32 devices in a mesh: dp: 16 (over z, y, x), tensor: 2 (over core).
Axes of the slice: x: 2, y: 2, z: 4, core: 2. Of those that a mesh axis runs over, the one named last changes fastest.
Arguments:
- layer_input: bfloat16 [16, 1024, 768], P('dp', 'tensor'), may hold values from -6 to 6
- seq_lengths: int32 [16], P('dp'), may hold values from 576 to 1024, as said below
- expert_routes: int32 [16, 1024, 2], P('dp'), may hold values from 0 to 7, all different within a row; in each aligned block of 1024 rows (0 to 1023, 1024 to 2047, ..., all dimensions but the last counted through in order) at most 512 rows name the same one
- w_query: float32 [768, 768], P('dp', 'tensor'), may hold values from -0.21875 to 0.21875
- w_key: float32 [768, 768], P('dp', 'tensor'), may hold values from -0.21875 to 0.21875
- w_value: float32 [768, 768], P('dp', 'tensor'), may hold values from -0.21875 to 0.21875
- w_output: float32 [768, 768], P('dp', 'tensor'), may hold values from -3.5 to 3.5
- gain_attn: float32 [768], P('dp'), may hold values from 0.1 to 1.9
- gain_ffn: float32 [768], P('dp'), may hold values from 0.1 to 1.9
- router_weight: float32 [768, 8], P('dp'), may hold values from -0.15625 to 0.15625
- expert_gate: float32 [768, 8, 2048], P('dp', None, 'tensor'), may hold values from -0.21875 to 0.21875
- expert_up: float32 [768, 8, 2048], P('dp', None, 'tensor'), may hold values from -0.21875 to 0.21875
- expert_down: float32 [768, 8, 2048], P('dp', None, 'tensor'), may hold values from -0.125 to 0.125
- shared_gate: float32 [768, 2048], P('dp', 'tensor'), may hold values from -0.21875 to 0.21875
- shared_up: float32 [768, 2048], P('dp', 'tensor'), may hold values from -0.21875 to 0.21875
- shared_down: float32 [768, 2048], P('dp', 'tensor'), may hold values from -0.125 to 0.125
- out_cotangent: bfloat16 [16, 1024, 768], P('dp', 'tensor'), may hold values from -6 to 6
Outputs:
- layer_output: bfloat16 [16, 1024, 768], P('dp', 'tensor')
- grad_input: bfloat16 [16, 1024, 768], P('dp', 'tensor')
- grad_query: float32 [768, 768], P('dp', 'tensor')
- grad_key: float32 [768, 768], P('dp', 'tensor')
- grad_value: float32 [768, 768], P('dp', 'tensor')
- grad_output_proj: float32 [768, 768], P('dp', 'tensor')
- grad_gain_attn: float32 [768], P('dp')
- grad_gain_ffn: float32 [768], P('dp')
- grad_router: float32 [768, 8], P('dp')
- grad_expert_gate: float32 [768, 8, 2048], P('dp', None, 'tensor')
- grad_expert_up: float32 [768, 8, 2048], P('dp', None, 'tensor')
- grad_expert_down: float32 [768, 8, 2048], P('dp', None, 'tensor')
- grad_shared_gate: float32 [768, 2048], P('dp', 'tensor')
- grad_shared_up: float32 [768, 2048], P('dp', 'tensor')
- grad_shared_down: float32 [768, 2048], P('dp', 'tensor')
The draws below stay inside these ranges and needn't reach their ends.
Inputs may be any that keep to these rules, and one draw needn't show every extreme that they name: `seq_lengths`: every sequence has more than half of its 1024 slots valid, and in every draw some sequence fills all 1024. `expert_routes`: A token's two experts differ. Among the 1024 tokens of one dp group no expert is named more than 512 times, and in some group an expert is named exactly 512 times.
All inputs are finite; a program needn't handle non-finite values.
Results may differ from the reference program's by a relative error of at most 0.017.
The reference program's roundings to bfloat16 on the way count: a program that leaves them out, or rounds other values in their place, can miss the bound.
Values may be sent and summed in bfloat16 or wider, within the bound.
A program may use at most 320 MiB of HBM per device.

```python
import math
import jax
import jax.numpy as jnp
import numpy as np
from jax import lax

D = 768
HEADS = 12
HD = 64
FF = 2048
E = 8
SLOT = 1024
SEQS = 1
NSEQ = 16
TOK_DEV = 1024
CAP = 512
MINLEN = 576
N_DP = 16


def draw_seq_lengths(key, part):
    key = jax.random.fold_in(key, 7)
    first_key, second_key = jax.random.split(key)
    drawn_lengths = jax.random.randint(first_key, (NSEQ,), MINLEN, SLOT + 1)
    chosen_one = jax.random.randint(second_key, (), 0, NSEQ)
    filled = jnp.where(jnp.arange(NSEQ) == chosen_one, SLOT, drawn_lengths)
    return filled.astype(jnp.int32)


def shard_levels(own_key, dims, shards, low, top_value):
    factor_of, own = 1.0, jax.random.fold_in(own_key, 6)
    for dim, blocks in shards:
        steps = jnp.exp(jax.random.uniform(jax.random.fold_in(own, dim), (blocks,), jnp.float32, low / len(shards), top_value / len(shards)))
        factor_of = factor_of * jnp.repeat(steps, dims[dim] // blocks).reshape([-1 if axis == dim else 1 for axis in range(len(dims))])
    return factor_of


def deal_out(key, own, number, rows, amount, top, most, slope):
    order = jax.random.permutation(key, amount)
    crowded, ordinary = portions_of(amount, rows * top, most, slope, True), portions_of(amount, rows * top, most, slope, False)
    places = jnp.arange(amount)

    def named(tallies, offset_by):
        used = int((tallies > 0).sum())
        fixed = max(1, used // 4)
        moved = fixed + (places - fixed + offset_by * (used - fixed)) % max(1, amount - fixed)
        return jnp.zeros((amount,), jnp.int32).at[order[jnp.where(places < fixed, places, moved)]].set(jnp.asarray(tallies, jnp.int32))

    tallies = jnp.where(number % 4 == 0, named(crowded, number // 4), named(ordinary, number - number // 4 - 1))
    mixed = jax.random.permutation(jax.random.fold_in(own, 3), amount)
    source_of, taker = mixed[0:amount // 2 * 2:2], mixed[1:amount // 2 * 2:2]
    margin = jnp.minimum(tallies[source_of] - 1, most - tallies[taker]) // 2
    margin = jnp.where((source_of == order[0]) | (taker == order[0]) | (tallies[taker] == 0), 0, jnp.maximum(margin, 0))
    moved = jax.random.randint(jax.random.fold_in(own, 4), (amount // 2,), 0, 1 << 20) % (margin + 1)
    tallies = tallies.at[source_of].add(-moved).at[taker].add(moved)
    items = jnp.searchsorted(jnp.cumsum(tallies), jnp.arange(rows * top), side="right").astype(jnp.int32)
    listing = items.reshape(top, rows).T
    listing = listing[jax.random.permutation(jax.random.fold_in(own, 1), rows)]
    offset_by = jax.random.randint(jax.random.fold_in(own, 2), (rows, 1), 0, top)
    return jnp.take_along_axis(listing, (jnp.arange(top)[None, :] + offset_by) % top, axis=1)


def portions_of(count, total, bound, lean, full):
    portions = [(1 << 20) // math.isqrt(rank ** lean) + 1 for rank in range(1, count + 1)]
    largest = bound if full else min(bound, max(-(-total // count), total * portions[0] // sum(portions)))
    least = 1 if total - largest >= count - 1 else 0
    counts, rest = [largest] + [least] * (count - 1), total - largest - least * (count - 1)
    while rest > 0:
        movable = [i for i in range(1, count) if counts[i] < largest] or [i for i in range(1, count) if counts[i] < bound]
        mass, remaining = sum([portions[i] for i in movable]), rest
        for i in movable:
            more = min(bound - counts[i], max(1, remaining * portions[i] // mass), rest)
            counts[i] = counts[i] + more
            rest = rest - more
    return np.array(counts)


def gaussian(stream_key, dims, spread, bound, pieces=(), kind=jnp.bfloat16):
    gain = shard_levels(stream_key, dims, pieces, -0.22, 0.18) if pieces else 1.0
    values = jax.random.normal(stream_key, dims, jnp.float32) * spread * gain
    return jnp.minimum(jnp.maximum(values, -bound), bound).astype(kind)


def setup_inputs(seed: int = 0) -> dict:
    arg_keys = jax.random.split(jax.random.key(seed), 18)
    layer_input = gaussian(arg_keys[0], (NSEQ, SLOT, D), 1.0, 6.0, ((0, 16), (1, 2)))
    seq_lengths = draw_seq_lengths(jax.random.fold_in(arg_keys[17], 71), 0)
    expert_routes_keys = jax.random.split(jax.random.fold_in(arg_keys[2], 1), NSEQ * SLOT // TOK_DEV)
    expert_routes_turns = jax.random.permutation(jax.random.fold_in(arg_keys[2], 3), NSEQ * SLOT // TOK_DEV)
    expert_routes = jax.vmap(lambda own, number: deal_out(jax.random.fold_in(arg_keys[2], 2), own, number, TOK_DEV, E, 2, CAP, 1))(expert_routes_keys, expert_routes_turns).reshape((NSEQ, SLOT, 2))
    w_query = gaussian(arg_keys[3], (D, D), D ** -0.5, 0.21875, ((0, 16), (1, 2)), jnp.float32)
    w_key = gaussian(arg_keys[4], (D, D), D ** -0.5, 0.21875, ((0, 16), (1, 2)), jnp.float32)
    w_value = gaussian(arg_keys[5], (D, D), D ** -0.5, 0.21875, ((0, 16), (1, 2)), jnp.float32)
    w_output = gaussian(arg_keys[6], (D, D), 3 ** -0.5, 3.5, ((0, 16), (1, 2)), jnp.float32)
    gain_attn = jnp.clip(1.0 + 0.18 * jax.random.normal(arg_keys[7], (D,), jnp.float32), 0.1, 1.9)
    gain_ffn = jnp.clip(1.0 + 0.18 * jax.random.normal(arg_keys[8], (D,), jnp.float32), 0.1, 1.9)
    router_weight = gaussian(arg_keys[9], (D, E), (2 * D) ** -0.5, 0.15625, ((0, 16),), jnp.float32)
    expert_gate = gaussian(arg_keys[10], (D, E, FF), D ** -0.5, 0.21875, ((0, 16), (2, 2)), jnp.float32)
    expert_up = gaussian(arg_keys[11], (D, E, FF), D ** -0.5, 0.21875, ((0, 16), (2, 2)), jnp.float32)
    expert_down = gaussian(arg_keys[12], (D, E, FF), FF ** -0.5, 0.125, ((0, 16), (2, 2)), jnp.float32)
    shared_gate = gaussian(arg_keys[13], (D, FF), D ** -0.5, 0.21875, ((0, 16), (1, 2)), jnp.float32)
    shared_up = gaussian(arg_keys[14], (D, FF), D ** -0.5, 0.21875, ((0, 16), (1, 2)), jnp.float32)
    shared_down = gaussian(arg_keys[15], (D, FF), FF ** -0.5, 0.125, ((0, 16), (1, 2)), jnp.float32)
    out_cotangent = gaussian(arg_keys[16], (NSEQ, SLOT, D), 1.0, 6.0, ((0, 16), (1, 2)))
    return dict(layer_input=layer_input, seq_lengths=seq_lengths, expert_routes=expert_routes, w_query=w_query, w_key=w_key, w_value=w_value, w_output=w_output, gain_attn=gain_attn, gain_ffn=gain_ffn, router_weight=router_weight, expert_gate=expert_gate, expert_up=expert_up, expert_down=expert_down, shared_gate=shared_gate, shared_up=shared_up, shared_down=shared_down, out_cotangent=out_cotangent)


@jax.custom_vjp
def low(v):
    return lax.optimization_barrier(v.astype(jnp.bfloat16)).astype(jnp.float32)

@jax.custom_vjp
def low_back(v):
    return v

def low_keep(v):
    return (low(v), None)

def low_pass(kept, grad):
    return (grad,)

def back_keep(v):
    return (v, None)

def back_low(kept, grad):
    return (low(grad),)
low.defvjp(low_keep, low_pass)
low_back.defvjp(back_keep, back_low)
epsilon = 1e-06
highest = lax.Precision.HIGHEST

def matmul_high(left, right):
    return jnp.dot(left, right, precision=highest)

def rms_norm(values, gain_row):
    factor = lax.rsqrt(lax.optimization_barrier(jnp.mean(values * values, axis=-1, keepdims=True)) + epsilon)
    return values * factor * gain_row

def rope_tables(length, half_size):
    places = jnp.arange(length, dtype=jnp.float32)[:, None]
    inverse = jnp.exp(jnp.arange(half_size, dtype=jnp.float32) * (-math.log(10000.0) / half_size))
    angles = places * inverse[None, :]
    return (jnp.cos(angles), jnp.sin(angles))

def rotate(values, cosine, sine_table):
    half_size = values.shape[-1] // 2
    first_half = values[..., :half_size]
    second = values[..., half_size:]
    cos_b = cosine[:, None, :]
    sin_b = sine_table[:, None, :]
    return jnp.concatenate([first_half * cos_b - second * sin_b, second * cos_b + first_half * sin_b], axis=-1)

def attend(query_rot, key_rot, value_rows, length):
    score_scale = 1.0 / math.sqrt(HD)
    scores = low_back(jnp.einsum('qhd,khd->hqk', query_rot, key_rot, precision=highest) * score_scale)
    row_pos = jnp.arange(SLOT)[:, None]
    column = jnp.arange(SLOT)[None, :]
    allowed = (column <= row_pos) & (column < length)
    masked = jnp.where(allowed[None], scores, -1e+30)
    weights = low(jax.nn.softmax(masked, axis=-1))
    return jnp.einsum('hqk,khd->qhd', weights, value_rows, precision=highest)

def group_layer(weights, group_input, group_lengths, group_routes):
    query_w, key_w, value_w, out_w, gain_one, gain_two, router_w, gate_w, up_w, down_w, sgate_w, sup_w, sdown_w = weights
    row_count = SEQS * SLOT
    cosine, sine_table = rope_tables(SLOT, HD // 2)
    normed_one = low(rms_norm(group_input, gain_one))
    attn_flat = normed_one.reshape(row_count, D)
    query_pre = low_back(matmul_high(attn_flat, query_w)).reshape(SEQS, SLOT, HEADS, HD)
    key_pre = low_back(matmul_high(attn_flat, key_w)).reshape(SEQS, SLOT, HEADS, HD)
    query_rot = low(rotate(query_pre, cosine, sine_table))
    key_rot = low(rotate(key_pre, cosine, sine_table))
    value_rows = low(low_back(matmul_high(attn_flat, value_w))).reshape(SEQS, SLOT, HEADS, HD)
    contexts = lax.map(jax.checkpoint(lambda seq_item: attend(*seq_item)), (query_rot, key_rot, value_rows, group_lengths))
    context_flat = low(low_back(contexts.reshape(row_count, D)))
    attn_out = low_back(matmul_high(context_flat, out_w.T))
    hidden_residual = group_input.reshape(row_count, D) + attn_out
    normed_two = low(rms_norm(hidden_residual, gain_two))
    logits = matmul_high(normed_two, router_w)
    route_rows = group_routes.astype(jnp.int32)
    chosen = (route_rows[..., None] == jnp.arange(E, dtype=jnp.int32)[None, None, :]).astype(jnp.float32)
    picked = lax.optimization_barrier(jnp.sum(chosen * logits[:, None, :], axis=-1))
    gate_mix = jax.nn.softmax(picked, axis=-1)
    flat_route = route_rows.reshape(2 * row_count)
    route_hot = (flat_route[:, None] == jnp.arange(E, dtype=jnp.int32)[None, :]).astype(jnp.int32)
    before = (jnp.cumsum(route_hot, axis=0) - route_hot).astype(jnp.int32)
    position = lax.optimization_barrier(jnp.sum(before * route_hot, axis=-1)).astype(jnp.int32)
    slot_index = (flat_route * CAP + position).astype(jnp.int32)
    slot_owner = jnp.full((E * CAP,), row_count, jnp.int32).at[slot_index].set(jnp.arange(2 * row_count, dtype=jnp.int32) // 2)
    padded_rows = jnp.concatenate([normed_two, jnp.zeros((1, D), jnp.float32)], axis=0)
    buffer = padded_rows[slot_owner].reshape(E, CAP, D)
    gate_pre = low_back(jnp.einsum('ecd,def->ecf', buffer, gate_w, precision=highest))
    up_pre = low_back(jnp.einsum('ecd,def->ecf', buffer, up_w, precision=highest))
    inner_act = low(jax.nn.silu(gate_pre) * up_pre)
    expert_out = low_back(jnp.einsum('ecf,def->ecd', inner_act, down_w, precision=highest))
    picked_out = expert_out.reshape(E * CAP, D)[slot_index].reshape(row_count, 2, D)
    routed = lax.optimization_barrier(jnp.sum(gate_mix[..., None] * picked_out, axis=1))
    shared_gate_pre = low_back(matmul_high(normed_two, sgate_w))
    shared_up_pre = low_back(matmul_high(normed_two, sup_w))
    shared_act = low(jax.nn.silu(shared_gate_pre) * shared_up_pre)
    shared_out = matmul_high(shared_act, sdown_w.T)
    ffn_out = low_back(shared_out + routed)
    return (hidden_residual + ffn_out).reshape(SEQS, SLOT, D)

def reference(layer_input, seq_lengths, expert_routes, w_query, w_key, w_value, w_output, gain_attn, gain_ffn, router_weight, expert_gate, expert_up, expert_down, shared_gate, shared_up, shared_down, out_cotangent):
    masters = (w_query, w_key, w_value, w_output, gain_attn, gain_ffn, router_weight, expert_gate, expert_up, expert_down, shared_gate, shared_up, shared_down)
    input_rows = layer_input.astype(jnp.float32).reshape(N_DP, SEQS, SLOT, D)
    group_lengths = seq_lengths.astype(jnp.int32).reshape(N_DP, SEQS)
    group_routes = expert_routes.astype(jnp.int32).reshape(N_DP, SEQS * SLOT, 2)

    def forward(params, group_inputs):
        weights = tuple((low(master) for master in params))
        step_fn = jax.checkpoint(lambda seq_item: group_layer(weights, seq_item[0], seq_item[1], seq_item[2]))
        return lax.map(step_fn, (group_inputs, group_lengths, group_routes))
    output, pullback = jax.vjp(forward, masters, input_rows)
    valid_rows = (jnp.arange(SLOT, dtype=jnp.int32)[None, :] < seq_lengths.astype(jnp.int32)[:, None]).astype(jnp.float32)
    cotangent = out_cotangent.astype(jnp.float32) * valid_rows[..., None]
    grads, grad_in = pullback(cotangent.reshape(N_DP, SEQS, SLOT, D))
    return (output.reshape(NSEQ, SLOT, D).astype(jnp.bfloat16), grad_in.reshape(NSEQ, SLOT, D).astype(jnp.bfloat16), grads[0], grads[1], grads[2], grads[3], grads[4], grads[5], grads[6], grads[7], grads[8], grads[9], grads[10], grads[11], grads[12])
```

```python
import functools
import math

import jax
import jax.numpy as jnp
from jax import lax
from jax.experimental import pallas as pl
from jax.experimental.pallas import tpu as pltpu
from jax.sharding import PartitionSpec as P

HD = 64
LANES = 128
EPS = 1e-06
F32 = jnp.float32
BF16 = jnp.bfloat16
HIGHEST = lax.Precision.HIGHEST
VMEM_LIMIT = 56 * 1024 * 1024

NN = (((1,), (0,)), ((), ()))
NT = (((1,), (1,)), ((), ()))
TN = (((0,), (0,)), ((), ()))


def mm(left, right, dims):
    return lax.dot_general(left, right, dims, preferred_element_type=F32)


def params(count):
    return pltpu.CompilerParams(
        dimension_semantics=("arbitrary",) * count, vmem_limit_bytes=VMEM_LIMIT
    )


def cost(flops, nbytes, trans=0):
    return pl.CostEstimate(flops=int(flops), bytes_accessed=int(nbytes), transcendentals=int(trans))


def partner(values):
    lane = lax.broadcasted_iota(jnp.int32, values.shape, 1)
    return jnp.where(
        lane % HD < HD // 2,
        pltpu.roll(values, LANES - HD // 2, 1),
        pltpu.roll(values, HD // 2, 1),
    )


def head_lanes(shape, head):
    lane = lax.broadcasted_iota(jnp.int32, shape, 1)
    return (lane // HD) == head


def attn_fwd_kernel(len_ref, a_ref, w_ref, cos_ref, sin_ref, qkv_ref, ctx_ref, *, block):
    span = a_ref.shape[0]
    length = len_ref[0]
    raw = mm(a_ref[...], w_ref[...], NN)
    cosine, sine = cos_ref[...], sin_ref[...]
    query, key = raw[:, :LANES], raw[:, LANES : 2 * LANES]
    qkv_ref[:, :LANES] = (query * cosine + partner(query) * sine).astype(BF16)
    qkv_ref[:, LANES : 2 * LANES] = (key * cosine + partner(key) * sine).astype(BF16)
    qkv_ref[:, 2 * LANES :] = raw[:, 2 * LANES :].astype(BF16)
    for index in range(span // block):
        keys = (index + 1) * block
        query_rows = qkv_ref[index * block : keys, :LANES] * jnp.asarray(HD**-0.5, BF16)
        key_rows = qkv_ref[:keys, LANES : 2 * LANES]
        value_rows = qkv_ref[:keys, 2 * LANES :]
        row = index * block + lax.broadcasted_iota(jnp.int32, (block, keys), 0)
        column = lax.broadcasted_iota(jnp.int32, (block, keys), 1)
        allowed = (column <= row) & (column < length)
        parts = []
        for head in range(LANES // HD):
            masked_query = jnp.where(
                head_lanes(query_rows.shape, head), query_rows, jnp.zeros_like(query_rows)
            )
            scores = jnp.where(allowed, mm(masked_query, key_rows, NT), -1e30)
            peak = jnp.max(scores, axis=1, keepdims=True)
            powers = jnp.exp(scores - peak)
            total = jnp.sum(powers, axis=1, keepdims=True)
            prob = (powers * (1.0 / total)).astype(BF16)
            parts.append(mm(prob, value_rows, NN))
        context = jnp.where(head_lanes(parts[0].shape, 0), parts[0], parts[1])
        ctx_ref[index * block : keys, :] = context.astype(BF16)


def attn_forward(length, attn_in, qkv_w, cosine, sine):
    span, width = attn_in.shape
    pairs = qkv_w.shape[1] // (3 * LANES)
    return pl.pallas_call(
        functools.partial(attn_fwd_kernel, block=256),
        grid=(pairs,),
        in_specs=[
            pl.BlockSpec(memory_space=pltpu.SMEM),
            pl.BlockSpec((span, width), lambda i: (0, 0)),
            pl.BlockSpec((width, 3 * LANES), lambda i: (0, i)),
            pl.BlockSpec((span, LANES), lambda i: (0, 0)),
            pl.BlockSpec((span, LANES), lambda i: (0, 0)),
        ],
        out_specs=[
            pl.BlockSpec((span, 3 * LANES), lambda i: (0, i)),
            pl.BlockSpec((span, LANES), lambda i: (0, i)),
        ],
        out_shape=[
            jax.ShapeDtypeStruct((span, pairs * 3 * LANES), BF16),
            jax.ShapeDtypeStruct((span, pairs * LANES), BF16),
        ],
        compiler_params=params(1),
        cost_estimate=cost(2 * span * width * pairs * 384 + 12 * span * span * 128, 12e6, 6e6),
        name="attn_fwd",
    )(length, attn_in, qkv_w, cosine, sine)


def attn_bwd_kernel(
    len_ref, a_ref, da_in_ref, w_ref, wo_ref, qkv_ref, ctx_ref, cos_ref, sin_ref,
    gw_ref, da_ref, dctx_s, dq_s, dk_s, dv_s, *, block,
):
    span = a_ref.shape[0]
    length = len_ref[0]
    grad_rows = da_in_ref[...]
    dctx_s[...] = mm(grad_rows, wo_ref[...], NN).astype(BF16)
    gw_ref[:, 3 * LANES :] = mm(grad_rows, ctx_ref[...], TN).astype(BF16)
    dk_s[...] = jnp.zeros_like(dk_s)
    dv_s[...] = jnp.zeros_like(dv_s)
    scale = jnp.asarray(HD**-0.5, BF16)
    for index in range(span // block):
        keys = (index + 1) * block
        start = index * block
        query_rows = qkv_ref[start:keys, :LANES] * scale
        key_rows = qkv_ref[:keys, LANES : 2 * LANES]
        value_rows = qkv_ref[:keys, 2 * LANES :]
        context_grad = dctx_s[start:keys, :]
        row = lax.broadcasted_iota(jnp.int32, (keys, block), 0)
        column = start + lax.broadcasted_iota(jnp.int32, (keys, block), 1)
        allowed = (row <= column) & (row < length)
        dq_total = None
        for head in range(LANES // HD):
            lanes = head_lanes((block, LANES), head)
            masked_query = jnp.where(lanes, query_rows, jnp.zeros_like(query_rows))
            masked_grad = jnp.where(lanes, context_grad, jnp.zeros_like(context_grad))
            scores = jnp.where(allowed, mm(key_rows, masked_query, NT), -1e30)
            peak = jnp.max(scores, axis=0, keepdims=True)
            powers = jnp.exp(scores - peak)
            total = jnp.sum(powers, axis=0, keepdims=True)
            prob = powers * (1.0 / total)
            prob_grad = mm(value_rows, masked_grad, NT)
            inner = jnp.sum(prob * prob_grad, axis=0, keepdims=True)
            score_grad = (prob * (prob_grad - inner)).astype(BF16)
            dk_s[:keys, :] += mm(score_grad, masked_query, NN)
            dv_s[:keys, :] += mm(prob.astype(BF16), masked_grad, NN)
            dq_part = mm(score_grad, key_rows, TN)
            dq_total = dq_part if head == 0 else jnp.where(lanes, dq_part, dq_total)
        dq_s[start:keys, :] = dq_total * (HD**-0.5)
    cosine, sine = cos_ref[...], sin_ref[...]
    dq, dk = dq_s[...], dk_s[...]
    dq = (dq * cosine - partner(dq) * sine).astype(BF16)
    dk = (dk * cosine - partner(dk) * sine).astype(BF16)
    grads = jnp.concatenate([dq, dk, dv_s[...].astype(BF16)], axis=1)
    gw_ref[:, : 3 * LANES] = mm(a_ref[...], grads, TN).astype(BF16)
    part = mm(grads, w_ref[...], NT)

    @pl.when(pl.program_id(0) == 0)
    def _():
        da_ref[...] = part

    @pl.when(pl.program_id(0) > 0)
    def _():
        da_ref[...] += part


def attn_backward(length, attn_in, grad_attn, qkv_w, out_w, qkv_rot, context, cosine, sine):
    span, width = attn_in.shape
    pairs = qkv_w.shape[1] // (3 * LANES)
    return pl.pallas_call(
        functools.partial(attn_bwd_kernel, block=256),
        grid=(pairs,),
        in_specs=[
            pl.BlockSpec(memory_space=pltpu.SMEM),
            pl.BlockSpec((span, width), lambda i: (0, 0)),
            pl.BlockSpec((span, width), lambda i: (0, 0)),
            pl.BlockSpec((width, 3 * LANES), lambda i: (0, i)),
            pl.BlockSpec((width, LANES), lambda i: (0, i)),
            pl.BlockSpec((span, 3 * LANES), lambda i: (0, i)),
            pl.BlockSpec((span, LANES), lambda i: (0, i)),
            pl.BlockSpec((span, LANES), lambda i: (0, 0)),
            pl.BlockSpec((span, LANES), lambda i: (0, 0)),
        ],
        out_specs=[
            pl.BlockSpec((width, 4 * LANES), lambda i: (0, i)),
            pl.BlockSpec((span, width), lambda i: (0, 0)),
        ],
        out_shape=[
            jax.ShapeDtypeStruct((width, pairs * 4 * LANES), BF16),
            jax.ShapeDtypeStruct((span, width), F32),
        ],
        scratch_shapes=[
            pltpu.VMEM((span, LANES), BF16),
            pltpu.VMEM((span, LANES), F32),
            pltpu.VMEM((span, LANES), F32),
            pltpu.VMEM((span, LANES), F32),
        ],
        compiler_params=params(1),
        cost_estimate=cost(20e9, 16e6, 6e6),
        name="attn_bwd",
    )(length, attn_in, grad_attn, qkv_w, out_w, qkv_rot, context, cosine, sine)


def ffn_kernel(
    x_ref, d_ref, g_ref, wg_ref, wu_ref, wd_ref,
    y_ref, dx_ref, dg_ref, og_ref, ou_ref, od_ref, ag, au, ad,
):
    step = pl.program_id(0)
    rows = x_ref.shape[0]
    diagonal = lax.broadcasted_iota(jnp.int32, (rows, rows), 0) == lax.broadcasted_iota(
        jnp.int32, (rows, rows), 1
    )
    gate = jnp.sum(jnp.where(diagonal, g_ref[...], 0.0), axis=1, keepdims=True)
    x = x_ref[...]
    grad = d_ref[...].astype(F32)
    gate_pre = mm(x, wg_ref[...], NN)
    up_pre = mm(x, wu_ref[...], NN)
    sig = jax.nn.sigmoid(gate_pre)
    act = gate_pre * sig
    inner = (act * up_pre).astype(BF16)
    out = mm(inner, wd_ref[...], NT)
    gate_grad = jnp.sum(out * grad, axis=1, keepdims=True)
    dg_ref[...] = jnp.sum(jnp.where(diagonal, gate_grad, 0.0), axis=0, keepdims=True)
    y_ref[...] = (out * gate).astype(BF16)
    out_grad = (grad * gate).astype(BF16)
    inner_grad = mm(out_grad, wd_ref[...], NN)
    gate_pre_grad = (inner_grad * up_pre * (sig + act * (1.0 - sig))).astype(BF16)
    up_pre_grad = (inner_grad * act).astype(BF16)
    dx_ref[...] = (
        mm(gate_pre_grad, wg_ref[...], NT) + mm(up_pre_grad, wu_ref[...], NT)
    ).astype(BF16)

    @pl.when(step == 0)
    def _():
        ag[...] = jnp.zeros_like(ag)
        au[...] = jnp.zeros_like(au)
        ad[...] = jnp.zeros_like(ad)

    ag[...] += mm(x, gate_pre_grad, TN)
    au[...] += mm(x, up_pre_grad, TN)
    ad[...] += mm(out_grad, inner, TN)

    @pl.when(step == pl.num_programs(0) - 1)
    def _():
        og_ref[...] = ag[...].astype(BF16)
        ou_ref[...] = au[...].astype(BF16)
        od_ref[...] = ad[...].astype(BF16)


def ffn(rows_in, grad_in, gates, gate_w, up_w, down_w, name):
    count, width = rows_in.shape
    hidden = gate_w.shape[1]
    blocks, _, block = gates.shape
    token = pl.BlockSpec((block, width), lambda i: (i, 0))
    weight = pl.BlockSpec((width, hidden), lambda i: (0, 0), pipeline_mode=pl.Buffered(1))
    row = pl.BlockSpec((None, 1, block), lambda i: (i, 0, 0))
    return pl.pallas_call(
        ffn_kernel,
        grid=(blocks,),
        in_specs=[token, token, row, weight, weight, weight],
        out_specs=[token, token, row, weight, weight, weight],
        out_shape=[
            jax.ShapeDtypeStruct((count, width), BF16),
            jax.ShapeDtypeStruct((count, width), BF16),
            jax.ShapeDtypeStruct((blocks, 1, block), F32),
        ]
        + [jax.ShapeDtypeStruct((width, hidden), BF16)] * 3,
        scratch_shapes=[pltpu.VMEM((width, hidden), F32)] * 3,
        compiler_params=params(1),
        cost_estimate=cost(18 * count * width * hidden, 8 * count * width + 12 * width * hidden, count * hidden),
        name=name,
    )(rows_in, grad_in, gates, gate_w, up_w, down_w)


def dispatch_kernel(pos_ref, b_ref, x_ref):
    slots = x_ref.shape[0]
    tokens = b_ref.shape[0]
    slot = lax.broadcasted_iota(jnp.int32, (slots, tokens), 0)
    hot = jnp.where(slot == pos_ref[...], 1.0, 0.0).astype(BF16)
    x_ref[...] = mm(hot, b_ref[...], NN).astype(BF16)


def dispatch(places, rows, slots, name):
    experts, _, tokens = places.shape
    width = rows.shape[1]
    return pl.pallas_call(
        dispatch_kernel,
        grid=(experts,),
        in_specs=[
            pl.BlockSpec((None, 1, tokens), lambda i: (i, 0, 0)),
            pl.BlockSpec((tokens, width), lambda i: (0, 0)),
        ],
        out_specs=pl.BlockSpec((None, slots, width), lambda i: (i, 0, 0)),
        out_shape=jax.ShapeDtypeStruct((experts, slots, width), BF16),
        compiler_params=params(1),
        cost_estimate=cost(2 * experts * slots * tokens * width, 6e6),
        name=name,
    )(places, rows)


def gate_slots_kernel(pos_ref, gate_ref, out_ref):
    slots = out_ref.shape[1]
    tokens = pos_ref.shape[1]
    slot = lax.broadcasted_iota(jnp.int32, (slots, tokens), 0)
    column = jnp.sum(jnp.where(slot == pos_ref[...], gate_ref[...], 0.0), axis=1, keepdims=True)
    diagonal = lax.broadcasted_iota(jnp.int32, (slots, slots), 0) == lax.broadcasted_iota(
        jnp.int32, (slots, slots), 1
    )
    out_ref[...] = jnp.sum(jnp.where(diagonal, column, 0.0), axis=0, keepdims=True)


def gate_slots(places, gates, slots):
    experts, _, tokens = places.shape
    row = pl.BlockSpec((None, 1, tokens), lambda i: (i, 0, 0))
    return pl.pallas_call(
        gate_slots_kernel,
        grid=(experts,),
        in_specs=[row, row],
        out_specs=pl.BlockSpec((None, 1, slots), lambda i: (i, 0, 0)),
        out_shape=jax.ShapeDtypeStruct((experts, 1, slots), F32),
        compiler_params=params(1),
        cost_estimate=cost(4 * experts * slots * tokens, 1e5),
        name="gate_slots",
    )(places, gates)


def combine_hot(pos_ref, offset, experts, slots):
    tokens = pos_ref.shape[0]
    slot = lax.broadcasted_iota(jnp.int32, (tokens, slots), 1) + offset
    return jnp.concatenate(
        [
            jnp.where(slot == pos_ref[:, e : e + 1], 1.0, 0.0).astype(BF16)
            for e in range(experts)
        ],
        axis=1,
    )


def combine_kernel(core_ref, pos_ref, y_ref, base_ref, out_ref):
    experts, slots, width = y_ref.shape
    hot = combine_hot(pos_ref, core_ref[0] * slots, experts, slots)
    part = mm(hot, y_ref[...].reshape(experts * slots, width), NN)
    out_ref[...] = (part + base_ref[...].astype(F32)).astype(BF16)


def combine_grad_kernel(
    core_ref, pos_ref, y_ref, base_ref, gate_ref, dgate_ref, router_ref, out_ref, dl_ref
):
    experts, slots, width = y_ref.shape
    tokens = pos_ref.shape[0]
    hot = combine_hot(pos_ref, core_ref[0] * slots, experts, slots)
    part = mm(hot, y_ref[...].reshape(experts * slots, width), NN)
    slot = lax.broadcasted_iota(jnp.int32, (tokens, 2 * slots), 1)
    lane = lax.broadcasted_iota(jnp.int32, (tokens, experts), 1)
    gate_grad = jnp.zeros((tokens, experts), F32)
    for e in range(experts):
        found = jnp.sum(
            jnp.where(slot == pos_ref[:, e : e + 1], dgate_ref[e], 0.0), axis=1, keepdims=True
        )
        gate_grad = jnp.where(lane == e, found, gate_grad)
    gate = gate_ref[...]
    mean = jnp.sum(gate * gate_grad, axis=1, keepdims=True)
    logit_grad = gate * (gate_grad - mean)
    dl_ref[...] = logit_grad
    part += lax.dot_general(
        logit_grad, router_ref[...], NN, precision=HIGHEST, preferred_element_type=F32
    )
    out_ref[...] = (part + base_ref[...].astype(F32)).astype(BF16)


def combine(core, places, slots_in, base, extra=None, block=256):
    tokens, experts = places.shape
    _, slots, width = slots_in.shape
    token = pl.BlockSpec((block, width), lambda i: (i, 0))
    small = pl.BlockSpec((block, experts), lambda i: (i, 0))
    in_specs = [
        pl.BlockSpec(memory_space=pltpu.SMEM),
        small,
        pl.BlockSpec((experts, slots, width), lambda i: (0, 0, 0)),
        token,
    ]
    out_specs, out_shape = token, jax.ShapeDtypeStruct((tokens, width), BF16)
    kernel, args = combine_kernel, [core, places, slots_in, base]
    if extra is not None:
        gates, gate_grads, router = extra
        kernel = combine_grad_kernel
        in_specs += [
            small,
            pl.BlockSpec(gate_grads.shape, lambda i: (0, 0, 0)),
            pl.BlockSpec(router.shape, lambda i: (0, 0)),
        ]
        args += [gates, gate_grads, router]
        out_specs = [token, small]
        out_shape = [out_shape, jax.ShapeDtypeStruct((tokens, experts), F32)]
    return pl.pallas_call(
        kernel,
        grid=(tokens // block,),
        in_specs=in_specs,
        out_specs=out_specs,
        out_shape=out_shape,
        compiler_params=params(1),
        cost_estimate=cost(2 * tokens * experts * slots * width, 8e6),
        name="combine" if extra is None else "combine_grad",
    )(*args)


def swap(values):
    return lax.ppermute(values, "tensor", [(0, 1), (1, 0)])


def both_halves(own):
    other = swap(own)
    first = lax.axis_index("tensor") == 0
    return jnp.concatenate([jnp.where(first, own, other), jnp.where(first, other, own)], axis=0)


def half_of(values, index):
    rows = values.shape[0] // 2
    return lax.dynamic_slice_in_dim(values, index * rows, rows, 0)


def sum_halves(part):
    core = lax.axis_index("tensor")
    other = swap(half_of(part, 1 - core))
    return half_of(part, core).astype(F32) + other.astype(F32)


def to_all(values, groups=None):
    count = lax.axis_size("dp") if groups is None else len(groups[0])
    copies = jnp.broadcast_to(values[None], (count,) + values.shape)
    return lax.all_to_all(copies, "dp", 0, 0, axis_index_groups=groups, tiled=True)


def after(values, *earlier):
    return lax.optimization_barrier((values,) + earlier)[0]


def rms_parts(values):
    factor = lax.rsqrt(jnp.mean(values * values, axis=-1, keepdims=True) + EPS)
    return values * factor, factor


def norm_back(grad, normed, factor, gain):
    hat = grad * gain
    back = factor * (hat - normed * jnp.mean(hat * normed, axis=-1, keepdims=True))
    return back, jnp.sum(grad * normed, axis=0)


def per_device(
    layer_input, seq_lengths, expert_routes, w_query, w_key, w_value, w_output,
    gain_attn, gain_ffn, router_weight, expert_gate, expert_up, expert_down,
    shared_gate, shared_up, shared_down, out_cotangent,
):
    ranks = lax.axis_size("dp")
    core = lax.axis_index("tensor")
    _, own_len, width = layer_input.shape
    span = 2 * own_len
    shard = w_query.shape[0]
    pairs = w_query.shape[1] // LANES
    experts, hidden = expert_gate.shape[1:]
    capacity = 4 * span // experts
    slots = capacity // 2
    groups = [list(range(s, s + experts)) for s in range(0, ranks, experts)]

    qkv_own = jnp.stack([w_query, w_key, w_value], axis=1).reshape(shard, 3, pairs, LANES)
    qkv_own = qkv_own.transpose(0, 2, 1, 3).reshape(shard, pairs * 3 * LANES)
    small_own = jnp.concatenate(
        [gain_attn[:, None], gain_ffn[:, None], router_weight], axis=1
    )
    small_own = jnp.pad(small_own, ((0, 0), (0, LANES - small_own.shape[1])))
    first_own = jnp.concatenate([qkv_own, small_own], axis=1).astype(BF16)
    first_all = to_all(first_own).reshape(width, pairs * 3 * LANES + LANES)
    qkv_w = first_all[:, : pairs * 3 * LANES]
    small = first_all[:, pairs * 3 * LANES :]
    gain_one = small[:, 0].astype(F32)
    gain_two = small[:, 1].astype(F32)
    router_w = small[:, 2 : 2 + experts]

    routes = expert_routes.reshape(span, 2)
    names = jnp.arange(experts, dtype=jnp.int32)
    chosen = (routes[:, 0:1] == names[None, :]) | (routes[:, 1:2] == names[None, :])
    counts = jnp.cumsum(chosen.astype(jnp.int32), axis=0)
    places = jnp.where(chosen, counts - 1, -1)
    own_places = jnp.where(chosen, counts - 1 - core * slots, -1).T[:, None, :]
    core_arg = core.reshape(1).astype(jnp.int32)

    length = seq_lengths[0]
    valid = (core * own_len + jnp.arange(own_len, dtype=jnp.int32)) < length
    cotangent = out_cotangent[0].astype(F32) * valid.astype(F32)[:, None]
    grad_ffn = both_halves(cotangent.astype(BF16))
    grad_slots = dispatch(own_places, grad_ffn, slots, "dispatch_grad")
    grad_slots = after(grad_slots, first_all)
    grad_slots = lax.all_to_all(grad_slots, "dp", 0, 0, axis_index_groups=groups, tiled=True)
    grad_rows = grad_slots.reshape(experts * slots, width)
    grad_rows = jnp.concatenate([grad_rows, swap(grad_rows)], axis=0)

    expert_own = jnp.stack([expert_gate, expert_up, expert_down], axis=0).astype(BF16)
    expert_own = expert_own.transpose(2, 0, 1, 3).reshape(1, experts, 3 * shard, hidden)
    expert_own = jnp.broadcast_to(
        expert_own, (ranks // experts, experts, 3 * shard, hidden)
    ).reshape(ranks, 3 * shard, hidden)
    expert_own = after(expert_own, first_all)
    expert_all = lax.all_to_all(expert_own, "dp", 0, 0, tiled=True)
    expert_all = expert_all.reshape(ranks, 3, shard, hidden).transpose(1, 0, 2, 3)
    expert_all = expert_all.reshape(3, width, hidden)

    shared_own = jnp.concatenate(
        [w_output, shared_gate, shared_up, shared_down], axis=1
    ).astype(BF16)
    near = [list(range(s, s + 4)) for s in range(0, ranks, 4)]
    far = [list(range(s, ranks, 4)) for s in range(4)]
    shared_own = after(shared_own, first_all)
    shared_all = to_all(to_all(shared_own, far), near)
    heads_width = w_output.shape[1]
    shared_all = shared_all.reshape(4, ranks // 4, shard, heads_width + 3 * hidden)
    shared_all = shared_all.transpose(1, 0, 2, 3).reshape(width, heads_width + 3 * hidden)
    out_w = shared_all[:, :heads_width]
    sgate_w, sup_w, sdown_w = (
        shared_all[:, heads_width + k * hidden : heads_width + (k + 1) * hidden] for k in range(3)
    )

    half = HD // 2
    inverse = jnp.exp(jnp.arange(half, dtype=F32) * (-math.log(10000.0) / half))
    angles = jnp.arange(span, dtype=F32)[:, None] * inverse[None, :]
    cos_half, sin_half = jnp.cos(angles), jnp.sin(angles)
    cosine = jnp.concatenate([cos_half] * 4, axis=1)
    sine = jnp.concatenate([-sin_half, sin_half] * 2, axis=1)
    input_rows = layer_input[0].astype(F32)
    unit_one, factor_one = rms_parts(input_rows)
    attn_in = both_halves((unit_one * gain_one).astype(BF16))
    qkv_rot, context = attn_forward(seq_lengths, attn_in, qkv_w, cosine, sine)
    attn_part = mm(context, out_w, NT)
    hidden_rows = input_rows + sum_halves(attn_part)
    unit_two, factor_two = rms_parts(hidden_rows)
    ffn_in = both_halves((unit_two * gain_two).astype(BF16))

    logits = mm(ffn_in, router_w, NN)
    top = jnp.max(jnp.where(chosen, logits, -jnp.inf), axis=1, keepdims=True)
    powers = jnp.where(chosen, jnp.exp(logits - top), 0.0)
    gates = powers / jnp.sum(powers, axis=1, keepdims=True)

    x_slots = dispatch(own_places, ffn_in, slots, "dispatch_rows")
    x_slots = lax.all_to_all(x_slots, "dp", 0, 0, axis_index_groups=groups, tiled=True)
    g_slots = gate_slots(own_places, gates.T[:, None, :], slots)
    g_slots = lax.all_to_all(g_slots, "dp", 0, 0, axis_index_groups=groups, tiled=True)
    x_rows = x_slots.reshape(experts * slots, width)
    x_rows = jnp.concatenate([x_rows, swap(x_rows)], axis=0)
    g_rows = g_slots.reshape(1, experts * slots)
    g_rows = jnp.concatenate([g_rows, swap(g_rows)], axis=0)
    block = 512
    g_rows = g_rows.reshape(2 * experts * slots // block, 1, block)

    ones = jnp.ones((span // block, 1, block), F32)
    shared_y, shared_dx, _, shared_gg, shared_gu, shared_gd = ffn(
        ffn_in, grad_ffn, ones, sgate_w, sup_w, sdown_w, "ffn_shared"
    )
    shared_grads = jnp.concatenate([shared_gg, shared_gu, shared_gd], axis=1)
    shared_grads = lax.all_to_all(
        shared_grads.reshape(ranks, shard, 3 * hidden), "dp", 0, 0, tiled=True
    )

    y_rows, dx_rows, gate_grads, expert_gg, expert_gu, expert_gd = ffn(
        x_rows, grad_rows, g_rows, expert_all[0], expert_all[1], expert_all[2], "ffn_expert"
    )
    half_rows = experts * slots

    def back_home(rows):
        total = rows[:half_rows].astype(F32) + swap(rows[half_rows:]).astype(F32)
        total = total.astype(BF16).reshape(experts, slots, width)
        return lax.all_to_all(total, "dp", 0, 0, axis_index_groups=groups, tiled=True)

    dx_home = back_home(dx_rows)
    gate_grads = gate_grads.reshape(2, experts, slots).transpose(1, 0, 2)
    gate_grads = lax.all_to_all(gate_grads, "dp", 0, 0, axis_index_groups=groups, tiled=True)
    first = core == 0
    gate_grads = jnp.concatenate(
        [
            jnp.where(first, gate_grads[:, 0], gate_grads[:, 1]),
            jnp.where(first, gate_grads[:, 1], gate_grads[:, 0]),
        ],
        axis=1,
    )[:, None, :]
    y_rows = after(y_rows, dx_home)
    y_home = back_home(y_rows)
    expert_grads = jnp.stack([expert_gg, expert_gu, expert_gd], axis=0)
    expert_grads = expert_grads.reshape(3, ranks, shard, hidden).transpose(1, 0, 2, 3)
    expert_grads = after(expert_grads, dx_home)
    expert_grads = lax.all_to_all(expert_grads, "dp", 0, 0, tiled=True)

    db_part, logit_grads = combine(
        core_arg, places, dx_home, shared_dx,
        (gates, gate_grads, router_w.astype(F32).T),
    )
    grad_router = lax.dot_general(
        ffn_in.astype(F32), logit_grads, TN, precision=HIGHEST, preferred_element_type=F32
    )
    back_two, gain_two_grad = norm_back(sum_halves(db_part), unit_two, factor_two, gain_two)
    grad_hidden = cotangent + back_two
    grad_attn = both_halves(grad_hidden.astype(BF16))
    attn_grads, da_part = attn_backward(
        seq_lengths, attn_in, grad_attn, qkv_w, out_w, qkv_rot, context, cosine, sine
    )
    attn_grads = lax.all_to_all(
        attn_grads.reshape(ranks, shard, pairs * 4 * LANES), "dp", 0, 0, tiled=True
    )
    back_one, gain_one_grad = norm_back(
        sum_halves(da_part.astype(BF16)), unit_one, factor_one, gain_one
    )
    grad_input = (grad_hidden + back_one).astype(BF16)

    ffn_part = combine(core_arg, places, y_home, shared_y)
    layer_output = (hidden_rows + sum_halves(ffn_part)).astype(BF16)

    small_grads = jnp.concatenate(
        [gain_one_grad[:, None], gain_two_grad[:, None], grad_router], axis=1
    )
    small_grads = lax.all_to_all(
        small_grads.reshape(ranks, shard, 2 + experts), "dp", 0, 0, tiled=True
    )
    small_grads = jnp.sum(small_grads, axis=0)
    small_grads = small_grads + swap(small_grads)

    attn_grads = jnp.sum(attn_grads.astype(F32), axis=0).reshape(shard, pairs, 4, LANES)
    attn_grads = [attn_grads[:, :, k].reshape(shard, pairs * LANES) for k in range(4)]
    shared_grads = jnp.sum(shared_grads.astype(F32), axis=0)
    shared_grads = [shared_grads[:, k * hidden : (k + 1) * hidden] for k in range(3)]
    expert_grads = expert_grads.reshape(ranks // experts, experts, 3, shard, hidden)
    expert_grads = jnp.sum(expert_grads.astype(F32), axis=0)
    expert_grads = [expert_grads[:, k].transpose(1, 0, 2) for k in range(3)]
    return (
        layer_output[None], grad_input[None],
        attn_grads[0], attn_grads[1], attn_grads[2], attn_grads[3],
        small_grads[:, 0], small_grads[:, 1], small_grads[:, 2:],
        expert_grads[0], expert_grads[1], expert_grads[2],
        shared_grads[0], shared_grads[1], shared_grads[2],
    )


def solution(mesh):
    tokens = P("dp", "tensor", None)
    matrix = P("dp", "tensor")
    expert = P("dp", None, "tensor")
    in_specs = (
        (tokens, P("dp"), P("dp", None, None))
        + (matrix,) * 4
        + (P("dp"), P("dp"), P("dp", None))
        + (expert,) * 3
        + (matrix,) * 3
        + (tokens,)
    )
    out_specs = (
        (tokens, tokens)
        + (matrix,) * 4
        + (P("dp"), P("dp"), P("dp", None))
        + (expert,) * 3
        + (matrix,) * 3
    )
    return jax.shard_map(
        per_device, mesh=mesh, in_specs=in_specs, out_specs=out_specs, check_vma=False
    )
```

```python
import functools
import math

import jax
import jax.numpy as jnp
from jax import lax
from jax.experimental import pallas as pl
from jax.experimental.pallas import tpu as pltpu
from jax.sharding import PartitionSpec as P

HD = 64
LANES = 128
EPS = 1e-06
F32 = jnp.float32
BF16 = jnp.bfloat16
HIGHEST = lax.Precision.HIGHEST
VMEM_LIMIT = 56 * 1024 * 1024

NN = (((1,), (0,)), ((), ()))
NT = (((1,), (1,)), ((), ()))
TN = (((0,), (0,)), ((), ()))


def mm(left, right, dims):
    return lax.dot_general(left, right, dims, preferred_element_type=F32)


def params(count):
    return pltpu.CompilerParams(
        dimension_semantics=("arbitrary",) * count, vmem_limit_bytes=VMEM_LIMIT
    )


def cost(flops, nbytes, trans=0):
    return pl.CostEstimate(flops=int(flops), bytes_accessed=int(nbytes), transcendentals=int(trans))


def flip(index, offset):
    bit = 1
    while bit <= offset:
        if offset & bit:
            index = index + bit - 2 * bit * lax.rem(lax.div(index, bit), 2)
        bit *= 2
    return index


def device(rank, core):
    return {"dp": rank, "tensor": core}


def greet(devices):
    barrier = pltpu.get_barrier_semaphore()
    for target in devices:
        pl.semaphore_signal(barrier, inc=1, device_id=target, device_id_type=pl.DeviceIdType.MESH)
    pl.semaphore_wait(barrier, len(devices))


def remote(src, dst, send, recv, target):
    return pltpu.make_async_remote_copy(
        src_ref=src, dst_ref=dst, send_sem=send, recv_sem=recv,
        device_id=target, device_id_type=pl.DeviceIdType.MESH,
    )


def gather_kernel(own_ref, out_ref, own_sem, z_send, z_recv, s_send, s_recv, f_send, f_recv, *, cut):
    me, core = lax.axis_index("dp"), lax.axis_index("tensor")
    z = lax.div(me, 4)
    x_rank, y_rank = flip(me, 1), flip(me, 2)
    up, down = lax.min(me + 4, 15), lax.max(me - 4, 0)
    barrier = pltpu.get_barrier_semaphore()

    def hello(target):
        pl.semaphore_signal(
            barrier, inc=1, device_id=device(target, core), device_id_type=pl.DeviceIdType.MESH
        )

    hello(x_rank)
    hello(y_rank)
    pl.when(z < 3)(lambda: hello(up))
    pl.when(z > 0)(lambda: hello(down))
    pl.semaphore_wait(barrier, 2 + lax.min(z, 1) + lax.min(3 - z, 1))

    own = pltpu.make_async_copy(own_ref, out_ref.at[me], own_sem)
    own.start()

    def z_copy(rank, step, upward):
        src = own_ref if step == 1 else out_ref.at[rank]
        index = step - 1 if upward else step + 2
        return remote(
            src, out_ref.at[rank], z_send.at[index], z_recv.at[index],
            device(up if upward else down, core),
        )

    def side_copy(rank, place, axis):
        src = own_ref if place == 0 else out_ref.at[rank]
        return remote(
            src, out_ref.at[rank], s_send.at[axis, place], s_recv.at[axis, place],
            device(x_rank if axis == 0 else y_rank, core),
        )

    def onward_copy(rank, place, axis):
        columns = pl.ds(0, cut) if axis == 0 else pl.ds(cut, own_ref.shape[1] - cut)
        return remote(
            out_ref.at[rank, :, columns], out_ref.at[rank, :, columns],
            f_send.at[axis, place], f_recv.at[axis, place],
            device(y_rank if axis == 0 else x_rank, core),
        )

    def has(place):
        if place == 0:
            return None
        return z >= place if place <= 3 else z + (place - 3) <= 3

    def rank_at(place):
        return me - 4 * place if place <= 3 else me + 4 * (place - 3)

    def guarded(condition, body):
        if condition is None:
            body()
        else:
            pl.when(condition)(body)

    def sides(place):
        for axis in range(2):
            side_copy(rank_at(place), place, axis).start()

    def onward(place):
        for axis in range(2):
            rank = flip(rank_at(place), 1 + axis)
            side_copy(rank, place, axis).wait_recv()
            onward_copy(rank, place, axis).start()

    def arrive(place):
        step = place if place <= 3 else place - 3
        upward = place <= 3
        rank = rank_at(place)
        z_copy(rank, step, upward).wait_recv()
        if step < 3:
            further = z < 3 if upward else z > 0
            pl.when(further)(lambda: z_copy(rank, step + 1, upward).start())
        sides(place)

    pl.when(z < 3)(lambda: z_copy(me, 1, True).start())
    pl.when(z > 0)(lambda: z_copy(me, 1, False).start())
    sides(0)
    order = (0, 1, 4, 2, 5, 3, 6)
    for turn, place in enumerate(order):
        if place > 0:
            guarded(has(place), functools.partial(arrive, place))
        if turn >= 2:
            guarded(has(order[turn - 2]), functools.partial(onward, order[turn - 2]))
    for place in order[-2:]:
        guarded(has(place), functools.partial(onward, place))

    def finish(place):
        for axis in range(2):
            rank = flip(rank_at(place), 1 + axis)
            side_copy(rank_at(place), place, axis).wait_send()
            onward_copy(rank, place, axis).wait_send()
            onward_copy(flip(rank_at(place), 3), place, axis).wait_recv()

    for place in order:
        guarded(has(place), functools.partial(finish, place))
    for step in range(1, 4):
        pl.when((z < 3) & (z >= step - 1))(
            lambda step=step: z_copy(me - 4 * (step - 1), step, True).wait_send()
        )
        pl.when((z > 0) & (z + step - 1 <= 3))(
            lambda step=step: z_copy(me + 4 * (step - 1), step, False).wait_send()
        )
    own.wait()


def gather_all(own):
    ranks = lax.axis_size("dp")
    rows, width = own.shape
    if ranks != 16:
        return to_all(own)
    return pl.pallas_call(
        functools.partial(gather_kernel, cut=width // 2 // LANES * LANES),
        in_specs=[pl.BlockSpec(memory_space=pl.ANY)],
        out_specs=pl.BlockSpec(memory_space=pl.ANY),
        out_shape=jax.ShapeDtypeStruct((ranks, rows, width), own.dtype),
        scratch_shapes=[
            pltpu.SemaphoreType.DMA,
            pltpu.SemaphoreType.DMA((6,)),
            pltpu.SemaphoreType.DMA((6,)),
            pltpu.SemaphoreType.DMA((2, 7)),
            pltpu.SemaphoreType.DMA((2, 7)),
            pltpu.SemaphoreType.DMA((2, 7)),
            pltpu.SemaphoreType.DMA((2, 7)),
        ],
        compiler_params=pltpu.CompilerParams(collective_id=1, has_side_effects=True),
        cost_estimate=cost(1e6, 60e6),
        name="gather_attn",
    )(own)


def partner(values):
    lane = lax.broadcasted_iota(jnp.int32, values.shape, 1)
    return jnp.where(
        lane % HD < HD // 2,
        pltpu.roll(values, LANES - HD // 2, 1),
        pltpu.roll(values, HD // 2, 1),
    )


def head_lanes(shape, head):
    lane = lax.broadcasted_iota(jnp.int32, shape, 1)
    return (lane // HD) == head


def attn_fwd_kernel(len_ref, a_ref, w_ref, cos_ref, sin_ref, qkv_ref, ctx_ref, *, block):
    span = a_ref.shape[0]
    length = len_ref[0]
    raw = mm(a_ref[...], w_ref[...], NN)
    cosine, sine = cos_ref[...], sin_ref[...]
    query, key = raw[:, :LANES], raw[:, LANES : 2 * LANES]
    qkv_ref[:, :LANES] = (query * cosine + partner(query) * sine).astype(BF16)
    qkv_ref[:, LANES : 2 * LANES] = (key * cosine + partner(key) * sine).astype(BF16)
    qkv_ref[:, 2 * LANES :] = raw[:, 2 * LANES :].astype(BF16)
    for index in range(span // block):
        keys = (index + 1) * block
        query_rows = qkv_ref[index * block : keys, :LANES] * jnp.asarray(HD**-0.5, BF16)
        key_rows = qkv_ref[:keys, LANES : 2 * LANES]
        value_rows = qkv_ref[:keys, 2 * LANES :]
        row = index * block + lax.broadcasted_iota(jnp.int32, (block, keys), 0)
        column = lax.broadcasted_iota(jnp.int32, (block, keys), 1)
        allowed = (column <= row) & (column < length)
        parts = []
        for head in range(LANES // HD):
            masked_query = jnp.where(
                head_lanes(query_rows.shape, head), query_rows, jnp.zeros_like(query_rows)
            )
            scores = jnp.where(allowed, mm(masked_query, key_rows, NT), -1e30)
            peak = jnp.max(scores, axis=1, keepdims=True)
            powers = jnp.exp(scores - peak)
            total = jnp.sum(powers, axis=1, keepdims=True)
            prob = (powers * (1.0 / total)).astype(BF16)
            parts.append(mm(prob, value_rows, NN))
        context = jnp.where(head_lanes(parts[0].shape, 0), parts[0], parts[1])
        ctx_ref[index * block : keys, :] = context.astype(BF16)


def attn_forward(length, attn_in, qkv_w, cosine, sine):
    span, width = attn_in.shape
    pairs = qkv_w.shape[1] // (3 * LANES)
    return pl.pallas_call(
        functools.partial(attn_fwd_kernel, block=256),
        grid=(pairs,),
        in_specs=[
            pl.BlockSpec(memory_space=pltpu.SMEM),
            pl.BlockSpec((span, width), lambda i: (0, 0)),
            pl.BlockSpec((width, 3 * LANES), lambda i: (0, i)),
            pl.BlockSpec((span, LANES), lambda i: (0, 0)),
            pl.BlockSpec((span, LANES), lambda i: (0, 0)),
        ],
        out_specs=[
            pl.BlockSpec((span, 3 * LANES), lambda i: (0, i)),
            pl.BlockSpec((span, LANES), lambda i: (0, i)),
        ],
        out_shape=[
            jax.ShapeDtypeStruct((span, pairs * 3 * LANES), BF16),
            jax.ShapeDtypeStruct((span, pairs * LANES), BF16),
        ],
        compiler_params=params(1),
        cost_estimate=cost(2 * span * width * pairs * 384 + 12 * span * span * 128, 12e6, 6e6),
        name="attn_fwd",
    )(length, attn_in, qkv_w, cosine, sine)


def attn_bwd_kernel(
    len_ref, a_ref, da_in_ref, w_ref, wo_ref, qkv_ref, ctx_ref, cos_ref, sin_ref,
    gw_ref, da_ref, dctx_s, dq_s, dk_s, dv_s, *, block,
):
    span = a_ref.shape[0]
    length = len_ref[0]
    grad_rows = da_in_ref[...]
    dctx_s[...] = mm(grad_rows, wo_ref[...], NN).astype(BF16)
    gw_ref[:, 3 * LANES :] = mm(grad_rows, ctx_ref[...], TN).astype(BF16)
    dk_s[...] = jnp.zeros_like(dk_s)
    dv_s[...] = jnp.zeros_like(dv_s)
    scale = jnp.asarray(HD**-0.5, BF16)
    for index in range(span // block):
        keys = (index + 1) * block
        start = index * block
        query_rows = qkv_ref[start:keys, :LANES] * scale
        key_rows = qkv_ref[:keys, LANES : 2 * LANES]
        value_rows = qkv_ref[:keys, 2 * LANES :]
        context_grad = dctx_s[start:keys, :]
        row = lax.broadcasted_iota(jnp.int32, (keys, block), 0)
        column = start + lax.broadcasted_iota(jnp.int32, (keys, block), 1)
        allowed = (row <= column) & (row < length)
        dq_total = None
        for head in range(LANES // HD):
            lanes = head_lanes((block, LANES), head)
            masked_query = jnp.where(lanes, query_rows, jnp.zeros_like(query_rows))
            masked_grad = jnp.where(lanes, context_grad, jnp.zeros_like(context_grad))
            scores = jnp.where(allowed, mm(key_rows, masked_query, NT), -1e30)
            peak = jnp.max(scores, axis=0, keepdims=True)
            powers = jnp.exp(scores - peak)
            total = jnp.sum(powers, axis=0, keepdims=True)
            prob = powers * (1.0 / total)
            prob_grad = mm(value_rows, masked_grad, NT)
            inner = jnp.sum(prob * prob_grad, axis=0, keepdims=True)
            score_grad = (prob * (prob_grad - inner)).astype(BF16)
            dk_s[:keys, :] += mm(score_grad, masked_query, NN)
            dv_s[:keys, :] += mm(prob.astype(BF16), masked_grad, NN)
            dq_part = mm(score_grad, key_rows, TN)
            dq_total = dq_part if head == 0 else jnp.where(lanes, dq_part, dq_total)
        dq_s[start:keys, :] = dq_total * (HD**-0.5)
    cosine, sine = cos_ref[...], sin_ref[...]
    dq, dk = dq_s[...], dk_s[...]
    dq = (dq * cosine - partner(dq) * sine).astype(BF16)
    dk = (dk * cosine - partner(dk) * sine).astype(BF16)
    grads = jnp.concatenate([dq, dk, dv_s[...].astype(BF16)], axis=1)
    gw_ref[:, : 3 * LANES] = mm(a_ref[...], grads, TN).astype(BF16)
    part = mm(grads, w_ref[...], NT)

    @pl.when(pl.program_id(0) == 0)
    def _():
        da_ref[...] = part

    @pl.when(pl.program_id(0) > 0)
    def _():
        da_ref[...] += part


def attn_backward(length, attn_in, grad_attn, qkv_w, out_w, qkv_rot, context, cosine, sine):
    span, width = attn_in.shape
    pairs = qkv_w.shape[1] // (3 * LANES)
    return pl.pallas_call(
        functools.partial(attn_bwd_kernel, block=256),
        grid=(pairs,),
        in_specs=[
            pl.BlockSpec(memory_space=pltpu.SMEM),
            pl.BlockSpec((span, width), lambda i: (0, 0)),
            pl.BlockSpec((span, width), lambda i: (0, 0)),
            pl.BlockSpec((width, 3 * LANES), lambda i: (0, i)),
            pl.BlockSpec((width, LANES), lambda i: (0, i)),
            pl.BlockSpec((span, 3 * LANES), lambda i: (0, i)),
            pl.BlockSpec((span, LANES), lambda i: (0, i)),
            pl.BlockSpec((span, LANES), lambda i: (0, 0)),
            pl.BlockSpec((span, LANES), lambda i: (0, 0)),
        ],
        out_specs=[
            pl.BlockSpec((width, 4 * LANES), lambda i: (0, i)),
            pl.BlockSpec((span, width), lambda i: (0, 0)),
        ],
        out_shape=[
            jax.ShapeDtypeStruct((width, pairs * 4 * LANES), BF16),
            jax.ShapeDtypeStruct((span, width), F32),
        ],
        scratch_shapes=[
            pltpu.VMEM((span, LANES), BF16),
            pltpu.VMEM((span, LANES), F32),
            pltpu.VMEM((span, LANES), F32),
            pltpu.VMEM((span, LANES), F32),
        ],
        compiler_params=params(1),
        cost_estimate=cost(20e9, 16e6, 6e6),
        name="attn_bwd",
    )(length, attn_in, grad_attn, qkv_w, out_w, qkv_rot, context, cosine, sine)


def column_of(row):
    count = row.shape[1]
    shape = (count, count)
    same = lax.broadcasted_iota(jnp.int32, shape, 0) == lax.broadcasted_iota(jnp.int32, shape, 1)
    return jnp.sum(jnp.where(same, row, 0.0), axis=1, keepdims=True)


def row_of(column):
    count = column.shape[0]
    shape = (count, count)
    same = lax.broadcasted_iota(jnp.int32, shape, 0) == lax.broadcasted_iota(jnp.int32, shape, 1)
    return jnp.sum(jnp.where(same, column, 0.0), axis=0, keepdims=True)


def ffn_block(x, grad, gate, gate_w, up_w, down_w, sums):
    gate_pre = mm(x, gate_w, NN)
    up_pre = mm(x, up_w, NN)
    sig = jax.nn.sigmoid(gate_pre)
    act = gate_pre * sig
    inner = (act * up_pre).astype(BF16)
    out = mm(inner, down_w, NT)
    gate_grad, out_grad = None, grad
    if gate is not None:
        wide = grad.astype(F32)
        gate_grad = jnp.sum(out * wide, axis=1, keepdims=True)
        out = out * gate
        out_grad = (wide * gate).astype(BF16)
    inner_grad = mm(out_grad, down_w, NN)
    gate_pre_grad = (inner_grad * up_pre * (sig + act * (1.0 - sig))).astype(BF16)
    up_pre_grad = (inner_grad * act).astype(BF16)
    row_grad = mm(gate_pre_grad, gate_w, NT) + mm(up_pre_grad, up_w, NT)
    sums[0][...] += mm(x, gate_pre_grad, TN)
    sums[1][...] += mm(x, up_pre_grad, TN)
    sums[2][...] += mm(out_grad, inner, TN)
    return out, row_grad, gate_grad


def slots_kernel(
    places_ref, gates_ref, b_ref, d_ref, wg_ref, wu_ref, wd_ref,
    xr, dr, gr, y_ref, dx_ref, og_ref, ou_ref, od_ref,
    xs, ds, gs, ag, au, ad, send, recv, core_send, core_recv, local, *, block,
):
    me, core = lax.axis_index("dp"), lax.axis_index("tensor")
    experts, slots, width = xs.shape
    mine = lax.rem(me, experts)
    other = device(me, 1 - core)
    greet([device(flip(me, k), core) for k in range(1, experts)] + [other])
    tokens = b_ref.shape[0]
    slot = lax.broadcasted_iota(jnp.int32, (slots, tokens), 0)
    outs, ins = (xr, dr, gr), (xs, ds, gs)

    def copy(k, part):
        return remote(
            ins[part].at[k], outs[part].at[k, 0], send.at[part, k], recv.at[part, k],
            device(flip(me, k), core),
        )

    def core_copy(k, part):
        src = ins[part].at[0] if k == 0 else outs[part].at[k, 0]
        return remote(
            src, outs[part].at[k, 1], core_send.at[part, k], core_recv.at[part, k], other
        )

    def own_copy(part):
        return pltpu.make_async_copy(ins[part].at[0], outs[part].at[0, 0], local.at[part])

    order = tuple(sorted(range(1, experts), key=lambda k: (bin(k).count("1"), k)))
    for k in order + (0,):
        target = flip(mine, k)
        found = slot == places_ref[target]
        hot = jnp.where(found, 1.0, 0.0).astype(BF16)
        xs[k] = mm(hot, b_ref[...], NN).astype(BF16)
        ds[k] = mm(hot, d_ref[...], NN).astype(BF16)
        gate = jnp.sum(jnp.where(found, gates_ref[target], 0.0), axis=1, keepdims=True)
        gs[k] = jnp.broadcast_to(row_of(gate), (8, slots))
        for part in range(3):
            if k:
                copy(k, part).start()
            else:
                own_copy(part).start()
                core_copy(k, part).start()
    for total in (ag, au, ad):
        total[...] = jnp.zeros_like(total)

    def shared(index, carry):
        rows = pl.ds(index * block, block)
        out, row_grad, _ = ffn_block(
            b_ref[rows, :], d_ref[rows, :], None, wg_ref[...], wu_ref[...], wd_ref[...],
            (ag, au, ad),
        )
        y_ref[rows, :] = out.astype(BF16)
        dx_ref[rows, :] = row_grad.astype(BF16)
        return carry

    lax.fori_loop(0, tokens // block, shared, 0)
    og_ref[...] = ag[...].astype(BF16)
    ou_ref[...] = au[...].astype(BF16)
    od_ref[...] = ad[...].astype(BF16)
    for k in order:
        for part in range(3):
            copy(k, part).wait_recv()
            core_copy(k, part).start()
    for part in range(3):
        own_copy(part).wait()
        for k in range(experts):
            core_copy(k, part).wait()
            if k:
                copy(k, part).wait_send()


def slots_and_shared(places, gates, rows, grads, shared_w, slots, block):
    experts, _, tokens = places.shape
    width = rows.shape[1]
    hidden = shared_w.shape[1] // 3
    vmem = pl.BlockSpec(memory_space=pltpu.VMEM)
    far = pl.BlockSpec(memory_space=pl.ANY)
    one = pl.Buffered(1)

    def whole(shape):
        return pl.BlockSpec(shape, lambda i: (0,) * len(shape), pipeline_mode=one)

    weights = [
        pl.BlockSpec((width, hidden), lambda i, k=k: (0, k), pipeline_mode=one) for k in range(3)
    ]
    return pl.pallas_call(
        functools.partial(slots_kernel, block=block),
        grid=(1,),
        in_specs=[whole(places.shape)] * 2 + [whole(rows.shape)] * 2 + weights,
        out_specs=[far] * 3 + [whole(rows.shape)] * 2 + [whole((width, hidden))] * 3,
        out_shape=[
            jax.ShapeDtypeStruct((experts, 2, slots, width), BF16),
            jax.ShapeDtypeStruct((experts, 2, slots, width), BF16),
            jax.ShapeDtypeStruct((experts, 2, 8, slots), F32),
        ]
        + [jax.ShapeDtypeStruct(rows.shape, BF16)] * 2
        + [jax.ShapeDtypeStruct((width, hidden), BF16)] * 3,
        scratch_shapes=[
            pltpu.VMEM((experts, slots, width), BF16),
            pltpu.VMEM((experts, slots, width), BF16),
            pltpu.VMEM((experts, 8, slots), F32),
        ]
        + [pltpu.VMEM((width, hidden), F32)] * 3
        + [pltpu.SemaphoreType.DMA((3, experts))] * 4
        + [pltpu.SemaphoreType.DMA((3,))],
        compiler_params=pltpu.CompilerParams(
            collective_id=2, has_side_effects=True, vmem_limit_bytes=VMEM_LIMIT,
            dimension_semantics=("arbitrary",),
        ),
        cost_estimate=cost(18 * tokens * width * hidden + 4 * experts * slots * tokens * width, 40e6),
        name="slots_shared",
    )(places, gates, rows, grads, shared_w, shared_w, shared_w)


def expert_kernel(
    x_ref, d_ref, g_ref, wg_ref, wu_ref, wd_ref,
    y_home, dx_home, dg_home, og_ref,
    ag, au, ad, own_y, own_dx, ys, dxs, yp, dxp, yt, dxt, dgs,
    core_send, core_recv, send, recv, local, *, experts,
):
    step = pl.program_id(0)
    block = experts - 1 - step
    me, core = lax.axis_index("dp"), lax.axis_index("tensor")
    mine = lax.rem(me, experts)
    other = device(me, 1 - core)
    slots = x_ref.shape[1]
    width = x_ref.shape[2]
    shape = (width, wg_ref.shape[-1])

    def rank_at(k):
        total, bit = me - mine, 1
        while bit < experts:
            total += bit * lax.rem(lax.div(mine, bit) + lax.div(k, bit), 2)
            bit *= 2
        return total

    def core_copy(k, part):
        src, dst = ((ys, yp), (dxs, dxp))[part]
        return remote(
            src.at[lax.rem(k, 2)], dst.at[k], core_send.at[part, k], core_recv.at[part, k], other
        )

    def home_copy(k, part):
        src, dst = ((yt, y_home), (dxt, dx_home), (dgs, dg_home))[part]
        return remote(
            src.at[k], dst.at[mine], send.at[part, k], recv.at[part, k],
            device(rank_at(k), core),
        )

    def own_copy(part):
        src, dst = ((yt, y_home), (dxt, dx_home), (dgs, dg_home))[part]
        return pltpu.make_async_copy(src.at[0], dst.at[mine], local.at[part])

    def go_home(k, part):
        @pl.when(k == 0)
        def _():
            own_copy(part).start()

        @pl.when(k > 0)
        def _():
            home_copy(k, part).start()

    @pl.when(step == 0)
    def _():
        greet([device(flip(me, k), core) for k in range(1, experts)] + [other])
        for total in (ag, au, ad):
            total[...] = jnp.zeros_like(total)

    def settle(k):
        for part in (1, 0):
            core_copy(k, part).wait_recv()
            own, shared, total = ((own_y, yp, yt), (own_dx, dxp, dxt))[part]
            total[k] = (own[...] + shared[k].astype(F32)).astype(BF16)
            go_home(k, part)

    @pl.when(step < experts)
    def _():
        gate = column_of(jnp.concatenate([g_ref[0, 0:1, :], g_ref[1, 0:1, :]], axis=1))
        out, row_grad, gate_grad = ffn_block(
            x_ref[...].reshape(2 * slots, width), d_ref[...].reshape(2 * slots, width), gate,
            wg_ref[...].reshape(shape), wu_ref[...].reshape(shape), wd_ref[...].reshape(shape),
            (ag, au, ad),
        )

        @pl.when(step >= 1)
        def _():
            settle(block + 1)

        for part in (1, 0):

            @pl.when(step >= 2)
            def _():
                core_copy(block + 2, part).wait_send()

            own, half = ((own_y, ys), (own_dx, dxs))[part]
            value = (out, row_grad)[part]
            own[...] = value[:slots]
            half[lax.rem(block, 2)] = value[slots:].astype(BF16)
            core_copy(block, part).start()
        dgs[block] = jnp.broadcast_to(row_of(gate_grad), (8, 2 * slots))
        go_home(block, 2)

    @pl.when(step == experts)
    def _():
        settle(block + 1)
        for index, total in enumerate((ag, au, ad)):
            og_ref[:, index] = total[...].astype(BF16).reshape(og_ref.shape[0], *og_ref.shape[2:])
        for part in (0, 1):
            for k in (0, 1):
                core_copy(k, part).wait_send()
        for part in range(3):
            own_copy(part).wait()
            for k in range(1, experts):
                home_copy(k, part).wait()


def expert_ffn(x_slots, d_slots, g_slots, weights):
    experts, _, slots, width = x_slots.shape
    parts, _, shard, hidden = weights.shape
    far = pl.BlockSpec(memory_space=pl.ANY)
    one = pl.Buffered(1)

    def group(shape):
        return pl.BlockSpec(
            (None,) + shape, lambda i: (jnp.maximum(experts - 1 - i, 0),) + (0,) * len(shape)
        )

    rows = group((2, slots, width))
    matrices = [
        pl.BlockSpec(
            (parts, None, shard, hidden), lambda i, k=k: (0, k, 0, 0), pipeline_mode=one
        )
        for k in range(3)
    ]
    return pl.pallas_call(
        functools.partial(expert_kernel, experts=experts),
        grid=(experts + 1,),
        in_specs=[rows, rows, group((2, 8, slots))] + matrices,
        out_specs=[far, far, far]
        + [pl.BlockSpec(weights.shape, lambda i: (0, 0, 0, 0), pipeline_mode=one)],
        out_shape=[
            jax.ShapeDtypeStruct((experts, slots, width), BF16),
            jax.ShapeDtypeStruct((experts, slots, width), BF16),
            jax.ShapeDtypeStruct((experts, 8, 2 * slots), F32),
            jax.ShapeDtypeStruct(weights.shape, BF16),
        ],
        scratch_shapes=[pltpu.VMEM((width, hidden), F32)] * 3
        + [pltpu.VMEM((slots, width), F32)] * 2
        + [pltpu.VMEM((2, slots, width), BF16)] * 2
        + [pltpu.VMEM((experts, slots, width), BF16)] * 4
        + [pltpu.VMEM((experts, 8, 2 * slots), F32)]
        + [pltpu.SemaphoreType.DMA((2, experts))] * 2
        + [pltpu.SemaphoreType.DMA((3, experts))] * 2
        + [pltpu.SemaphoreType.DMA((3,))],
        compiler_params=pltpu.CompilerParams(
            collective_id=3, has_side_effects=True, vmem_limit_bytes=VMEM_LIMIT,
            dimension_semantics=("arbitrary",),
        ),
        cost_estimate=cost(36 * experts * slots * width * hidden, 40e6),
        name="ffn_expert",
    )(x_slots, d_slots, g_slots, weights, weights, weights)


def combine_hot(pos_ref, offset, experts, slots):
    tokens = pos_ref.shape[0]
    slot = lax.broadcasted_iota(jnp.int32, (tokens, slots), 1) + offset
    return jnp.concatenate(
        [
            jnp.where(slot == pos_ref[:, e : e + 1], 1.0, 0.0).astype(BF16)
            for e in range(experts)
        ],
        axis=1,
    )


def combine_kernel(core_ref, pos_ref, y_ref, base_ref, out_ref):
    experts, slots, width = y_ref.shape
    hot = combine_hot(pos_ref, core_ref[0] * slots, experts, slots)
    part = mm(hot, y_ref[...].reshape(experts * slots, width), NN)
    out_ref[...] = (part + base_ref[...].astype(F32)).astype(BF16)


def combine_grad_kernel(
    core_ref, pos_ref, y_ref, base_ref, gate_ref, dgate_ref, router_ref, out_ref, dl_ref
):
    experts, slots, width = y_ref.shape
    tokens = pos_ref.shape[0]
    hot = combine_hot(pos_ref, core_ref[0] * slots, experts, slots)
    part = mm(hot, y_ref[...].reshape(experts * slots, width), NN)
    slot = lax.broadcasted_iota(jnp.int32, (tokens, 2 * slots), 1)
    slot = jnp.where(
        slot < slots, slot + core_ref[0] * slots, slot - core_ref[0] * slots
    )
    lane = lax.broadcasted_iota(jnp.int32, (tokens, experts), 1)
    gate_grad = jnp.zeros((tokens, experts), F32)
    for e in range(experts):
        found = jnp.sum(
            jnp.where(slot == pos_ref[:, e : e + 1], dgate_ref[e, 0:1, :], 0.0), axis=1, keepdims=True
        )
        gate_grad = jnp.where(lane == e, found, gate_grad)
    gate = gate_ref[...]
    mean = jnp.sum(gate * gate_grad, axis=1, keepdims=True)
    logit_grad = gate * (gate_grad - mean)
    dl_ref[...] = logit_grad
    part += lax.dot_general(
        logit_grad, router_ref[...], NN, precision=HIGHEST, preferred_element_type=F32
    )
    out_ref[...] = (part + base_ref[...].astype(F32)).astype(BF16)


def combine(core, places, slots_in, base, extra=None, block=256):
    tokens, experts = places.shape
    _, slots, width = slots_in.shape
    token = pl.BlockSpec((block, width), lambda i: (i, 0))
    small = pl.BlockSpec((block, experts), lambda i: (i, 0))
    in_specs = [
        pl.BlockSpec(memory_space=pltpu.SMEM),
        small,
        pl.BlockSpec((experts, slots, width), lambda i: (0, 0, 0)),
        token,
    ]
    out_specs, out_shape = token, jax.ShapeDtypeStruct((tokens, width), BF16)
    kernel, args = combine_kernel, [core, places, slots_in, base]
    if extra is not None:
        gates, gate_grads, router = extra
        kernel = combine_grad_kernel
        in_specs += [
            small,
            pl.BlockSpec(gate_grads.shape, lambda i: (0, 0, 0)),
            pl.BlockSpec(router.shape, lambda i: (0, 0)),
        ]
        args += [gates, gate_grads, router]
        out_specs = [token, small]
        out_shape = [out_shape, jax.ShapeDtypeStruct((tokens, experts), F32)]
    return pl.pallas_call(
        kernel,
        grid=(tokens // block,),
        in_specs=in_specs,
        out_specs=out_specs,
        out_shape=out_shape,
        compiler_params=params(1),
        cost_estimate=cost(2 * tokens * experts * slots * width, 8e6),
        name="combine" if extra is None else "combine_grad",
    )(*args)


def swap(values):
    return lax.ppermute(values, "tensor", [(0, 1), (1, 0)])


def both_halves(own):
    other = swap(own)
    first = lax.axis_index("tensor") == 0
    return jnp.concatenate([jnp.where(first, own, other), jnp.where(first, other, own)], axis=0)


def half_of(values, index):
    rows = values.shape[0] // 2
    return lax.dynamic_slice_in_dim(values, index * rows, rows, 0)


def sum_halves(part):
    core = lax.axis_index("tensor")
    other = swap(half_of(part, 1 - core))
    return half_of(part, core).astype(F32) + other.astype(F32)


def to_all(values, groups=None):
    count = lax.axis_size("dp") if groups is None else len(groups[0])
    copies = jnp.broadcast_to(values[None], (count,) + values.shape)
    return lax.all_to_all(copies, "dp", 0, 0, axis_index_groups=groups, tiled=True)


def after(values, *earlier):
    return lax.optimization_barrier((values,) + earlier)[0]


def rms_parts(values):
    factor = lax.rsqrt(jnp.mean(values * values, axis=-1, keepdims=True) + EPS)
    return values * factor, factor


def norm_back(grad, normed, factor, gain):
    hat = grad * gain
    back = factor * (hat - normed * jnp.mean(hat * normed, axis=-1, keepdims=True))
    return back, jnp.sum(grad * normed, axis=0)


def per_device(
    layer_input, seq_lengths, expert_routes, w_query, w_key, w_value, w_output,
    gain_attn, gain_ffn, router_weight, expert_gate, expert_up, expert_down,
    shared_gate, shared_up, shared_down, out_cotangent,
):
    ranks = lax.axis_size("dp")
    core = lax.axis_index("tensor")
    _, own_len, width = layer_input.shape
    span = 2 * own_len
    shard = w_query.shape[0]
    pairs = w_query.shape[1] // LANES
    experts, hidden = expert_gate.shape[1:]
    capacity = 4 * span // experts
    slots = capacity // 2
    groups = [list(range(s, s + experts)) for s in range(0, ranks, experts)]

    qkv_own = jnp.stack([w_query, w_key, w_value], axis=1).reshape(shard, 3, pairs, LANES)
    qkv_own = qkv_own.transpose(0, 2, 1, 3).reshape(shard, pairs * 3 * LANES)
    small_own = jnp.concatenate(
        [gain_attn[:, None], gain_ffn[:, None], router_weight], axis=1
    )
    small_own = jnp.pad(small_own, ((0, 0), (0, LANES - small_own.shape[1])))
    first_own = jnp.concatenate([qkv_own, w_output, small_own], axis=1).astype(BF16)
    first_all = gather_all(first_own).reshape(width, first_own.shape[1])
    qkv_w = first_all[:, : pairs * 3 * LANES]
    out_w = first_all[:, pairs * 3 * LANES : pairs * 4 * LANES]
    small = first_all[:, pairs * 4 * LANES :]
    gain_one = small[:, 0].astype(F32)
    gain_two = small[:, 1].astype(F32)
    router_w = small[:, 2 : 2 + experts]

    routes = expert_routes.reshape(span, 2)
    names = jnp.arange(experts, dtype=jnp.int32)
    chosen = (routes[:, 0:1] == names[None, :]) | (routes[:, 1:2] == names[None, :])
    counts = jnp.cumsum(chosen.astype(jnp.int32), axis=0)
    places = jnp.where(chosen, counts - 1, -1)
    own_places = jnp.where(chosen, counts - 1 - core * slots, -1).T[:, None, :]
    core_arg = core.reshape(1).astype(jnp.int32)

    length = seq_lengths[0]
    valid = (core * own_len + jnp.arange(own_len, dtype=jnp.int32)) < length
    cotangent = out_cotangent[0].astype(F32) * valid.astype(F32)[:, None]
    grad_ffn = both_halves(cotangent.astype(BF16))

    expert_own = jnp.stack([expert_gate, expert_up, expert_down], axis=0).astype(BF16)
    expert_own = expert_own.transpose(2, 0, 1, 3).reshape(1, experts, 3 * shard, hidden)
    expert_own = jnp.broadcast_to(
        expert_own, (ranks // experts, experts, 3 * shard, hidden)
    ).reshape(ranks, 3 * shard, hidden)
    expert_own = after(expert_own, first_all)
    expert_all = lax.all_to_all(expert_own, "dp", 0, 0, tiled=True)
    expert_all = expert_all.reshape(ranks, 3, shard, hidden)
    direct = shard % 16 == 0
    if not direct:
        expert_all = expert_all.transpose(1, 0, 2, 3).reshape(1, 3, width, hidden)

    shared_own = jnp.concatenate([shared_gate, shared_up, shared_down], axis=1).astype(BF16)
    shared_all = lax.all_gather(shared_own, "dp", axis=0, tiled=True)

    half = HD // 2
    inverse = jnp.exp(jnp.arange(half, dtype=F32) * (-math.log(10000.0) / half))
    angles = jnp.arange(span, dtype=F32)[:, None] * inverse[None, :]
    cos_half, sin_half = jnp.cos(angles), jnp.sin(angles)
    cosine = jnp.concatenate([cos_half] * 4, axis=1)
    sine = jnp.concatenate([-sin_half, sin_half] * 2, axis=1)
    input_rows = layer_input[0].astype(F32)
    unit_one, factor_one = rms_parts(input_rows)
    attn_in = both_halves((unit_one * gain_one).astype(BF16))
    qkv_rot, context = attn_forward(seq_lengths, attn_in, qkv_w, cosine, sine)
    attn_part = mm(context, out_w, NT)
    hidden_rows = input_rows + sum_halves(attn_part)
    unit_two, factor_two = rms_parts(hidden_rows)
    ffn_in = both_halves((unit_two * gain_two).astype(BF16))

    logits = mm(ffn_in, router_w, NN)
    top = jnp.max(jnp.where(chosen, logits, -jnp.inf), axis=1, keepdims=True)
    powers = jnp.where(chosen, jnp.exp(logits - top), 0.0)
    gates = powers / jnp.sum(powers, axis=1, keepdims=True)

    x_slots, d_slots, g_slots, shared_y, shared_dx, shared_gg, shared_gu, shared_gd = (
        slots_and_shared(
            own_places, gates.T[:, None, :], ffn_in, grad_ffn, shared_all, slots, 512
        )
    )
    shared_grads = jnp.concatenate([shared_gg, shared_gu, shared_gd], axis=1)
    shared_grads = lax.all_to_all(
        shared_grads.reshape(ranks, shard, 3 * hidden), "dp", 0, 0, tiled=True
    )

    y_home, dx_home, gate_grads, expert_grads = expert_ffn(x_slots, d_slots, g_slots, expert_all)
    if not direct:
        expert_grads = expert_grads.reshape(3, ranks, shard, hidden).transpose(1, 0, 2, 3)
    dx_home = after(dx_home, shared_grads)
    expert_grads = lax.all_to_all(expert_grads, "dp", 0, 0, tiled=True)

    db_part, logit_grads = combine(
        core_arg, places, dx_home, shared_dx,
        (gates, gate_grads, router_w.astype(F32).T),
    )
    grad_router = lax.dot_general(
        ffn_in.astype(F32), logit_grads, TN, precision=HIGHEST, preferred_element_type=F32
    )
    back_two, gain_two_grad = norm_back(sum_halves(db_part), unit_two, factor_two, gain_two)
    grad_hidden = cotangent + back_two
    grad_attn = both_halves(grad_hidden.astype(BF16))
    attn_grads, da_part = attn_backward(
        seq_lengths, attn_in, grad_attn, qkv_w, out_w, qkv_rot, context, cosine, sine
    )
    attn_grads = after(attn_grads, expert_grads)
    attn_grads = lax.all_to_all(
        attn_grads.reshape(ranks, shard, pairs * 4 * LANES), "dp", 0, 0, tiled=True
    )
    back_one, gain_one_grad = norm_back(
        sum_halves(da_part.astype(BF16)), unit_one, factor_one, gain_one
    )
    grad_input = (grad_hidden + back_one).astype(BF16)

    ffn_part = combine(core_arg, places, y_home, shared_y)
    layer_output = (hidden_rows + sum_halves(ffn_part)).astype(BF16)

    small_grads = jnp.concatenate(
        [gain_one_grad[:, None], gain_two_grad[:, None], grad_router], axis=1
    )
    small_grads = lax.all_to_all(
        small_grads.reshape(ranks, shard, 2 + experts), "dp", 0, 0, tiled=True
    )
    small_grads = jnp.sum(small_grads, axis=0)
    small_grads = small_grads + swap(small_grads)

    attn_grads = jnp.sum(attn_grads.astype(F32), axis=0).reshape(shard, pairs, 4, LANES)
    attn_grads = [attn_grads[:, :, k].reshape(shard, pairs * LANES) for k in range(4)]
    shared_grads = jnp.sum(shared_grads.astype(F32), axis=0)
    shared_grads = [shared_grads[:, k * hidden : (k + 1) * hidden] for k in range(3)]
    expert_grads = expert_grads.reshape(ranks // experts, experts, 3, shard, hidden)
    expert_grads = jnp.sum(expert_grads.astype(F32), axis=0)
    expert_grads = [expert_grads[:, k].transpose(1, 0, 2) for k in range(3)]
    return (
        layer_output[None], grad_input[None],
        attn_grads[0], attn_grads[1], attn_grads[2], attn_grads[3],
        small_grads[:, 0], small_grads[:, 1], small_grads[:, 2:],
        expert_grads[0], expert_grads[1], expert_grads[2],
        shared_grads[0], shared_grads[1], shared_grads[2],
    )


def solution(mesh):
    tokens = P("dp", "tensor", None)
    matrix = P("dp", "tensor")
    expert = P("dp", None, "tensor")
    in_specs = (
        (tokens, P("dp"), P("dp", None, None))
        + (matrix,) * 4
        + (P("dp"), P("dp"), P("dp", None))
        + (expert,) * 3
        + (matrix,) * 3
        + (tokens,)
    )
    out_specs = (
        (tokens, tokens)
        + (matrix,) * 4
        + (P("dp"), P("dp"), P("dp", None))
        + (expert,) * 3
        + (matrix,) * 3
    )
    return jax.shard_map(
        per_device, mesh=mesh, in_specs=in_specs, out_specs=out_specs, check_vma=False
    )
```

```python
import functools
import math

import jax
import jax.numpy as jnp
import numpy as np
from jax import lax
from jax.experimental import pallas as pl
from jax.experimental.pallas import tpu as pltpu
from jax.sharding import PartitionSpec as P

HD = 64
LANES = 128
EPS = 1e-06
F32 = jnp.float32
BF16 = jnp.bfloat16
HIGHEST = lax.Precision.HIGHEST
VMEM_LIMIT = 60 * 1024 * 1024

NN = (((1,), (0,)), ((), ()))
NT = (((1,), (1,)), ((), ()))
TN = (((0,), (0,)), ((), ()))


def mm(left, right, dims):
    return lax.dot_general(left, right, dims, preferred_element_type=F32)


def params(count):
    return pltpu.CompilerParams(
        dimension_semantics=("arbitrary",) * count, vmem_limit_bytes=VMEM_LIMIT
    )


def remote_params(number):
    return pltpu.CompilerParams(
        collective_id=number, has_side_effects=True, vmem_limit_bytes=VMEM_LIMIT,
        dimension_semantics=("arbitrary",),
    )


def cost(flops, nbytes, trans=0):
    return pl.CostEstimate(flops=int(flops), bytes_accessed=int(nbytes), transcendentals=int(trans))


def flip(index, offset):
    bit = 1
    while bit <= offset:
        if offset & bit:
            index = index + bit - 2 * bit * lax.rem(lax.div(index, bit), 2)
        bit *= 2
    return index


def device(rank, core):
    return {"dp": rank, "tensor": core}


def greet(devices):
    barrier = pltpu.get_barrier_semaphore()
    for target in devices:
        pl.semaphore_signal(barrier, inc=1, device_id=target, device_id_type=pl.DeviceIdType.MESH)
    pl.semaphore_wait(barrier, len(devices))


def remote(src, dst, send, recv, target):
    return pltpu.make_async_remote_copy(
        src_ref=src, dst_ref=dst, send_sem=send, recv_sem=recv,
        device_id=target, device_id_type=pl.DeviceIdType.MESH,
    )


class Gather:
    order = (0, 1, 4, 2, 5, 3, 6)
    turns = 9

    def __init__(self, own_ref, out_ref, sems, which):
        self.own_ref, self.out_ref = own_ref, out_ref
        self.own_sem, self.z_send, self.z_recv, self.s_send, self.s_recv, self.f_send, self.f_recv = (
            sem.at[which] for sem in sems
        )
        self.cut = own_ref.shape[1] // 2 // LANES * LANES
        self.me, self.core = lax.axis_index("dp"), lax.axis_index("tensor")
        self.z = lax.div(self.me, 4)
        self.up, self.down = lax.min(self.me + 4, 15), lax.max(self.me - 4, 0)
        self.sides_of = (flip(self.me, 1), flip(self.me, 2))

    @staticmethod
    def semaphores(count):
        dma = pltpu.SemaphoreType.DMA
        return [dma((count,)), dma((count, 6)), dma((count, 6))] + [dma((count, 2, 7))] * 4

    def rank_at(self, place):
        return self.me - 4 * place if place <= 3 else self.me + 4 * (place - 3)

    def at(self, place, body):
        if place == 0:
            body()
        else:
            pl.when(self.z >= place if place <= 3 else self.z + (place - 3) <= 3)(body)

    def own_copy(self):
        return pltpu.make_async_copy(self.own_ref, self.out_ref.at[self.me], self.own_sem)

    def z_copy(self, rank, step, upward):
        index = step - 1 if upward else step + 2
        return remote(
            self.own_ref if step == 1 else self.out_ref.at[rank], self.out_ref.at[rank],
            self.z_send.at[index], self.z_recv.at[index],
            device(self.up if upward else self.down, self.core),
        )

    def side_copy(self, rank, place, axis):
        return remote(
            self.own_ref if place == 0 else self.out_ref.at[rank], self.out_ref.at[rank],
            self.s_send.at[axis, place], self.s_recv.at[axis, place],
            device(self.sides_of[axis], self.core),
        )

    def onward_copy(self, rank, place, axis):
        width = self.own_ref.shape[1]
        columns = pl.ds(0, self.cut) if axis == 0 else pl.ds(self.cut, width - self.cut)
        part = self.out_ref.at[rank, :, columns]
        return remote(
            part, part, self.f_send.at[axis, place], self.f_recv.at[axis, place],
            device(self.sides_of[1 - axis], self.core),
        )

    def begin(self):
        self.own_copy().start()
        pl.when(self.z < 3)(lambda: self.z_copy(self.me, 1, True).start())
        pl.when(self.z > 0)(lambda: self.z_copy(self.me, 1, False).start())
        for axis in range(2):
            self.side_copy(self.me, 0, axis).start()

    def arrive(self, place):
        upward = place <= 3
        step = place if upward else place - 3
        rank = self.rank_at(place)
        self.z_copy(rank, step, upward).wait_recv()
        if step < 3:
            further = self.z < 3 if upward else self.z > 0
            pl.when(further)(lambda: self.z_copy(rank, step + 1, upward).start())
        for axis in range(2):
            self.side_copy(rank, place, axis).start()

    def onward(self, place):
        for axis in range(2):
            rank = flip(self.rank_at(place), 1 + axis)
            self.side_copy(rank, place, axis).wait_recv()
            self.onward_copy(rank, place, axis).start()

    def turn(self, index):
        if index < 7:
            self.at(self.order[index], functools.partial(self.arrive, self.order[index]))
        if index >= 2:
            self.at(self.order[index - 2], functools.partial(self.onward, self.order[index - 2]))

    def finish(self, place):
        for axis in range(2):
            rank = flip(self.rank_at(place), 1 + axis)
            self.side_copy(self.rank_at(place), place, axis).wait_send()
            self.onward_copy(rank, place, axis).wait_send()
            self.onward_copy(flip(self.rank_at(place), 3), place, axis).wait_recv()

    def end(self):
        z = self.z
        for place in self.order:
            self.at(place, functools.partial(self.finish, place))
        for step in range(1, 4):
            pl.when((z < 3) & (z >= step - 1))(
                lambda step=step: self.z_copy(self.me - 4 * (step - 1), step, True).wait_send()
            )
            pl.when((z > 0) & (z + step - 1 <= 3))(
                lambda step=step: self.z_copy(self.me + 4 * (step - 1), step, False).wait_send()
            )
        self.own_copy().wait()


def gather_kernel(own_ref, out_ref, *sems):
    gather = Gather(own_ref, out_ref, sems, 0)
    z, core = gather.z, gather.core
    barrier = pltpu.get_barrier_semaphore()

    def hello(rank):
        pl.semaphore_signal(
            barrier, inc=1, device_id=device(rank, core), device_id_type=pl.DeviceIdType.MESH
        )

    for rank in gather.sides_of:
        hello(rank)
    pl.when(z < 3)(lambda: hello(gather.up))
    pl.when(z > 0)(lambda: hello(gather.down))
    pl.semaphore_wait(barrier, 2 + lax.min(z, 1) + lax.min(3 - z, 1))
    gather.begin()
    for turn in range(1, gather.turns):
        gather.turn(turn)
    gather.end()


def gather_all(own):
    ranks = lax.axis_size("dp")
    if ranks != 16:
        return to_all(own)
    return pl.pallas_call(
        gather_kernel,
        in_specs=[pl.BlockSpec(memory_space=pl.ANY)],
        out_specs=pl.BlockSpec(memory_space=pl.ANY),
        out_shape=jax.ShapeDtypeStruct((ranks,) + own.shape, own.dtype),
        scratch_shapes=Gather.semaphores(1),
        compiler_params=pltpu.CompilerParams(collective_id=1, has_side_effects=True),
        cost_estimate=cost(1e6, 60e6),
        name="gather_attn",
    )(own)


def partner(values):
    lane = lax.broadcasted_iota(jnp.int32, values.shape, 1)
    return jnp.where(
        lane % HD < HD // 2,
        pltpu.roll(values, LANES - HD // 2, 1),
        pltpu.roll(values, HD // 2, 1),
    )


def head_lanes(shape, head):
    lane = lax.broadcasted_iota(jnp.int32, shape, 1)
    return (lane // HD) == head


def offsets(count):
    return sorted(range(1, count), key=lambda k: (bin(k).count("1"), k))


class Trip:
    def __init__(self, ins, outs, send, recv, core_send, core_recv, local, part):
        self.ins, self.outs, self.part = ins, outs, part
        self.send, self.recv, self.local = send, recv, local
        self.core_send, self.core_recv = core_send, core_recv
        self.me, self.core = lax.axis_index("dp"), lax.axis_index("tensor")
        self.count = ins.shape[0]

    def copy(self, k):
        return remote(
            self.ins.at[k], self.outs.at[k, 0],
            self.send.at[self.part, k], self.recv.at[self.part, k],
            device(flip(self.me, k), self.core),
        )

    def core_copy(self, k):
        src = self.ins.at[0] if k == 0 else self.outs.at[k, 0]
        return remote(
            src, self.outs.at[k, 1],
            self.core_send.at[self.part, k], self.core_recv.at[self.part, k],
            device(self.me, 1 - self.core),
        )

    def own(self):
        return pltpu.make_async_copy(self.ins.at[0], self.outs.at[0, 0], self.local.at[self.part])

    def go(self, k):
        if k:
            self.copy(k).start()
        else:
            self.own().start()
            self.core_copy(0).start()

    def pass_on(self, k):
        self.copy(k).wait_recv()
        self.core_copy(k).start()

    def end(self):
        self.own().wait()
        for k in range(self.count):
            self.core_copy(k).wait()
            if k:
                self.copy(k).wait_send()


def cluster_and_core(count):
    me, core = lax.axis_index("dp"), lax.axis_index("tensor")
    return [device(flip(me, k), core) for k in range(1, count)] + [device(me, 1 - core)]


def rms(values):
    return values * lax.rsqrt(jnp.mean(values * values, axis=-1, keepdims=True) + EPS)


def whole(shape):
    return pl.BlockSpec(shape, lambda i: (0,) * len(shape), pipeline_mode=pl.Buffered(1))


def attn_fwd_kernel(
    len_ref, x_ref, c_ref, routes_ref, w_ref, wo_ref, small_ref, shared_ref, cos_ref, sin_ref,
    a_ref, qkv_ref, ctx_ref, h_ref, b_ref, d_ref, places_ref, rows_ref, gates_ref, y_ref, dx_ref, dr, xr, gr, og_ref, shared_all,
    ds, xs, gs, ag, au, ad, shared_w, part, x_in, h_in, b_out, b_in, c_out, c_in,
    send, recv, core_send, core_recv, local, pair_send, pair_recv, load, *gather_sems,
    block, gathers,
):
    step = pl.program_id(0)
    me, core = lax.axis_index("dp"), lax.axis_index("tensor")
    other = device(me, 1 - core)
    experts, slots, _ = ds.shape
    trips = [
        Trip(ins, outs, send, recv, core_send, core_recv, local, index)
        for index, (ins, outs) in enumerate(((ds, dr), (xs, xr), (gs, gr)))
    ]
    slot = core * slots + lax.broadcasted_iota(jnp.int32, (slots, a_ref.shape[0]), 0)
    slot = slot.astype(F32)
    mine = lax.rem(me, experts)
    span, width = a_ref.shape
    half = span // 2
    length = len_ref[0]
    own = pl.ds(pl.multiple_of(core * half, half), half)
    away = pl.ds(pl.multiple_of((1 - core) * half, half), half)
    pairs = pl.num_programs(0)
    if gathers:
        shared = Gather(shared_ref, shared_all, gather_sems, 0)

    def to_other(src, dst, index):
        return remote(src, dst, pair_send.at[index], pair_recv.at[index], other)

    @pl.when(step == 0)
    def _():
        if gathers:
            z = lax.div(me, 4)
            barrier = pltpu.get_barrier_semaphore()

            def hello(target):
                pl.semaphore_signal(
                    barrier, inc=1, device_id=target, device_id_type=pl.DeviceIdType.MESH
                )

            for target in cluster_and_core(experts):
                hello(target)
            pl.when(z == 1)(lambda: hello(device(shared.up, core)))
            pl.when(z == 2)(lambda: hello(device(shared.down, core)))
            pl.semaphore_wait(barrier, experts + lax.min(z, 1) * lax.min(3 - z, 1))
        else:
            greet(cluster_and_core(experts))
        token = core * half + lax.broadcasted_iota(jnp.int32, c_ref.shape, 0)
        valid = jnp.where(token < length, c_ref[...].astype(F32), 0.0).astype(BF16)
        c_out[...] = valid
        d_ref[own, :] = valid
        swap_c = to_other(c_out, c_in, 0)
        swap_c.start()
        swap_x = to_other(x_ref, x_in, 1)
        swap_x.start()

        name = lax.broadcasted_iota(jnp.int32, (experts, span), 0)
        chosen = (name == routes_ref[0:1, :]) | (name == routes_ref[1:2, :])
        earlier = lax.broadcasted_iota(jnp.int32, (span, span), 0) < lax.broadcasted_iota(
            jnp.int32, (span, span), 1
        )
        counts = mm(
            jnp.where(chosen, 1.0, 0.0).astype(BF16), jnp.where(earlier, 1.0, 0.0).astype(BF16), NN
        )
        places_ref[...] = jnp.where(chosen, counts, -1.0)

        swap_c.wait_recv()
        d_ref[away, :] = c_in[...]
        for k in offsets(experts) + [0]:
            place = places_ref[pl.ds(flip(mine, k), 1), :]
            hot = jnp.where(slot == place, 1.0, 0.0).astype(BF16)
            ds[k] = mm(hot, d_ref[...], NN).astype(BF16)
            trips[0].go(k)
        if gathers:
            shared.begin()
        rows_ref[...] = small_ref[...].astype(F32).T[: rows_ref.shape[0], :]
        swap_x.wait_recv()
        gain = rows_ref[0:1, :]
        a_ref[own, :] = (rms(x_ref[...].astype(F32)) * gain).astype(BF16)
        a_ref[away, :] = (rms(x_in[...].astype(F32)) * gain).astype(BF16)
        part[...] = jnp.zeros_like(part)
        swap_c.wait_send()
        swap_x.wait_send()

    raw = mm(a_ref[...], w_ref[...], NN)
    cosine, sine = cos_ref[...], sin_ref[...]
    query, key = raw[:, :LANES], raw[:, LANES : 2 * LANES]
    qkv_ref[:, :LANES] = (query * cosine + partner(query) * sine).astype(BF16)
    qkv_ref[:, LANES : 2 * LANES] = (key * cosine + partner(key) * sine).astype(BF16)
    qkv_ref[:, 2 * LANES :] = raw[:, 2 * LANES :].astype(BF16)
    for index in range(span // block):
        keys = (index + 1) * block
        query_rows = qkv_ref[index * block : keys, :LANES] * jnp.asarray(HD**-0.5, BF16)
        key_rows = qkv_ref[:keys, LANES : 2 * LANES]
        value_rows = qkv_ref[:keys, 2 * LANES :]
        row = index * block + lax.broadcasted_iota(jnp.int32, (block, keys), 0)
        column = lax.broadcasted_iota(jnp.int32, (block, keys), 1)
        allowed = (column <= row) & (column < length)
        parts = []
        for head in range(LANES // HD):
            masked_query = jnp.where(
                head_lanes(query_rows.shape, head), query_rows, jnp.zeros_like(query_rows)
            )
            scores = jnp.where(allowed, mm(masked_query, key_rows, NT), -1e30)
            peak = jnp.max(scores, axis=1, keepdims=True)
            powers = jnp.exp(scores - peak)
            total = jnp.sum(powers, axis=1, keepdims=True)
            prob = (powers * (1.0 / total)).astype(BF16)
            parts.append(mm(prob, value_rows, NN))
        context = jnp.where(head_lanes(parts[0].shape, 0), parts[0], parts[1]).astype(BF16)
        ctx_ref[index * block : keys, :] = context
        part[index * block : keys, :] += mm(context, wo_ref[...], NT)

    if gathers:
        for turn in range(1, 3):
            pl.when(step == turn - 1)(functools.partial(shared.turn, turn))

    @pl.when(step == pairs - 1)
    def _():
        swap_h = to_other(part.at[away], h_in, 2)
        swap_h.start()
        rows = x_ref[...].astype(F32) + part[own, :]
        swap_h.wait_recv()
        rows = rows + h_in[...]
        h_ref[...] = rows
        normed = (rms(rows) * rows_ref[1:2, :]).astype(BF16)
        b_out[...] = normed
        swap_b = to_other(b_out, b_in, 3)
        swap_b.start()
        b_ref[own, :] = normed
        swap_b.wait_recv()
        b_ref[away, :] = b_in[...]
        chosen = places_ref[...] >= 0
        logits = mm(rows_ref[2 : 2 + experts, :].astype(BF16), b_ref[...], NT)
        top = jnp.max(jnp.where(chosen, logits, -1e30), axis=0, keepdims=True)
        powers = jnp.where(chosen, jnp.exp(jnp.minimum(logits - top, 0.0)), 0.0)
        gates_ref[...] = powers / jnp.sum(powers, axis=0, keepdims=True)
        for k in offsets(experts) + [0]:
            target = pl.ds(flip(mine, k), 1)
            found = slot == places_ref[target, :]
            xs[k] = mm(jnp.where(found, 1.0, 0.0).astype(BF16), b_ref[...], NN).astype(BF16)
            trips[1].go(k)
            gate = jnp.sum(jnp.where(found, gates_ref[target, :], 0.0), axis=1, keepdims=True)
            gs[k] = jnp.broadcast_to(row_of(gate), gs.shape[1:])
            trips[2].go(k)
        swap_h.wait_send()
        swap_b.wait_send()
        for total in (ag, au, ad):
            total[...] = jnp.zeros_like(total)
        if gathers:
            for turn in range(3, shared.turns):
                shared.turn(turn)
            shared.end()
        read = pltpu.make_async_copy(shared_all if gathers else shared_ref, shared_w, load)
        read.start()
        read.wait()
        for k in offsets(experts):
            trips[0].pass_on(k)
        hidden = ag.shape[1]

        def matrix(index):
            return shared_w[:, :, index * hidden : (index + 1) * hidden].reshape(width, hidden)

        def branch(index, carry):
            rows = pl.ds(pl.multiple_of(index * block, block), block)
            out, row_grad, _ = ffn_block(
                b_ref[rows, :], d_ref[rows, :], None, matrix(0), matrix(1), matrix(2), (ag, au, ad)
            )
            y_ref[rows, :] = out.astype(BF16)
            dx_ref[rows, :] = row_grad.astype(BF16)
            return carry

        lax.fori_loop(0, span // block, branch, 0)
        for index, total in enumerate((ag, au, ad)):
            shared_w[:, :, index * hidden : (index + 1) * hidden] = (
                total[...].astype(BF16).reshape(shared_w.shape[0], -1, hidden)
            )
        write = pltpu.make_async_copy(shared_w, og_ref, load)
        write.start()
        for k in offsets(experts):
            trips[1].pass_on(k)
            trips[2].pass_on(k)
        for trip in trips:
            trip.end()
        write.wait()


def attn_forward(length, rows, cotangent, routes, first_all, shared_own, cosine, sine, experts, slots):
    half, width = rows.shape
    span = 2 * half
    ranks = lax.axis_size("dp")
    pairs = (first_all.shape[1] - LANES) // (4 * LANES)
    gathers = ranks == 16
    far = pl.BlockSpec(memory_space=pl.ANY)
    hidden = shared_own.shape[1] // 3
    if gathers:
        shared, parts = shared_own, (ranks,) + shared_own.shape
    else:
        parts = (1, width, shared_own.shape[1])
        shared = to_all(shared_own).reshape(parts)
    return pl.pallas_call(
        functools.partial(attn_fwd_kernel, block=256, gathers=gathers),
        grid=(pairs,),
        in_specs=[
            pl.BlockSpec(memory_space=pltpu.SMEM),
            whole((half, width)),
            whole((half, width)),
            whole(routes.shape),
            pl.BlockSpec((width, 3 * LANES), lambda i: (0, i)),
            pl.BlockSpec((width, LANES), lambda i: (0, 3 * pairs + i)),
            pl.BlockSpec((width, LANES), lambda i: (0, 4 * pairs)),
            far,
            whole((span, LANES)),
            whole((span, LANES)),
        ],
        out_specs=[
            whole((span, width)),
            pl.BlockSpec((span, 3 * LANES), lambda i: (0, i)),
            pl.BlockSpec((span, LANES), lambda i: (0, i)),
            whole((half, width)),
            whole((span, width)),
            whole((span, width)),
            whole((experts, span)),
            whole((16, width)),
            whole((experts, span)),
            whole((span, width)),
            whole((span, width)),
        ]
        + [far] * 5,
        out_shape=[
            jax.ShapeDtypeStruct((span, width), BF16),
            jax.ShapeDtypeStruct((span, pairs * 3 * LANES), BF16),
            jax.ShapeDtypeStruct((span, pairs * LANES), BF16),
            jax.ShapeDtypeStruct((half, width), F32),
            jax.ShapeDtypeStruct((span, width), BF16),
            jax.ShapeDtypeStruct((span, width), BF16),
            jax.ShapeDtypeStruct((experts, span), F32),
            jax.ShapeDtypeStruct((16, width), F32),
            jax.ShapeDtypeStruct((experts, span), F32),
            jax.ShapeDtypeStruct((span, width), BF16),
            jax.ShapeDtypeStruct((span, width), BF16),
            jax.ShapeDtypeStruct((experts, 2, slots, width), BF16),
            jax.ShapeDtypeStruct((experts, 2, slots, width), BF16),
            jax.ShapeDtypeStruct((experts, 2, 8, slots), F32),
            jax.ShapeDtypeStruct(parts, BF16),
            jax.ShapeDtypeStruct(parts if gathers else (1, 16, LANES), BF16),
        ],
        scratch_shapes=[
            pltpu.VMEM((experts, slots, width), BF16),
            pltpu.VMEM((experts, slots, width), BF16),
            pltpu.VMEM((experts, 8, slots), F32),
            pltpu.VMEM((width, hidden), F32),
            pltpu.VMEM((width, hidden), F32),
            pltpu.VMEM((width, hidden), F32),
            pltpu.VMEM(parts, BF16),
            pltpu.VMEM((span, width), F32),
            pltpu.VMEM((half, width), BF16),
            pltpu.VMEM((half, width), F32),
        ]
        + [pltpu.VMEM((half, width), BF16)] * 4
        + [pltpu.SemaphoreType.DMA((3, experts))] * 4
        + [pltpu.SemaphoreType.DMA((3,))]
        + [pltpu.SemaphoreType.DMA((4,))] * 2
        + [pltpu.SemaphoreType.DMA]
        + Gather.semaphores(1),
        compiler_params=remote_params(4),
        cost_estimate=cost(20e9, 60e6, 6e6),
        name="attn_fwd",
    )(length, rows, cotangent, routes, first_all, first_all, first_all, shared, cosine, sine)


def norm_back(grad, values, gain):
    factor = lax.rsqrt(jnp.mean(values * values, axis=-1, keepdims=True) + EPS)
    normed = values * factor
    hat = grad * gain
    back = factor * (hat - normed * jnp.mean(hat * normed, axis=-1, keepdims=True))
    return back, jnp.sum(grad * normed, axis=0, keepdims=True)


def slot_table(places, experts, slots, offset):
    slot = lax.broadcasted_iota(jnp.int32, (places.shape[0], slots), 1) + offset
    slot = slot.astype(F32)
    return jnp.concatenate(
        [jnp.where(slot == places[:, e : e + 1], 1.0, 0.0).astype(BF16) for e in range(experts)],
        axis=1,
    )


def attn_bwd_kernel(
    len_ref, places_ref, gates_ref, rows_ref, dx_ref, dg_ref, base_ref, b_ref, h_ref, d_ref,
    x_ref, a_ref, w_ref, wo_ref, qkv_ref, ctx_ref, cos_ref, sin_ref, sy_ref, y_ref, share_ref, late_ref, early_ref,
    gi_ref, lo_ref, *rest, block, ranks, halves, sends,
):
    if sends:
        go_refs, gx_refs, gsh_refs, gs_ref = rest[:4], rest[4:7], rest[7:10], rest[10]
        gw_ref, total_ref, late_in, early_in, small_in = rest[11:16]
        rest = rest[16:]
    else:
        gw_ref, gs_ref = rest[:2]
        rest = rest[2:]
    (
        db_s, dl_s, db_out, db_in, dh_s, grad_s, da_s, sums_s, sums_in, turned_s,
        yh_s, gw_s, dctx_s, dq_s, dk_s, dv_s, send, recv, local, pair_send, pair_recv,
        y_send, y_recv, y_local, z_send, z_recv,
    ) = rest
    step = pl.program_id(0)
    last = pl.num_programs(0) - 1
    me, core = lax.axis_index("dp"), lax.axis_index("tensor")
    other = device(me, 1 - core)
    experts, slots, width = dx_ref.shape
    span = a_ref.shape[0]
    half = span // 2
    length = len_ref[0]
    own = pl.ds(pl.multiple_of(core * half, half), half)
    away = pl.ds(pl.multiple_of((1 - core) * half, half), half)
    shard = width // ranks
    pairs = gw_s.shape[0]

    def to_other(src, dst, index):
        return remote(src, dst, pair_send.at[index], pair_recv.at[index], other)

    small, late = pairs, pairs + 1

    def part_of(index, rank):
        rows = pl.ds(pl.multiple_of(rank * shard, shard), shard)
        if index is late:
            return late_ref.at[rank]
        return turned_s.at[rows] if index is small else gw_s.at[index, rows]

    def place_of(index, rank):
        if index is late:
            return late_in.at[rank]
        return small_in.at[rank] if index is small else gw_ref.at[rank, index]

    def share(index, offset):
        rank = lax.rem(me + offset, ranks)
        return remote(
            part_of(index, rank), place_of(index, me), send.at[index, offset],
            recv.at[index, offset], device(rank, core),
        )

    def own_share(index):
        return pltpu.make_async_copy(part_of(index, me), place_of(index, me), local.at[index])

    def give(index):
        own_share(index).start()

        def one(offset, carry):
            share(index, offset).start()
            return carry

        lax.fori_loop(1, ranks, one, 0)

    def take(index):
        own_share(index).wait()

        def done(offset, carry):
            share(index, offset).wait()
            return carry

        lax.fori_loop(1, ranks, done, 0)

    def all_ranks(ref, *index):
        total = ref[(0,) + index].astype(F32)
        for rank in range(1, ref.shape[0]):
            total += ref[(rank,) + index].astype(F32)
        return total

    def put_experts(ref, columns):
        for kind in range(3):
            for expert in range(experts):
                total = ref[expert, kind].astype(F32)
                for cluster in range(1, ranks // experts):
                    total += ref[cluster * experts + expert, kind].astype(F32)
                gx_refs[kind][:, expert, columns] = total

    def y_copy(k):
        return remote(
            y_ref.at[k], yh_s.at[k], y_send.at[k], y_recv.at[k], device(flip(me, k), core)
        )

    def z_copy(k):
        rank = flip(me, 4 * k)
        return remote(
            share_ref.at[lax.div(rank, 4)], total_ref.at[k], z_send.at[k], z_recv.at[k],
            device(rank, core),
        )

    def own_rows():
        copies = [pltpu.make_async_copy(y_ref.at[0], yh_s.at[0], y_local.at[0])]
        if halves:
            copies.append(
                pltpu.make_async_copy(share_ref.at[lax.div(me, 4)], total_ref.at[0], y_local.at[1])
            )
        return copies

    def put_together(table, values, index, tokens):
        here = pl.ds(pl.multiple_of(index * tokens, tokens), tokens)
        places = table(here)
        hot = slot_table(places, experts, slots, core * slots)
        return here, places, mm(hot, values[...].reshape(experts * slots, width), NN)

    @pl.when(step == 0)
    def _():
        if sends:
            greet([device(lax.rem(me + k, ranks), core) for k in range(1, ranks)] + [other])
        else:
            greet(cluster_and_core(experts))
        for copy in own_rows():
            copy.start()
        for k in range(1, experts):
            y_copy(k).start()
        if halves:
            for k in range(1, 4):
                z_copy(k).start()
        if sends:
            give(late)
            pltpu.make_async_copy(early_ref, early_in, y_local.at[2]).start()
        router = rows_ref[2 : 2 + experts, :]
        tokens = 256

        def gather(index, carry):
            here, places, total = put_together(
                lambda rows: places_ref[:, rows].T, dx_ref, index, tokens
            )
            gate = gates_ref[:, here].T
            slot = lax.broadcasted_iota(jnp.int32, (tokens, 2 * slots), 1)
            slot = jnp.where(slot < slots, slot + core * slots, slot - core * slots).astype(F32)
            lane = lax.broadcasted_iota(jnp.int32, (tokens, experts), 1)
            gate_grad = jnp.zeros((tokens, experts), F32)
            for e in range(experts):
                found = jnp.where(slot == places[:, e : e + 1], dg_ref[e, 0:1, :], 0.0)
                gate_grad = jnp.where(lane == e, jnp.sum(found, axis=1, keepdims=True), gate_grad)
            mean = jnp.sum(gate * gate_grad, axis=1, keepdims=True)
            logit_grad = gate * (gate_grad - mean)
            dl_s[here, :] = logit_grad
            total += lax.dot_general(
                logit_grad, router, NN, precision=HIGHEST, preferred_element_type=F32
            )
            db_s[here, :] = total + base_ref[here, :].astype(F32)
            return carry

        lax.fori_loop(0, span // tokens, gather, 0)
        db_out[...] = db_s[away, :].astype(BF16)
        swap_b = to_other(db_out, db_in.at[0], 0)
        swap_b.start()
        sums_s[...] = jnp.zeros_like(sums_s)
        sums_s[2 : 2 + experts, :] = lax.dot_general(
            dl_s[...], b_ref[...].astype(F32), TN, precision=HIGHEST, preferred_element_type=F32
        )
        swap_b.wait()
        db = db_s[own, :] + db_in[0].astype(F32)
        back, sums_s[1:2, :] = norm_back(db, h_ref[...], rows_ref[1:2, :])
        rows = d_ref[own, :].astype(F32) + back
        dh_s[...] = rows
        db_out[...] = rows.astype(BF16)
        grad_s[own, :] = rows.astype(BF16)
        swap_a = to_other(db_out, db_in.at[1], 1)
        swap_a.start()
        da_s[...] = jnp.zeros_like(da_s)
        swap_a.wait()
        grad_s[away, :] = db_in[1]

    grad_rows = grad_s[...]
    dctx_s[...] = mm(grad_rows, wo_ref[...], NN).astype(BF16)
    gw_s[step, :, 3 * LANES :] = mm(grad_rows, ctx_ref[...], TN).astype(BF16)
    dk_s[...] = jnp.zeros_like(dk_s)
    dv_s[...] = jnp.zeros_like(dv_s)
    scale = jnp.asarray(HD**-0.5, BF16)
    for index in range(span // block):
        keys = (index + 1) * block
        start = index * block
        query_rows = qkv_ref[start:keys, :LANES] * scale
        key_rows = qkv_ref[:keys, LANES : 2 * LANES]
        value_rows = qkv_ref[:keys, 2 * LANES :]
        context_grad = dctx_s[start:keys, :]
        row = lax.broadcasted_iota(jnp.int32, (keys, block), 0)
        column = start + lax.broadcasted_iota(jnp.int32, (keys, block), 1)
        allowed = (row <= column) & (row < length)
        dq_total = None
        for head in range(LANES // HD):
            lanes = head_lanes((block, LANES), head)
            masked_query = jnp.where(lanes, query_rows, jnp.zeros_like(query_rows))
            masked_grad = jnp.where(lanes, context_grad, jnp.zeros_like(context_grad))
            scores = jnp.where(allowed, mm(key_rows, masked_query, NT), -1e30)
            peak = jnp.max(scores, axis=0, keepdims=True)
            powers = jnp.exp(scores - peak)
            total = jnp.sum(powers, axis=0, keepdims=True)
            prob = powers * (1.0 / total)
            prob_grad = mm(value_rows, masked_grad, NT)
            inner = jnp.sum(prob * prob_grad, axis=0, keepdims=True)
            score_grad = (prob * (prob_grad - inner)).astype(BF16)
            dk_s[:keys, :] += mm(score_grad, masked_query, NN)
            dv_s[:keys, :] += mm(prob.astype(BF16), masked_grad, NN)
            dq_part = mm(score_grad, key_rows, TN)
            dq_total = dq_part if head == 0 else jnp.where(lanes, dq_part, dq_total)
        dq_s[start:keys, :] = dq_total * (HD**-0.5)
    cosine, sine = cos_ref[...], sin_ref[...]
    dq, dk = dq_s[...], dk_s[...]
    dq = (dq * cosine - partner(dq) * sine).astype(BF16)
    dk = (dk * cosine - partner(dk) * sine).astype(BF16)
    grads = jnp.concatenate([dq, dk, dv_s[...].astype(BF16)], axis=1)
    gw_s[step, :, : 3 * LANES] = mm(a_ref[...], grads, TN).astype(BF16)
    if sends:
        give(step)
    else:
        gw_ref[step] = gw_s[step]
    da_s[...] += mm(grads, w_ref[...], NT)

    @pl.when(step == last)
    def _():
        db_out[...] = da_s[away, :].astype(BF16)
        swap_d = to_other(db_out, db_in.at[0], 2)
        swap_d.start()
        swap_d.wait()
        da = da_s[own, :] + db_in[0].astype(F32)
        back, sums_s[0:1, :] = norm_back(da, x_ref[...].astype(F32), rows_ref[0:1, :])
        swap_s = to_other(sums_s, sums_in, 3)
        swap_s.start()
        gi_ref[...] = (dh_s[...] + back).astype(BF16)
        swap_s.wait()
        turned = (sums_s[...] + sums_in[...]).T
        if sends:
            turned_s[...] = jnp.zeros_like(turned_s)
            turned_s[:, : turned.shape[1]] = turned
            give(small)
            pltpu.make_async_copy(early_ref, early_in, y_local.at[2]).wait()
            put_experts(early_in, pl.ds(0, early_in.shape[-1]))
        for copy in own_rows():
            copy.wait()
        for k in range(1, experts):
            y_copy(k).wait()
        mine = lax.rem(me, experts)

        def near(rows):
            table = [places_ref[pl.ds(flip(mine, k), 1), rows] for k in range(experts)]
            return jnp.concatenate(table, axis=0).T

        def add(index, carry):
            here, _, total = put_together(near, yh_s, index, 256)
            db_s[here, :] = total + sy_ref[here, :].astype(F32)
            return carry

        lax.fori_loop(0, span // 256, add, 0)
        db_out[...] = db_s[away, :].astype(BF16)
        swap_y = to_other(db_out, db_in.at[1], 4)
        swap_y.start()
        swap_y.wait()
        out = db_s[own, :] + db_in[1].astype(F32)
        lo_ref[...] = (h_ref[...] + out).astype(BF16)
        if sends:
            take(late)
            put_experts(late_in, pl.ds(early_in.shape[-1], late_in.shape[-1]))
            for k in range(1, 4):
                z_copy(k).wait()
            total = all_ranks(total_ref)
            hidden = total.shape[1] // 3
            for kind in range(3):
                gsh_refs[kind][...] = total[:, kind * hidden : (kind + 1) * hidden]
            for pair in range(pairs):
                take(pair)
                total = all_ranks(gw_ref, pair)
                for kind in range(4):
                    go_refs[kind][:, pair * LANES : (pair + 1) * LANES] = total[
                        :, kind * LANES : (kind + 1) * LANES
                    ]
            take(small)
            gs_ref[...] = all_ranks(small_in)
        else:
            gs_ref[:, : turned.shape[1]] = turned


def attn_backward(
    length, places, gates, rows, dx_home, gate_grads, y_near, shared_y, shares, late, early,
    shared_dx, ffn_in, hidden_rows, grad_ffn, layer_rows, attn_in, first_all, qkv_rot, context,
    cosine, sine, ranks, halves,
):
    span, width = attn_in.shape
    half = span // 2
    experts = places.shape[0]
    pairs = context.shape[1] // LANES
    shard = width // ranks
    sends = halves
    far = pl.BlockSpec(memory_space=pl.ANY)
    if sends:
        hidden = shares.shape[-1] // 3
        forms = (
            [(shard, pairs * LANES)] * 4
            + [(shard, experts, hidden)] * 3
            + [(shard, hidden)] * 3
            + [(shard, LANES)]
        )
        outs = [(form, F32) for form in forms]
        extra = [
            pltpu.VMEM((ranks, pairs, shard, 4 * LANES), BF16),
            pltpu.VMEM(shares.shape, BF16),
            pltpu.VMEM(late.shape, BF16),
            pltpu.VMEM(early.shape, BF16),
            pltpu.VMEM((ranks, shard, LANES), F32),
        ]
    else:
        outs = [((pairs, width, 4 * LANES), BF16), ((width, LANES), F32)]
        extra = []
    outs = [((half, width), BF16)] * 2 + outs
    return pl.pallas_call(
        functools.partial(attn_bwd_kernel, block=256, ranks=ranks, halves=halves, sends=sends),
        grid=(pairs,),
        in_specs=[pl.BlockSpec(memory_space=pltpu.SMEM)]
        + [
            whole(v.shape)
            for v in (
                places, gates, rows, dx_home, gate_grads, shared_dx, ffn_in, hidden_rows, grad_ffn,
                layer_rows, attn_in,
            )
        ]
        + [
            pl.BlockSpec((width, 3 * LANES), lambda i: (0, i)),
            pl.BlockSpec((width, LANES), lambda i: (0, 3 * pairs + i)),
            pl.BlockSpec((span, 3 * LANES), lambda i: (0, i)),
            pl.BlockSpec((span, LANES), lambda i: (0, i)),
            whole((span, LANES)),
            whole((span, LANES)),
            whole((span, width)),
        ]
        + [far] * 4,
        out_specs=[whole(form) for form, _ in outs],
        out_shape=[jax.ShapeDtypeStruct(form, kind) for form, kind in outs],
        scratch_shapes=extra
        + [
            pltpu.VMEM((span, width), F32),
            pltpu.VMEM((span, experts), F32),
            pltpu.VMEM((half, width), BF16),
            pltpu.VMEM((2, half, width), BF16),
            pltpu.VMEM((half, width), F32),
            pltpu.VMEM((span, width), BF16),
            pltpu.VMEM((span, width), F32),
            pltpu.VMEM((16, width), F32),
            pltpu.VMEM((16, width), F32),
            pltpu.VMEM((width, LANES), F32),
            pltpu.VMEM(y_near.shape, BF16),
            pltpu.VMEM((pairs, width, 4 * LANES), BF16),
            pltpu.VMEM((span, LANES), BF16),
            pltpu.VMEM((span, LANES), F32),
            pltpu.VMEM((span, LANES), F32),
            pltpu.VMEM((span, LANES), F32),
            pltpu.SemaphoreType.DMA((pairs + 2, ranks)),
            pltpu.SemaphoreType.DMA((pairs + 2, ranks)),
            pltpu.SemaphoreType.DMA((pairs + 2,)),
            pltpu.SemaphoreType.DMA((5,)),
            pltpu.SemaphoreType.DMA((5,)),
            pltpu.SemaphoreType.DMA((experts,)),
            pltpu.SemaphoreType.DMA((experts,)),
            pltpu.SemaphoreType.DMA((3,)),
            pltpu.SemaphoreType.DMA((4,)),
            pltpu.SemaphoreType.DMA((4,)),
        ],
        compiler_params=remote_params(5),
        cost_estimate=cost(40e9, 40e6, 6e6),
        name="attn_bwd",
    )(
        length, places, gates, rows, dx_home, gate_grads, shared_dx, ffn_in, hidden_rows, grad_ffn,
        layer_rows, attn_in, first_all, first_all, qkv_rot, context, cosine, sine, shared_y,
        y_near, shares, late, early,
    )


def column_of(row):
    count = row.shape[1]
    shape = (count, count)
    same = lax.broadcasted_iota(jnp.int32, shape, 0) == lax.broadcasted_iota(jnp.int32, shape, 1)
    return jnp.sum(jnp.where(same, row, 0.0), axis=1, keepdims=True)


def row_of(column):
    count = column.shape[0]
    shape = (count, count)
    same = lax.broadcasted_iota(jnp.int32, shape, 0) == lax.broadcasted_iota(jnp.int32, shape, 1)
    return jnp.sum(jnp.where(same, column, 0.0), axis=0, keepdims=True)


def ffn_block(x, grad, gate, gate_w, up_w, down_w, sums):
    gate_pre = mm(x, gate_w, NN)
    up_pre = mm(x, up_w, NN)
    sig = jax.nn.sigmoid(gate_pre)
    act = gate_pre * sig
    inner = (act * up_pre).astype(BF16)
    out = mm(inner, down_w, NT)
    gate_grad, out_grad = None, grad
    if gate is not None:
        wide = grad.astype(F32)
        gate_grad = jnp.sum(out * wide, axis=1, keepdims=True)
        out = out * gate
        out_grad = (wide * gate).astype(BF16)
    inner_grad = mm(out_grad, down_w, NN)
    gate_pre_grad = (inner_grad * up_pre * (sig + act * (1.0 - sig))).astype(BF16)
    up_pre_grad = (inner_grad * act).astype(BF16)
    row_grad = mm(gate_pre_grad, gate_w, NT) + mm(up_pre_grad, up_w, NT)
    sums[0][...] += mm(x, gate_pre_grad, TN)
    sums[1][...] += mm(x, up_pre_grad, TN)
    sums[2][...] += mm(out_grad, inner, TN)
    return out, row_grad, gate_grad


def sides(rank):
    x, y = lax.rem(rank, 2), lax.rem(lax.div(rank, 2), 2)
    return x, y, flip(rank, 1), flip(rank, 2)


def block_of(x_ref, d_ref, g_ref, w_refs, sums):
    slots, width = x_ref.shape[1:]
    shape = (width, w_refs[0].shape[-1])
    gate = column_of(jnp.concatenate([g_ref[0, 0:1, :], g_ref[1, 0:1, :]], axis=1))
    return ffn_block(
        x_ref[...].reshape(2 * slots, width), d_ref[...].reshape(2 * slots, width), gate,
        *(w_ref[...].reshape(shape) for w_ref in w_refs), sums,
    )


def put_sums(og_ref, sums):
    for index, total in enumerate(sums):
        og_ref[:, index] = total[...].astype(BF16).reshape(og_ref.shape[0], *og_ref.shape[2:])


def expert_first_kernel(
    x_ref, d_ref, g_ref, wg_ref, wu_ref, wd_ref, share_ref,
    y_ref, dx_ref, dg_ref, og_ref, sx_ref, sy_ref,
    ag, au, ad, own_x, own_y, in_x, in_y, send, recv, local, *, halves,
):
    step = pl.program_id(0)
    sums = (ag, au, ad)
    me, core = lax.axis_index("dp"), lax.axis_index("tensor")
    x, y, x_rank, y_rank = sides(me)
    cut = share_ref.shape[-1] // 2
    low, high = pl.ds(0, cut), pl.ds(cut, cut)

    def over_x(place):
        return share_ref.at[:, :, place, :, low]

    def over_y(place):
        return share_ref.at[:, place, :, :, high]

    def copies():
        return (
            remote(over_x(1 - x), in_x, send.at[0], recv.at[0], device(x_rank, core)),
            remote(over_y(1 - y), in_y, send.at[1], recv.at[1], device(y_rank, core)),
        )

    def loads():
        return (
            pltpu.make_async_copy(over_x(x), own_x, local.at[0]),
            pltpu.make_async_copy(over_y(y), own_y, local.at[1]),
        )

    @pl.when(step == 0)
    def _():
        for total in sums:
            total[...] = jnp.zeros_like(total)
        if halves:
            greet([device(x_rank, core), device(y_rank, core)])
            for copy in copies() + loads():
                copy.start()

    out, row_grad, gate_grad = block_of(x_ref, d_ref, g_ref, (wg_ref, wu_ref, wd_ref), sums)
    y_ref[...] = out
    dx_ref[...] = row_grad
    dg_ref[...] = jnp.broadcast_to(row_of(gate_grad), dg_ref.shape)

    @pl.when(step == pl.num_programs(0) - 1)
    def _():
        put_sums(og_ref, sums)
        if halves:
            for copy in copies() + loads():
                copy.wait()
            sx_ref[...] = (own_x[...].astype(F32) + in_x[...].astype(F32)).astype(BF16)
            sy_ref[...] = (own_y[...].astype(F32) + in_y[...].astype(F32)).astype(BF16)


def expert_specs(experts, slots, width, weights, order):
    def group(shape):
        return pl.BlockSpec((None,) + shape, lambda i: (order(i),) + (0,) * len(shape))

    parts, _, shard, hidden = weights.shape
    matrices = [
        pl.BlockSpec(
            (parts, None, shard, hidden), lambda i, k=k: (0, k, 0, 0),
            pipeline_mode=pl.Buffered(1),
        )
        for k in range(3)
    ]
    return group, matrices, [pltpu.VMEM((width, hidden), F32)] * 3


def expert_first(x_slots, d_slots, g_slots, weights, shares, halves):
    experts, _, slots, width = x_slots.shape
    hidden = weights.shape[-1]
    group, matrices, sums = expert_specs(experts, slots, width, weights, lambda i: i)
    rows = group((2, slots, width))
    if halves:
        _, _, _, shard, columns = shares.shape
        part = (shares.shape[0], 2, shard, columns // 2)
    else:
        part = (1, 1, 16, LANES)
    return pl.pallas_call(
        functools.partial(expert_first_kernel, halves=halves),
        grid=(experts,),
        in_specs=[rows, rows, group((2, 8, slots))]
        + matrices
        + [pl.BlockSpec(memory_space=pl.ANY)],
        out_specs=[group((2 * slots, width))] * 2
        + [group((8, 2 * slots)), whole(weights.shape), whole(part), whole(part)],
        out_shape=[jax.ShapeDtypeStruct((experts, 2 * slots, width), F32)] * 2
        + [
            jax.ShapeDtypeStruct((experts, 8, 2 * slots), F32),
            jax.ShapeDtypeStruct(weights.shape, BF16),
            jax.ShapeDtypeStruct(part, BF16),
            jax.ShapeDtypeStruct(part, BF16),
        ],
        scratch_shapes=sums
        + [pltpu.VMEM(part, BF16)] * 4
        + [pltpu.SemaphoreType.DMA((2,))] * 3,
        compiler_params=remote_params(6) if halves else params(1),
        cost_estimate=cost(36 * experts * slots * width * hidden, 40e6),
        name="expert_first",
    )(x_slots, d_slots, g_slots, weights, weights, weights, shares)


def expert_second_kernel(
    x_ref, d_ref, g_ref, wg_ref, wu_ref, wd_ref, yf_ref, dxf_ref, dgf_ref, sx_ref, sy_ref,
    y_ref, dx_home, dg_home, og_ref, share_ref,
    ag, au, ad, own_y, own_dx, ys, dxs, yp, dxp, dgs, out_x, out_y, in_x, in_y,
    core_send, core_recv, send, recv, local, share_send, share_recv, *, experts, halves,
):
    step = pl.program_id(0)
    block = experts - 1 - step
    sums = (ag, au, ad)
    me, core = lax.axis_index("dp"), lax.axis_index("tensor")
    mine = lax.rem(me, experts)
    other = device(me, 1 - core)
    slots = x_ref.shape[1]
    x, y, x_rank, y_rank = sides(me)

    def rank_at(k):
        total, bit = me - mine, 1
        while bit < experts:
            total += bit * lax.rem(lax.div(mine, bit) + lax.div(k, bit), 2)
            bit *= 2
        return total

    def core_copy(k, part):
        src, dst = ((ys, yp), (dxs, dxp))[part]
        return remote(
            src.at[lax.rem(k, 2)], dst.at[k], core_send.at[part, k], core_recv.at[part, k], other
        )

    def home_copy(k, part):
        src, dst = ((dxp, dx_home), (dgs, dg_home))[part]
        return remote(
            src.at[k], dst.at[mine], send.at[part, k], recv.at[part, k],
            device(rank_at(k), core),
        )

    def own_copy(part):
        src, dst = ((dxp, dx_home), (dgs, dg_home))[part]
        return pltpu.make_async_copy(src.at[0], dst.at[mine], local.at[part])

    def go_home(k, part):
        @pl.when(k == 0)
        def _():
            own_copy(part).start()

        @pl.when(k > 0)
        def _():
            home_copy(k, part).start()

    def share_copies():
        return (
            remote(out_x, in_x, share_send.at[0], share_recv.at[0], device(y_rank, core)),
            remote(out_y, in_y, share_send.at[1], share_recv.at[1], device(x_rank, core)),
        )

    @pl.when(step == 0)
    def _():
        greet(cluster_and_core(experts))
        for total in sums:
            total[...] = jnp.zeros_like(total)
        if halves:
            out_x[...] = sx_ref[:, pl.ds(1 - y, 1)]
            out_y[...] = sy_ref[:, pl.ds(1 - x, 1)]
            for copy in share_copies():
                copy.start()

    def settle(k):
        for part in (1, 0):
            core_copy(k, part).wait_recv()
            own, shared = ((own_y, yp), (own_dx, dxp))[part]
            total = (own[...] + shared[k].astype(F32)).astype(BF16)
            if part:
                dxp[k] = total
                go_home(k, 0)
            else:
                y_ref[...] = total

    @pl.when(step < experts)
    def _():
        out, row_grad, gate_grad = block_of(x_ref, d_ref, g_ref, (wg_ref, wu_ref, wd_ref), sums)
        out += yf_ref[...]
        row_grad += dxf_ref[...]

        @pl.when(step >= 1)
        def _():
            settle(block + 1)

        for part in (1, 0):

            @pl.when(step >= 2)
            def _():
                core_copy(block + 2, part).wait_send()

            own, half = ((own_y, ys), (own_dx, dxs))[part]
            value = (out, row_grad)[part]
            own[...] = value[:slots]
            half[lax.rem(block, 2)] = value[slots:].astype(BF16)
            core_copy(block, part).start()
        dgs[block] = jnp.broadcast_to(row_of(gate_grad), dgs.shape[1:]) + dgf_ref[...]
        go_home(block, 1)

    @pl.when(step == experts)
    def _():
        settle(block + 1)
        put_sums(og_ref, sums)
        if halves:
            cut = out_x.shape[-1]
            for copy in share_copies():
                copy.wait()
            kept_x, kept_y = sx_ref[:, pl.ds(y, 1)], sy_ref[:, pl.ds(x, 1)]
            total_x = kept_x.astype(F32) + in_x[...].astype(F32)
            total_y = kept_y.astype(F32) + in_y[...].astype(F32)
            share_ref[:, :, :cut] = total_x.astype(BF16).reshape(share_ref.shape[0], -1, cut)
            share_ref[:, :, cut:] = total_y.astype(BF16).reshape(share_ref.shape[0], -1, cut)
        for part in (0, 1):
            for k in (0, 1):
                core_copy(k, part).wait_send()
            own_copy(part).wait()
            for k in range(1, experts):
                home_copy(k, part).wait()


def expert_second(x_slots, d_slots, g_slots, weights, first, halves):
    experts, _, slots, width = x_slots.shape
    hidden = weights.shape[-1]
    y_first, dx_first, dg_first, sx, sy = first
    far = pl.BlockSpec(memory_space=pl.ANY)
    group, matrices, sums = expert_specs(
        experts, slots, width, weights, lambda i: jnp.maximum(experts - 1 - i, 0)
    )
    rows = group((2, slots, width))
    long, _, shard, cut = sx.shape
    share = (long, shard, 2 * cut)
    return pl.pallas_call(
        functools.partial(expert_second_kernel, experts=experts, halves=halves),
        grid=(experts + 1,),
        in_specs=[rows, rows, group((2, 8, slots))]
        + matrices
        + [group((2 * slots, width))] * 2
        + [group((8, 2 * slots)), whole(sx.shape), whole(sy.shape)],
        out_specs=[
            pl.BlockSpec((None, slots, width), lambda i: (jnp.minimum(experts - i, experts - 1), 0, 0)),
            far,
            far,
            whole(weights.shape),
            whole(share),
        ],
        out_shape=[
            jax.ShapeDtypeStruct((experts, slots, width), BF16),
            jax.ShapeDtypeStruct((experts, slots, width), BF16),
            jax.ShapeDtypeStruct((experts, 8, 2 * slots), F32),
            jax.ShapeDtypeStruct(weights.shape, BF16),
            jax.ShapeDtypeStruct(share, BF16),
        ],
        scratch_shapes=sums
        + [pltpu.VMEM((slots, width), F32)] * 2
        + [pltpu.VMEM((2, slots, width), BF16)] * 2
        + [pltpu.VMEM((experts, slots, width), BF16)] * 2
        + [pltpu.VMEM((experts, 8, 2 * slots), F32)]
        + [pltpu.VMEM((long, 1, shard, cut), BF16)] * 4
        + [pltpu.SemaphoreType.DMA((2, experts))] * 4
        + [pltpu.SemaphoreType.DMA((2,))] * 3,
        compiler_params=remote_params(3),
        cost_estimate=cost(36 * experts * slots * width * hidden, 40e6),
        name="expert_second",
    )(x_slots, d_slots, g_slots, weights, weights, weights, y_first, dx_first, dg_first, sx, sy)


def to_all(values, groups=None):
    count = lax.axis_size("dp") if groups is None else len(groups[0])
    copies = jnp.broadcast_to(values[None], (count,) + values.shape)
    return lax.all_to_all(copies, "dp", 0, 0, axis_index_groups=groups, tiled=True)


def after(values, *earlier):
    return lax.optimization_barrier((values,) + earlier)[0]


def per_device(
    layer_input, seq_lengths, expert_routes, w_query, w_key, w_value, w_output,
    gain_attn, gain_ffn, router_weight, expert_gate, expert_up, expert_down,
    shared_gate, shared_up, shared_down, out_cotangent,
):
    ranks = lax.axis_size("dp")
    _, own_len, width = layer_input.shape
    span = 2 * own_len
    shard = w_query.shape[0]
    pairs = w_query.shape[1] // LANES
    experts, hidden = expert_gate.shape[1:]
    capacity = 4 * span // experts
    slots = capacity // 2
    groups = [list(range(s, s + experts)) for s in range(0, ranks, experts)]

    qkv_own = jnp.stack([w_query, w_key, w_value], axis=1).reshape(shard, 3, pairs, LANES)
    qkv_own = qkv_own.transpose(0, 2, 1, 3).reshape(shard, pairs * 3 * LANES)
    small_own = jnp.concatenate(
        [gain_attn[:, None], gain_ffn[:, None], router_weight], axis=1
    )
    small_own = jnp.pad(small_own, ((0, 0), (0, LANES - small_own.shape[1])))
    first_own = jnp.concatenate([qkv_own, w_output, small_own], axis=1).astype(BF16)
    half = HD // 2
    inverse = np.exp(np.arange(half, dtype=np.float32) * np.float32(-math.log(10000.0) / half))
    angles = np.arange(span, dtype=np.float32)[:, None] * inverse[None, :]
    cos_half, sin_half = np.cos(angles), np.sin(angles)
    cosine = np.concatenate([cos_half] * 4, axis=1)
    sine = np.concatenate([-sin_half, sin_half] * 2, axis=1)

    direct = shard % 16 == 0
    halves = ranks == 16
    first_all = gather_all(first_own).reshape(width, first_own.shape[1])

    def to_experts(columns, *earlier):
        stack = jnp.stack(
            [w[:, :, columns] for w in (expert_gate, expert_up, expert_down)], axis=0
        ).astype(BF16)
        part = stack.shape[-1]
        stack = stack.transpose(2, 0, 1, 3).reshape(1, experts, 3 * shard, part)
        stack = jnp.broadcast_to(stack, (ranks // experts, experts, 3 * shard, part))
        stack = after(stack.reshape(ranks, 3 * shard, part), *earlier)
        gathered = lax.all_to_all(stack, "dp", 0, 0, tiled=True).reshape(ranks, 3, shard, part)
        if not direct:
            gathered = gathered.transpose(1, 0, 2, 3).reshape(1, 3, width, part)
        return gathered

    def from_experts(grads):
        if not direct:
            grads = grads.reshape(3, ranks, shard, grads.shape[-1]).transpose(1, 0, 2, 3)
        return lax.all_to_all(grads, "dp", 0, 0, tiled=True)

    def to_outputs(grads):
        grads = grads.reshape(ranks // experts, experts, 3, shard, grads.shape[-1])
        return jnp.sum(grads.astype(F32), axis=0)

    early = to_experts(slice(0, hidden // 2), first_all)

    shared_own = jnp.concatenate([shared_gate, shared_up, shared_down], axis=1).astype(BF16)
    (
        attn_in, qkv_rot, context, hidden_rows, ffn_in, grad_ffn, places, small, gates, shared_y,
        shared_dx, d_slots, x_slots, g_slots, shared_grads, _,
    ) = attn_forward(
        seq_lengths, layer_input[0], out_cotangent[0], expert_routes.reshape(span, 2).T,
        first_all, shared_own, cosine, sine, experts, slots,
    )
    late = to_experts(slice(hidden // 2, hidden), early, places)

    if halves:
        shares = shared_grads.reshape(4, 2, 2, shard, 3 * hidden)
    else:
        shares = shared_grads[0, :16, :LANES]
        shared_grads = lax.all_to_all(
            shared_grads.reshape(ranks, shard, 3 * hidden), "dp", 0, 0, tiled=True
        )

    y_first, dx_first, dg_first, early_grads, sx, sy = expert_first(
        x_slots, d_slots, g_slots, early, shares, halves
    )
    early_grads = from_experts(early_grads)
    y_near, dx_home, gate_grads, late_grads, shares = expert_second(
        x_slots, d_slots, g_slots, late, (y_first, dx_first, dg_first, sx, sy), halves
    )

    grad_input, layer_output, *grads = attn_backward(
        seq_lengths, places, gates, small, dx_home, gate_grads, y_near, shared_y, shares,
        late_grads, early_grads, shared_dx, ffn_in, hidden_rows, grad_ffn, layer_input[0], attn_in,
        first_all, qkv_rot, context, cosine, sine, ranks, halves,
    )
    if halves:
        attn_grads, expert_grads, shared_grads, small_grads = (
            grads[:4], grads[4:7], grads[7:10], grads[10]
        )
    else:
        attn_grads = grads[0].reshape(pairs, ranks, shard, 4 * LANES).transpose(1, 0, 2, 3)
        attn_grads = lax.all_to_all(attn_grads, "dp", 0, 0, tiled=True)
        attn_grads = jnp.sum(attn_grads.astype(F32), axis=0).reshape(pairs, shard, 4, LANES)
        attn_grads = [
            attn_grads[:, :, k].transpose(1, 0, 2).reshape(shard, pairs * LANES) for k in range(4)
        ]
        small_grads = lax.all_to_all(grads[1].reshape(ranks, shard, LANES), "dp", 0, 0, tiled=True)
        small_grads = jnp.sum(small_grads, axis=0)
        shared_grads = jnp.sum(shared_grads.astype(F32), axis=0)
        shared_grads = [shared_grads[:, k * hidden : (k + 1) * hidden] for k in range(3)]
        late_grads = from_experts(late_grads)
        expert_grads = jnp.concatenate([to_outputs(early_grads), to_outputs(late_grads)], axis=-1)
        expert_grads = [expert_grads[:, k].transpose(1, 0, 2) for k in range(3)]
    return (
        layer_output[None], grad_input[None],
        attn_grads[0], attn_grads[1], attn_grads[2], attn_grads[3],
        small_grads[:, 0], small_grads[:, 1], small_grads[:, 2 : 2 + experts],
        expert_grads[0], expert_grads[1], expert_grads[2],
        shared_grads[0], shared_grads[1], shared_grads[2],
    )


def solution(mesh):
    tokens = P("dp", "tensor", None)
    matrix = P("dp", "tensor")
    expert = P("dp", None, "tensor")
    in_specs = (
        (tokens, P("dp"), P("dp", None, None))
        + (matrix,) * 4
        + (P("dp"), P("dp"), P("dp", None))
        + (expert,) * 3
        + (matrix,) * 3
        + (tokens,)
    )
    out_specs = (
        (tokens, tokens)
        + (matrix,) * 4
        + (P("dp"), P("dp"), P("dp", None))
        + (expert,) * 3
        + (matrix,) * 3
    )
    return jax.shard_map(
        per_device, mesh=mesh, in_specs=in_specs, out_specs=out_specs, check_vma=False
    )
```

```python
import functools
import math

import jax
import jax.numpy as jnp
import numpy as np
from jax import lax
from jax.experimental import pallas as pl
from jax.experimental.pallas import tpu as pltpu
from jax.sharding import PartitionSpec as P

HD = 64
LANES = 128
EPS = 1e-06
F32 = jnp.float32
BF16 = jnp.bfloat16
HIGHEST = lax.Precision.HIGHEST
VMEM_LIMIT = 60 * 1024 * 1024

NN = (((1,), (0,)), ((), ()))
NT = (((1,), (1,)), ((), ()))
TN = (((0,), (0,)), ((), ()))


def mm(left, right, dims):
    return lax.dot_general(left, right, dims, preferred_element_type=F32)


def params(count):
    return pltpu.CompilerParams(
        dimension_semantics=("arbitrary",) * count, vmem_limit_bytes=VMEM_LIMIT
    )


def remote_params(number):
    return pltpu.CompilerParams(
        collective_id=number, has_side_effects=True, vmem_limit_bytes=VMEM_LIMIT,
        dimension_semantics=("arbitrary",),
    )


def cost(flops, nbytes, trans=0):
    return pl.CostEstimate(flops=int(flops), bytes_accessed=int(nbytes), transcendentals=int(trans))


def flip(index, offset):
    bit = 1
    while bit <= offset:
        if offset & bit:
            index = index + bit - 2 * bit * lax.rem(lax.div(index, bit), 2)
        bit *= 2
    return index


def device(rank, core):
    return {"dp": rank, "tensor": core}


def greet(devices):
    barrier = pltpu.get_barrier_semaphore()
    for target in devices:
        pl.semaphore_signal(barrier, inc=1, device_id=target, device_id_type=pl.DeviceIdType.MESH)
    pl.semaphore_wait(barrier, len(devices))


def remote(src, dst, send, recv, target):
    return pltpu.make_async_remote_copy(
        src_ref=src, dst_ref=dst, send_sem=send, recv_sem=recv,
        device_id=target, device_id_type=pl.DeviceIdType.MESH,
    )


class Gather:
    order = (0, 1, 4, 2, 5, 3, 6)
    turns = 9

    def __init__(self, own_ref, out_ref, sems, which):
        self.own_ref, self.out_ref = own_ref, out_ref
        self.own_sem, self.z_send, self.z_recv, self.s_send, self.s_recv, self.f_send, self.f_recv = (
            sem.at[which] for sem in sems
        )
        self.cut = own_ref.shape[1] // 2 // LANES * LANES
        self.me, self.core = lax.axis_index("dp"), lax.axis_index("tensor")
        self.z = lax.div(self.me, 4)
        self.up, self.down = lax.min(self.me + 4, 15), lax.max(self.me - 4, 0)
        self.sides_of = (flip(self.me, 1), flip(self.me, 2))

    @staticmethod
    def semaphores(count):
        dma = pltpu.SemaphoreType.DMA
        return [dma((count,)), dma((count, 6)), dma((count, 6))] + [dma((count, 2, 7))] * 4

    def rank_at(self, place):
        return self.me - 4 * place if place <= 3 else self.me + 4 * (place - 3)

    def at(self, place, body):
        if place == 0:
            body()
        else:
            pl.when(self.z >= place if place <= 3 else self.z + (place - 3) <= 3)(body)

    def own_copy(self):
        return pltpu.make_async_copy(self.own_ref, self.out_ref.at[self.me], self.own_sem)

    def z_copy(self, rank, step, upward):
        index = step - 1 if upward else step + 2
        return remote(
            self.own_ref if step == 1 else self.out_ref.at[rank], self.out_ref.at[rank],
            self.z_send.at[index], self.z_recv.at[index],
            device(self.up if upward else self.down, self.core),
        )

    def side_copy(self, rank, place, axis):
        return remote(
            self.own_ref if place == 0 else self.out_ref.at[rank], self.out_ref.at[rank],
            self.s_send.at[axis, place], self.s_recv.at[axis, place],
            device(self.sides_of[axis], self.core),
        )

    def onward_copy(self, rank, place, axis):
        width = self.own_ref.shape[1]
        columns = pl.ds(0, self.cut) if axis == 0 else pl.ds(self.cut, width - self.cut)
        part = self.out_ref.at[rank, :, columns]
        return remote(
            part, part, self.f_send.at[axis, place], self.f_recv.at[axis, place],
            device(self.sides_of[1 - axis], self.core),
        )

    def begin(self):
        self.own_copy().start()
        pl.when(self.z < 3)(lambda: self.z_copy(self.me, 1, True).start())
        pl.when(self.z > 0)(lambda: self.z_copy(self.me, 1, False).start())
        for axis in range(2):
            self.side_copy(self.me, 0, axis).start()

    def arrive(self, place):
        upward = place <= 3
        step = place if upward else place - 3
        rank = self.rank_at(place)
        self.z_copy(rank, step, upward).wait_recv()
        if step < 3:
            further = self.z < 3 if upward else self.z > 0
            pl.when(further)(lambda: self.z_copy(rank, step + 1, upward).start())
        for axis in range(2):
            self.side_copy(rank, place, axis).start()

    def onward(self, place):
        for axis in range(2):
            rank = flip(self.rank_at(place), 1 + axis)
            self.side_copy(rank, place, axis).wait_recv()
            self.onward_copy(rank, place, axis).start()

    def turn(self, index):
        if index < 7:
            self.at(self.order[index], functools.partial(self.arrive, self.order[index]))
        if index >= 2:
            self.at(self.order[index - 2], functools.partial(self.onward, self.order[index - 2]))

    def finish(self, place):
        for axis in range(2):
            rank = flip(self.rank_at(place), 1 + axis)
            self.side_copy(self.rank_at(place), place, axis).wait_send()
            self.onward_copy(rank, place, axis).wait_send()
            self.onward_copy(flip(self.rank_at(place), 3), place, axis).wait_recv()

    def end(self):
        z = self.z
        for place in self.order:
            self.at(place, functools.partial(self.finish, place))
        for step in range(1, 4):
            pl.when((z < 3) & (z >= step - 1))(
                lambda step=step: self.z_copy(self.me - 4 * (step - 1), step, True).wait_send()
            )
            pl.when((z > 0) & (z + step - 1 <= 3))(
                lambda step=step: self.z_copy(self.me + 4 * (step - 1), step, False).wait_send()
            )
        self.own_copy().wait()


def gather_kernel(
    wq_ref, wk_ref, wv_ref, wo_ref, small_ref, sg_ref, su_ref, sd_ref, first_out, shared_out,
    first_s, shared_s, *sems,
):
    pairs = wq_ref.shape[1] // LANES
    for pair in range(pairs):
        columns = slice(pair * LANES, (pair + 1) * LANES)
        for kind, ref in enumerate((wq_ref, wk_ref, wv_ref)):
            start = (3 * pair + kind) * LANES
            first_s[:, start : start + LANES] = ref[:, columns].astype(BF16)
    first_s[:, 3 * pairs * LANES : 4 * pairs * LANES] = wo_ref[...].astype(BF16)
    first_s[:, 4 * pairs * LANES :] = small_ref[...].astype(BF16)
    hidden = sg_ref.shape[1]
    for kind, ref in enumerate((sg_ref, su_ref, sd_ref)):
        shared_s[:, kind * hidden : (kind + 1) * hidden] = ref[...].astype(BF16)

    gathers = Gather(first_s, first_out, sems, 0), Gather(shared_s, shared_out, sems, 1)
    z, core = gathers[0].z, gathers[0].core
    barrier = pltpu.get_barrier_semaphore()

    def hello(rank):
        pl.semaphore_signal(
            barrier, inc=1, device_id=device(rank, core), device_id_type=pl.DeviceIdType.MESH
        )

    for rank in gathers[0].sides_of:
        hello(rank)
    pl.when(z < 3)(lambda: hello(gathers[0].up))
    pl.when(z > 0)(lambda: hello(gathers[0].down))
    pl.semaphore_wait(barrier, 2 + lax.min(z, 1) + lax.min(3 - z, 1))
    for gather in gathers:
        gather.begin()
    for turn in range(1, Gather.turns):
        for gather in gathers:
            gather.turn(turn)
    for gather in gathers:
        gather.end()


def gather_weights(attention, small, shared):
    ranks = lax.axis_size("dp")
    rows, heads_width = attention[0].shape
    columns = 4 * heads_width + LANES
    hidden = shared[0].shape[1]
    if ranks != 16:
        pairs = heads_width // LANES
        qkv = jnp.stack(attention[:3], axis=1).reshape(rows, 3, pairs, LANES)
        qkv = qkv.transpose(0, 2, 1, 3).reshape(rows, 3 * heads_width)
        first = jnp.concatenate([qkv, attention[3], small], axis=1).astype(BF16)
        return to_all(first), to_all(jnp.concatenate(shared, axis=1).astype(BF16))
    vmem = pl.BlockSpec(memory_space=pltpu.VMEM)
    return pl.pallas_call(
        gather_kernel,
        in_specs=[vmem] * 8,
        out_specs=[pl.BlockSpec(memory_space=pl.ANY)] * 2,
        out_shape=[
            jax.ShapeDtypeStruct((ranks, rows, columns), BF16),
            jax.ShapeDtypeStruct((ranks, rows, 3 * hidden), BF16),
        ],
        scratch_shapes=[
            pltpu.VMEM((rows, columns), BF16),
            pltpu.VMEM((rows, 3 * hidden), BF16),
        ]
        + Gather.semaphores(2),
        compiler_params=pltpu.CompilerParams(
            collective_id=1, has_side_effects=True, vmem_limit_bytes=VMEM_LIMIT
        ),
        cost_estimate=cost(1e6, 100e6),
        name="gather_weights",
    )(*attention, small, *shared)


def partner(values):
    lane = lax.broadcasted_iota(jnp.int32, values.shape, 1)
    return jnp.where(
        lane % HD < HD // 2,
        pltpu.roll(values, LANES - HD // 2, 1),
        pltpu.roll(values, HD // 2, 1),
    )


def head_lanes(shape, head):
    lane = lax.broadcasted_iota(jnp.int32, shape, 1)
    return (lane // HD) == head


def offsets(count):
    return sorted(range(1, count), key=lambda k: (bin(k).count("1"), k))


class Trip:
    def __init__(self, ins, outs, send, recv, core_send, core_recv, local, part):
        self.ins, self.outs, self.part = ins, outs, part
        self.send, self.recv, self.local = send, recv, local
        self.core_send, self.core_recv = core_send, core_recv
        self.me, self.core = lax.axis_index("dp"), lax.axis_index("tensor")
        self.count = ins.shape[0]

    def copy(self, k):
        return remote(
            self.ins.at[k], self.outs.at[k, 0],
            self.send.at[self.part, k], self.recv.at[self.part, k],
            device(flip(self.me, k), self.core),
        )

    def core_copy(self, k):
        src = self.ins.at[0] if k == 0 else self.outs.at[k, 0]
        return remote(
            src, self.outs.at[k, 1],
            self.core_send.at[self.part, k], self.core_recv.at[self.part, k],
            device(self.me, 1 - self.core),
        )

    def own(self):
        return pltpu.make_async_copy(self.ins.at[0], self.outs.at[0, 0], self.local.at[self.part])

    def go(self, k):
        if k:
            self.copy(k).start()
        else:
            self.own().start()
            self.core_copy(0).start()

    def pass_on(self, k):
        self.copy(k).wait_recv()
        self.core_copy(k).start()

    def end(self):
        self.own().wait()
        for k in range(self.count):
            self.core_copy(k).wait()
            if k:
                self.copy(k).wait_send()


def cluster_and_core(count):
    me, core = lax.axis_index("dp"), lax.axis_index("tensor")
    return [device(flip(me, k), core) for k in range(1, count)] + [device(me, 1 - core)]


def rms(values):
    return values * lax.rsqrt(jnp.mean(values * values, axis=-1, keepdims=True) + EPS)


def whole(shape):
    return pl.BlockSpec(shape, lambda i: (0,) * len(shape), pipeline_mode=pl.Buffered(1))


def attn_fwd_kernel(
    len_ref, x_ref, c_ref, routes_ref, w_ref, wo_ref, small_ref, shared_ref, cos_ref, sin_ref,
    a_ref, qkv_ref, ctx_ref, h_ref, b_ref, d_ref, places_ref, rows_ref, gates_ref, y_ref, dx_ref, dr, xr, gr, og_ref,
    ds, xs, gs, ag, au, ad, shared_w, part, x_in, h_in, b_out, b_in, c_out, c_in,
    send, recv, core_send, core_recv, local, pair_send, pair_recv, load, *, block,
):
    step = pl.program_id(0)
    me, core = lax.axis_index("dp"), lax.axis_index("tensor")
    other = device(me, 1 - core)
    experts, slots, _ = ds.shape
    trips = [
        Trip(ins, outs, send, recv, core_send, core_recv, local, index)
        for index, (ins, outs) in enumerate(((ds, dr), (xs, xr), (gs, gr)))
    ]
    slot = core * slots + lax.broadcasted_iota(jnp.int32, (slots, a_ref.shape[0]), 0)
    slot = slot.astype(F32)
    mine = lax.rem(me, experts)
    span, width = a_ref.shape
    half = span // 2
    length = len_ref[0]
    own = pl.ds(pl.multiple_of(core * half, half), half)
    away = pl.ds(pl.multiple_of((1 - core) * half, half), half)
    pairs = pl.num_programs(0)

    def to_other(src, dst, index):
        return remote(src, dst, pair_send.at[index], pair_recv.at[index], other)

    @pl.when(step == 0)
    def _():
        greet(cluster_and_core(experts))
        pltpu.make_async_copy(shared_ref, shared_w, load).start()
        token = core * half + lax.broadcasted_iota(jnp.int32, c_ref.shape, 0)
        valid = jnp.where(token < length, c_ref[...].astype(F32), 0.0).astype(BF16)
        c_out[...] = valid
        d_ref[own, :] = valid
        swap_c = to_other(c_out, c_in, 0)
        swap_c.start()
        swap_x = to_other(x_ref, x_in, 1)
        swap_x.start()

        name = lax.broadcasted_iota(jnp.int32, (experts, span), 0)
        chosen = (name == routes_ref[0:1, :]) | (name == routes_ref[1:2, :])
        earlier = lax.broadcasted_iota(jnp.int32, (span, span), 0) < lax.broadcasted_iota(
            jnp.int32, (span, span), 1
        )
        counts = mm(
            jnp.where(chosen, 1.0, 0.0).astype(BF16), jnp.where(earlier, 1.0, 0.0).astype(BF16), NN
        )
        places_ref[...] = jnp.where(chosen, counts, -1.0)

        swap_c.wait_recv()
        d_ref[away, :] = c_in[...]
        for k in offsets(experts) + [0]:
            place = places_ref[pl.ds(flip(mine, k), 1), :]
            hot = jnp.where(slot == place, 1.0, 0.0).astype(BF16)
            ds[k] = mm(hot, d_ref[...], NN).astype(BF16)
            trips[0].go(k)
        rows_ref[...] = small_ref[...].astype(F32).T[: rows_ref.shape[0], :]
        swap_x.wait_recv()
        gain = rows_ref[0:1, :]
        a_ref[own, :] = (rms(x_ref[...].astype(F32)) * gain).astype(BF16)
        a_ref[away, :] = (rms(x_in[...].astype(F32)) * gain).astype(BF16)
        part[...] = jnp.zeros_like(part)
        swap_c.wait_send()
        swap_x.wait_send()

    raw = mm(a_ref[...], w_ref[...], NN)
    cosine, sine = cos_ref[...], sin_ref[...]
    query, key = raw[:, :LANES], raw[:, LANES : 2 * LANES]
    qkv_ref[:, :LANES] = (query * cosine + partner(query) * sine).astype(BF16)
    qkv_ref[:, LANES : 2 * LANES] = (key * cosine + partner(key) * sine).astype(BF16)
    qkv_ref[:, 2 * LANES :] = raw[:, 2 * LANES :].astype(BF16)
    for index in range(span // block):
        keys = (index + 1) * block
        query_rows = qkv_ref[index * block : keys, :LANES] * jnp.asarray(HD**-0.5, BF16)
        key_rows = qkv_ref[:keys, LANES : 2 * LANES]
        value_rows = qkv_ref[:keys, 2 * LANES :]
        row = index * block + lax.broadcasted_iota(jnp.int32, (block, keys), 0)
        column = lax.broadcasted_iota(jnp.int32, (block, keys), 1)
        allowed = (column <= row) & (column < length)
        parts = []
        for head in range(LANES // HD):
            masked_query = jnp.where(
                head_lanes(query_rows.shape, head), query_rows, jnp.zeros_like(query_rows)
            )
            scores = jnp.where(allowed, mm(masked_query, key_rows, NT), -1e30)
            peak = jnp.max(scores, axis=1, keepdims=True)
            powers = jnp.exp(scores - peak)
            total = jnp.sum(powers, axis=1, keepdims=True)
            prob = (powers * (1.0 / total)).astype(BF16)
            parts.append(mm(prob, value_rows, NN))
        context = jnp.where(head_lanes(parts[0].shape, 0), parts[0], parts[1]).astype(BF16)
        ctx_ref[index * block : keys, :] = context
        part[index * block : keys, :] += mm(context, wo_ref[...], NT)

    @pl.when(step == pairs - 1)
    def _():
        swap_h = to_other(part.at[away], h_in, 2)
        swap_h.start()
        rows = x_ref[...].astype(F32) + part[own, :]
        swap_h.wait_recv()
        rows = rows + h_in[...]
        h_ref[...] = rows
        normed = (rms(rows) * rows_ref[1:2, :]).astype(BF16)
        b_out[...] = normed
        swap_b = to_other(b_out, b_in, 3)
        swap_b.start()
        b_ref[own, :] = normed
        swap_b.wait_recv()
        b_ref[away, :] = b_in[...]
        chosen = places_ref[...] >= 0
        logits = mm(rows_ref[2 : 2 + experts, :].astype(BF16), b_ref[...], NT)
        top = jnp.max(jnp.where(chosen, logits, -1e30), axis=0, keepdims=True)
        powers = jnp.where(chosen, jnp.exp(jnp.minimum(logits - top, 0.0)), 0.0)
        gates_ref[...] = powers / jnp.sum(powers, axis=0, keepdims=True)
        for k in offsets(experts) + [0]:
            target = pl.ds(flip(mine, k), 1)
            found = slot == places_ref[target, :]
            xs[k] = mm(jnp.where(found, 1.0, 0.0).astype(BF16), b_ref[...], NN).astype(BF16)
            trips[1].go(k)
            gate = jnp.sum(jnp.where(found, gates_ref[target, :], 0.0), axis=1, keepdims=True)
            gs[k] = jnp.broadcast_to(row_of(gate), gs.shape[1:])
            trips[2].go(k)
        swap_h.wait_send()
        swap_b.wait_send()
        for total in (ag, au, ad):
            total[...] = jnp.zeros_like(total)
        pltpu.make_async_copy(shared_ref, shared_w, load).wait()
        for k in offsets(experts):
            trips[0].pass_on(k)
        hidden = ag.shape[1]

        def matrix(index):
            return shared_w[:, :, index * hidden : (index + 1) * hidden].reshape(width, hidden)

        def branch(index, carry):
            rows = pl.ds(pl.multiple_of(index * block, block), block)
            out, row_grad, _ = ffn_block(
                b_ref[rows, :], d_ref[rows, :], None, matrix(0), matrix(1), matrix(2), (ag, au, ad)
            )
            y_ref[rows, :] = out.astype(BF16)
            dx_ref[rows, :] = row_grad.astype(BF16)
            return carry

        lax.fori_loop(0, span // block, branch, 0)
        for index, total in enumerate((ag, au, ad)):
            shared_w[:, :, index * hidden : (index + 1) * hidden] = (
                total[...].astype(BF16).reshape(shared_w.shape[0], -1, hidden)
            )
        write = pltpu.make_async_copy(shared_w, og_ref, load)
        write.start()
        for k in offsets(experts):
            trips[1].pass_on(k)
            trips[2].pass_on(k)
        for trip in trips:
            trip.end()
        write.wait()


def attn_forward(length, rows, cotangent, routes, first_all, shared_all, cosine, sine, experts, slots):
    half, width = rows.shape
    span = 2 * half
    pairs = (first_all.shape[1] - LANES) // (4 * LANES)
    far = pl.BlockSpec(memory_space=pl.ANY)
    hidden = shared_all.shape[-1] // 3
    return pl.pallas_call(
        functools.partial(attn_fwd_kernel, block=256),
        grid=(pairs,),
        in_specs=[
            pl.BlockSpec(memory_space=pltpu.SMEM),
            whole((half, width)),
            whole((half, width)),
            whole(routes.shape),
            pl.BlockSpec((width, 3 * LANES), lambda i: (0, i)),
            pl.BlockSpec((width, LANES), lambda i: (0, 3 * pairs + i)),
            pl.BlockSpec((width, LANES), lambda i: (0, 4 * pairs)),
            far,
            whole((span, LANES)),
            whole((span, LANES)),
        ],
        out_specs=[
            whole((span, width)),
            pl.BlockSpec((span, 3 * LANES), lambda i: (0, i)),
            pl.BlockSpec((span, LANES), lambda i: (0, i)),
            whole((half, width)),
            whole((span, width)),
            whole((span, width)),
            whole((experts, span)),
            whole((16, width)),
            whole((experts, span)),
            whole((span, width)),
            whole((span, width)),
        ]
        + [far] * 4,
        out_shape=[
            jax.ShapeDtypeStruct((span, width), BF16),
            jax.ShapeDtypeStruct((span, pairs * 3 * LANES), BF16),
            jax.ShapeDtypeStruct((span, pairs * LANES), BF16),
            jax.ShapeDtypeStruct((half, width), F32),
            jax.ShapeDtypeStruct((span, width), BF16),
            jax.ShapeDtypeStruct((span, width), BF16),
            jax.ShapeDtypeStruct((experts, span), F32),
            jax.ShapeDtypeStruct((16, width), F32),
            jax.ShapeDtypeStruct((experts, span), F32),
            jax.ShapeDtypeStruct((span, width), BF16),
            jax.ShapeDtypeStruct((span, width), BF16),
            jax.ShapeDtypeStruct((experts, 2, slots, width), BF16),
            jax.ShapeDtypeStruct((experts, 2, slots, width), BF16),
            jax.ShapeDtypeStruct((experts, 2, 8, slots), F32),
            jax.ShapeDtypeStruct(shared_all.shape, BF16),
        ],
        scratch_shapes=[
            pltpu.VMEM((experts, slots, width), BF16),
            pltpu.VMEM((experts, slots, width), BF16),
            pltpu.VMEM((experts, 8, slots), F32),
            pltpu.VMEM((width, hidden), F32),
            pltpu.VMEM((width, hidden), F32),
            pltpu.VMEM((width, hidden), F32),
            pltpu.VMEM(shared_all.shape, BF16),
            pltpu.VMEM((span, width), F32),
            pltpu.VMEM((half, width), BF16),
            pltpu.VMEM((half, width), F32),
        ]
        + [pltpu.VMEM((half, width), BF16)] * 4
        + [pltpu.SemaphoreType.DMA((3, experts))] * 4
        + [pltpu.SemaphoreType.DMA((3,))]
        + [pltpu.SemaphoreType.DMA((4,))] * 2
        + [pltpu.SemaphoreType.DMA],
        compiler_params=remote_params(4),
        cost_estimate=cost(20e9, 60e6, 6e6),
        name="attn_fwd",
    )(length, rows, cotangent, routes, first_all, first_all, first_all, shared_all, cosine, sine)


def norm_back(grad, values, gain):
    factor = lax.rsqrt(jnp.mean(values * values, axis=-1, keepdims=True) + EPS)
    normed = values * factor
    hat = grad * gain
    back = factor * (hat - normed * jnp.mean(hat * normed, axis=-1, keepdims=True))
    return back, jnp.sum(grad * normed, axis=0, keepdims=True)


def slot_table(places, experts, slots, offset):
    slot = lax.broadcasted_iota(jnp.int32, (places.shape[0], slots), 1) + offset
    slot = slot.astype(F32)
    return jnp.concatenate(
        [jnp.where(slot == places[:, e : e + 1], 1.0, 0.0).astype(BF16) for e in range(experts)],
        axis=1,
    )


def attn_bwd_kernel(
    len_ref, places_ref, gates_ref, rows_ref, dx_ref, dg_ref, base_ref, b_ref, h_ref, d_ref,
    x_ref, a_ref, w_ref, wo_ref, qkv_ref, ctx_ref, cos_ref, sin_ref, sy_ref, y_ref, share_ref, late_ref, early_ref,
    gi_ref, lo_ref, *rest, block, ranks, halves, sends,
):
    if sends:
        go_refs, gx_refs, gsh_refs, gs_ref = rest[:4], rest[4:7], rest[7:10], rest[10]
        sum_x, sum_y, in_x, in_y, sums, in_z, total_ref, late_in, early_in, small_in = rest[11:21]
        step_send, step_recv = rest[21:23]
        rest = rest[23:]
    else:
        gw_ref, gs_ref = rest[:2]
        rest = rest[2:]
    (
        db_s, dl_s, db_out, db_in, dh_s, grad_s, da_s, sums_s, sums_in, turned_s,
        yh_s, gw_s, dctx_s, dq_s, dk_s, dv_s, send, recv, local, pair_send, pair_recv,
        y_send, y_recv, y_local, z_send, z_recv,
    ) = rest
    step = pl.program_id(0)
    last = pl.num_programs(0) - 1
    me, core = lax.axis_index("dp"), lax.axis_index("tensor")
    other = device(me, 1 - core)
    experts, slots, width = dx_ref.shape
    span = a_ref.shape[0]
    half = span // 2
    length = len_ref[0]
    own = pl.ds(pl.multiple_of(core * half, half), half)
    away = pl.ds(pl.multiple_of((1 - core) * half, half), half)
    shard = width // ranks
    pairs = gw_s.shape[0]

    def to_other(src, dst, index):
        return remote(src, dst, pair_send.at[index], pair_recv.at[index], other)

    small, late = 0, 1

    def part_of(index, rank):
        rows = pl.ds(pl.multiple_of(rank * shard, shard), shard)
        return late_ref.at[rank] if index == late else turned_s.at[rows]

    def place_of(index, rank):
        return late_in.at[rank] if index == late else small_in.at[rank]

    def share(index, offset):
        rank = lax.rem(me + offset, ranks)
        return remote(
            part_of(index, rank), place_of(index, me), send.at[index, offset],
            recv.at[index, offset], device(rank, core),
        )

    def own_share(index):
        return pltpu.make_async_copy(part_of(index, me), place_of(index, me), local.at[index])

    def give(index):
        own_share(index).start()

        def one(offset, carry):
            share(index, offset).start()
            return carry

        lax.fori_loop(1, ranks, one, 0)

    def take(index):
        own_share(index).wait()

        def done(offset, carry):
            share(index, offset).wait()
            return carry

        lax.fori_loop(1, ranks, done, 0)

    def all_ranks(ref, *index):
        total = ref[(0,) + index].astype(F32)
        for rank in range(1, ref.shape[0]):
            total += ref[(rank,) + index].astype(F32)
        return total

    x, y, x_rank, y_rank = sides(me)
    z = lax.div(me, 4)
    cut = gw_s.shape[-1] // 2
    low, high = slice(0, cut), slice(cut, 2 * cut)

    def step_copy(src, dst, index, pair, rank):
        return remote(
            src, dst, step_send.at[index, pair], step_recv.at[index, pair], device(rank, core)
        )

    def sides_first(pair):
        return (
            step_copy(gw_s.at[pair, :, :, 1 - x, :, low], sum_x.at[pair], 0, pair, x_rank),
            step_copy(gw_s.at[pair, :, 1 - y, :, :, high], sum_y.at[pair], 1, pair, y_rank),
        )

    def sides_second(pair):
        return (
            step_copy(sum_x.at[pair, :, 1 - y], in_x.at[pair], 2, pair, y_rank),
            step_copy(sum_y.at[pair, :, 1 - x], in_y.at[pair], 3, pair, x_rank),
        )

    def along_z(pair):
        copies = []
        for offset in range(1, 4):
            rank = flip(me, 4 * offset)
            copies.append(
                step_copy(
                    sums.at[pair, lax.div(rank, 4)], in_z.at[pair, offset - 1], 3 + offset, pair, rank
                )
            )
        return copies

    def begin_sum(pair):
        for copy in sides_first(pair):
            copy.start()

    def go_on(pair):
        for copy in sides_first(pair):
            copy.wait()
        own_x = gw_s[pair, :, :, pl.ds(x, 1), :, low].reshape(sum_x.shape[1:])
        own_y = gw_s[pair, :, pl.ds(y, 1), :, :, high].reshape(sum_y.shape[1:])
        sum_x[pair] = (sum_x[pair].astype(F32) + own_x.astype(F32)).astype(BF16)
        sum_y[pair] = (sum_y[pair].astype(F32) + own_y.astype(F32)).astype(BF16)
        for copy in sides_second(pair):
            copy.start()

    def go_along(pair):
        for copy in sides_second(pair):
            copy.wait()
        own_x = sum_x[pair, :, pl.ds(y, 1)].reshape(in_x.shape[1:])
        own_y = sum_y[pair, :, pl.ds(x, 1)].reshape(in_y.shape[1:])
        sums[pair, :, :, low] = (in_x[pair].astype(F32) + own_x.astype(F32)).astype(BF16)
        sums[pair, :, :, high] = (in_y[pair].astype(F32) + own_y.astype(F32)).astype(BF16)
        for copy in along_z(pair):
            copy.start()

    def end_sum(pair):
        for copy in along_z(pair):
            copy.wait()
        total = sums[pair, pl.ds(z, 1)].reshape(shard, 2 * cut).astype(F32)
        for offset in range(3):
            total += in_z[pair, offset].astype(F32)
        for kind in range(4):
            go_refs[kind][:, pair * LANES : (pair + 1) * LANES] = total[
                :, kind * LANES : (kind + 1) * LANES
            ]

    def put_experts(ref, columns):
        for kind in range(3):
            for expert in range(experts):
                total = ref[expert, kind].astype(F32)
                for cluster in range(1, ranks // experts):
                    total += ref[cluster * experts + expert, kind].astype(F32)
                gx_refs[kind][:, expert, columns] = total

    def y_copy(k):
        return remote(
            y_ref.at[k], yh_s.at[k], y_send.at[k], y_recv.at[k], device(flip(me, k), core)
        )

    def z_copy(k):
        rank = flip(me, 4 * k)
        return remote(
            share_ref.at[lax.div(rank, 4)], total_ref.at[k], z_send.at[k], z_recv.at[k],
            device(rank, core),
        )

    def own_rows():
        copies = [pltpu.make_async_copy(y_ref.at[0], yh_s.at[0], y_local.at[0])]
        if halves:
            copies.append(
                pltpu.make_async_copy(share_ref.at[lax.div(me, 4)], total_ref.at[0], y_local.at[1])
            )
        return copies

    def put_together(table, values, index, tokens):
        here = pl.ds(pl.multiple_of(index * tokens, tokens), tokens)
        places = table(here)
        hot = slot_table(places, experts, slots, core * slots)
        return here, places, mm(hot, values[...].reshape(experts * slots, width), NN)

    @pl.when(step == 0)
    def _():
        if sends:
            greet([device(lax.rem(me + k, ranks), core) for k in range(1, ranks)] + [other])
        else:
            greet(cluster_and_core(experts))
        for copy in own_rows():
            copy.start()
        for k in range(1, experts):
            y_copy(k).start()
        if halves:
            for k in range(1, 4):
                z_copy(k).start()
        if sends:
            give(late)
            pltpu.make_async_copy(early_ref, early_in, y_local.at[2]).start()
        router = rows_ref[2 : 2 + experts, :]
        tokens = 256

        def gather(index, carry):
            here, places, total = put_together(
                lambda rows: places_ref[:, rows].T, dx_ref, index, tokens
            )
            gate = gates_ref[:, here].T
            slot = lax.broadcasted_iota(jnp.int32, (tokens, 2 * slots), 1)
            slot = jnp.where(slot < slots, slot + core * slots, slot - core * slots).astype(F32)
            lane = lax.broadcasted_iota(jnp.int32, (tokens, experts), 1)
            gate_grad = jnp.zeros((tokens, experts), F32)
            for e in range(experts):
                found = jnp.where(slot == places[:, e : e + 1], dg_ref[e, 0:1, :], 0.0)
                gate_grad = jnp.where(lane == e, jnp.sum(found, axis=1, keepdims=True), gate_grad)
            mean = jnp.sum(gate * gate_grad, axis=1, keepdims=True)
            logit_grad = gate * (gate_grad - mean)
            dl_s[here, :] = logit_grad
            total += lax.dot_general(
                logit_grad, router, NN, precision=HIGHEST, preferred_element_type=F32
            )
            db_s[here, :] = total + base_ref[here, :].astype(F32)
            return carry

        lax.fori_loop(0, span // tokens, gather, 0)
        db_out[...] = db_s[away, :].astype(BF16)
        swap_b = to_other(db_out, db_in.at[0], 0)
        swap_b.start()
        sums_s[...] = jnp.zeros_like(sums_s)
        sums_s[2 : 2 + experts, :] = lax.dot_general(
            dl_s[...], b_ref[...].astype(F32), TN, precision=HIGHEST, preferred_element_type=F32
        )
        swap_b.wait()
        db = db_s[own, :] + db_in[0].astype(F32)
        back, sums_s[1:2, :] = norm_back(db, h_ref[...], rows_ref[1:2, :])
        rows = d_ref[own, :].astype(F32) + back
        dh_s[...] = rows
        db_out[...] = rows.astype(BF16)
        grad_s[own, :] = rows.astype(BF16)
        swap_a = to_other(db_out, db_in.at[1], 1)
        swap_a.start()
        da_s[...] = jnp.zeros_like(da_s)
        swap_a.wait()
        grad_s[away, :] = db_in[1]

    grad_rows = grad_s[...]
    dctx_s[...] = mm(grad_rows, wo_ref[...], NN).astype(BF16)
    out_grads = mm(grad_rows, ctx_ref[...], TN).astype(BF16)
    dk_s[...] = jnp.zeros_like(dk_s)
    dv_s[...] = jnp.zeros_like(dv_s)
    scale = jnp.asarray(HD**-0.5, BF16)
    for index in range(span // block):
        keys = (index + 1) * block
        start = index * block
        query_rows = qkv_ref[start:keys, :LANES] * scale
        key_rows = qkv_ref[:keys, LANES : 2 * LANES]
        value_rows = qkv_ref[:keys, 2 * LANES :]
        context_grad = dctx_s[start:keys, :]
        row = lax.broadcasted_iota(jnp.int32, (keys, block), 0)
        column = start + lax.broadcasted_iota(jnp.int32, (keys, block), 1)
        allowed = (row <= column) & (row < length)
        dq_total = None
        for head in range(LANES // HD):
            lanes = head_lanes((block, LANES), head)
            masked_query = jnp.where(lanes, query_rows, jnp.zeros_like(query_rows))
            masked_grad = jnp.where(lanes, context_grad, jnp.zeros_like(context_grad))
            scores = jnp.where(allowed, mm(key_rows, masked_query, NT), -1e30)
            peak = jnp.max(scores, axis=0, keepdims=True)
            powers = jnp.exp(scores - peak)
            total = jnp.sum(powers, axis=0, keepdims=True)
            prob = powers * (1.0 / total)
            prob_grad = mm(value_rows, masked_grad, NT)
            inner = jnp.sum(prob * prob_grad, axis=0, keepdims=True)
            score_grad = (prob * (prob_grad - inner)).astype(BF16)
            dk_s[:keys, :] += mm(score_grad, masked_query, NN)
            dv_s[:keys, :] += mm(prob.astype(BF16), masked_grad, NN)
            dq_part = mm(score_grad, key_rows, TN)
            dq_total = dq_part if head == 0 else jnp.where(lanes, dq_part, dq_total)
        dq_s[start:keys, :] = dq_total * (HD**-0.5)
    cosine, sine = cos_ref[...], sin_ref[...]
    dq, dk = dq_s[...], dk_s[...]
    dq = (dq * cosine - partner(dq) * sine).astype(BF16)
    dk = (dk * cosine - partner(dk) * sine).astype(BF16)
    grads = jnp.concatenate([dq, dk, dv_s[...].astype(BF16)], axis=1)
    in_grads = mm(a_ref[...], grads, TN).astype(BF16)
    shape = gw_s.shape[1:-1]
    gw_s[step, ..., : 3 * LANES] = in_grads.reshape(*shape, 3 * LANES)
    gw_s[step, ..., 3 * LANES :] = out_grads.reshape(*shape, LANES)
    if sends:
        for pair in range(pairs):
            pl.when(step == pair)(functools.partial(begin_sum, pair))
            pl.when(step == pair + 1)(functools.partial(go_on, pair))
            pl.when(step == pair + 2)(functools.partial(go_along, pair))
    else:
        gw_ref[step] = gw_s[step]
    da_s[...] += mm(grads, w_ref[...], NT)

    @pl.when(step == last)
    def _():
        db_out[...] = da_s[away, :].astype(BF16)
        swap_d = to_other(db_out, db_in.at[0], 2)
        swap_d.start()
        swap_d.wait()
        da = da_s[own, :] + db_in[0].astype(F32)
        back, sums_s[0:1, :] = norm_back(da, x_ref[...].astype(F32), rows_ref[0:1, :])
        swap_s = to_other(sums_s, sums_in, 3)
        swap_s.start()
        if sends:
            go_on(pairs - 1)
            go_along(pairs - 2)
        gi_ref[...] = (dh_s[...] + back).astype(BF16)
        swap_s.wait()
        turned = (sums_s[...] + sums_in[...]).T
        if sends:
            turned_s[...] = jnp.zeros_like(turned_s)
            turned_s[:, : turned.shape[1]] = turned
            give(small)
            pltpu.make_async_copy(early_ref, early_in, y_local.at[2]).wait()
            go_along(pairs - 1)
            put_experts(early_in, pl.ds(0, early_in.shape[-1]))
        for copy in own_rows():
            copy.wait()
        for k in range(1, experts):
            y_copy(k).wait()
        mine = lax.rem(me, experts)

        def near(rows):
            table = [places_ref[pl.ds(flip(mine, k), 1), rows] for k in range(experts)]
            return jnp.concatenate(table, axis=0).T

        def add(index, carry):
            here, _, total = put_together(near, yh_s, index, 256)
            db_s[here, :] = total + sy_ref[here, :].astype(F32)
            return carry

        lax.fori_loop(0, span // 256, add, 0)
        db_out[...] = db_s[away, :].astype(BF16)
        swap_y = to_other(db_out, db_in.at[1], 4)
        swap_y.start()
        swap_y.wait()
        out = db_s[own, :] + db_in[1].astype(F32)
        lo_ref[...] = (h_ref[...] + out).astype(BF16)
        if sends:
            take(late)
            put_experts(late_in, pl.ds(early_in.shape[-1], late_in.shape[-1]))
            for k in range(1, 4):
                z_copy(k).wait()
            total = all_ranks(total_ref)
            hidden = total.shape[1] // 3
            for kind in range(3):
                gsh_refs[kind][...] = total[:, kind * hidden : (kind + 1) * hidden]
            for pair in range(pairs):
                end_sum(pair)
            take(small)
            gs_ref[...] = all_ranks(small_in)
        else:
            gs_ref[:, : turned.shape[1]] = turned


def attn_backward(
    length, places, gates, rows, dx_home, gate_grads, y_near, shared_y, shares, late, early,
    shared_dx, ffn_in, hidden_rows, grad_ffn, layer_rows, attn_in, first_all, qkv_rot, context,
    cosine, sine, ranks, halves,
):
    span, width = attn_in.shape
    half = span // 2
    experts = places.shape[0]
    pairs = context.shape[1] // LANES
    shard = width // ranks
    sends = halves
    far = pl.BlockSpec(memory_space=pl.ANY)
    if sends:
        hidden = shares.shape[-1] // 3
        forms = (
            [(shard, pairs * LANES)] * 4
            + [(shard, experts, hidden)] * 3
            + [(shard, hidden)] * 3
            + [(shard, LANES)]
        )
        outs = [(form, F32) for form in forms]
        extra = [
            pltpu.VMEM((pairs, 4, 2, shard, 2 * LANES), BF16),
            pltpu.VMEM((pairs, 4, 2, shard, 2 * LANES), BF16),
            pltpu.VMEM((pairs, 4, shard, 2 * LANES), BF16),
            pltpu.VMEM((pairs, 4, shard, 2 * LANES), BF16),
            pltpu.VMEM((pairs, 4, shard, 4 * LANES), BF16),
            pltpu.VMEM((pairs, 3, shard, 4 * LANES), BF16),
            pltpu.VMEM(shares.shape, BF16),
            pltpu.VMEM(late.shape, BF16),
            pltpu.VMEM(early.shape, BF16),
            pltpu.VMEM((ranks, shard, LANES), F32),
            pltpu.SemaphoreType.DMA((7, pairs)),
            pltpu.SemaphoreType.DMA((7, pairs)),
        ]
        blocks = (4, 2, 2, shard)
    else:
        outs = [((pairs, width, 4 * LANES), BF16), ((width, LANES), F32)]
        extra = []
        blocks = (width,)
    outs = [((half, width), BF16)] * 2 + outs
    return pl.pallas_call(
        functools.partial(attn_bwd_kernel, block=256, ranks=ranks, halves=halves, sends=sends),
        grid=(pairs,),
        in_specs=[pl.BlockSpec(memory_space=pltpu.SMEM)]
        + [
            whole(v.shape)
            for v in (
                places, gates, rows, dx_home, gate_grads, shared_dx, ffn_in, hidden_rows, grad_ffn,
                layer_rows, attn_in,
            )
        ]
        + [
            pl.BlockSpec((width, 3 * LANES), lambda i: (0, i)),
            pl.BlockSpec((width, LANES), lambda i: (0, 3 * pairs + i)),
            pl.BlockSpec((span, 3 * LANES), lambda i: (0, i)),
            pl.BlockSpec((span, LANES), lambda i: (0, i)),
            whole((span, LANES)),
            whole((span, LANES)),
            whole((span, width)),
        ]
        + [far] * 4,
        out_specs=[whole(form) for form, _ in outs],
        out_shape=[jax.ShapeDtypeStruct(form, kind) for form, kind in outs],
        scratch_shapes=extra
        + [
            pltpu.VMEM((span, width), F32),
            pltpu.VMEM((span, experts), F32),
            pltpu.VMEM((half, width), BF16),
            pltpu.VMEM((2, half, width), BF16),
            pltpu.VMEM((half, width), F32),
            pltpu.VMEM((span, width), BF16),
            pltpu.VMEM((span, width), F32),
            pltpu.VMEM((16, width), F32),
            pltpu.VMEM((16, width), F32),
            pltpu.VMEM((width, LANES), F32),
            pltpu.VMEM(y_near.shape, BF16),
            pltpu.VMEM((pairs,) + blocks + (4 * LANES,), BF16),
            pltpu.VMEM((span, LANES), BF16),
            pltpu.VMEM((span, LANES), F32),
            pltpu.VMEM((span, LANES), F32),
            pltpu.VMEM((span, LANES), F32),
            pltpu.SemaphoreType.DMA((2, ranks)),
            pltpu.SemaphoreType.DMA((2, ranks)),
            pltpu.SemaphoreType.DMA((2,)),
            pltpu.SemaphoreType.DMA((5,)),
            pltpu.SemaphoreType.DMA((5,)),
            pltpu.SemaphoreType.DMA((experts,)),
            pltpu.SemaphoreType.DMA((experts,)),
            pltpu.SemaphoreType.DMA((3,)),
            pltpu.SemaphoreType.DMA((4,)),
            pltpu.SemaphoreType.DMA((4,)),
        ],
        compiler_params=remote_params(5),
        cost_estimate=cost(40e9, 40e6, 6e6),
        name="attn_bwd",
    )(
        length, places, gates, rows, dx_home, gate_grads, shared_dx, ffn_in, hidden_rows, grad_ffn,
        layer_rows, attn_in, first_all, first_all, qkv_rot, context, cosine, sine, shared_y,
        y_near, shares, late, early,
    )


def column_of(row):
    count = row.shape[1]
    shape = (count, count)
    same = lax.broadcasted_iota(jnp.int32, shape, 0) == lax.broadcasted_iota(jnp.int32, shape, 1)
    return jnp.sum(jnp.where(same, row, 0.0), axis=1, keepdims=True)


def row_of(column):
    count = column.shape[0]
    shape = (count, count)
    same = lax.broadcasted_iota(jnp.int32, shape, 0) == lax.broadcasted_iota(jnp.int32, shape, 1)
    return jnp.sum(jnp.where(same, column, 0.0), axis=0, keepdims=True)


def ffn_block(x, grad, gate, gate_w, up_w, down_w, sums):
    gate_pre = mm(x, gate_w, NN)
    up_pre = mm(x, up_w, NN)
    sig = jax.nn.sigmoid(gate_pre)
    act = gate_pre * sig
    inner = (act * up_pre).astype(BF16)
    out = mm(inner, down_w, NT)
    gate_grad, out_grad = None, grad
    if gate is not None:
        wide = grad.astype(F32)
        gate_grad = jnp.sum(out * wide, axis=1, keepdims=True)
        out = out * gate
        out_grad = (wide * gate).astype(BF16)
    inner_grad = mm(out_grad, down_w, NN)
    gate_pre_grad = (inner_grad * up_pre * (sig + act * (1.0 - sig))).astype(BF16)
    up_pre_grad = (inner_grad * act).astype(BF16)
    row_grad = mm(gate_pre_grad, gate_w, NT) + mm(up_pre_grad, up_w, NT)
    sums[0][...] += mm(x, gate_pre_grad, TN)
    sums[1][...] += mm(x, up_pre_grad, TN)
    sums[2][...] += mm(out_grad, inner, TN)
    return out, row_grad, gate_grad


def sides(rank):
    x, y = lax.rem(rank, 2), lax.rem(lax.div(rank, 2), 2)
    return x, y, flip(rank, 1), flip(rank, 2)


def block_of(x_ref, d_ref, g_ref, w_refs, sums):
    slots, width = x_ref.shape[1:]
    shape = (width, w_refs[0].shape[-1])
    gate = column_of(jnp.concatenate([g_ref[0, 0:1, :], g_ref[1, 0:1, :]], axis=1))
    return ffn_block(
        x_ref[...].reshape(2 * slots, width), d_ref[...].reshape(2 * slots, width), gate,
        *(w_ref[...].reshape(shape) for w_ref in w_refs), sums,
    )


def put_sums(og_ref, sums):
    for index, total in enumerate(sums):
        og_ref[:, index] = total[...].astype(BF16).reshape(og_ref.shape[0], *og_ref.shape[2:])


def expert_first_kernel(
    x_ref, d_ref, g_ref, wg_ref, wu_ref, wd_ref, share_ref,
    y_ref, dx_ref, dg_ref, og_ref, sx_ref, sy_ref,
    ag, au, ad, own_x, own_y, in_x, in_y, send, recv, local, *, halves,
):
    step = pl.program_id(0)
    sums = (ag, au, ad)
    me, core = lax.axis_index("dp"), lax.axis_index("tensor")
    x, y, x_rank, y_rank = sides(me)
    cut = share_ref.shape[-1] // 2
    low, high = pl.ds(0, cut), pl.ds(cut, cut)

    def over_x(place):
        return share_ref.at[:, :, place, :, low]

    def over_y(place):
        return share_ref.at[:, place, :, :, high]

    def copies():
        return (
            remote(over_x(1 - x), in_x, send.at[0], recv.at[0], device(x_rank, core)),
            remote(over_y(1 - y), in_y, send.at[1], recv.at[1], device(y_rank, core)),
        )

    def loads():
        return (
            pltpu.make_async_copy(over_x(x), own_x, local.at[0]),
            pltpu.make_async_copy(over_y(y), own_y, local.at[1]),
        )

    @pl.when(step == 0)
    def _():
        for total in sums:
            total[...] = jnp.zeros_like(total)
        if halves:
            greet([device(x_rank, core), device(y_rank, core)])
            for copy in copies() + loads():
                copy.start()

    out, row_grad, gate_grad = block_of(x_ref, d_ref, g_ref, (wg_ref, wu_ref, wd_ref), sums)
    y_ref[...] = out
    dx_ref[...] = row_grad
    dg_ref[...] = jnp.broadcast_to(row_of(gate_grad), dg_ref.shape)

    @pl.when(step == pl.num_programs(0) - 1)
    def _():
        put_sums(og_ref, sums)
        if halves:
            for copy in copies() + loads():
                copy.wait()
            sx_ref[...] = (own_x[...].astype(F32) + in_x[...].astype(F32)).astype(BF16)
            sy_ref[...] = (own_y[...].astype(F32) + in_y[...].astype(F32)).astype(BF16)


def expert_specs(experts, slots, width, weights, order):
    def group(shape):
        return pl.BlockSpec((None,) + shape, lambda i: (order(i),) + (0,) * len(shape))

    parts, _, shard, hidden = weights.shape
    matrices = [
        pl.BlockSpec(
            (parts, None, shard, hidden), lambda i, k=k: (0, k, 0, 0),
            pipeline_mode=pl.Buffered(1),
        )
        for k in range(3)
    ]
    return group, matrices, [pltpu.VMEM((width, hidden), F32)] * 3


def expert_first(x_slots, d_slots, g_slots, weights, shares, halves):
    experts, _, slots, width = x_slots.shape
    hidden = weights.shape[-1]
    group, matrices, sums = expert_specs(experts, slots, width, weights, lambda i: i)
    rows = group((2, slots, width))
    if halves:
        _, _, _, shard, columns = shares.shape
        part = (shares.shape[0], 2, shard, columns // 2)
    else:
        part = (1, 1, 16, LANES)
    return pl.pallas_call(
        functools.partial(expert_first_kernel, halves=halves),
        grid=(experts,),
        in_specs=[rows, rows, group((2, 8, slots))]
        + matrices
        + [pl.BlockSpec(memory_space=pl.ANY)],
        out_specs=[group((2 * slots, width))] * 2
        + [group((8, 2 * slots)), whole(weights.shape), whole(part), whole(part)],
        out_shape=[jax.ShapeDtypeStruct((experts, 2 * slots, width), F32)] * 2
        + [
            jax.ShapeDtypeStruct((experts, 8, 2 * slots), F32),
            jax.ShapeDtypeStruct(weights.shape, BF16),
            jax.ShapeDtypeStruct(part, BF16),
            jax.ShapeDtypeStruct(part, BF16),
        ],
        scratch_shapes=sums
        + [pltpu.VMEM(part, BF16)] * 4
        + [pltpu.SemaphoreType.DMA((2,))] * 3,
        compiler_params=remote_params(6) if halves else params(1),
        cost_estimate=cost(36 * experts * slots * width * hidden, 40e6),
        name="expert_first",
    )(x_slots, d_slots, g_slots, weights, weights, weights, shares)


def expert_second_kernel(
    x_ref, d_ref, g_ref, wg_ref, wu_ref, wd_ref, yf_ref, dxf_ref, dgf_ref, sx_ref, sy_ref,
    y_ref, dx_home, dg_home, og_ref, share_ref,
    ag, au, ad, own_y, own_dx, ys, dxs, yp, dxp, dgs, out_x, out_y, in_x, in_y,
    core_send, core_recv, send, recv, local, share_send, share_recv, *, experts, halves,
):
    step = pl.program_id(0)
    block = experts - 1 - step
    sums = (ag, au, ad)
    me, core = lax.axis_index("dp"), lax.axis_index("tensor")
    mine = lax.rem(me, experts)
    other = device(me, 1 - core)
    slots = x_ref.shape[1]
    x, y, x_rank, y_rank = sides(me)

    def rank_at(k):
        total, bit = me - mine, 1
        while bit < experts:
            total += bit * lax.rem(lax.div(mine, bit) + lax.div(k, bit), 2)
            bit *= 2
        return total

    def core_copy(k, part):
        src, dst = ((ys, yp), (dxs, dxp))[part]
        return remote(
            src.at[lax.rem(k, 2)], dst.at[k], core_send.at[part, k], core_recv.at[part, k], other
        )

    def home_copy(k, part):
        src, dst = ((dxp, dx_home), (dgs, dg_home))[part]
        return remote(
            src.at[k], dst.at[mine], send.at[part, k], recv.at[part, k],
            device(rank_at(k), core),
        )

    def own_copy(part):
        src, dst = ((dxp, dx_home), (dgs, dg_home))[part]
        return pltpu.make_async_copy(src.at[0], dst.at[mine], local.at[part])

    def go_home(k, part):
        @pl.when(k == 0)
        def _():
            own_copy(part).start()

        @pl.when(k > 0)
        def _():
            home_copy(k, part).start()

    def share_copies():
        return (
            remote(out_x, in_x, share_send.at[0], share_recv.at[0], device(y_rank, core)),
            remote(out_y, in_y, share_send.at[1], share_recv.at[1], device(x_rank, core)),
        )

    @pl.when(step == 0)
    def _():
        greet(cluster_and_core(experts))
        for total in sums:
            total[...] = jnp.zeros_like(total)
        if halves:
            out_x[...] = sx_ref[:, pl.ds(1 - y, 1)]
            out_y[...] = sy_ref[:, pl.ds(1 - x, 1)]
            for copy in share_copies():
                copy.start()

    def settle(k):
        for part in (1, 0):
            core_copy(k, part).wait_recv()
            own, shared = ((own_y, yp), (own_dx, dxp))[part]
            total = (own[...] + shared[k].astype(F32)).astype(BF16)
            if part:
                dxp[k] = total
                go_home(k, 0)
            else:
                y_ref[...] = total

    @pl.when(step < experts)
    def _():
        out, row_grad, gate_grad = block_of(x_ref, d_ref, g_ref, (wg_ref, wu_ref, wd_ref), sums)
        out += yf_ref[...]
        row_grad += dxf_ref[...]

        @pl.when(step >= 1)
        def _():
            settle(block + 1)

        for part in (1, 0):

            @pl.when(step >= 2)
            def _():
                core_copy(block + 2, part).wait_send()

            own, half = ((own_y, ys), (own_dx, dxs))[part]
            value = (out, row_grad)[part]
            own[...] = value[:slots]
            half[lax.rem(block, 2)] = value[slots:].astype(BF16)
            core_copy(block, part).start()
        dgs[block] = jnp.broadcast_to(row_of(gate_grad), dgs.shape[1:]) + dgf_ref[...]
        go_home(block, 1)

    @pl.when(step == experts)
    def _():
        settle(block + 1)
        put_sums(og_ref, sums)
        if halves:
            cut = out_x.shape[-1]
            for copy in share_copies():
                copy.wait()
            kept_x, kept_y = sx_ref[:, pl.ds(y, 1)], sy_ref[:, pl.ds(x, 1)]
            total_x = kept_x.astype(F32) + in_x[...].astype(F32)
            total_y = kept_y.astype(F32) + in_y[...].astype(F32)
            share_ref[:, :, :cut] = total_x.astype(BF16).reshape(share_ref.shape[0], -1, cut)
            share_ref[:, :, cut:] = total_y.astype(BF16).reshape(share_ref.shape[0], -1, cut)
        for part in (0, 1):
            for k in (0, 1):
                core_copy(k, part).wait_send()
            own_copy(part).wait()
            for k in range(1, experts):
                home_copy(k, part).wait()


def expert_second(x_slots, d_slots, g_slots, weights, first, halves):
    experts, _, slots, width = x_slots.shape
    hidden = weights.shape[-1]
    y_first, dx_first, dg_first, sx, sy = first
    far = pl.BlockSpec(memory_space=pl.ANY)
    group, matrices, sums = expert_specs(
        experts, slots, width, weights, lambda i: jnp.maximum(experts - 1 - i, 0)
    )
    rows = group((2, slots, width))
    long, _, shard, cut = sx.shape
    share = (long, shard, 2 * cut)
    return pl.pallas_call(
        functools.partial(expert_second_kernel, experts=experts, halves=halves),
        grid=(experts + 1,),
        in_specs=[rows, rows, group((2, 8, slots))]
        + matrices
        + [group((2 * slots, width))] * 2
        + [group((8, 2 * slots)), whole(sx.shape), whole(sy.shape)],
        out_specs=[
            pl.BlockSpec((None, slots, width), lambda i: (jnp.minimum(experts - i, experts - 1), 0, 0)),
            far,
            far,
            whole(weights.shape),
            whole(share),
        ],
        out_shape=[
            jax.ShapeDtypeStruct((experts, slots, width), BF16),
            jax.ShapeDtypeStruct((experts, slots, width), BF16),
            jax.ShapeDtypeStruct((experts, 8, 2 * slots), F32),
            jax.ShapeDtypeStruct(weights.shape, BF16),
            jax.ShapeDtypeStruct(share, BF16),
        ],
        scratch_shapes=sums
        + [pltpu.VMEM((slots, width), F32)] * 2
        + [pltpu.VMEM((2, slots, width), BF16)] * 2
        + [pltpu.VMEM((experts, slots, width), BF16)] * 2
        + [pltpu.VMEM((experts, 8, 2 * slots), F32)]
        + [pltpu.VMEM((long, 1, shard, cut), BF16)] * 4
        + [pltpu.SemaphoreType.DMA((2, experts))] * 4
        + [pltpu.SemaphoreType.DMA((2,))] * 3,
        compiler_params=remote_params(3),
        cost_estimate=cost(36 * experts * slots * width * hidden, 40e6),
        name="expert_second",
    )(x_slots, d_slots, g_slots, weights, weights, weights, y_first, dx_first, dg_first, sx, sy)


def to_all(values, groups=None):
    count = lax.axis_size("dp") if groups is None else len(groups[0])
    copies = jnp.broadcast_to(values[None], (count,) + values.shape)
    return lax.all_to_all(copies, "dp", 0, 0, axis_index_groups=groups, tiled=True)


def after(values, *earlier):
    return lax.optimization_barrier((values,) + earlier)[0]


def per_device(
    layer_input, seq_lengths, expert_routes, w_query, w_key, w_value, w_output,
    gain_attn, gain_ffn, router_weight, expert_gate, expert_up, expert_down,
    shared_gate, shared_up, shared_down, out_cotangent,
):
    ranks = lax.axis_size("dp")
    _, own_len, width = layer_input.shape
    span = 2 * own_len
    shard = w_query.shape[0]
    pairs = w_query.shape[1] // LANES
    experts, hidden = expert_gate.shape[1:]
    capacity = 4 * span // experts
    slots = capacity // 2
    groups = [list(range(s, s + experts)) for s in range(0, ranks, experts)]

    small_own = jnp.concatenate(
        [gain_attn[:, None], gain_ffn[:, None], router_weight], axis=1
    )
    small_own = jnp.pad(small_own, ((0, 0), (0, LANES - small_own.shape[1])))
    first_all, shared_all = gather_weights(
        (w_query, w_key, w_value, w_output), small_own, (shared_gate, shared_up, shared_down)
    )
    first_all = first_all.reshape(width, first_all.shape[-1])

    half = HD // 2
    inverse = np.exp(np.arange(half, dtype=np.float32) * np.float32(-math.log(10000.0) / half))
    angles = np.arange(span, dtype=np.float32)[:, None] * inverse[None, :]
    cos_half, sin_half = np.cos(angles), np.sin(angles)
    cosine = np.concatenate([cos_half] * 4, axis=1)
    sine = np.concatenate([-sin_half, sin_half] * 2, axis=1)

    direct = shard % 16 == 0
    halves = ranks == 16

    def to_experts(columns, *earlier):
        stack = jnp.stack(
            [w[:, :, columns] for w in (expert_gate, expert_up, expert_down)], axis=0
        ).astype(BF16)
        part = stack.shape[-1]
        stack = stack.transpose(2, 0, 1, 3).reshape(1, experts, 3 * shard, part)
        stack = jnp.broadcast_to(stack, (ranks // experts, experts, 3 * shard, part))
        stack = after(stack.reshape(ranks, 3 * shard, part), *earlier)
        gathered = lax.all_to_all(stack, "dp", 0, 0, tiled=True).reshape(ranks, 3, shard, part)
        if not direct:
            gathered = gathered.transpose(1, 0, 2, 3).reshape(1, 3, width, part)
        return gathered

    def from_experts(grads):
        if not direct:
            grads = grads.reshape(3, ranks, shard, grads.shape[-1]).transpose(1, 0, 2, 3)
        return lax.all_to_all(grads, "dp", 0, 0, tiled=True)

    def to_outputs(grads):
        grads = grads.reshape(ranks // experts, experts, 3, shard, grads.shape[-1])
        return jnp.sum(grads.astype(F32), axis=0)

    early = to_experts(slice(0, hidden // 2), first_all)

    (
        attn_in, qkv_rot, context, hidden_rows, ffn_in, grad_ffn, places, small, gates, shared_y,
        shared_dx, d_slots, x_slots, g_slots, shared_grads,
    ) = attn_forward(
        seq_lengths, layer_input[0], out_cotangent[0], expert_routes.reshape(span, 2).T,
        first_all, shared_all if direct else shared_all.reshape(1, width, 3 * hidden), cosine, sine,
        experts, slots,
    )
    late = to_experts(slice(hidden // 2, hidden), early, places)

    if halves:
        shares = shared_grads.reshape(4, 2, 2, shard, 3 * hidden)
    else:
        shares = shared_grads[0, :16, :LANES]
        shared_grads = lax.all_to_all(
            shared_grads.reshape(ranks, shard, 3 * hidden), "dp", 0, 0, tiled=True
        )

    y_first, dx_first, dg_first, early_grads, sx, sy = expert_first(
        x_slots, d_slots, g_slots, early, shares, halves
    )
    early_grads = from_experts(early_grads)
    y_near, dx_home, gate_grads, late_grads, shares = expert_second(
        x_slots, d_slots, g_slots, late, (y_first, dx_first, dg_first, sx, sy), halves
    )

    grad_input, layer_output, *grads = attn_backward(
        seq_lengths, places, gates, small, dx_home, gate_grads, y_near, shared_y, shares,
        late_grads, early_grads, shared_dx, ffn_in, hidden_rows, grad_ffn, layer_input[0], attn_in,
        first_all, qkv_rot, context, cosine, sine, ranks, halves,
    )
    if halves:
        attn_grads, expert_grads, shared_grads, small_grads = (
            grads[:4], grads[4:7], grads[7:10], grads[10]
        )
    else:
        attn_grads = grads[0].reshape(pairs, ranks, shard, 4 * LANES).transpose(1, 0, 2, 3)
        attn_grads = lax.all_to_all(attn_grads, "dp", 0, 0, tiled=True)
        attn_grads = jnp.sum(attn_grads.astype(F32), axis=0).reshape(pairs, shard, 4, LANES)
        attn_grads = [
            attn_grads[:, :, k].transpose(1, 0, 2).reshape(shard, pairs * LANES) for k in range(4)
        ]
        small_grads = lax.all_to_all(grads[1].reshape(ranks, shard, LANES), "dp", 0, 0, tiled=True)
        small_grads = jnp.sum(small_grads, axis=0)
        shared_grads = jnp.sum(shared_grads.astype(F32), axis=0)
        shared_grads = [shared_grads[:, k * hidden : (k + 1) * hidden] for k in range(3)]
        late_grads = from_experts(late_grads)
        expert_grads = jnp.concatenate([to_outputs(early_grads), to_outputs(late_grads)], axis=-1)
        expert_grads = [expert_grads[:, k].transpose(1, 0, 2) for k in range(3)]
    return (
        layer_output[None], grad_input[None],
        attn_grads[0], attn_grads[1], attn_grads[2], attn_grads[3],
        small_grads[:, 0], small_grads[:, 1], small_grads[:, 2 : 2 + experts],
        expert_grads[0], expert_grads[1], expert_grads[2],
        shared_grads[0], shared_grads[1], shared_grads[2],
    )


def solution(mesh):
    tokens = P("dp", "tensor", None)
    matrix = P("dp", "tensor")
    expert = P("dp", None, "tensor")
    in_specs = (
        (tokens, P("dp"), P("dp", None, None))
        + (matrix,) * 4
        + (P("dp"), P("dp"), P("dp", None))
        + (expert,) * 3
        + (matrix,) * 3
        + (tokens,)
    )
    out_specs = (
        (tokens, tokens)
        + (matrix,) * 4
        + (P("dp"), P("dp"), P("dp", None))
        + (expert,) * 3
        + (matrix,) * 3
    )
    return jax.shard_map(
        per_device, mesh=mesh, in_specs=in_specs, out_specs=out_specs, check_vma=False
    )
```

```python
import functools
import math

import jax
import jax.numpy as jnp
import numpy as np
from jax import lax
from jax.experimental import pallas as pl
from jax.experimental.pallas import tpu as pltpu
from jax.sharding import PartitionSpec as P

HD = 64
LANES = 128
EPS = 1e-06
F32 = jnp.float32
BF16 = jnp.bfloat16
HIGHEST = lax.Precision.HIGHEST
VMEM_LIMIT = 60 * 1024 * 1024

NN = (((1,), (0,)), ((), ()))
NT = (((1,), (1,)), ((), ()))
TN = (((0,), (0,)), ((), ()))


def mm(left, right, dims):
    return lax.dot_general(left, right, dims, preferred_element_type=F32)


def params(count):
    return pltpu.CompilerParams(
        dimension_semantics=("arbitrary",) * count, vmem_limit_bytes=VMEM_LIMIT
    )


def remote_params(number):
    return pltpu.CompilerParams(
        collective_id=number, has_side_effects=True, vmem_limit_bytes=VMEM_LIMIT,
        dimension_semantics=("arbitrary",),
    )


def cost(flops, nbytes, trans=0):
    return pl.CostEstimate(flops=int(flops), bytes_accessed=int(nbytes), transcendentals=int(trans))


def flip(index, offset):
    bit = 1
    while bit <= offset:
        if offset & bit:
            index = index + bit - 2 * bit * lax.rem(lax.div(index, bit), 2)
        bit *= 2
    return index


def device(rank, core):
    return {"dp": rank, "tensor": core}


def greet(devices):
    barrier = pltpu.get_barrier_semaphore()
    for target in devices:
        pl.semaphore_signal(barrier, inc=1, device_id=target, device_id_type=pl.DeviceIdType.MESH)
    pl.semaphore_wait(barrier, len(devices))


def remote(src, dst, send, recv, target):
    return pltpu.make_async_remote_copy(
        src_ref=src, dst_ref=dst, send_sem=send, recv_sem=recv,
        device_id=target, device_id_type=pl.DeviceIdType.MESH,
    )


class Deal:
    def __init__(self, source, place, send, recv, local, ranks):
        self.source, self.place, self.ranks = source, place, ranks
        self.send, self.recv, self.local = send, recv, local
        self.me, self.core = lax.axis_index("dp"), lax.axis_index("tensor")

    @staticmethod
    def semaphores(ranks):
        dma = pltpu.SemaphoreType.DMA
        return [dma((ranks,)), dma((ranks,)), dma]

    def own(self):
        return pltpu.make_async_copy(self.source(self.me), self.place(self.me), self.local)

    order = (12, 1, 8, 2, 13, 4, 9, 3, 14, 5, 10, 6, 15, 7, 11)

    def share(self, offset):
        rank = flip(self.me, offset)
        return remote(
            self.source(rank), self.place(self.me), self.send.at[offset], self.recv.at[offset],
            device(rank, self.core),
        )

    def each(self, body):
        for offset in self.order:
            body(self.share(offset))

    def start(self, pieces=1):
        self.own().start()
        for piece in range(pieces):
            for offset in self.order:
                rank = flip(self.me, offset)
                source, place = self.source(rank), self.place(self.me)
                rows = source.shape[0] // pieces
                here = pl.ds(piece * rows, rows)
                remote(
                    source.at[here], place.at[here], self.send.at[offset], self.recv.at[offset],
                    device(rank, self.core),
                ).start()

    def wait(self):
        self.own().wait()
        self.each(lambda copy: copy.wait())


def all_and_core(ranks):
    me, core = lax.axis_index("dp"), lax.axis_index("tensor")
    return [device(lax.rem(me + k, ranks), core) for k in range(1, ranks)] + [device(me, 1 - core)]


class Gather:
    order = (0, 1, 4, 2, 5, 3, 6)
    turns = 9

    def __init__(self, own_ref, out_ref, sems, which):
        self.own_ref, self.out_ref = own_ref, out_ref
        self.own_sem, self.z_send, self.z_recv, self.s_send, self.s_recv, self.f_send, self.f_recv = (
            sem.at[which] for sem in sems
        )
        self.cut = own_ref.shape[1] // 2 // LANES * LANES
        self.me, self.core = lax.axis_index("dp"), lax.axis_index("tensor")
        self.z = lax.div(self.me, 4)
        self.up, self.down = lax.min(self.me + 4, 15), lax.max(self.me - 4, 0)
        self.sides_of = (flip(self.me, 1), flip(self.me, 2))

    @staticmethod
    def semaphores(count):
        dma = pltpu.SemaphoreType.DMA
        return [dma((count,)), dma((count, 6)), dma((count, 6))] + [dma((count, 2, 7))] * 4

    def rank_at(self, place):
        return self.me - 4 * place if place <= 3 else self.me + 4 * (place - 3)

    def at(self, place, body):
        if place == 0:
            body()
        else:
            pl.when(self.z >= place if place <= 3 else self.z + (place - 3) <= 3)(body)

    def own_copy(self):
        return pltpu.make_async_copy(self.own_ref, self.out_ref.at[self.me], self.own_sem)

    def z_copy(self, rank, step, upward):
        index = step - 1 if upward else step + 2
        return remote(
            self.own_ref if step == 1 else self.out_ref.at[rank], self.out_ref.at[rank],
            self.z_send.at[index], self.z_recv.at[index],
            device(self.up if upward else self.down, self.core),
        )

    def side_copy(self, rank, place, axis):
        return remote(
            self.own_ref if place == 0 else self.out_ref.at[rank], self.out_ref.at[rank],
            self.s_send.at[axis, place], self.s_recv.at[axis, place],
            device(self.sides_of[axis], self.core),
        )

    def onward_copy(self, rank, place, axis):
        width = self.own_ref.shape[1]
        columns = pl.ds(0, self.cut) if axis == 0 else pl.ds(self.cut, width - self.cut)
        part = self.out_ref.at[rank, :, columns]
        return remote(
            part, part, self.f_send.at[axis, place], self.f_recv.at[axis, place],
            device(self.sides_of[1 - axis], self.core),
        )

    def begin(self):
        self.own_copy().start()
        pl.when(self.z < 3)(lambda: self.z_copy(self.me, 1, True).start())
        pl.when(self.z > 0)(lambda: self.z_copy(self.me, 1, False).start())
        for axis in range(2):
            self.side_copy(self.me, 0, axis).start()

    def arrive(self, place):
        upward = place <= 3
        step = place if upward else place - 3
        rank = self.rank_at(place)
        self.z_copy(rank, step, upward).wait_recv()
        if step < 3:
            further = self.z < 3 if upward else self.z > 0
            pl.when(further)(lambda: self.z_copy(rank, step + 1, upward).start())
        for axis in range(2):
            self.side_copy(rank, place, axis).start()

    def onward(self, place):
        for axis in range(2):
            rank = flip(self.rank_at(place), 1 + axis)
            self.side_copy(rank, place, axis).wait_recv()
            self.onward_copy(rank, place, axis).start()

    def turn(self, index):
        if index < 7:
            self.at(self.order[index], functools.partial(self.arrive, self.order[index]))
        if index >= 2:
            self.at(self.order[index - 2], functools.partial(self.onward, self.order[index - 2]))

    def finish(self, place):
        for axis in range(2):
            rank = flip(self.rank_at(place), 1 + axis)
            self.side_copy(self.rank_at(place), place, axis).wait_send()
            self.onward_copy(rank, place, axis).wait_send()
            self.onward_copy(flip(self.rank_at(place), 3), place, axis).wait_recv()

    def end(self):
        z = self.z
        for place in self.order:
            self.at(place, functools.partial(self.finish, place))
        for step in range(1, 4):
            pl.when((z < 3) & (z >= step - 1))(
                lambda step=step: self.z_copy(self.me - 4 * (step - 1), step, True).wait_send()
            )
            pl.when((z > 0) & (z + step - 1 <= 3))(
                lambda step=step: self.z_copy(self.me + 4 * (step - 1), step, False).wait_send()
            )
        self.own_copy().wait()


def gather_kernel(
    wq_ref, wk_ref, wv_ref, wo_ref, small_ref, sg_ref, su_ref, sd_ref, first_out, shared_out,
    first_s, shared_s, *sems,
):
    pairs = wq_ref.shape[1] // LANES
    for pair in range(pairs):
        columns = slice(pair * LANES, (pair + 1) * LANES)
        for kind, ref in enumerate((wq_ref, wk_ref, wv_ref)):
            start = (3 * pair + kind) * LANES
            first_s[:, start : start + LANES] = ref[:, columns].astype(BF16)
    first_s[:, 3 * pairs * LANES : 4 * pairs * LANES] = wo_ref[...].astype(BF16)
    first_s[:, 4 * pairs * LANES :] = small_ref[...].astype(BF16)
    hidden = sg_ref.shape[1]
    for kind, ref in enumerate((sg_ref, su_ref, sd_ref)):
        shared_s[:, kind * hidden : (kind + 1) * hidden] = ref[...].astype(BF16)

    gathers = Gather(first_s, first_out, sems, 0), Gather(shared_s, shared_out, sems, 1)
    z, core = gathers[0].z, gathers[0].core
    barrier = pltpu.get_barrier_semaphore()

    def hello(rank):
        pl.semaphore_signal(
            barrier, inc=1, device_id=device(rank, core), device_id_type=pl.DeviceIdType.MESH
        )

    for rank in gathers[0].sides_of:
        hello(rank)
    pl.when(z < 3)(lambda: hello(gathers[0].up))
    pl.when(z > 0)(lambda: hello(gathers[0].down))
    pl.semaphore_wait(barrier, 2 + lax.min(z, 1) + lax.min(3 - z, 1))
    for gather in gathers:
        gather.begin()
    for turn in range(1, Gather.turns):
        for gather in gathers:
            gather.turn(turn)
    for gather in gathers:
        gather.end()


def gather_weights(attention, small, shared):
    ranks = lax.axis_size("dp")
    rows, heads_width = attention[0].shape
    columns = 4 * heads_width + LANES
    hidden = shared[0].shape[1]
    if ranks != 16:
        pairs = heads_width // LANES
        qkv = jnp.stack(attention[:3], axis=1).reshape(rows, 3, pairs, LANES)
        qkv = qkv.transpose(0, 2, 1, 3).reshape(rows, 3 * heads_width)
        first = jnp.concatenate([qkv, attention[3], small], axis=1).astype(BF16)
        return to_all(first), to_all(jnp.concatenate(shared, axis=1).astype(BF16))
    vmem = pl.BlockSpec(memory_space=pltpu.VMEM)
    return pl.pallas_call(
        gather_kernel,
        in_specs=[vmem] * 8,
        out_specs=[pl.BlockSpec(memory_space=pl.ANY)] * 2,
        out_shape=[
            jax.ShapeDtypeStruct((ranks, rows, columns), BF16),
            jax.ShapeDtypeStruct((ranks, rows, 3 * hidden), BF16),
        ],
        scratch_shapes=[
            pltpu.VMEM((rows, columns), BF16),
            pltpu.VMEM((rows, 3 * hidden), BF16),
        ]
        + Gather.semaphores(2),
        compiler_params=pltpu.CompilerParams(
            collective_id=1, has_side_effects=True, vmem_limit_bytes=VMEM_LIMIT
        ),
        cost_estimate=cost(1e6, 100e6),
        name="gather_weights",
    )(*attention, small, *shared)


def partner(values):
    lane = lax.broadcasted_iota(jnp.int32, values.shape, 1)
    return jnp.where(
        lane % HD < HD // 2,
        pltpu.roll(values, LANES - HD // 2, 1),
        pltpu.roll(values, HD // 2, 1),
    )


def head_lanes(shape, head):
    lane = lax.broadcasted_iota(jnp.int32, shape, 1)
    return (lane // HD) == head


def offsets(count):
    return sorted(range(1, count), key=lambda k: (bin(k).count("1"), k))


class Trip:
    def __init__(self, ins, outs, send, recv, core_send, core_recv, local, part):
        self.ins, self.outs, self.part = ins, outs, part
        self.send, self.recv, self.local = send, recv, local
        self.core_send, self.core_recv = core_send, core_recv
        self.me, self.core = lax.axis_index("dp"), lax.axis_index("tensor")
        self.count = ins.shape[0]

    def copy(self, k):
        return remote(
            self.ins.at[k], self.outs.at[k, 0],
            self.send.at[self.part, k], self.recv.at[self.part, k],
            device(flip(self.me, k), self.core),
        )

    def core_copy(self, k):
        src = self.ins.at[0] if k == 0 else self.outs.at[k, 0]
        return remote(
            src, self.outs.at[k, 1],
            self.core_send.at[self.part, k], self.core_recv.at[self.part, k],
            device(self.me, 1 - self.core),
        )

    def own(self):
        return pltpu.make_async_copy(self.ins.at[0], self.outs.at[0, 0], self.local.at[self.part])

    def go(self, k):
        if k:
            self.copy(k).start()
        else:
            self.own().start()
            self.core_copy(0).start()

    def pass_on(self, k):
        self.copy(k).wait_recv()
        self.core_copy(k).start()

    def end(self):
        self.own().wait()
        for k in range(self.count):
            self.core_copy(k).wait()
            if k:
                self.copy(k).wait_send()


def cluster_and_core(count):
    me, core = lax.axis_index("dp"), lax.axis_index("tensor")
    return [device(flip(me, k), core) for k in range(1, count)] + [device(me, 1 - core)]


def rms(values):
    return values * lax.rsqrt(jnp.mean(values * values, axis=-1, keepdims=True) + EPS)


def whole(shape):
    return pl.BlockSpec(shape, lambda i: (0,) * len(shape), pipeline_mode=pl.Buffered(1))


def attn_fwd_kernel(
    len_ref, x_ref, c_ref, routes_ref, w_ref, wo_ref, small_ref, cos_ref, sin_ref, shared_ref, own_ref,
    a_ref, qkv_ref, ctx_ref, h_ref, b_ref, d_ref, places_ref, rows_ref, gates_ref, y_ref, dx_ref, dr, xr, gr, og_ref, early_ref,
    ds, xs, gs, ag, au, ad, shared_w, part, x_in, h_in, b_out, b_in, c_out, c_in,
    send, recv, core_send, core_recv, local, pair_send, pair_recv, load, *sems,
    block, ranks, deals,
):
    step = pl.program_id(0)
    me, core = lax.axis_index("dp"), lax.axis_index("tensor")
    other = device(me, 1 - core)
    experts, slots, _ = ds.shape
    trips = [
        Trip(ins, outs, send, recv, core_send, core_recv, local, index)
        for index, (ins, outs) in enumerate(((ds, dr), (xs, xr), (gs, gr)))
    ]
    if deals:
        deal = Deal(
            lambda rank: own_ref.at[lax.rem(rank, experts)], lambda rank: early_ref.at[rank],
            *sems, ranks,
        )
    slot = core * slots + lax.broadcasted_iota(jnp.int32, (slots, a_ref.shape[0]), 0)
    slot = slot.astype(F32)
    mine = lax.rem(me, experts)
    span, width = a_ref.shape
    half = span // 2
    length = len_ref[0]
    own = pl.ds(pl.multiple_of(core * half, half), half)
    away = pl.ds(pl.multiple_of((1 - core) * half, half), half)
    pairs = pl.num_programs(0)

    def to_other(src, dst, index):
        return remote(src, dst, pair_send.at[index], pair_recv.at[index], other)

    @pl.when(step == 0)
    def _():
        greet(all_and_core(ranks) if deals else cluster_and_core(experts))
        if deals:
            deal.start(3)
        pltpu.make_async_copy(shared_ref, shared_w, load).start()
        token = core * half + lax.broadcasted_iota(jnp.int32, c_ref.shape, 0)
        valid = jnp.where(token < length, c_ref[...].astype(F32), 0.0).astype(BF16)
        c_out[...] = valid
        d_ref[own, :] = valid
        swap_c = to_other(c_out, c_in, 0)
        swap_c.start()
        swap_x = to_other(x_ref, x_in, 1)
        swap_x.start()

        name = lax.broadcasted_iota(jnp.int32, (experts, span), 0)
        chosen = (name == routes_ref[0:1, :]) | (name == routes_ref[1:2, :])
        earlier = lax.broadcasted_iota(jnp.int32, (span, span), 0) < lax.broadcasted_iota(
            jnp.int32, (span, span), 1
        )
        counts = mm(
            jnp.where(chosen, 1.0, 0.0).astype(BF16), jnp.where(earlier, 1.0, 0.0).astype(BF16), NN
        )
        places_ref[...] = jnp.where(chosen, counts, -1.0)

        swap_c.wait_recv()
        d_ref[away, :] = c_in[...]
        for k in offsets(experts) + [0]:
            place = places_ref[pl.ds(flip(mine, k), 1), :]
            hot = jnp.where(slot == place, 1.0, 0.0).astype(BF16)
            ds[k] = mm(hot, d_ref[...], NN).astype(BF16)
            trips[0].go(k)
        rows_ref[...] = small_ref[...].astype(F32).T[: rows_ref.shape[0], :]
        swap_x.wait_recv()
        gain = rows_ref[0:1, :]
        a_ref[own, :] = (rms(x_ref[...].astype(F32)) * gain).astype(BF16)
        a_ref[away, :] = (rms(x_in[...].astype(F32)) * gain).astype(BF16)
        part[...] = jnp.zeros_like(part)
        swap_c.wait_send()
        swap_x.wait_send()

    raw = mm(a_ref[...], w_ref[...], NN)
    cosine, sine = cos_ref[...], sin_ref[...]
    query, key = raw[:, :LANES], raw[:, LANES : 2 * LANES]
    qkv_ref[:, :LANES] = (query * cosine + partner(query) * sine).astype(BF16)
    qkv_ref[:, LANES : 2 * LANES] = (key * cosine + partner(key) * sine).astype(BF16)
    qkv_ref[:, 2 * LANES :] = raw[:, 2 * LANES :].astype(BF16)
    for index in range(span // block):
        keys = (index + 1) * block
        query_rows = qkv_ref[index * block : keys, :LANES] * jnp.asarray(HD**-0.5, BF16)
        key_rows = qkv_ref[:keys, LANES : 2 * LANES]
        value_rows = qkv_ref[:keys, 2 * LANES :]
        row = index * block + lax.broadcasted_iota(jnp.int32, (block, keys), 0)
        column = lax.broadcasted_iota(jnp.int32, (block, keys), 1)
        allowed = (column <= row) & (column < length)
        parts = []
        for head in range(LANES // HD):
            masked_query = jnp.where(
                head_lanes(query_rows.shape, head), query_rows, jnp.zeros_like(query_rows)
            )
            scores = jnp.where(allowed, mm(masked_query, key_rows, NT), -1e30)
            peak = jnp.max(scores, axis=1, keepdims=True)
            powers = jnp.exp(scores - peak)
            total = jnp.sum(powers, axis=1, keepdims=True)
            prob = (powers * (1.0 / total)).astype(BF16)
            parts.append(mm(prob, value_rows, NN))
        context = jnp.where(head_lanes(parts[0].shape, 0), parts[0], parts[1]).astype(BF16)
        ctx_ref[index * block : keys, :] = context
        part[index * block : keys, :] += mm(context, wo_ref[...], NT)

    @pl.when(step == pairs - 1)
    def _():
        swap_h = to_other(part.at[away], h_in, 2)
        swap_h.start()
        rows = x_ref[...].astype(F32) + part[own, :]
        swap_h.wait_recv()
        rows = rows + h_in[...]
        h_ref[...] = rows
        normed = (rms(rows) * rows_ref[1:2, :]).astype(BF16)
        b_out[...] = normed
        swap_b = to_other(b_out, b_in, 3)
        swap_b.start()
        b_ref[own, :] = normed
        swap_b.wait_recv()
        b_ref[away, :] = b_in[...]
        chosen = places_ref[...] >= 0
        logits = mm(rows_ref[2 : 2 + experts, :].astype(BF16), b_ref[...], NT)
        top = jnp.max(jnp.where(chosen, logits, -1e30), axis=0, keepdims=True)
        powers = jnp.where(chosen, jnp.exp(jnp.minimum(logits - top, 0.0)), 0.0)
        gates_ref[...] = powers / jnp.sum(powers, axis=0, keepdims=True)
        for k in offsets(experts) + [0]:
            target = pl.ds(flip(mine, k), 1)
            found = slot == places_ref[target, :]
            xs[k] = mm(jnp.where(found, 1.0, 0.0).astype(BF16), b_ref[...], NN).astype(BF16)
            trips[1].go(k)
            gate = jnp.sum(jnp.where(found, gates_ref[target, :], 0.0), axis=1, keepdims=True)
            gs[k] = jnp.broadcast_to(row_of(gate), gs.shape[1:])
            trips[2].go(k)
        swap_h.wait_send()
        swap_b.wait_send()
        for total in (ag, au, ad):
            total[...] = jnp.zeros_like(total)
        pltpu.make_async_copy(shared_ref, shared_w, load).wait()
        hidden = ag.shape[1]

        def matrix(index):
            return shared_w[:, :, index * hidden : (index + 1) * hidden].reshape(width, hidden)

        def branch(index, carry):
            rows = pl.ds(pl.multiple_of(index * block, block), block)
            out, row_grad, _ = ffn_block(
                b_ref[rows, :], d_ref[rows, :], None, matrix(0), matrix(1), matrix(2), (ag, au, ad)
            )
            y_ref[rows, :] = out.astype(BF16)
            dx_ref[rows, :] = row_grad.astype(BF16)
            return carry

        lax.fori_loop(0, span // block, branch, 0)
        for index, total in enumerate((ag, au, ad)):
            shared_w[:, :, index * hidden : (index + 1) * hidden] = (
                total[...].astype(BF16).reshape(shared_w.shape[0], -1, hidden)
            )
        write = pltpu.make_async_copy(shared_w, og_ref, load)
        write.start()
        for trip in trips:
            for k in offsets(experts):
                trip.pass_on(k)
        for trip in trips:
            trip.end()
        write.wait()
        if deals:
            deal.wait()


def attn_forward(length, rows, cotangent, routes, first_all, shared_all, own, cosine, sine, slots):
    half, width = rows.shape
    span = 2 * half
    pairs = (first_all.shape[1] - LANES) // (4 * LANES)
    far = pl.BlockSpec(memory_space=pl.ANY)
    ranks = lax.axis_size("dp")
    experts, own_rows, part = own.shape
    deals = ranks == 16
    hidden = shared_all.shape[-1] // 3
    return pl.pallas_call(
        functools.partial(attn_fwd_kernel, block=256, ranks=ranks, deals=deals),
        grid=(pairs,),
        in_specs=[
            pl.BlockSpec(memory_space=pltpu.SMEM),
            whole((half, width)),
            whole((half, width)),
            whole(routes.shape),
            pl.BlockSpec((width, 3 * LANES), lambda i: (0, i)),
            pl.BlockSpec((width, LANES), lambda i: (0, 3 * pairs + i)),
            pl.BlockSpec((width, LANES), lambda i: (0, 4 * pairs)),
            whole((span, LANES)),
            whole((span, LANES)),
        ]
        + [far] * 2,
        out_specs=[
            whole((span, width)),
            pl.BlockSpec((span, 3 * LANES), lambda i: (0, i)),
            pl.BlockSpec((span, LANES), lambda i: (0, i)),
            whole((half, width)),
            whole((span, width)),
            whole((span, width)),
            whole((experts, span)),
            whole((16, width)),
            whole((experts, span)),
            whole((span, width)),
            whole((span, width)),
        ]
        + [far] * 5,
        out_shape=[
            jax.ShapeDtypeStruct((span, width), BF16),
            jax.ShapeDtypeStruct((span, pairs * 3 * LANES), BF16),
            jax.ShapeDtypeStruct((span, pairs * LANES), BF16),
            jax.ShapeDtypeStruct((half, width), F32),
            jax.ShapeDtypeStruct((span, width), BF16),
            jax.ShapeDtypeStruct((span, width), BF16),
            jax.ShapeDtypeStruct((experts, span), F32),
            jax.ShapeDtypeStruct((16, width), F32),
            jax.ShapeDtypeStruct((experts, span), F32),
            jax.ShapeDtypeStruct((span, width), BF16),
            jax.ShapeDtypeStruct((span, width), BF16),
            jax.ShapeDtypeStruct((experts, 2, slots, width), BF16),
            jax.ShapeDtypeStruct((experts, 2, slots, width), BF16),
            jax.ShapeDtypeStruct((experts, 2, 8, slots), F32),
            jax.ShapeDtypeStruct(shared_all.shape, BF16),
            jax.ShapeDtypeStruct((ranks, own_rows, part) if deals else (1, 16, LANES), BF16),
        ],
        scratch_shapes=[
            pltpu.VMEM((experts, slots, width), BF16),
            pltpu.VMEM((experts, slots, width), BF16),
            pltpu.VMEM((experts, 8, slots), F32),
            pltpu.VMEM((width, hidden), F32),
            pltpu.VMEM((width, hidden), F32),
            pltpu.VMEM((width, hidden), F32),
            pltpu.VMEM(shared_all.shape, BF16),
            pltpu.VMEM((span, width), F32),
            pltpu.VMEM((half, width), BF16),
            pltpu.VMEM((half, width), F32),
        ]
        + [pltpu.VMEM((half, width), BF16)] * 4
        + [pltpu.SemaphoreType.DMA((3, experts))] * 4
        + [pltpu.SemaphoreType.DMA((3,))]
        + [pltpu.SemaphoreType.DMA((4,))] * 2
        + [pltpu.SemaphoreType.DMA]
        + Deal.semaphores(ranks),
        compiler_params=remote_params(4),
        cost_estimate=cost(20e9, 60e6, 6e6),
        name="attn_fwd",
    )(length, rows, cotangent, routes, first_all, first_all, first_all, cosine, sine, shared_all, own)


def norm_back(grad, values, gain):
    factor = lax.rsqrt(jnp.mean(values * values, axis=-1, keepdims=True) + EPS)
    normed = values * factor
    hat = grad * gain
    back = factor * (hat - normed * jnp.mean(hat * normed, axis=-1, keepdims=True))
    return back, jnp.sum(grad * normed, axis=0, keepdims=True)


def slot_table(places, experts, slots, offset):
    slot = lax.broadcasted_iota(jnp.int32, (places.shape[0], slots), 1) + offset
    slot = slot.astype(F32)
    return jnp.concatenate(
        [jnp.where(slot == places[:, e : e + 1], 1.0, 0.0).astype(BF16) for e in range(experts)],
        axis=1,
    )


def attn_bwd_kernel(
    len_ref, places_ref, gates_ref, rows_ref, dx_ref, dg_ref, base_ref, b_ref, h_ref, d_ref,
    x_ref, a_ref, w_ref, wo_ref, qkv_ref, ctx_ref, cos_ref, sin_ref, sy_ref, y_ref, share_ref, late_ref,
    gi_ref, lo_ref, *rest, block, ranks, halves, sends,
):
    if sends:
        go_ref, late_in, total_ref, small_in = rest[:4]
        sum_x, sum_y, in_x, in_y, sums, in_z, step_send, step_recv = rest[4:12]
        rest = rest[12:]
    else:
        gw_ref, gs_ref = rest[:2]
        rest = rest[2:]
    (
        db_s, dl_s, db_out, y_out, db_in, dh_s, grad_s, da_s, sums_s, sums_in, turned_s,
        yh_s, gw_s, dctx_s, dq_s, dk_s, dv_s, send, recv, local, pair_send, pair_recv,
        y_send, y_recv, y_local, z_send, z_recv,
    ) = rest
    step = pl.program_id(0)
    last = pl.num_programs(0) - 1
    me, core = lax.axis_index("dp"), lax.axis_index("tensor")
    other = device(me, 1 - core)
    experts, slots, width = dx_ref.shape
    span = a_ref.shape[0]
    half = span // 2
    length = len_ref[0]
    own = pl.ds(pl.multiple_of(core * half, half), half)
    away = pl.ds(pl.multiple_of((1 - core) * half, half), half)
    shard = width // ranks
    pairs = gw_s.shape[0]

    def to_other(src, dst, index):
        return remote(src, dst, pair_send.at[index], pair_recv.at[index], other)

    if sends:
        rows_at = lambda rank: pl.ds(pl.multiple_of(rank * shard, shard), shard)
        small = Deal(
            lambda rank: turned_s.at[rows_at(rank)], lambda rank: small_in.at[rank],
            send.at[0], recv.at[0], local.at[0], ranks,
        )
        late = Deal(
            lambda rank: late_ref.at[rank], lambda rank: late_in.at[rank],
            send.at[1], recv.at[1], local.at[1], ranks,
        )

    x, y, x_rank, y_rank = sides(me)
    z = lax.div(me, 4)
    cut = gw_s.shape[-1] // 2
    low, high = slice(0, cut), slice(cut, 2 * cut)

    def step_copy(src, dst, index, pair, rank):
        return remote(
            src, dst, step_send.at[index, pair], step_recv.at[index, pair], device(rank, core)
        )

    def sides_first(pair):
        return (
            step_copy(gw_s.at[pair, :, :, 1 - x, :, low], sum_x.at[pair], 0, pair, x_rank),
            step_copy(gw_s.at[pair, :, 1 - y, :, :, high], sum_y.at[pair], 1, pair, y_rank),
        )

    def sides_second(pair):
        return (
            step_copy(sum_x.at[pair, :, 1 - y], in_x.at[pair], 2, pair, y_rank),
            step_copy(sum_y.at[pair, :, 1 - x], in_y.at[pair], 3, pair, x_rank),
        )

    def along_z(pair):
        copies = []
        for offset in range(1, 4):
            rank = flip(me, 4 * offset)
            copies.append(
                step_copy(
                    sums.at[pair, lax.div(rank, 4)], in_z.at[pair, offset - 1], 3 + offset, pair, rank
                )
            )
        return copies

    def begin_sum(pair):
        for copy in sides_first(pair):
            copy.start()

    def go_on(pair):
        for copy in sides_first(pair):
            copy.wait()
        own_x = gw_s[pair, :, :, pl.ds(x, 1), :, low].reshape(sum_x.shape[1:])
        own_y = gw_s[pair, :, pl.ds(y, 1), :, :, high].reshape(sum_y.shape[1:])
        sum_x[pair] = (sum_x[pair].astype(F32) + own_x.astype(F32)).astype(BF16)
        sum_y[pair] = (sum_y[pair].astype(F32) + own_y.astype(F32)).astype(BF16)
        for copy in sides_second(pair):
            copy.start()

    def go_along(pair):
        for copy in sides_second(pair):
            copy.wait()
        own_x = sum_x[pair, :, pl.ds(y, 1)].reshape(in_x.shape[1:])
        own_y = sum_y[pair, :, pl.ds(x, 1)].reshape(in_y.shape[1:])
        sums[pair, :, :, low] = (in_x[pair].astype(F32) + own_x.astype(F32)).astype(BF16)
        sums[pair, :, :, high] = (in_y[pair].astype(F32) + own_y.astype(F32)).astype(BF16)
        for copy in along_z(pair):
            copy.start()

    def end_sum(pair):
        for copy in along_z(pair):
            copy.wait()
        total = sums[pair, pl.ds(z, 1)].reshape(shard, 2 * cut).astype(F32)
        for offset in range(3):
            total += in_z[pair, offset].astype(F32)
        go_ref[pair] = total

    def y_copy(k):
        return remote(
            y_ref.at[k], yh_s.at[k], y_send.at[k], y_recv.at[k], device(flip(me, k), core)
        )

    def z_copy(k):
        rank = flip(me, 4 * k)
        return remote(
            share_ref.at[lax.div(rank, 4)], total_ref.at[k], z_send.at[k], z_recv.at[k],
            device(rank, core),
        )

    def own_rows():
        copies = [pltpu.make_async_copy(y_ref.at[0], yh_s.at[0], y_local.at[0])]
        if halves:
            copies.append(
                pltpu.make_async_copy(share_ref.at[lax.div(me, 4)], total_ref.at[0], y_local.at[1])
            )
        return copies

    def put_together(table, values, index, tokens):
        here = pl.ds(pl.multiple_of(index * tokens, tokens), tokens)
        places = table(here)
        hot = slot_table(places, experts, slots, core * slots)
        return here, places, mm(hot, values[...].reshape(experts * slots, width), NN)

    @pl.when(step == 0)
    def _():
        if sends:
            greet([device(lax.rem(me + k, ranks), core) for k in range(1, ranks)] + [other])
        else:
            greet(cluster_and_core(experts))
        for copy in own_rows():
            copy.start()
        for k in range(1, experts):
            y_copy(k).start()
        if sends:
            for k in range(1, 4):
                z_copy(k).start()
            late.start(3)
        router = rows_ref[2 : 2 + experts, :]
        tokens = 256

        def gather(index, carry):
            here, places, total = put_together(
                lambda rows: places_ref[:, rows].T, dx_ref, index, tokens
            )
            gate = gates_ref[:, here].T
            slot = lax.broadcasted_iota(jnp.int32, (tokens, 2 * slots), 1)
            slot = jnp.where(slot < slots, slot + core * slots, slot - core * slots).astype(F32)
            lane = lax.broadcasted_iota(jnp.int32, (tokens, experts), 1)
            gate_grad = jnp.zeros((tokens, experts), F32)
            for e in range(experts):
                found = jnp.where(slot == places[:, e : e + 1], dg_ref[e, 0:1, :], 0.0)
                gate_grad = jnp.where(lane == e, jnp.sum(found, axis=1, keepdims=True), gate_grad)
            mean = jnp.sum(gate * gate_grad, axis=1, keepdims=True)
            logit_grad = gate * (gate_grad - mean)
            dl_s[here, :] = logit_grad
            total += lax.dot_general(
                logit_grad, router, NN, precision=HIGHEST, preferred_element_type=F32
            )
            db_s[here, :] = total + base_ref[here, :].astype(F32)
            return carry

        lax.fori_loop(0, span // tokens, gather, 0)
        db_out[...] = db_s[away, :].astype(BF16)
        swap_b = to_other(db_out, db_in.at[0], 0)
        swap_b.start()
        sums_s[...] = jnp.zeros_like(sums_s)
        sums_s[2 : 2 + experts, :] = lax.dot_general(
            dl_s[...], b_ref[...].astype(F32), TN, precision=HIGHEST, preferred_element_type=F32
        )
        swap_b.wait()
        db = db_s[own, :] + db_in[0].astype(F32)
        back, sums_s[1:2, :] = norm_back(db, h_ref[...], rows_ref[1:2, :])
        rows = d_ref[own, :].astype(F32) + back
        dh_s[...] = rows
        db_out[...] = rows.astype(BF16)
        grad_s[own, :] = rows.astype(BF16)
        swap_a = to_other(db_out, db_in.at[1], 1)
        swap_a.start()
        da_s[...] = jnp.zeros_like(da_s)
        swap_a.wait()
        grad_s[away, :] = db_in[1]

    grad_rows = grad_s[...]
    dctx_s[...] = mm(grad_rows, wo_ref[...], NN).astype(BF16)
    out_grads = mm(grad_rows, ctx_ref[...], TN).astype(BF16)
    dk_s[...] = jnp.zeros_like(dk_s)
    dv_s[...] = jnp.zeros_like(dv_s)
    scale = jnp.asarray(HD**-0.5, BF16)
    for index in range(span // block):
        keys = (index + 1) * block
        start = index * block
        query_rows = qkv_ref[start:keys, :LANES] * scale
        key_rows = qkv_ref[:keys, LANES : 2 * LANES]
        value_rows = qkv_ref[:keys, 2 * LANES :]
        context_grad = dctx_s[start:keys, :]
        row = lax.broadcasted_iota(jnp.int32, (keys, block), 0)
        column = start + lax.broadcasted_iota(jnp.int32, (keys, block), 1)
        allowed = (row <= column) & (row < length)
        dq_total = None
        for head in range(LANES // HD):
            lanes = head_lanes((block, LANES), head)
            masked_query = jnp.where(lanes, query_rows, jnp.zeros_like(query_rows))
            masked_grad = jnp.where(lanes, context_grad, jnp.zeros_like(context_grad))
            scores = jnp.where(allowed, mm(key_rows, masked_query, NT), -1e30)
            peak = jnp.max(scores, axis=0, keepdims=True)
            powers = jnp.exp(scores - peak)
            total = jnp.sum(powers, axis=0, keepdims=True)
            prob = powers * (1.0 / total)
            prob_grad = mm(value_rows, masked_grad, NT)
            inner = jnp.sum(prob * prob_grad, axis=0, keepdims=True)
            score_grad = (prob * (prob_grad - inner)).astype(BF16)
            dk_s[:keys, :] += mm(score_grad, masked_query, NN)
            dv_s[:keys, :] += mm(prob.astype(BF16), masked_grad, NN)
            dq_part = mm(score_grad, key_rows, TN)
            dq_total = dq_part if head == 0 else jnp.where(lanes, dq_part, dq_total)
        dq_s[start:keys, :] = dq_total * (HD**-0.5)
    cosine, sine = cos_ref[...], sin_ref[...]
    dq, dk = dq_s[...], dk_s[...]
    dq = (dq * cosine - partner(dq) * sine).astype(BF16)
    dk = (dk * cosine - partner(dk) * sine).astype(BF16)
    grads = jnp.concatenate([dq, dk, dv_s[...].astype(BF16)], axis=1)
    in_grads = mm(a_ref[...], grads, TN).astype(BF16)
    shape = gw_s.shape[1:-1]
    gw_s[step, ..., : 3 * LANES] = in_grads.reshape(*shape, 3 * LANES)
    gw_s[step, ..., 3 * LANES :] = out_grads.reshape(*shape, LANES)
    if sends:
        for pair in range(pairs):
            pl.when(step == pair)(functools.partial(begin_sum, pair))
            pl.when(step == pair + 1)(functools.partial(go_on, pair))
            pl.when(step == pair + 2)(functools.partial(go_along, pair))
    else:
        gw_ref[step] = gw_s[step]
    da_s[...] += mm(grads, w_ref[...], NT)

    @pl.when(step == last)
    def _():
        db_out[...] = da_s[away, :].astype(BF16)
        swap_d = to_other(db_out, db_in.at[0], 2)
        swap_d.start()

        for copy in own_rows():
            copy.wait()
        for k in range(1, experts):
            y_copy(k).wait()
        mine = lax.rem(me, experts)

        def near(rows):
            table = [places_ref[pl.ds(flip(mine, k), 1), rows] for k in range(experts)]
            return jnp.concatenate(table, axis=0).T

        def add(index, carry):
            here, _, total = put_together(near, yh_s, index, 256)
            db_s[here, :] = total + sy_ref[here, :].astype(F32)
            return carry

        lax.fori_loop(0, span // 256, add, 0)
        y_out[...] = db_s[away, :].astype(BF16)
        swap_y = to_other(y_out, db_in.at[2], 4)
        swap_y.start()

        swap_d.wait()
        da = da_s[own, :] + db_in[0].astype(F32)
        back, sums_s[0:1, :] = norm_back(da, x_ref[...].astype(F32), rows_ref[0:1, :])
        swap_s = to_other(sums_s, sums_in, 3)
        swap_s.start()
        if sends:
            go_on(pairs - 1)
            go_along(pairs - 2)
        gi_ref[...] = (dh_s[...] + back).astype(BF16)
        swap_s.wait()
        turned = (sums_s[...] + sums_in[...]).T
        if sends:
            turned_s[...] = jnp.zeros_like(turned_s)
            turned_s[:, : turned.shape[1]] = turned
            small.start()
            go_along(pairs - 1)
        else:
            gs_ref[:, : turned.shape[1]] = turned
        swap_y.wait()
        out = db_s[own, :] + db_in[2].astype(F32)
        lo_ref[...] = (h_ref[...] + out).astype(BF16)
        if sends:
            late.wait()
            for k in range(1, 4):
                z_copy(k).wait()
            for pair in range(pairs):
                end_sum(pair)
            small.wait()


def attn_backward(
    length, places, gates, rows, dx_home, gate_grads, y_near, shared_y, shares, late,
    shared_dx, ffn_in, hidden_rows, grad_ffn, layer_rows, attn_in, first_all, qkv_rot, context,
    cosine, sine, ranks, halves,
):
    span, width = attn_in.shape
    half = span // 2
    experts = places.shape[0]
    pairs = context.shape[1] // LANES
    shard = width // ranks
    sends = halves
    far = pl.BlockSpec(memory_space=pl.ANY)
    if sends:
        outs = [
            (whole((pairs, shard, 4 * LANES)), (pairs, shard, 4 * LANES), F32),
            (far, late.shape, BF16),
            (far, shares.shape, BF16),
            (far, (ranks, shard, LANES), F32),
        ]
        extra = [
            pltpu.VMEM((pairs, 4, 2, shard, 2 * LANES), BF16),
            pltpu.VMEM((pairs, 4, 2, shard, 2 * LANES), BF16),
            pltpu.VMEM((pairs, 4, shard, 2 * LANES), BF16),
            pltpu.VMEM((pairs, 4, shard, 2 * LANES), BF16),
            pltpu.VMEM((pairs, 4, shard, 4 * LANES), BF16),
            pltpu.VMEM((pairs, 3, shard, 4 * LANES), BF16),
            pltpu.SemaphoreType.DMA((7, pairs)),
            pltpu.SemaphoreType.DMA((7, pairs)),
        ]
        blocks = (4, 2, 2, shard)
    else:
        forms = (pairs, width, 4 * LANES), (width, LANES)
        outs = [(whole(forms[0]), forms[0], BF16), (whole(forms[1]), forms[1], F32)]
        extra = []
        blocks = (width,)
    outs = [(whole((half, width)), (half, width), BF16)] * 2 + outs
    return pl.pallas_call(
        functools.partial(attn_bwd_kernel, block=256, ranks=ranks, halves=halves, sends=sends),
        grid=(pairs,),
        in_specs=[pl.BlockSpec(memory_space=pltpu.SMEM)]
        + [
            whole(v.shape)
            for v in (
                places, gates, rows, dx_home, gate_grads, shared_dx, ffn_in, hidden_rows, grad_ffn,
                layer_rows, attn_in,
            )
        ]
        + [
            pl.BlockSpec((width, 3 * LANES), lambda i: (0, i)),
            pl.BlockSpec((width, LANES), lambda i: (0, 3 * pairs + i)),
            pl.BlockSpec((span, 3 * LANES), lambda i: (0, i)),
            pl.BlockSpec((span, LANES), lambda i: (0, i)),
            whole((span, LANES)),
            whole((span, LANES)),
            whole((span, width)),
        ]
        + [far] * 3,
        out_specs=[spec for spec, _, _ in outs],
        out_shape=[jax.ShapeDtypeStruct(form, kind) for _, form, kind in outs],
        scratch_shapes=extra
        + [
            pltpu.VMEM((span, width), F32),
            pltpu.VMEM((span, experts), F32),
            pltpu.VMEM((half, width), BF16),
            pltpu.VMEM((half, width), BF16),
            pltpu.VMEM((3, half, width), BF16),
            pltpu.VMEM((half, width), F32),
            pltpu.VMEM((span, width), BF16),
            pltpu.VMEM((span, width), F32),
            pltpu.VMEM((16, width), F32),
            pltpu.VMEM((16, width), F32),
            pltpu.VMEM((width, LANES), F32),
            pltpu.VMEM(y_near.shape, BF16),
            pltpu.VMEM((pairs,) + blocks + (4 * LANES,), BF16),
            pltpu.VMEM((span, LANES), BF16),
            pltpu.VMEM((span, LANES), F32),
            pltpu.VMEM((span, LANES), F32),
            pltpu.VMEM((span, LANES), F32),
            pltpu.SemaphoreType.DMA((2, ranks)),
            pltpu.SemaphoreType.DMA((2, ranks)),
            pltpu.SemaphoreType.DMA((2,)),
            pltpu.SemaphoreType.DMA((5,)),
            pltpu.SemaphoreType.DMA((5,)),
            pltpu.SemaphoreType.DMA((experts,)),
            pltpu.SemaphoreType.DMA((experts,)),
            pltpu.SemaphoreType.DMA((3,)),
            pltpu.SemaphoreType.DMA((4,)),
            pltpu.SemaphoreType.DMA((4,)),
        ],
        compiler_params=remote_params(5),
        cost_estimate=cost(40e9, 40e6, 6e6),
        name="attn_bwd",
    )(
        length, places, gates, rows, dx_home, gate_grads, shared_dx, ffn_in, hidden_rows, grad_ffn,
        layer_rows, attn_in, first_all, first_all, qkv_rot, context, cosine, sine, shared_y,
        y_near, shares, late,
    )


def finish_kernel(
    gi_in, lo_in, proj_ref, early_ref, late_ref, total_ref, small_ref, gi_ref, lo_ref, *refs
):
    gi_ref[...] = gi_in[...]
    lo_ref[...] = lo_in[...]
    for pair in range(proj_ref.shape[0]):
        for kind in range(4):
            refs[kind][:, pair * LANES : (pair + 1) * LANES] = proj_ref[
                pair, :, kind * LANES : (kind + 1) * LANES
            ]
    experts = refs[4].shape[1]
    part = early_ref.shape[-1]
    for kind in range(3):
        for index, ref in enumerate((early_ref, late_ref)):
            for expert in range(experts):
                total = ref[expert, kind].astype(F32)
                for rank in range(expert + experts, ref.shape[0], experts):
                    total += ref[rank, kind].astype(F32)
                refs[4 + kind][:, expert, index * part : (index + 1) * part] = total
    hidden = total_ref.shape[-1] // 3
    for kind in range(3):
        columns = slice(kind * hidden, (kind + 1) * hidden)
        total = total_ref[0, :, columns].astype(F32)
        for place in range(1, total_ref.shape[0]):
            total += total_ref[place, :, columns].astype(F32)
        refs[7 + kind][...] = total
    total = small_ref[0]
    for rank in range(1, small_ref.shape[0]):
        total += small_ref[rank]
    refs[10][...] = total


def finish(rows, outputs, proj, early, late, total, small, experts):
    pairs, shard, _ = proj.shape
    hidden = total.shape[-1] // 3
    forms = (
        [(rows.shape, BF16)] * 2
        + [((shard, pairs * LANES), F32)] * 4
        + [((shard, experts, hidden), F32)] * 3
        + [((shard, hidden), F32)] * 3
        + [((shard, LANES), F32)]
    )
    args = (rows, outputs, proj, early, late, total, small)
    return pl.pallas_call(
        finish_kernel,
        grid=(1,),
        in_specs=[whole(v.shape) for v in args],
        out_specs=[whole(form) for form, _ in forms],
        out_shape=[jax.ShapeDtypeStruct(form, kind) for form, kind in forms],
        compiler_params=params(1),
        cost_estimate=cost(1e7, 2e7),
        name="finish",
    )(*args)


def column_of(row):
    count = row.shape[1]
    shape = (count, count)
    same = lax.broadcasted_iota(jnp.int32, shape, 0) == lax.broadcasted_iota(jnp.int32, shape, 1)
    return jnp.sum(jnp.where(same, row, 0.0), axis=1, keepdims=True)


def row_of(column):
    count = column.shape[0]
    shape = (count, count)
    same = lax.broadcasted_iota(jnp.int32, shape, 0) == lax.broadcasted_iota(jnp.int32, shape, 1)
    return jnp.sum(jnp.where(same, column, 0.0), axis=0, keepdims=True)


def ffn_block(x, grad, gate, gate_w, up_w, down_w, sums):
    gate_pre = mm(x, gate_w, NN)
    up_pre = mm(x, up_w, NN)
    sig = jax.nn.sigmoid(gate_pre)
    act = gate_pre * sig
    inner = (act * up_pre).astype(BF16)
    out = mm(inner, down_w, NT)
    gate_grad, out_grad = None, grad
    if gate is not None:
        wide = grad.astype(F32)
        gate_grad = jnp.sum(out * wide, axis=1, keepdims=True)
        out = out * gate
        out_grad = (wide * gate).astype(BF16)
    inner_grad = mm(out_grad, down_w, NN)
    gate_pre_grad = (inner_grad * up_pre * (sig + act * (1.0 - sig))).astype(BF16)
    up_pre_grad = (inner_grad * act).astype(BF16)
    row_grad = mm(gate_pre_grad, gate_w, NT) + mm(up_pre_grad, up_w, NT)
    sums[0][...] += mm(x, gate_pre_grad, TN)
    sums[1][...] += mm(x, up_pre_grad, TN)
    sums[2][...] += mm(out_grad, inner, TN)
    return out, row_grad, gate_grad


def sides(rank):
    x, y = lax.rem(rank, 2), lax.rem(lax.div(rank, 2), 2)
    return x, y, flip(rank, 1), flip(rank, 2)


def block_of(x_ref, d_ref, g_ref, w_refs, sums):
    slots, width = x_ref.shape[1:]
    shape = (width, w_refs[0].shape[-1])
    gate = column_of(jnp.concatenate([g_ref[0, 0:1, :], g_ref[1, 0:1, :]], axis=1))
    return ffn_block(
        x_ref[...].reshape(2 * slots, width), d_ref[...].reshape(2 * slots, width), gate,
        *(w_ref[...].reshape(shape) for w_ref in w_refs), sums,
    )


def put_sums(og_ref, sums):
    for index, total in enumerate(sums):
        og_ref[:, index] = total[...].astype(BF16).reshape(og_ref.shape[0], *og_ref.shape[2:])


def expert_first_kernel(
    x_ref, d_ref, g_ref, wg_ref, wu_ref, wd_ref, share_ref, late_ref,
    y_ref, dx_ref, dg_ref, og_ref, sx_ref, sy_ref, late_out,
    ag, au, ad, own_x, own_y, in_x, in_y, send, recv, local, *sems,
    experts, ranks, halves,
):
    step = pl.program_id(0)
    sums = (ag, au, ad)
    me, core = lax.axis_index("dp"), lax.axis_index("tensor")
    x, y, x_rank, y_rank = sides(me)
    cut = share_ref.shape[-1] // 2
    low, high = pl.ds(0, cut), pl.ds(cut, cut)

    def over_x(place):
        return share_ref.at[:, :, place, :, low]

    def over_y(place):
        return share_ref.at[:, place, :, :, high]

    deal = Deal(
        lambda rank: late_ref.at[lax.rem(rank, experts)], lambda rank: late_out.at[rank], *sems, ranks
    )

    def copies():
        return (
            remote(over_x(1 - x), in_x, send.at[0], recv.at[0], device(x_rank, core)),
            remote(over_y(1 - y), in_y, send.at[1], recv.at[1], device(y_rank, core)),
        )

    def loads():
        return (
            pltpu.make_async_copy(over_x(x), own_x, local.at[0]),
            pltpu.make_async_copy(over_y(y), own_y, local.at[1]),
        )

    @pl.when(step == 0)
    def _():
        for total in sums:
            total[...] = jnp.zeros_like(total)
        if halves:
            greet(all_and_core(ranks))
            for copy in copies() + loads():
                copy.start()
            deal.start(3)

    out, row_grad, gate_grad = block_of(x_ref, d_ref, g_ref, (wg_ref, wu_ref, wd_ref), sums)
    y_ref[...] = out
    dx_ref[...] = row_grad
    dg_ref[...] = jnp.broadcast_to(row_of(gate_grad), dg_ref.shape)

    @pl.when(step == pl.num_programs(0) - 1)
    def _():
        put_sums(og_ref, sums)
        if halves:
            for copy in copies() + loads():
                copy.wait()
            sx_ref[...] = (own_x[...].astype(F32) + in_x[...].astype(F32)).astype(BF16)
            sy_ref[...] = (own_y[...].astype(F32) + in_y[...].astype(F32)).astype(BF16)
            deal.wait()


def expert_specs(experts, slots, width, weights, order):
    def group(shape):
        return pl.BlockSpec((None,) + shape, lambda i: (order(i),) + (0,) * len(shape))

    parts, _, shard, hidden = weights.shape
    matrices = [
        pl.BlockSpec(
            (parts, None, shard, hidden), lambda i, k=k: (0, k, 0, 0),
            pipeline_mode=pl.Buffered(1),
        )
        for k in range(3)
    ]
    return group, matrices, [pltpu.VMEM((width, hidden), F32)] * 3


def expert_first(x_slots, d_slots, g_slots, weights, shares, late, halves):
    experts, _, slots, width = x_slots.shape
    hidden = weights.shape[-1]
    ranks = lax.axis_size("dp")
    group, matrices, sums = expert_specs(experts, slots, width, weights, lambda i: i)
    rows = group((2, slots, width))
    if halves:
        _, _, _, shard, columns = shares.shape
        part = (shares.shape[0], 2, shard, columns // 2)
    else:
        part = (1, 1, 16, LANES)
    return pl.pallas_call(
        functools.partial(expert_first_kernel, experts=experts, ranks=ranks, halves=halves),
        grid=(experts,),
        in_specs=[rows, rows, group((2, 8, slots))]
        + matrices
        + [pl.BlockSpec(memory_space=pl.ANY)] * 2,
        out_specs=[group((2 * slots, width))] * 2
        + [group((8, 2 * slots)), whole(weights.shape), whole(part), whole(part)]
        + [pl.BlockSpec(memory_space=pl.ANY)],
        out_shape=[jax.ShapeDtypeStruct((experts, 2 * slots, width), F32)] * 2
        + [
            jax.ShapeDtypeStruct((experts, 8, 2 * slots), F32),
            jax.ShapeDtypeStruct(weights.shape, BF16),
            jax.ShapeDtypeStruct(part, BF16),
            jax.ShapeDtypeStruct(part, BF16),
            jax.ShapeDtypeStruct((ranks,) + late.shape[1:] if halves else (1, 16, LANES), BF16),
        ],
        scratch_shapes=sums
        + [pltpu.VMEM(part, BF16)] * 4
        + [pltpu.SemaphoreType.DMA((2,))] * 3
        + Deal.semaphores(ranks),
        compiler_params=remote_params(6) if halves else params(1),
        cost_estimate=cost(36 * experts * slots * width * hidden, 40e6),
        name="expert_first",
    )(x_slots, d_slots, g_slots, weights, weights, weights, shares, late)


def expert_second_kernel(
    x_ref, d_ref, g_ref, wg_ref, wu_ref, wd_ref, yf_ref, dxf_ref, dgf_ref, sx_ref, sy_ref,
    y_ref, dx_home, dg_home, og_ref, share_ref,
    ag, au, ad, own_y, own_dx, ys, dxs, yp, dxp, dgs, out_x, out_y, in_x, in_y,
    core_send, core_recv, send, recv, local, share_send, share_recv, *, experts, halves,
):
    step = pl.program_id(0)
    block = experts - 1 - step
    sums = (ag, au, ad)
    me, core = lax.axis_index("dp"), lax.axis_index("tensor")
    mine = lax.rem(me, experts)
    other = device(me, 1 - core)
    slots = x_ref.shape[1]
    x, y, x_rank, y_rank = sides(me)

    def rank_at(k):
        total, bit = me - mine, 1
        while bit < experts:
            total += bit * lax.rem(lax.div(mine, bit) + lax.div(k, bit), 2)
            bit *= 2
        return total

    def core_copy(k, part):
        src, dst = ((ys, yp), (dxs, dxp))[part]
        return remote(
            src.at[lax.rem(k, 2)], dst.at[k], core_send.at[part, k], core_recv.at[part, k], other
        )

    def home_copy(k, part):
        src, dst = ((dxp, dx_home), (dgs, dg_home))[part]
        return remote(
            src.at[k], dst.at[mine], send.at[part, k], recv.at[part, k],
            device(rank_at(k), core),
        )

    def own_copy(part):
        src, dst = ((dxp, dx_home), (dgs, dg_home))[part]
        return pltpu.make_async_copy(src.at[0], dst.at[mine], local.at[part])

    def go_home(k, part):
        @pl.when(k == 0)
        def _():
            own_copy(part).start()

        @pl.when(k > 0)
        def _():
            home_copy(k, part).start()

    def share_copies():
        return (
            remote(out_x, in_x, share_send.at[0], share_recv.at[0], device(y_rank, core)),
            remote(out_y, in_y, share_send.at[1], share_recv.at[1], device(x_rank, core)),
        )

    @pl.when(step == 0)
    def _():
        greet(cluster_and_core(experts))
        for total in sums:
            total[...] = jnp.zeros_like(total)
        if halves:
            out_x[...] = sx_ref[:, pl.ds(1 - y, 1)]
            out_y[...] = sy_ref[:, pl.ds(1 - x, 1)]
            for copy in share_copies():
                copy.start()

    def settle(k):
        for part in (1, 0):
            core_copy(k, part).wait_recv()
            own, shared = ((own_y, yp), (own_dx, dxp))[part]
            total = (own[...] + shared[k].astype(F32)).astype(BF16)
            if part:
                dxp[k] = total
                go_home(k, 0)
            else:
                y_ref[...] = total

    @pl.when(step < experts)
    def _():
        out, row_grad, gate_grad = block_of(x_ref, d_ref, g_ref, (wg_ref, wu_ref, wd_ref), sums)
        out += yf_ref[...]
        row_grad += dxf_ref[...]

        @pl.when(step >= 1)
        def _():
            settle(block + 1)

        for part in (1, 0):

            @pl.when(step >= 2)
            def _():
                core_copy(block + 2, part).wait_send()

            own, half = ((own_y, ys), (own_dx, dxs))[part]
            value = (out, row_grad)[part]
            own[...] = value[:slots]
            half[lax.rem(block, 2)] = value[slots:].astype(BF16)
            core_copy(block, part).start()
        dgs[block] = jnp.broadcast_to(row_of(gate_grad), dgs.shape[1:]) + dgf_ref[...]
        go_home(block, 1)

    @pl.when(step == experts)
    def _():
        settle(block + 1)
        put_sums(og_ref, sums)
        if halves:
            cut = out_x.shape[-1]
            for copy in share_copies():
                copy.wait()
            kept_x, kept_y = sx_ref[:, pl.ds(y, 1)], sy_ref[:, pl.ds(x, 1)]
            total_x = kept_x.astype(F32) + in_x[...].astype(F32)
            total_y = kept_y.astype(F32) + in_y[...].astype(F32)
            share_ref[:, :, :cut] = total_x.astype(BF16).reshape(share_ref.shape[0], -1, cut)
            share_ref[:, :, cut:] = total_y.astype(BF16).reshape(share_ref.shape[0], -1, cut)
        for part in (0, 1):
            for k in (0, 1):
                core_copy(k, part).wait_send()
            own_copy(part).wait()
            for k in range(1, experts):
                home_copy(k, part).wait()


def expert_second(x_slots, d_slots, g_slots, weights, first, halves):
    experts, _, slots, width = x_slots.shape
    hidden = weights.shape[-1]
    y_first, dx_first, dg_first, sx, sy = first
    far = pl.BlockSpec(memory_space=pl.ANY)
    group, matrices, sums = expert_specs(
        experts, slots, width, weights, lambda i: jnp.maximum(experts - 1 - i, 0)
    )
    rows = group((2, slots, width))
    long, _, shard, cut = sx.shape
    share = (long, shard, 2 * cut)
    return pl.pallas_call(
        functools.partial(expert_second_kernel, experts=experts, halves=halves),
        grid=(experts + 1,),
        in_specs=[rows, rows, group((2, 8, slots))]
        + matrices
        + [group((2 * slots, width))] * 2
        + [group((8, 2 * slots)), whole(sx.shape), whole(sy.shape)],
        out_specs=[
            pl.BlockSpec((None, slots, width), lambda i: (jnp.minimum(experts - i, experts - 1), 0, 0)),
            far,
            far,
            whole(weights.shape),
            whole(share),
        ],
        out_shape=[
            jax.ShapeDtypeStruct((experts, slots, width), BF16),
            jax.ShapeDtypeStruct((experts, slots, width), BF16),
            jax.ShapeDtypeStruct((experts, 8, 2 * slots), F32),
            jax.ShapeDtypeStruct(weights.shape, BF16),
            jax.ShapeDtypeStruct(share, BF16),
        ],
        scratch_shapes=sums
        + [pltpu.VMEM((slots, width), F32)] * 2
        + [pltpu.VMEM((2, slots, width), BF16)] * 2
        + [pltpu.VMEM((experts, slots, width), BF16)] * 2
        + [pltpu.VMEM((experts, 8, 2 * slots), F32)]
        + [pltpu.VMEM((long, 1, shard, cut), BF16)] * 4
        + [pltpu.SemaphoreType.DMA((2, experts))] * 4
        + [pltpu.SemaphoreType.DMA((2,))] * 3,
        compiler_params=remote_params(3),
        cost_estimate=cost(36 * experts * slots * width * hidden, 40e6),
        name="expert_second",
    )(x_slots, d_slots, g_slots, weights, weights, weights, y_first, dx_first, dg_first, sx, sy)


def to_all(values, groups=None):
    count = lax.axis_size("dp") if groups is None else len(groups[0])
    copies = jnp.broadcast_to(values[None], (count,) + values.shape)
    return lax.all_to_all(copies, "dp", 0, 0, axis_index_groups=groups, tiled=True)


def after(values, *earlier):
    return lax.optimization_barrier((values,) + earlier)[0]


def per_device(
    layer_input, seq_lengths, expert_routes, w_query, w_key, w_value, w_output,
    gain_attn, gain_ffn, router_weight, expert_gate, expert_up, expert_down,
    shared_gate, shared_up, shared_down, out_cotangent,
):
    ranks = lax.axis_size("dp")
    _, own_len, width = layer_input.shape
    span = 2 * own_len
    shard = w_query.shape[0]
    pairs = w_query.shape[1] // LANES
    experts, hidden = expert_gate.shape[1:]
    capacity = 4 * span // experts
    slots = capacity // 2
    groups = [list(range(s, s + experts)) for s in range(0, ranks, experts)]

    small_own = jnp.concatenate(
        [gain_attn[:, None], gain_ffn[:, None], router_weight], axis=1
    )
    small_own = jnp.pad(small_own, ((0, 0), (0, LANES - small_own.shape[1])))
    first_all, shared_all = gather_weights(
        (w_query, w_key, w_value, w_output), small_own, (shared_gate, shared_up, shared_down)
    )
    first_all = first_all.reshape(width, first_all.shape[-1])
    if shard % 16:
        shared_all = shared_all.reshape(1, width, shared_all.shape[-1])

    half = HD // 2
    inverse = np.exp(np.arange(half, dtype=np.float32) * np.float32(-math.log(10000.0) / half))
    angles = np.arange(span, dtype=np.float32)[:, None] * inverse[None, :]
    cos_half, sin_half = np.cos(angles), np.sin(angles)
    cosine = np.concatenate([cos_half] * 4, axis=1)
    sine = np.concatenate([-sin_half, sin_half] * 2, axis=1)

    direct = shard % 16 == 0
    halves = ranks == 16

    def by_expert(columns):
        stack = jnp.stack(
            [w[:, :, columns] for w in (expert_gate, expert_up, expert_down)], axis=0
        ).astype(BF16)
        return stack.transpose(2, 0, 1, 3).reshape(experts, 3 * shard, stack.shape[-1])

    def to_experts(own):
        part = own.shape[-1]
        copies = jnp.broadcast_to(own[None], (ranks // experts,) + own.shape)
        return lax.all_to_all(copies.reshape(ranks, 3 * shard, part), "dp", 0, 0, tiled=True)

    def matrices(gathered):
        gathered = gathered.reshape(ranks, 3, shard, gathered.shape[-1])
        if direct:
            return gathered
        return gathered.transpose(1, 0, 2, 3).reshape(1, 3, width, gathered.shape[-1])

    def from_experts(grads):
        if not direct:
            grads = grads.reshape(3, ranks, shard, grads.shape[-1]).transpose(1, 0, 2, 3)
        return lax.all_to_all(grads, "dp", 0, 0, tiled=True)

    def to_outputs(grads):
        grads = grads.reshape(ranks // experts, experts, 3, shard, grads.shape[-1])
        return jnp.sum(grads.astype(F32), axis=0)

    early_own = by_expert(slice(0, hidden // 2))
    late_own = by_expert(slice(hidden // 2, hidden))

    (
        attn_in, qkv_rot, context, hidden_rows, ffn_in, grad_ffn, places, small, gates, shared_y,
        shared_dx, d_slots, x_slots, g_slots, shared_grads, early,
    ) = attn_forward(
        seq_lengths, layer_input[0], out_cotangent[0], expert_routes.reshape(span, 2).T,
        first_all, shared_all, early_own, cosine, sine, slots,
    )
    if not halves:
        early = to_experts(early_own)

    if halves:
        shares = shared_grads.reshape(4, 2, 2, shard, 3 * hidden)
    else:
        shares = shared_grads[0, :16, :LANES]
        shared_grads = lax.all_to_all(
            shared_grads.reshape(ranks, shard, 3 * hidden), "dp", 0, 0, tiled=True
        )

    y_first, dx_first, dg_first, early_grads, sx, sy, late = expert_first(
        x_slots, d_slots, g_slots, matrices(early), shares, late_own, halves
    )
    if not halves:
        late = to_experts(late_own)
    early_grads = from_experts(early_grads)
    y_near, dx_home, gate_grads, late_grads, shares = expert_second(
        x_slots, d_slots, g_slots, matrices(late), (y_first, dx_first, dg_first, sx, sy), halves
    )
    late_grads = after(late_grads, early_grads)

    grad_input, layer_output, *grads = attn_backward(
        seq_lengths, places, gates, small, dx_home, gate_grads, y_near, shared_y, shares,
        late_grads, shared_dx, ffn_in, hidden_rows, grad_ffn, layer_input[0], attn_in,
        first_all, qkv_rot, context, cosine, sine, ranks, halves,
    )
    if halves:
        proj, late_in, total, small_in = grads
        grad_input, layer_output, *grads = finish(
            grad_input, layer_output, proj, early_grads, late_in, total, small_in, experts
        )
        attn_grads, expert_grads, shared_grads, small_grads = (
            grads[:4], grads[4:7], grads[7:10], grads[10]
        )
    else:
        attn_grads = grads[0].reshape(pairs, ranks, shard, 4 * LANES).transpose(1, 0, 2, 3)
        attn_grads = lax.all_to_all(attn_grads, "dp", 0, 0, tiled=True)
        attn_grads = jnp.sum(attn_grads.astype(F32), axis=0).reshape(pairs, shard, 4, LANES)
        attn_grads = [
            attn_grads[:, :, k].transpose(1, 0, 2).reshape(shard, pairs * LANES) for k in range(4)
        ]
        small_grads = lax.all_to_all(grads[1].reshape(ranks, shard, LANES), "dp", 0, 0, tiled=True)
        small_grads = jnp.sum(small_grads, axis=0)
        shared_grads = jnp.sum(shared_grads.astype(F32), axis=0)
        shared_grads = [shared_grads[:, k * hidden : (k + 1) * hidden] for k in range(3)]
        late_grads = from_experts(late_grads)
        expert_grads = jnp.concatenate([to_outputs(early_grads), to_outputs(late_grads)], axis=-1)
        expert_grads = [expert_grads[:, k].transpose(1, 0, 2) for k in range(3)]
    return (
        layer_output[None], grad_input[None],
        attn_grads[0], attn_grads[1], attn_grads[2], attn_grads[3],
        small_grads[:, 0], small_grads[:, 1], small_grads[:, 2 : 2 + experts],
        expert_grads[0], expert_grads[1], expert_grads[2],
        shared_grads[0], shared_grads[1], shared_grads[2],
    )


def solution(mesh):
    tokens = P("dp", "tensor", None)
    matrix = P("dp", "tensor")
    expert = P("dp", None, "tensor")
    in_specs = (
        (tokens, P("dp"), P("dp", None, None))
        + (matrix,) * 4
        + (P("dp"), P("dp"), P("dp", None))
        + (expert,) * 3
        + (matrix,) * 3
        + (tokens,)
    )
    out_specs = (
        (tokens, tokens)
        + (matrix,) * 4
        + (P("dp"), P("dp"), P("dp", None))
        + (expert,) * 3
        + (matrix,) * 3
    )
    return jax.shard_map(
        per_device, mesh=mesh, in_specs=in_specs, out_specs=out_specs, check_vma=False
    )
```

```python
import functools
import math

import jax
import jax.numpy as jnp
import numpy as np
from jax import lax
from jax.experimental import pallas as pl
from jax.experimental.pallas import tpu as pltpu
from jax.sharding import PartitionSpec as P

HD = 64
LANES = 128
EPS = 1e-06
F32 = jnp.float32
BF16 = jnp.bfloat16
HIGHEST = lax.Precision.HIGHEST
VMEM_LIMIT = 60 * 1024 * 1024

NN = (((1,), (0,)), ((), ()))
NT = (((1,), (1,)), ((), ()))
TN = (((0,), (0,)), ((), ()))


def mm(left, right, dims):
    return lax.dot_general(left, right, dims, preferred_element_type=F32)


def params(count):
    return pltpu.CompilerParams(
        dimension_semantics=("arbitrary",) * count, vmem_limit_bytes=VMEM_LIMIT
    )


def remote_params(number):
    return pltpu.CompilerParams(
        collective_id=number, has_side_effects=True, vmem_limit_bytes=VMEM_LIMIT,
        dimension_semantics=("arbitrary",),
    )


def cost(flops, nbytes, trans=0):
    return pl.CostEstimate(flops=int(flops), bytes_accessed=int(nbytes), transcendentals=int(trans))


def flip(index, offset):
    bit = 1
    while bit <= offset:
        if offset & bit:
            index = index + bit - 2 * bit * lax.rem(lax.div(index, bit), 2)
        bit *= 2
    return index


def device(rank, core):
    return {"dp": rank, "tensor": core}


def greet(devices):
    barrier = pltpu.get_barrier_semaphore()
    for target in devices:
        pl.semaphore_signal(barrier, inc=1, device_id=target, device_id_type=pl.DeviceIdType.MESH)
    pl.semaphore_wait(barrier, len(devices))


def remote(src, dst, send, recv, target):
    return pltpu.make_async_remote_copy(
        src_ref=src, dst_ref=dst, send_sem=send, recv_sem=recv,
        device_id=target, device_id_type=pl.DeviceIdType.MESH,
    )


class Deal:
    def __init__(self, source, place, send, recv, local, ranks):
        self.source, self.place, self.ranks = source, place, ranks
        self.send, self.recv, self.local = send, recv, local
        self.me, self.core = lax.axis_index("dp"), lax.axis_index("tensor")

    @staticmethod
    def semaphores(ranks):
        dma = pltpu.SemaphoreType.DMA
        return [dma((ranks,)), dma((ranks,)), dma]

    def own(self):
        return pltpu.make_async_copy(self.source(self.me), self.place(self.me), self.local)

    order = (12, 1, 8, 2, 13, 4, 9, 3, 14, 5, 10, 6, 15, 7, 11)

    def share(self, offset):
        rank = flip(self.me, offset)
        return remote(
            self.source(rank), self.place(self.me), self.send.at[offset], self.recv.at[offset],
            device(rank, self.core),
        )

    def each(self, body):
        for offset in self.order:
            body(self.share(offset))

    def start(self, pieces=1):
        self.own().start()
        for piece in range(pieces):
            for offset in self.order:
                rank = flip(self.me, offset)
                source, place = self.source(rank), self.place(self.me)
                rows = source.shape[0] // pieces
                here = pl.ds(piece * rows, rows)
                remote(
                    source.at[here], place.at[here], self.send.at[offset], self.recv.at[offset],
                    device(rank, self.core),
                ).start()

    def wait(self):
        self.own().wait()
        self.each(lambda copy: copy.wait())


def all_and_core(ranks):
    me, core = lax.axis_index("dp"), lax.axis_index("tensor")
    return [device(lax.rem(me + k, ranks), core) for k in range(1, ranks)] + [device(me, 1 - core)]


class Gather:
    order = (0, 1, 4, 2, 5, 3, 6)
    turns = 9

    def __init__(self, own_ref, out_ref, sems, which):
        self.own_ref, self.out_ref = own_ref, out_ref
        self.own_sem, self.z_send, self.z_recv, self.s_send, self.s_recv, self.f_send, self.f_recv = (
            sem.at[which] for sem in sems
        )
        self.cut = own_ref.shape[1] // 2 // LANES * LANES
        self.me, self.core = lax.axis_index("dp"), lax.axis_index("tensor")
        self.z = lax.div(self.me, 4)
        self.up, self.down = lax.min(self.me + 4, 15), lax.max(self.me - 4, 0)
        self.sides_of = (flip(self.me, 1), flip(self.me, 2))

    @staticmethod
    def semaphores(count):
        dma = pltpu.SemaphoreType.DMA
        return [dma((count,)), dma((count, 6)), dma((count, 6))] + [dma((count, 2, 7))] * 4

    def rank_at(self, place):
        return self.me - 4 * place if place <= 3 else self.me + 4 * (place - 3)

    def at(self, place, body):
        if place == 0:
            body()
        else:
            pl.when(self.z >= place if place <= 3 else self.z + (place - 3) <= 3)(body)

    def own_copy(self):
        return pltpu.make_async_copy(self.own_ref, self.out_ref.at[self.me], self.own_sem)

    def z_copy(self, rank, step, upward):
        index = step - 1 if upward else step + 2
        return remote(
            self.own_ref if step == 1 else self.out_ref.at[rank], self.out_ref.at[rank],
            self.z_send.at[index], self.z_recv.at[index],
            device(self.up if upward else self.down, self.core),
        )

    def side_copy(self, rank, place, axis):
        return remote(
            self.own_ref if place == 0 else self.out_ref.at[rank], self.out_ref.at[rank],
            self.s_send.at[axis, place], self.s_recv.at[axis, place],
            device(self.sides_of[axis], self.core),
        )

    def onward_copy(self, rank, place, axis):
        width = self.own_ref.shape[1]
        columns = pl.ds(0, self.cut) if axis == 0 else pl.ds(self.cut, width - self.cut)
        part = self.out_ref.at[rank, :, columns]
        return remote(
            part, part, self.f_send.at[axis, place], self.f_recv.at[axis, place],
            device(self.sides_of[1 - axis], self.core),
        )

    def begin(self):
        self.own_copy().start()
        pl.when(self.z < 3)(lambda: self.z_copy(self.me, 1, True).start())
        pl.when(self.z > 0)(lambda: self.z_copy(self.me, 1, False).start())
        for axis in range(2):
            self.side_copy(self.me, 0, axis).start()

    def arrive(self, place):
        upward = place <= 3
        step = place if upward else place - 3
        rank = self.rank_at(place)
        self.z_copy(rank, step, upward).wait_recv()
        if step < 3:
            further = self.z < 3 if upward else self.z > 0
            pl.when(further)(lambda: self.z_copy(rank, step + 1, upward).start())
        for axis in range(2):
            self.side_copy(rank, place, axis).start()

    def onward(self, place):
        for axis in range(2):
            rank = flip(self.rank_at(place), 1 + axis)
            self.side_copy(rank, place, axis).wait_recv()
            self.onward_copy(rank, place, axis).start()

    def turn(self, index):
        if index < 7:
            self.at(self.order[index], functools.partial(self.arrive, self.order[index]))
        if index >= 2:
            self.at(self.order[index - 2], functools.partial(self.onward, self.order[index - 2]))

    def finish(self, place):
        for axis in range(2):
            rank = flip(self.rank_at(place), 1 + axis)
            self.side_copy(self.rank_at(place), place, axis).wait_send()
            self.onward_copy(rank, place, axis).wait_send()
            self.onward_copy(flip(self.rank_at(place), 3), place, axis).wait_recv()

    def end(self):
        z = self.z
        for place in self.order:
            self.at(place, functools.partial(self.finish, place))
        for step in range(1, 4):
            pl.when((z < 3) & (z >= step - 1))(
                lambda step=step: self.z_copy(self.me - 4 * (step - 1), step, True).wait_send()
            )
            pl.when((z > 0) & (z + step - 1 <= 3))(
                lambda step=step: self.z_copy(self.me + 4 * (step - 1), step, False).wait_send()
            )
        self.own_copy().wait()


def gather_kernel(
    wq_ref, wk_ref, wv_ref, wo_ref, small_ref, sg_ref, su_ref, sd_ref, eg_ref, eu_ref, ed_ref,
    first_out, shared_out, early_out, late_out,
    first_s, shared_s, raw_s, packed_s, load, store, *sems,
):
    loads = [
        pltpu.make_async_copy(ref, raw_s.at[kind], load.at[kind])
        for kind, ref in enumerate((eg_ref, eu_ref, ed_ref))
    ]
    for copy in loads:
        copy.start()
    pairs = wq_ref.shape[1] // LANES
    for pair in range(pairs):
        columns = slice(pair * LANES, (pair + 1) * LANES)
        for kind, ref in enumerate((wq_ref, wk_ref, wv_ref)):
            start = (3 * pair + kind) * LANES
            first_s[:, start : start + LANES] = ref[:, columns].astype(BF16)
    first_s[:, 3 * pairs * LANES : 4 * pairs * LANES] = wo_ref[...].astype(BF16)
    first_s[:, 4 * pairs * LANES :] = small_ref[...].astype(BF16)
    hidden = sg_ref.shape[1]
    for kind, ref in enumerate((sg_ref, su_ref, sd_ref)):
        shared_s[:, kind * hidden : (kind + 1) * hidden] = ref[...].astype(BF16)

    gathers = Gather(first_s, first_out, sems, 0), Gather(shared_s, shared_out, sems, 1)
    z, core = gathers[0].z, gathers[0].core
    barrier = pltpu.get_barrier_semaphore()

    def hello(rank):
        pl.semaphore_signal(
            barrier, inc=1, device_id=device(rank, core), device_id_type=pl.DeviceIdType.MESH
        )

    for rank in gathers[0].sides_of:
        hello(rank)
    pl.when(z < 3)(lambda: hello(gathers[0].up))
    pl.when(z > 0)(lambda: hello(gathers[0].down))
    pl.semaphore_wait(barrier, 2 + lax.min(z, 1) + lax.min(3 - z, 1))
    for gather in gathers:
        gather.begin()
    _, rows, experts, _ = raw_s.shape
    part = packed_s.shape[-1]
    for copy in loads:
        copy.wait()
    for turn in range(1, Gather.turns):
        for gather in gathers:
            gather.turn(turn)
        for expert in range(turn - 1, experts, Gather.turns - 1):
            for kind in range(3):
                for half in range(2):
                    packed_s[half, expert, kind * rows : (kind + 1) * rows, :] = raw_s[
                        kind, :, expert, half * part : (half + 1) * part
                    ].astype(BF16)
    count = early_out.shape[0] // experts
    stores = [
        pltpu.make_async_copy(
            packed_s.at[0], early_out.at[pl.ds(index * experts, experts)], store.at[index]
        )
        for index in range(count)
    ] + [pltpu.make_async_copy(packed_s.at[1], late_out, store.at[count])]
    for copy in stores:
        copy.start()
    for copy in stores:
        copy.wait()
    for gather in gathers:
        gather.end()


def gather_weights(attention, small, shared, expert):
    ranks = lax.axis_size("dp")
    rows, heads_width = attention[0].shape
    columns = 4 * heads_width + LANES
    hidden = shared[0].shape[1]
    if ranks != 16:
        pairs = heads_width // LANES
        qkv = jnp.stack(attention[:3], axis=1).reshape(rows, 3, pairs, LANES)
        qkv = qkv.transpose(0, 2, 1, 3).reshape(rows, 3 * heads_width)
        first = jnp.concatenate([qkv, attention[3], small], axis=1).astype(BF16)
        stack = jnp.stack(expert, axis=0).astype(BF16).transpose(2, 0, 1, 3)
        stack = stack.reshape(stack.shape[0], 3 * rows, hidden)
        early, late = stack[:, :, : hidden // 2], stack[:, :, hidden // 2 :]
        early = jnp.concatenate([early] * (ranks // early.shape[0]), axis=0)
        return (
            to_all(first), to_all(jnp.concatenate(shared, axis=1).astype(BF16)), early, late
        )
    vmem = pl.BlockSpec(memory_space=pltpu.VMEM)
    far = pl.BlockSpec(memory_space=pl.ANY)
    experts = expert[0].shape[1]
    return pl.pallas_call(
        gather_kernel,
        in_specs=[vmem] * 8 + [far] * 3,
        out_specs=[far] * 4,
        out_shape=[
            jax.ShapeDtypeStruct((ranks, rows, columns), BF16),
            jax.ShapeDtypeStruct((ranks, rows, 3 * hidden), BF16),
            jax.ShapeDtypeStruct((ranks, 3 * rows, hidden // 2), BF16),
            jax.ShapeDtypeStruct((experts, 3 * rows, hidden // 2), BF16),
        ],
        scratch_shapes=[
            pltpu.VMEM((rows, columns), BF16),
            pltpu.VMEM((rows, 3 * hidden), BF16),
            pltpu.VMEM((3, rows, experts, hidden), F32),
            pltpu.VMEM((2, experts, 3 * rows, hidden // 2), BF16),
            pltpu.SemaphoreType.DMA((3,)),
            pltpu.SemaphoreType.DMA((ranks // experts + 1,)),
        ]
        + Gather.semaphores(2),
        compiler_params=pltpu.CompilerParams(
            collective_id=1, has_side_effects=True, vmem_limit_bytes=VMEM_LIMIT
        ),
        cost_estimate=cost(1e6, 100e6),
        name="gather_weights",
    )(*attention, small, *shared, *expert)


def partner(values):
    lane = lax.broadcasted_iota(jnp.int32, values.shape, 1)
    return jnp.where(
        lane % HD < HD // 2,
        pltpu.roll(values, LANES - HD // 2, 1),
        pltpu.roll(values, HD // 2, 1),
    )


def head_lanes(shape, head):
    lane = lax.broadcasted_iota(jnp.int32, shape, 1)
    return (lane // HD) == head


def offsets(count):
    return sorted(range(1, count), key=lambda k: (bin(k).count("1"), k))


class Trip:
    def __init__(self, ins, outs, send, recv, core_send, core_recv, local, part):
        self.ins, self.outs, self.part = ins, outs, part
        self.send, self.recv, self.local = send, recv, local
        self.core_send, self.core_recv = core_send, core_recv
        self.me, self.core = lax.axis_index("dp"), lax.axis_index("tensor")
        self.count = ins.shape[0]

    def copy(self, k):
        return remote(
            self.ins.at[k], self.outs.at[k, 0],
            self.send.at[self.part, k], self.recv.at[self.part, k],
            device(flip(self.me, k), self.core),
        )

    def core_copy(self, k):
        src = self.ins.at[0] if k == 0 else self.outs.at[k, 0]
        return remote(
            src, self.outs.at[k, 1],
            self.core_send.at[self.part, k], self.core_recv.at[self.part, k],
            device(self.me, 1 - self.core),
        )

    def own(self):
        return pltpu.make_async_copy(self.ins.at[0], self.outs.at[0, 0], self.local.at[self.part])

    def go(self, k):
        if k:
            self.copy(k).start()
        else:
            self.own().start()
            self.core_copy(0).start()

    def pass_on(self, k):
        self.copy(k).wait_recv()
        self.core_copy(k).start()

    def end(self):
        self.own().wait()
        for k in range(self.count):
            self.core_copy(k).wait()
            if k:
                self.copy(k).wait_send()


def cluster_and_core(count):
    me, core = lax.axis_index("dp"), lax.axis_index("tensor")
    return [device(flip(me, k), core) for k in range(1, count)] + [device(me, 1 - core)]


def rms(values):
    return values * lax.rsqrt(jnp.mean(values * values, axis=-1, keepdims=True) + EPS)


def whole(shape):
    return pl.BlockSpec(shape, lambda i: (0,) * len(shape), pipeline_mode=pl.Buffered(1))


def attn_fwd_kernel(
    len_ref, x_ref, c_ref, routes_ref, w_ref, wo_ref, small_ref, cos_ref, sin_ref, shared_ref,
    a_ref, qkv_ref, ctx_ref, h_ref, b_ref, d_ref, places_ref, rows_ref, gates_ref, y_ref, dx_ref, dr, xr, gr, og_ref,
    ds, xs, gs, ag, au, ad, shared_w, part, x_in, h_in, b_out, b_in, c_out, c_in,
    send, recv, core_send, core_recv, local, pair_send, pair_recv, load, *, block,
):
    step = pl.program_id(0)
    me, core = lax.axis_index("dp"), lax.axis_index("tensor")
    other = device(me, 1 - core)
    experts, slots, _ = ds.shape
    trips = [
        Trip(ins, outs, send, recv, core_send, core_recv, local, index)
        for index, (ins, outs) in enumerate(((ds, dr), (xs, xr), (gs, gr)))
    ]
    slot = core * slots + lax.broadcasted_iota(jnp.int32, (slots, a_ref.shape[0]), 0)
    slot = slot.astype(F32)
    mine = lax.rem(me, experts)
    span, width = a_ref.shape
    half = span // 2
    length = len_ref[0]
    own = pl.ds(pl.multiple_of(core * half, half), half)
    away = pl.ds(pl.multiple_of((1 - core) * half, half), half)
    pairs = pl.num_programs(0)

    def to_other(src, dst, index):
        return remote(src, dst, pair_send.at[index], pair_recv.at[index], other)

    @pl.when(step == 0)
    def _():
        greet(cluster_and_core(experts))
        pltpu.make_async_copy(shared_ref, shared_w, load).start()
        token = core * half + lax.broadcasted_iota(jnp.int32, c_ref.shape, 0)
        valid = jnp.where(token < length, c_ref[...].astype(F32), 0.0).astype(BF16)
        c_out[...] = valid
        d_ref[own, :] = valid
        swap_c = to_other(c_out, c_in, 0)
        swap_c.start()
        swap_x = to_other(x_ref, x_in, 1)
        swap_x.start()

        name = lax.broadcasted_iota(jnp.int32, (experts, span), 0)
        chosen = (name == routes_ref[0:1, :]) | (name == routes_ref[1:2, :])
        earlier = lax.broadcasted_iota(jnp.int32, (span, span), 0) < lax.broadcasted_iota(
            jnp.int32, (span, span), 1
        )
        counts = mm(
            jnp.where(chosen, 1.0, 0.0).astype(BF16), jnp.where(earlier, 1.0, 0.0).astype(BF16), NN
        )
        places_ref[...] = jnp.where(chosen, counts, -1.0)

        swap_c.wait_recv()
        d_ref[away, :] = c_in[...]
        for k in offsets(experts) + [0]:
            place = places_ref[pl.ds(flip(mine, k), 1), :]
            hot = jnp.where(slot == place, 1.0, 0.0).astype(BF16)
            ds[k] = mm(hot, d_ref[...], NN).astype(BF16)
            trips[0].go(k)
        rows_ref[...] = small_ref[...].astype(F32).T[: rows_ref.shape[0], :]
        swap_x.wait_recv()
        gain = rows_ref[0:1, :]
        a_ref[own, :] = (rms(x_ref[...].astype(F32)) * gain).astype(BF16)
        a_ref[away, :] = (rms(x_in[...].astype(F32)) * gain).astype(BF16)
        part[...] = jnp.zeros_like(part)
        swap_c.wait_send()
        swap_x.wait_send()

    raw = mm(a_ref[...], w_ref[...], NN)
    cosine, sine = cos_ref[...], sin_ref[...]
    query, key = raw[:, :LANES], raw[:, LANES : 2 * LANES]
    qkv_ref[:, :LANES] = (query * cosine + partner(query) * sine).astype(BF16)
    qkv_ref[:, LANES : 2 * LANES] = (key * cosine + partner(key) * sine).astype(BF16)
    qkv_ref[:, 2 * LANES :] = raw[:, 2 * LANES :].astype(BF16)
    for index in range(span // block):
        keys = (index + 1) * block
        query_rows = qkv_ref[index * block : keys, :LANES] * jnp.asarray(HD**-0.5, BF16)
        key_rows = qkv_ref[:keys, LANES : 2 * LANES]
        value_rows = qkv_ref[:keys, 2 * LANES :]
        row = index * block + lax.broadcasted_iota(jnp.int32, (block, keys), 0)
        column = lax.broadcasted_iota(jnp.int32, (block, keys), 1)
        allowed = (column <= row) & (column < length)
        parts = []
        for head in range(LANES // HD):
            masked_query = jnp.where(
                head_lanes(query_rows.shape, head), query_rows, jnp.zeros_like(query_rows)
            )
            scores = jnp.where(allowed, mm(masked_query, key_rows, NT), -1e30)
            peak = jnp.max(scores, axis=1, keepdims=True)
            powers = jnp.exp(scores - peak)
            total = jnp.sum(powers, axis=1, keepdims=True)
            prob = (powers * (1.0 / total)).astype(BF16)
            parts.append(mm(prob, value_rows, NN))
        context = jnp.where(head_lanes(parts[0].shape, 0), parts[0], parts[1]).astype(BF16)
        ctx_ref[index * block : keys, :] = context
        part[index * block : keys, :] += mm(context, wo_ref[...], NT)

    @pl.when(step == pairs - 1)
    def _():
        swap_h = to_other(part.at[away], h_in, 2)
        swap_h.start()
        rows = x_ref[...].astype(F32) + part[own, :]
        swap_h.wait_recv()
        rows = rows + h_in[...]
        h_ref[...] = rows
        normed = (rms(rows) * rows_ref[1:2, :]).astype(BF16)
        b_out[...] = normed
        swap_b = to_other(b_out, b_in, 3)
        swap_b.start()
        b_ref[own, :] = normed
        swap_b.wait_recv()
        b_ref[away, :] = b_in[...]
        chosen = places_ref[...] >= 0
        logits = mm(rows_ref[2 : 2 + experts, :].astype(BF16), b_ref[...], NT)
        top = jnp.max(jnp.where(chosen, logits, -1e30), axis=0, keepdims=True)
        powers = jnp.where(chosen, jnp.exp(jnp.minimum(logits - top, 0.0)), 0.0)
        gates_ref[...] = powers / jnp.sum(powers, axis=0, keepdims=True)
        for k in offsets(experts) + [0]:
            target = pl.ds(flip(mine, k), 1)
            found = slot == places_ref[target, :]
            xs[k] = mm(jnp.where(found, 1.0, 0.0).astype(BF16), b_ref[...], NN).astype(BF16)
            trips[1].go(k)
            gate = jnp.sum(jnp.where(found, gates_ref[target, :], 0.0), axis=1, keepdims=True)
            gs[k] = jnp.broadcast_to(row_of(gate), gs.shape[1:])
            trips[2].go(k)
        swap_h.wait_send()
        swap_b.wait_send()
        for total in (ag, au, ad):
            total[...] = jnp.zeros_like(total)
        pltpu.make_async_copy(shared_ref, shared_w, load).wait()
        hidden = ag.shape[1]

        def matrix(index):
            return shared_w[:, :, index * hidden : (index + 1) * hidden].reshape(width, hidden)

        def branch(index, carry):
            rows = pl.ds(pl.multiple_of(index * block, block), block)
            out, row_grad, _ = ffn_block(
                b_ref[rows, :], d_ref[rows, :], None, matrix(0), matrix(1), matrix(2), (ag, au, ad)
            )
            y_ref[rows, :] = out.astype(BF16)
            dx_ref[rows, :] = row_grad.astype(BF16)
            return carry

        lax.fori_loop(0, span // block, branch, 0)
        for index, total in enumerate((ag, au, ad)):
            shared_w[:, :, index * hidden : (index + 1) * hidden] = (
                total[...].astype(BF16).reshape(shared_w.shape[0], -1, hidden)
            )
        write = pltpu.make_async_copy(shared_w, og_ref, load)
        write.start()
        for trip in trips:
            for k in offsets(experts):
                trip.pass_on(k)
        for trip in trips:
            trip.end()
        write.wait()


def attn_forward(length, rows, cotangent, routes, first_all, shared_all, cosine, sine, experts, slots):
    half, width = rows.shape
    span = 2 * half
    pairs = (first_all.shape[1] - LANES) // (4 * LANES)
    far = pl.BlockSpec(memory_space=pl.ANY)
    hidden = shared_all.shape[-1] // 3
    return pl.pallas_call(
        functools.partial(attn_fwd_kernel, block=256),
        grid=(pairs,),
        in_specs=[
            pl.BlockSpec(memory_space=pltpu.SMEM),
            whole((half, width)),
            whole((half, width)),
            whole(routes.shape),
            pl.BlockSpec((width, 3 * LANES), lambda i: (0, i)),
            pl.BlockSpec((width, LANES), lambda i: (0, 3 * pairs + i)),
            pl.BlockSpec((width, LANES), lambda i: (0, 4 * pairs)),
            whole((span, LANES)),
            whole((span, LANES)),
        ]
        + [far],
        out_specs=[
            whole((span, width)),
            pl.BlockSpec((span, 3 * LANES), lambda i: (0, i)),
            pl.BlockSpec((span, LANES), lambda i: (0, i)),
            whole((half, width)),
            whole((span, width)),
            whole((span, width)),
            whole((experts, span)),
            whole((16, width)),
            whole((experts, span)),
            whole((span, width)),
            whole((span, width)),
        ]
        + [far] * 4,
        out_shape=[
            jax.ShapeDtypeStruct((span, width), BF16),
            jax.ShapeDtypeStruct((span, pairs * 3 * LANES), BF16),
            jax.ShapeDtypeStruct((span, pairs * LANES), BF16),
            jax.ShapeDtypeStruct((half, width), F32),
            jax.ShapeDtypeStruct((span, width), BF16),
            jax.ShapeDtypeStruct((span, width), BF16),
            jax.ShapeDtypeStruct((experts, span), F32),
            jax.ShapeDtypeStruct((16, width), F32),
            jax.ShapeDtypeStruct((experts, span), F32),
            jax.ShapeDtypeStruct((span, width), BF16),
            jax.ShapeDtypeStruct((span, width), BF16),
            jax.ShapeDtypeStruct((experts, 2, slots, width), BF16),
            jax.ShapeDtypeStruct((experts, 2, slots, width), BF16),
            jax.ShapeDtypeStruct((experts, 2, 8, slots), F32),
            jax.ShapeDtypeStruct(shared_all.shape, BF16),
        ],
        scratch_shapes=[
            pltpu.VMEM((experts, slots, width), BF16),
            pltpu.VMEM((experts, slots, width), BF16),
            pltpu.VMEM((experts, 8, slots), F32),
            pltpu.VMEM((width, hidden), F32),
            pltpu.VMEM((width, hidden), F32),
            pltpu.VMEM((width, hidden), F32),
            pltpu.VMEM(shared_all.shape, BF16),
            pltpu.VMEM((span, width), F32),
            pltpu.VMEM((half, width), BF16),
            pltpu.VMEM((half, width), F32),
        ]
        + [pltpu.VMEM((half, width), BF16)] * 4
        + [pltpu.SemaphoreType.DMA((3, experts))] * 4
        + [pltpu.SemaphoreType.DMA((3,))]
        + [pltpu.SemaphoreType.DMA((4,))] * 2
        + [pltpu.SemaphoreType.DMA],
        compiler_params=remote_params(4),
        cost_estimate=cost(20e9, 60e6, 6e6),
        name="attn_fwd",
    )(length, rows, cotangent, routes, first_all, first_all, first_all, cosine, sine, shared_all)


def norm_back(grad, values, gain):
    factor = lax.rsqrt(jnp.mean(values * values, axis=-1, keepdims=True) + EPS)
    normed = values * factor
    hat = grad * gain
    back = factor * (hat - normed * jnp.mean(hat * normed, axis=-1, keepdims=True))
    return back, jnp.sum(grad * normed, axis=0, keepdims=True)


def slot_table(places, experts, slots, offset):
    slot = lax.broadcasted_iota(jnp.int32, (places.shape[0], slots), 1) + offset
    slot = slot.astype(F32)
    return jnp.concatenate(
        [jnp.where(slot == places[:, e : e + 1], 1.0, 0.0).astype(BF16) for e in range(experts)],
        axis=1,
    )


def attn_bwd_kernel(
    len_ref, places_ref, gates_ref, rows_ref, dx_ref, dg_ref, base_ref, b_ref, h_ref, d_ref,
    x_ref, a_ref, w_ref, wo_ref, qkv_ref, ctx_ref, cos_ref, sin_ref, sy_ref, y_ref, share_ref, late_ref,
    gi_ref, lo_ref, *rest, block, ranks, halves, sends,
):
    if sends:
        go_ref, late_in, total_ref, small_in = rest[:4]
        sum_x, sum_y, in_x, in_y, sums, in_z, step_send, step_recv = rest[4:12]
        rest = rest[12:]
    else:
        gw_ref, gs_ref = rest[:2]
        rest = rest[2:]
    (
        db_s, dl_s, db_out, y_out, db_in, dh_s, grad_s, da_s, sums_s, sums_in, turned_s,
        yh_s, gw_s, dctx_s, dq_s, dk_s, dv_s, send, recv, local, pair_send, pair_recv,
        y_send, y_recv, y_local, z_send, z_recv,
    ) = rest
    step = pl.program_id(0)
    last = pl.num_programs(0) - 1
    me, core = lax.axis_index("dp"), lax.axis_index("tensor")
    other = device(me, 1 - core)
    experts, slots, width = dx_ref.shape
    span = a_ref.shape[0]
    half = span // 2
    length = len_ref[0]
    own = pl.ds(pl.multiple_of(core * half, half), half)
    away = pl.ds(pl.multiple_of((1 - core) * half, half), half)
    shard = width // ranks
    pairs = gw_s.shape[0]

    def to_other(src, dst, index):
        return remote(src, dst, pair_send.at[index], pair_recv.at[index], other)

    if sends:
        rows_at = lambda rank: pl.ds(pl.multiple_of(rank * shard, shard), shard)
        small = Deal(
            lambda rank: turned_s.at[rows_at(rank)], lambda rank: small_in.at[rank],
            send.at[0], recv.at[0], local.at[0], ranks,
        )
        late = Deal(
            lambda rank: late_ref.at[rank], lambda rank: late_in.at[rank],
            send.at[1], recv.at[1], local.at[1], ranks,
        )

    x, y, x_rank, y_rank = sides(me)
    z = lax.div(me, 4)
    cut = gw_s.shape[-1] // 2
    low, high = slice(0, cut), slice(cut, 2 * cut)

    def step_copy(src, dst, index, pair, rank):
        return remote(
            src, dst, step_send.at[index, pair], step_recv.at[index, pair], device(rank, core)
        )

    def sides_first(pair):
        return (
            step_copy(gw_s.at[pair, :, :, 1 - x, :, low], sum_x.at[pair], 0, pair, x_rank),
            step_copy(gw_s.at[pair, :, 1 - y, :, :, high], sum_y.at[pair], 1, pair, y_rank),
        )

    def sides_second(pair):
        return (
            step_copy(sum_x.at[pair, :, 1 - y], in_x.at[pair], 2, pair, y_rank),
            step_copy(sum_y.at[pair, :, 1 - x], in_y.at[pair], 3, pair, x_rank),
        )

    def along_z(pair):
        copies = []
        for offset in range(1, 4):
            rank = flip(me, 4 * offset)
            copies.append(
                step_copy(
                    sums.at[pair, lax.div(rank, 4)], in_z.at[pair, offset - 1], 3 + offset, pair, rank
                )
            )
        return copies

    def begin_sum(pair):
        for copy in sides_first(pair):
            copy.start()

    def go_on(pair):
        for copy in sides_first(pair):
            copy.wait()
        own_x = gw_s[pair, :, :, pl.ds(x, 1), :, low].reshape(sum_x.shape[1:])
        own_y = gw_s[pair, :, pl.ds(y, 1), :, :, high].reshape(sum_y.shape[1:])
        sum_x[pair] = (sum_x[pair].astype(F32) + own_x.astype(F32)).astype(BF16)
        sum_y[pair] = (sum_y[pair].astype(F32) + own_y.astype(F32)).astype(BF16)
        for copy in sides_second(pair):
            copy.start()

    def go_along(pair):
        for copy in sides_second(pair):
            copy.wait()
        own_x = sum_x[pair, :, pl.ds(y, 1)].reshape(in_x.shape[1:])
        own_y = sum_y[pair, :, pl.ds(x, 1)].reshape(in_y.shape[1:])
        sums[pair, :, :, low] = (in_x[pair].astype(F32) + own_x.astype(F32)).astype(BF16)
        sums[pair, :, :, high] = (in_y[pair].astype(F32) + own_y.astype(F32)).astype(BF16)
        for copy in along_z(pair):
            copy.start()

    def end_sum(pair):
        for copy in along_z(pair):
            copy.wait()
        total = sums[pair, pl.ds(z, 1)].reshape(shard, 2 * cut).astype(F32)
        for offset in range(3):
            total += in_z[pair, offset].astype(F32)
        go_ref[pair] = total

    def y_copy(k):
        return remote(
            y_ref.at[k], yh_s.at[k], y_send.at[k], y_recv.at[k], device(flip(me, k), core)
        )

    def z_copy(k):
        rank = flip(me, 4 * k)
        return remote(
            share_ref.at[lax.div(rank, 4)], total_ref.at[k], z_send.at[k], z_recv.at[k],
            device(rank, core),
        )

    def own_rows():
        copies = [pltpu.make_async_copy(y_ref.at[0], yh_s.at[0], y_local.at[0])]
        if halves:
            copies.append(
                pltpu.make_async_copy(share_ref.at[lax.div(me, 4)], total_ref.at[0], y_local.at[1])
            )
        return copies

    def put_together(table, values, index, tokens):
        here = pl.ds(pl.multiple_of(index * tokens, tokens), tokens)
        places = table(here)
        hot = slot_table(places, experts, slots, core * slots)
        return here, places, mm(hot, values[...].reshape(experts * slots, width), NN)

    @pl.when(step == 0)
    def _():
        if sends:
            greet([device(lax.rem(me + k, ranks), core) for k in range(1, ranks)] + [other])
        else:
            greet(cluster_and_core(experts))
        for copy in own_rows():
            copy.start()
        for k in range(1, experts):
            y_copy(k).start()
        if sends:
            for k in range(1, 4):
                z_copy(k).start()
            late.start(3)
        router = rows_ref[2 : 2 + experts, :]
        tokens = 256

        def gather(index, carry):
            here, places, total = put_together(
                lambda rows: places_ref[:, rows].T, dx_ref, index, tokens
            )
            gate = gates_ref[:, here].T
            slot = lax.broadcasted_iota(jnp.int32, (tokens, 2 * slots), 1)
            slot = jnp.where(slot < slots, slot + core * slots, slot - core * slots).astype(F32)
            lane = lax.broadcasted_iota(jnp.int32, (tokens, experts), 1)
            gate_grad = jnp.zeros((tokens, experts), F32)
            for e in range(experts):
                found = jnp.where(slot == places[:, e : e + 1], dg_ref[e, 0:1, :], 0.0)
                gate_grad = jnp.where(lane == e, jnp.sum(found, axis=1, keepdims=True), gate_grad)
            mean = jnp.sum(gate * gate_grad, axis=1, keepdims=True)
            logit_grad = gate * (gate_grad - mean)
            dl_s[here, :] = logit_grad
            total += lax.dot_general(
                logit_grad, router, NN, precision=HIGHEST, preferred_element_type=F32
            )
            db_s[here, :] = total + base_ref[here, :].astype(F32)
            return carry

        lax.fori_loop(0, span // tokens, gather, 0)
        db_out[...] = db_s[away, :].astype(BF16)
        swap_b = to_other(db_out, db_in.at[0], 0)
        swap_b.start()
        sums_s[...] = jnp.zeros_like(sums_s)
        sums_s[2 : 2 + experts, :] = lax.dot_general(
            dl_s[...], b_ref[...].astype(F32), TN, precision=HIGHEST, preferred_element_type=F32
        )
        swap_b.wait()
        db = db_s[own, :] + db_in[0].astype(F32)
        back, sums_s[1:2, :] = norm_back(db, h_ref[...], rows_ref[1:2, :])
        rows = d_ref[own, :].astype(F32) + back
        dh_s[...] = rows
        db_out[...] = rows.astype(BF16)
        grad_s[own, :] = rows.astype(BF16)
        swap_a = to_other(db_out, db_in.at[1], 1)
        swap_a.start()
        da_s[...] = jnp.zeros_like(da_s)
        swap_a.wait()
        grad_s[away, :] = db_in[1]

    grad_rows = grad_s[...]
    dctx_s[...] = mm(grad_rows, wo_ref[...], NN).astype(BF16)
    out_grads = mm(grad_rows, ctx_ref[...], TN).astype(BF16)
    dk_s[...] = jnp.zeros_like(dk_s)
    dv_s[...] = jnp.zeros_like(dv_s)
    scale = jnp.asarray(HD**-0.5, BF16)
    for index in range(span // block):
        keys = (index + 1) * block
        start = index * block
        query_rows = qkv_ref[start:keys, :LANES] * scale
        key_rows = qkv_ref[:keys, LANES : 2 * LANES]
        value_rows = qkv_ref[:keys, 2 * LANES :]
        context_grad = dctx_s[start:keys, :]
        row = lax.broadcasted_iota(jnp.int32, (keys, block), 0)
        column = start + lax.broadcasted_iota(jnp.int32, (keys, block), 1)
        allowed = (row <= column) & (row < length)
        dq_total = None
        for head in range(LANES // HD):
            lanes = head_lanes((block, LANES), head)
            masked_query = jnp.where(lanes, query_rows, jnp.zeros_like(query_rows))
            masked_grad = jnp.where(lanes, context_grad, jnp.zeros_like(context_grad))
            scores = jnp.where(allowed, mm(key_rows, masked_query, NT), -1e30)
            peak = jnp.max(scores, axis=0, keepdims=True)
            powers = jnp.exp(scores - peak)
            total = jnp.sum(powers, axis=0, keepdims=True)
            prob = powers * (1.0 / total)
            prob_grad = mm(value_rows, masked_grad, NT)
            inner = jnp.sum(prob * prob_grad, axis=0, keepdims=True)
            score_grad = (prob * (prob_grad - inner)).astype(BF16)
            dk_s[:keys, :] += mm(score_grad, masked_query, NN)
            dv_s[:keys, :] += mm(prob.astype(BF16), masked_grad, NN)
            dq_part = mm(score_grad, key_rows, TN)
            dq_total = dq_part if head == 0 else jnp.where(lanes, dq_part, dq_total)
        dq_s[start:keys, :] = dq_total * (HD**-0.5)
    cosine, sine = cos_ref[...], sin_ref[...]
    dq, dk = dq_s[...], dk_s[...]
    dq = (dq * cosine - partner(dq) * sine).astype(BF16)
    dk = (dk * cosine - partner(dk) * sine).astype(BF16)
    grads = jnp.concatenate([dq, dk, dv_s[...].astype(BF16)], axis=1)
    in_grads = mm(a_ref[...], grads, TN).astype(BF16)
    shape = gw_s.shape[1:-1]
    gw_s[step, ..., : 3 * LANES] = in_grads.reshape(*shape, 3 * LANES)
    gw_s[step, ..., 3 * LANES :] = out_grads.reshape(*shape, LANES)
    if sends:
        for pair in range(pairs):
            pl.when(step == pair)(functools.partial(begin_sum, pair))
            pl.when(step == pair + 1)(functools.partial(go_on, pair))
            pl.when(step == pair + 2)(functools.partial(go_along, pair))
    else:
        gw_ref[step] = gw_s[step]
    da_s[...] += mm(grads, w_ref[...], NT)

    @pl.when(step == last)
    def _():
        db_out[...] = da_s[away, :].astype(BF16)
        swap_d = to_other(db_out, db_in.at[0], 2)
        swap_d.start()

        for copy in own_rows():
            copy.wait()
        for k in range(1, experts):
            y_copy(k).wait()
        mine = lax.rem(me, experts)

        def near(rows):
            table = [places_ref[pl.ds(flip(mine, k), 1), rows] for k in range(experts)]
            return jnp.concatenate(table, axis=0).T

        def add(index, carry):
            here, _, total = put_together(near, yh_s, index, 256)
            db_s[here, :] = total + sy_ref[here, :].astype(F32)
            return carry

        lax.fori_loop(0, span // 256, add, 0)
        y_out[...] = db_s[away, :].astype(BF16)
        swap_y = to_other(y_out, db_in.at[2], 4)
        swap_y.start()

        swap_d.wait()
        da = da_s[own, :] + db_in[0].astype(F32)
        back, sums_s[0:1, :] = norm_back(da, x_ref[...].astype(F32), rows_ref[0:1, :])
        swap_s = to_other(sums_s, sums_in, 3)
        swap_s.start()
        if sends:
            go_on(pairs - 1)
            go_along(pairs - 2)
        gi_ref[...] = (dh_s[...] + back).astype(BF16)
        swap_s.wait()
        turned = (sums_s[...] + sums_in[...]).T
        if sends:
            turned_s[...] = jnp.zeros_like(turned_s)
            turned_s[:, : turned.shape[1]] = turned
            small.start()
            go_along(pairs - 1)
        else:
            gs_ref[:, : turned.shape[1]] = turned
        swap_y.wait()
        out = db_s[own, :] + db_in[2].astype(F32)
        lo_ref[...] = (h_ref[...] + out).astype(BF16)
        if sends:
            late.wait()
            for k in range(1, 4):
                z_copy(k).wait()
            for pair in range(pairs):
                end_sum(pair)
            small.wait()


def attn_backward(
    length, places, gates, rows, dx_home, gate_grads, y_near, shared_y, shares, late,
    shared_dx, ffn_in, hidden_rows, grad_ffn, layer_rows, attn_in, first_all, qkv_rot, context,
    cosine, sine, ranks, halves,
):
    span, width = attn_in.shape
    half = span // 2
    experts = places.shape[0]
    pairs = context.shape[1] // LANES
    shard = width // ranks
    sends = halves
    far = pl.BlockSpec(memory_space=pl.ANY)
    if sends:
        outs = [
            (whole((pairs, shard, 4 * LANES)), (pairs, shard, 4 * LANES), F32),
            (far, late.shape, BF16),
            (far, shares.shape, BF16),
            (far, (ranks, shard, LANES), F32),
        ]
        extra = [
            pltpu.VMEM((pairs, 4, 2, shard, 2 * LANES), BF16),
            pltpu.VMEM((pairs, 4, 2, shard, 2 * LANES), BF16),
            pltpu.VMEM((pairs, 4, shard, 2 * LANES), BF16),
            pltpu.VMEM((pairs, 4, shard, 2 * LANES), BF16),
            pltpu.VMEM((pairs, 4, shard, 4 * LANES), BF16),
            pltpu.VMEM((pairs, 3, shard, 4 * LANES), BF16),
            pltpu.SemaphoreType.DMA((7, pairs)),
            pltpu.SemaphoreType.DMA((7, pairs)),
        ]
        blocks = (4, 2, 2, shard)
    else:
        forms = (pairs, width, 4 * LANES), (width, LANES)
        outs = [(whole(forms[0]), forms[0], BF16), (whole(forms[1]), forms[1], F32)]
        extra = []
        blocks = (width,)
    outs = [(whole((half, width)), (half, width), BF16)] * 2 + outs
    return pl.pallas_call(
        functools.partial(attn_bwd_kernel, block=256, ranks=ranks, halves=halves, sends=sends),
        grid=(pairs,),
        in_specs=[pl.BlockSpec(memory_space=pltpu.SMEM)]
        + [
            whole(v.shape)
            for v in (
                places, gates, rows, dx_home, gate_grads, shared_dx, ffn_in, hidden_rows, grad_ffn,
                layer_rows, attn_in,
            )
        ]
        + [
            pl.BlockSpec((width, 3 * LANES), lambda i: (0, i)),
            pl.BlockSpec((width, LANES), lambda i: (0, 3 * pairs + i)),
            pl.BlockSpec((span, 3 * LANES), lambda i: (0, i)),
            pl.BlockSpec((span, LANES), lambda i: (0, i)),
            whole((span, LANES)),
            whole((span, LANES)),
            whole((span, width)),
        ]
        + [far] * 3,
        out_specs=[spec for spec, _, _ in outs],
        out_shape=[jax.ShapeDtypeStruct(form, kind) for _, form, kind in outs],
        scratch_shapes=extra
        + [
            pltpu.VMEM((span, width), F32),
            pltpu.VMEM((span, experts), F32),
            pltpu.VMEM((half, width), BF16),
            pltpu.VMEM((half, width), BF16),
            pltpu.VMEM((3, half, width), BF16),
            pltpu.VMEM((half, width), F32),
            pltpu.VMEM((span, width), BF16),
            pltpu.VMEM((span, width), F32),
            pltpu.VMEM((16, width), F32),
            pltpu.VMEM((16, width), F32),
            pltpu.VMEM((width, LANES), F32),
            pltpu.VMEM(y_near.shape, BF16),
            pltpu.VMEM((pairs,) + blocks + (4 * LANES,), BF16),
            pltpu.VMEM((span, LANES), BF16),
            pltpu.VMEM((span, LANES), F32),
            pltpu.VMEM((span, LANES), F32),
            pltpu.VMEM((span, LANES), F32),
            pltpu.SemaphoreType.DMA((2, ranks)),
            pltpu.SemaphoreType.DMA((2, ranks)),
            pltpu.SemaphoreType.DMA((2,)),
            pltpu.SemaphoreType.DMA((5,)),
            pltpu.SemaphoreType.DMA((5,)),
            pltpu.SemaphoreType.DMA((experts,)),
            pltpu.SemaphoreType.DMA((experts,)),
            pltpu.SemaphoreType.DMA((3,)),
            pltpu.SemaphoreType.DMA((4,)),
            pltpu.SemaphoreType.DMA((4,)),
        ],
        compiler_params=remote_params(5),
        cost_estimate=cost(40e9, 40e6, 6e6),
        name="attn_bwd",
    )(
        length, places, gates, rows, dx_home, gate_grads, shared_dx, ffn_in, hidden_rows, grad_ffn,
        layer_rows, attn_in, first_all, first_all, qkv_rot, context, cosine, sine, shared_y,
        y_near, shares, late,
    )


def finish_kernel(
    gi_in, lo_in, proj_ref, early_ref, late_ref, total_ref, small_ref, gi_ref, lo_ref, *refs
):
    gi_ref[...] = gi_in[...]
    lo_ref[...] = lo_in[...]
    for pair in range(proj_ref.shape[0]):
        for kind in range(4):
            refs[kind][:, pair * LANES : (pair + 1) * LANES] = proj_ref[
                pair, :, kind * LANES : (kind + 1) * LANES
            ]
    experts = refs[4].shape[1]
    part = early_ref.shape[-1]
    for kind in range(3):
        for index, ref in enumerate((early_ref, late_ref)):
            for expert in range(experts):
                total = ref[expert, kind].astype(F32)
                for rank in range(expert + experts, ref.shape[0], experts):
                    total += ref[rank, kind].astype(F32)
                refs[4 + kind][:, expert, index * part : (index + 1) * part] = total
    hidden = total_ref.shape[-1] // 3
    for kind in range(3):
        columns = slice(kind * hidden, (kind + 1) * hidden)
        total = total_ref[0, :, columns].astype(F32)
        for place in range(1, total_ref.shape[0]):
            total += total_ref[place, :, columns].astype(F32)
        refs[7 + kind][...] = total
    total = small_ref[0]
    for rank in range(1, small_ref.shape[0]):
        total += small_ref[rank]
    refs[10][...] = total


def finish(rows, outputs, proj, early, late, total, small, experts):
    pairs, shard, _ = proj.shape
    hidden = total.shape[-1] // 3
    forms = (
        [(rows.shape, BF16)] * 2
        + [((shard, pairs * LANES), F32)] * 4
        + [((shard, experts, hidden), F32)] * 3
        + [((shard, hidden), F32)] * 3
        + [((shard, LANES), F32)]
    )
    args = (rows, outputs, proj, early, late, total, small)
    return pl.pallas_call(
        finish_kernel,
        grid=(1,),
        in_specs=[whole(v.shape) for v in args],
        out_specs=[whole(form) for form, _ in forms],
        out_shape=[jax.ShapeDtypeStruct(form, kind) for form, kind in forms],
        compiler_params=params(1),
        cost_estimate=cost(1e7, 2e7),
        name="finish",
    )(*args)


def column_of(row):
    count = row.shape[1]
    shape = (count, count)
    same = lax.broadcasted_iota(jnp.int32, shape, 0) == lax.broadcasted_iota(jnp.int32, shape, 1)
    return jnp.sum(jnp.where(same, row, 0.0), axis=1, keepdims=True)


def row_of(column):
    count = column.shape[0]
    shape = (count, count)
    same = lax.broadcasted_iota(jnp.int32, shape, 0) == lax.broadcasted_iota(jnp.int32, shape, 1)
    return jnp.sum(jnp.where(same, column, 0.0), axis=0, keepdims=True)


def ffn_block(x, grad, gate, gate_w, up_w, down_w, sums):
    gate_pre = mm(x, gate_w, NN)
    up_pre = mm(x, up_w, NN)
    sig = jax.nn.sigmoid(gate_pre)
    act = gate_pre * sig
    inner = (act * up_pre).astype(BF16)
    out = mm(inner, down_w, NT)
    gate_grad, out_grad = None, grad
    if gate is not None:
        wide = grad.astype(F32)
        gate_grad = jnp.sum(out * wide, axis=1, keepdims=True)
        out = out * gate
        out_grad = (wide * gate).astype(BF16)
    inner_grad = mm(out_grad, down_w, NN)
    gate_pre_grad = (inner_grad * up_pre * (sig + act * (1.0 - sig))).astype(BF16)
    up_pre_grad = (inner_grad * act).astype(BF16)
    row_grad = mm(gate_pre_grad, gate_w, NT) + mm(up_pre_grad, up_w, NT)
    sums[0][...] += mm(x, gate_pre_grad, TN)
    sums[1][...] += mm(x, up_pre_grad, TN)
    sums[2][...] += mm(out_grad, inner, TN)
    return out, row_grad, gate_grad


def sides(rank):
    x, y = lax.rem(rank, 2), lax.rem(lax.div(rank, 2), 2)
    return x, y, flip(rank, 1), flip(rank, 2)


def block_of(x_ref, d_ref, g_ref, w_refs, sums):
    slots, width = x_ref.shape[1:]
    shape = (width, w_refs[0].shape[-1])
    gate = column_of(jnp.concatenate([g_ref[0, 0:1, :], g_ref[1, 0:1, :]], axis=1))
    return ffn_block(
        x_ref[...].reshape(2 * slots, width), d_ref[...].reshape(2 * slots, width), gate,
        *(w_ref[...].reshape(shape) for w_ref in w_refs), sums,
    )


def put_sums(og_ref, sums):
    for index, total in enumerate(sums):
        og_ref[:, index] = total[...].astype(BF16).reshape(og_ref.shape[0], *og_ref.shape[2:])


def expert_first_kernel(
    x_ref, d_ref, g_ref, wg_ref, wu_ref, wd_ref, share_ref, late_ref,
    y_ref, dx_ref, dg_ref, og_ref, sx_ref, sy_ref, late_out,
    ag, au, ad, own_x, own_y, in_x, in_y, send, recv, local, *sems,
    experts, ranks, halves,
):
    step = pl.program_id(0)
    sums = (ag, au, ad)
    me, core = lax.axis_index("dp"), lax.axis_index("tensor")
    x, y, x_rank, y_rank = sides(me)
    cut = share_ref.shape[-1] // 2
    low, high = pl.ds(0, cut), pl.ds(cut, cut)

    def over_x(place):
        return share_ref.at[:, :, place, :, low]

    def over_y(place):
        return share_ref.at[:, place, :, :, high]

    deal = Deal(
        lambda rank: late_ref.at[lax.rem(rank, experts)], lambda rank: late_out.at[rank], *sems, ranks
    )

    def copies():
        return (
            remote(over_x(1 - x), in_x, send.at[0], recv.at[0], device(x_rank, core)),
            remote(over_y(1 - y), in_y, send.at[1], recv.at[1], device(y_rank, core)),
        )

    def loads():
        return (
            pltpu.make_async_copy(over_x(x), own_x, local.at[0]),
            pltpu.make_async_copy(over_y(y), own_y, local.at[1]),
        )

    @pl.when(step == 0)
    def _():
        for total in sums:
            total[...] = jnp.zeros_like(total)
        if halves:
            greet(all_and_core(ranks))
            for copy in copies() + loads():
                copy.start()
            deal.start(3)

    out, row_grad, gate_grad = block_of(x_ref, d_ref, g_ref, (wg_ref, wu_ref, wd_ref), sums)
    y_ref[...] = out
    dx_ref[...] = row_grad
    dg_ref[...] = jnp.broadcast_to(row_of(gate_grad), dg_ref.shape)

    @pl.when(step == pl.num_programs(0) - 1)
    def _():
        put_sums(og_ref, sums)
        if halves:
            for copy in copies() + loads():
                copy.wait()
            sx_ref[...] = (own_x[...].astype(F32) + in_x[...].astype(F32)).astype(BF16)
            sy_ref[...] = (own_y[...].astype(F32) + in_y[...].astype(F32)).astype(BF16)
            deal.wait()


def expert_specs(experts, slots, width, weights, order):
    def group(shape):
        return pl.BlockSpec((None,) + shape, lambda i: (order(i),) + (0,) * len(shape))

    parts, _, shard, hidden = weights.shape
    matrices = [
        pl.BlockSpec(
            (parts, None, shard, hidden), lambda i, k=k: (0, k, 0, 0),
            pipeline_mode=pl.Buffered(1),
        )
        for k in range(3)
    ]
    return group, matrices, [pltpu.VMEM((width, hidden), F32)] * 3


def expert_first(x_slots, d_slots, g_slots, weights, shares, late, halves):
    experts, _, slots, width = x_slots.shape
    hidden = weights.shape[-1]
    ranks = lax.axis_size("dp")
    group, matrices, sums = expert_specs(experts, slots, width, weights, lambda i: i)
    rows = group((2, slots, width))
    if halves:
        _, _, _, shard, columns = shares.shape
        part = (shares.shape[0], 2, shard, columns // 2)
    else:
        part = (1, 1, 16, LANES)
    return pl.pallas_call(
        functools.partial(expert_first_kernel, experts=experts, ranks=ranks, halves=halves),
        grid=(experts,),
        in_specs=[rows, rows, group((2, 8, slots))]
        + matrices
        + [pl.BlockSpec(memory_space=pl.ANY)] * 2,
        out_specs=[group((2 * slots, width))] * 2
        + [group((8, 2 * slots)), whole(weights.shape), whole(part), whole(part)]
        + [pl.BlockSpec(memory_space=pl.ANY)],
        out_shape=[jax.ShapeDtypeStruct((experts, 2 * slots, width), F32)] * 2
        + [
            jax.ShapeDtypeStruct((experts, 8, 2 * slots), F32),
            jax.ShapeDtypeStruct(weights.shape, BF16),
            jax.ShapeDtypeStruct(part, BF16),
            jax.ShapeDtypeStruct(part, BF16),
            jax.ShapeDtypeStruct((ranks,) + late.shape[1:] if halves else (1, 16, LANES), BF16),
        ],
        scratch_shapes=sums
        + [pltpu.VMEM(part, BF16)] * 4
        + [pltpu.SemaphoreType.DMA((2,))] * 3
        + Deal.semaphores(ranks),
        compiler_params=remote_params(6) if halves else params(1),
        cost_estimate=cost(36 * experts * slots * width * hidden, 40e6),
        name="expert_first",
    )(x_slots, d_slots, g_slots, weights, weights, weights, shares, late)


def expert_second_kernel(
    x_ref, d_ref, g_ref, wg_ref, wu_ref, wd_ref, yf_ref, dxf_ref, dgf_ref, sx_ref, sy_ref,
    y_ref, dx_home, dg_home, og_ref, share_ref,
    ag, au, ad, own_y, own_dx, ys, dxs, yp, dxp, dgs, out_x, out_y, in_x, in_y,
    core_send, core_recv, send, recv, local, share_send, share_recv, *, experts, halves,
):
    step = pl.program_id(0)
    block = experts - 1 - step
    sums = (ag, au, ad)
    me, core = lax.axis_index("dp"), lax.axis_index("tensor")
    mine = lax.rem(me, experts)
    other = device(me, 1 - core)
    slots = x_ref.shape[1]
    x, y, x_rank, y_rank = sides(me)

    def rank_at(k):
        total, bit = me - mine, 1
        while bit < experts:
            total += bit * lax.rem(lax.div(mine, bit) + lax.div(k, bit), 2)
            bit *= 2
        return total

    def core_copy(k, part):
        src, dst = ((ys, yp), (dxs, dxp))[part]
        return remote(
            src.at[lax.rem(k, 2)], dst.at[k], core_send.at[part, k], core_recv.at[part, k], other
        )

    def home_copy(k, part):
        src, dst = ((dxp, dx_home), (dgs, dg_home))[part]
        return remote(
            src.at[k], dst.at[mine], send.at[part, k], recv.at[part, k],
            device(rank_at(k), core),
        )

    def own_copy(part):
        src, dst = ((dxp, dx_home), (dgs, dg_home))[part]
        return pltpu.make_async_copy(src.at[0], dst.at[mine], local.at[part])

    def go_home(k, part):
        @pl.when(k == 0)
        def _():
            own_copy(part).start()

        @pl.when(k > 0)
        def _():
            home_copy(k, part).start()

    def share_copies():
        return (
            remote(out_x, in_x, share_send.at[0], share_recv.at[0], device(y_rank, core)),
            remote(out_y, in_y, share_send.at[1], share_recv.at[1], device(x_rank, core)),
        )

    @pl.when(step == 0)
    def _():
        greet(cluster_and_core(experts))
        for total in sums:
            total[...] = jnp.zeros_like(total)
        if halves:
            out_x[...] = sx_ref[:, pl.ds(1 - y, 1)]
            out_y[...] = sy_ref[:, pl.ds(1 - x, 1)]
            for copy in share_copies():
                copy.start()

    def settle(k):
        for part in (1, 0):
            core_copy(k, part).wait_recv()
            own, shared = ((own_y, yp), (own_dx, dxp))[part]
            total = (own[...] + shared[k].astype(F32)).astype(BF16)
            if part:
                dxp[k] = total
                go_home(k, 0)
            else:
                y_ref[...] = total

    @pl.when(step < experts)
    def _():
        out, row_grad, gate_grad = block_of(x_ref, d_ref, g_ref, (wg_ref, wu_ref, wd_ref), sums)
        out += yf_ref[...]
        row_grad += dxf_ref[...]

        @pl.when(step >= 1)
        def _():
            settle(block + 1)

        for part in (1, 0):

            @pl.when(step >= 2)
            def _():
                core_copy(block + 2, part).wait_send()

            own, half = ((own_y, ys), (own_dx, dxs))[part]
            value = (out, row_grad)[part]
            own[...] = value[:slots]
            half[lax.rem(block, 2)] = value[slots:].astype(BF16)
            core_copy(block, part).start()
        dgs[block] = jnp.broadcast_to(row_of(gate_grad), dgs.shape[1:]) + dgf_ref[...]
        go_home(block, 1)

    @pl.when(step == experts)
    def _():
        settle(block + 1)
        put_sums(og_ref, sums)
        if halves:
            cut = out_x.shape[-1]
            for copy in share_copies():
                copy.wait()
            kept_x, kept_y = sx_ref[:, pl.ds(y, 1)], sy_ref[:, pl.ds(x, 1)]
            total_x = kept_x.astype(F32) + in_x[...].astype(F32)
            total_y = kept_y.astype(F32) + in_y[...].astype(F32)
            share_ref[:, :, :cut] = total_x.astype(BF16).reshape(share_ref.shape[0], -1, cut)
            share_ref[:, :, cut:] = total_y.astype(BF16).reshape(share_ref.shape[0], -1, cut)
        for part in (0, 1):
            for k in (0, 1):
                core_copy(k, part).wait_send()
            own_copy(part).wait()
            for k in range(1, experts):
                home_copy(k, part).wait()


def expert_second(x_slots, d_slots, g_slots, weights, first, halves):
    experts, _, slots, width = x_slots.shape
    hidden = weights.shape[-1]
    y_first, dx_first, dg_first, sx, sy = first
    far = pl.BlockSpec(memory_space=pl.ANY)
    group, matrices, sums = expert_specs(
        experts, slots, width, weights, lambda i: jnp.maximum(experts - 1 - i, 0)
    )
    rows = group((2, slots, width))
    long, _, shard, cut = sx.shape
    share = (long, shard, 2 * cut)
    return pl.pallas_call(
        functools.partial(expert_second_kernel, experts=experts, halves=halves),
        grid=(experts + 1,),
        in_specs=[rows, rows, group((2, 8, slots))]
        + matrices
        + [group((2 * slots, width))] * 2
        + [group((8, 2 * slots)), whole(sx.shape), whole(sy.shape)],
        out_specs=[
            pl.BlockSpec((None, slots, width), lambda i: (jnp.minimum(experts - i, experts - 1), 0, 0)),
            far,
            far,
            whole(weights.shape),
            whole(share),
        ],
        out_shape=[
            jax.ShapeDtypeStruct((experts, slots, width), BF16),
            jax.ShapeDtypeStruct((experts, slots, width), BF16),
            jax.ShapeDtypeStruct((experts, 8, 2 * slots), F32),
            jax.ShapeDtypeStruct(weights.shape, BF16),
            jax.ShapeDtypeStruct(share, BF16),
        ],
        scratch_shapes=sums
        + [pltpu.VMEM((slots, width), F32)] * 2
        + [pltpu.VMEM((2, slots, width), BF16)] * 2
        + [pltpu.VMEM((experts, slots, width), BF16)] * 2
        + [pltpu.VMEM((experts, 8, 2 * slots), F32)]
        + [pltpu.VMEM((long, 1, shard, cut), BF16)] * 4
        + [pltpu.SemaphoreType.DMA((2, experts))] * 4
        + [pltpu.SemaphoreType.DMA((2,))] * 3,
        compiler_params=remote_params(3),
        cost_estimate=cost(36 * experts * slots * width * hidden, 40e6),
        name="expert_second",
    )(x_slots, d_slots, g_slots, weights, weights, weights, y_first, dx_first, dg_first, sx, sy)


def to_all(values, groups=None):
    count = lax.axis_size("dp") if groups is None else len(groups[0])
    copies = jnp.broadcast_to(values[None], (count,) + values.shape)
    return lax.all_to_all(copies, "dp", 0, 0, axis_index_groups=groups, tiled=True)


def after(values, *earlier):
    return lax.optimization_barrier((values,) + earlier)[0]


def per_device(
    layer_input, seq_lengths, expert_routes, w_query, w_key, w_value, w_output,
    gain_attn, gain_ffn, router_weight, expert_gate, expert_up, expert_down,
    shared_gate, shared_up, shared_down, out_cotangent,
):
    ranks = lax.axis_size("dp")
    _, own_len, width = layer_input.shape
    span = 2 * own_len
    shard = w_query.shape[0]
    pairs = w_query.shape[1] // LANES
    experts, hidden = expert_gate.shape[1:]
    capacity = 4 * span // experts
    slots = capacity // 2
    groups = [list(range(s, s + experts)) for s in range(0, ranks, experts)]

    small_own = jnp.concatenate(
        [gain_attn[:, None], gain_ffn[:, None], router_weight], axis=1
    )
    small_own = jnp.pad(small_own, ((0, 0), (0, LANES - small_own.shape[1])))
    first_all, shared_all, early_own, late_own = gather_weights(
        (w_query, w_key, w_value, w_output), small_own, (shared_gate, shared_up, shared_down),
        (expert_gate, expert_up, expert_down),
    )
    first_all = first_all.reshape(width, first_all.shape[-1])
    if shard % 16:
        shared_all = shared_all.reshape(1, width, shared_all.shape[-1])

    half = HD // 2
    inverse = np.exp(np.arange(half, dtype=np.float32) * np.float32(-math.log(10000.0) / half))
    angles = np.arange(span, dtype=np.float32)[:, None] * inverse[None, :]
    cos_half, sin_half = np.cos(angles), np.sin(angles)
    cosine = np.concatenate([cos_half] * 4, axis=1)
    sine = np.concatenate([-sin_half, sin_half] * 2, axis=1)

    direct = shard % 16 == 0
    halves = ranks == 16

    def matrices(gathered):
        gathered = gathered.reshape(ranks, 3, shard, gathered.shape[-1])
        if direct:
            return gathered
        return gathered.transpose(1, 0, 2, 3).reshape(1, 3, width, gathered.shape[-1])

    def from_experts(grads):
        if not direct:
            grads = grads.reshape(3, ranks, shard, grads.shape[-1]).transpose(1, 0, 2, 3)
        return lax.all_to_all(grads, "dp", 0, 0, tiled=True)

    def to_outputs(grads):
        grads = grads.reshape(ranks // experts, experts, 3, shard, grads.shape[-1])
        return jnp.sum(grads.astype(F32), axis=0)

    early = lax.all_to_all(early_own, "dp", 0, 0, tiled=True)
    (
        attn_in, qkv_rot, context, hidden_rows, ffn_in, grad_ffn, places, small, gates, shared_y,
        shared_dx, d_slots, x_slots, g_slots, shared_grads,
    ) = attn_forward(
        seq_lengths, layer_input[0], out_cotangent[0], expert_routes.reshape(span, 2).T,
        first_all, shared_all, cosine, sine, experts, slots,
    )

    if halves:
        shares = shared_grads.reshape(4, 2, 2, shard, 3 * hidden)
    else:
        shares = shared_grads[0, :16, :LANES]
        shared_grads = lax.all_to_all(
            shared_grads.reshape(ranks, shard, 3 * hidden), "dp", 0, 0, tiled=True
        )

    y_first, dx_first, dg_first, early_grads, sx, sy, late = expert_first(
        x_slots, d_slots, g_slots, matrices(early), shares, late_own, halves
    )
    if not halves:
        late = jnp.concatenate([late_own] * (ranks // experts), axis=0)
        late = lax.all_to_all(late, "dp", 0, 0, tiled=True)
    early_grads = from_experts(early_grads)
    y_near, dx_home, gate_grads, late_grads, shares = expert_second(
        x_slots, d_slots, g_slots, matrices(late), (y_first, dx_first, dg_first, sx, sy), halves
    )
    late_grads = after(late_grads, early_grads)

    grad_input, layer_output, *grads = attn_backward(
        seq_lengths, places, gates, small, dx_home, gate_grads, y_near, shared_y, shares,
        late_grads, shared_dx, ffn_in, hidden_rows, grad_ffn, layer_input[0], attn_in,
        first_all, qkv_rot, context, cosine, sine, ranks, halves,
    )
    if halves:
        proj, late_in, total, small_in = grads
        grad_input, layer_output, *grads = finish(
            grad_input, layer_output, proj, early_grads, late_in, total, small_in, experts
        )
        attn_grads, expert_grads, shared_grads, small_grads = (
            grads[:4], grads[4:7], grads[7:10], grads[10]
        )
    else:
        attn_grads = grads[0].reshape(pairs, ranks, shard, 4 * LANES).transpose(1, 0, 2, 3)
        attn_grads = lax.all_to_all(attn_grads, "dp", 0, 0, tiled=True)
        attn_grads = jnp.sum(attn_grads.astype(F32), axis=0).reshape(pairs, shard, 4, LANES)
        attn_grads = [
            attn_grads[:, :, k].transpose(1, 0, 2).reshape(shard, pairs * LANES) for k in range(4)
        ]
        small_grads = lax.all_to_all(grads[1].reshape(ranks, shard, LANES), "dp", 0, 0, tiled=True)
        small_grads = jnp.sum(small_grads, axis=0)
        shared_grads = jnp.sum(shared_grads.astype(F32), axis=0)
        shared_grads = [shared_grads[:, k * hidden : (k + 1) * hidden] for k in range(3)]
        late_grads = from_experts(late_grads)
        expert_grads = jnp.concatenate([to_outputs(early_grads), to_outputs(late_grads)], axis=-1)
        expert_grads = [expert_grads[:, k].transpose(1, 0, 2) for k in range(3)]
    return (
        layer_output[None], grad_input[None],
        attn_grads[0], attn_grads[1], attn_grads[2], attn_grads[3],
        small_grads[:, 0], small_grads[:, 1], small_grads[:, 2 : 2 + experts],
        expert_grads[0], expert_grads[1], expert_grads[2],
        shared_grads[0], shared_grads[1], shared_grads[2],
    )


def solution(mesh):
    tokens = P("dp", "tensor", None)
    matrix = P("dp", "tensor")
    expert = P("dp", None, "tensor")
    in_specs = (
        (tokens, P("dp"), P("dp", None, None))
        + (matrix,) * 4
        + (P("dp"), P("dp"), P("dp", None))
        + (expert,) * 3
        + (matrix,) * 3
        + (tokens,)
    )
    out_specs = (
        (tokens, tokens)
        + (matrix,) * 4
        + (P("dp"), P("dp"), P("dp", None))
        + (expert,) * 3
        + (matrix,) * 3
    )
    return jax.shard_map(
        per_device, mesh=mesh, in_specs=in_specs, out_specs=out_specs, check_vma=False
    )
```

```python
import functools
import math

import jax
import jax.numpy as jnp
import numpy as np
from jax import lax
from jax.experimental import pallas as pl
from jax.experimental.pallas import tpu as pltpu
from jax.sharding import PartitionSpec as P

HD = 64
LANES = 128
EPS = 1e-06
F32 = jnp.float32
BF16 = jnp.bfloat16
HIGHEST = lax.Precision.HIGHEST
VMEM_LIMIT = 60 * 1024 * 1024

NN = (((1,), (0,)), ((), ()))
NT = (((1,), (1,)), ((), ()))
TN = (((0,), (0,)), ((), ()))


def mm(left, right, dims):
    return lax.dot_general(left, right, dims, preferred_element_type=F32)


def params(count):
    return pltpu.CompilerParams(
        dimension_semantics=("arbitrary",) * count, vmem_limit_bytes=VMEM_LIMIT
    )


def remote_params(number):
    return pltpu.CompilerParams(
        collective_id=number, has_side_effects=True, vmem_limit_bytes=VMEM_LIMIT,
        dimension_semantics=("arbitrary",),
    )


def cost(flops, nbytes, trans=0):
    return pl.CostEstimate(flops=int(flops), bytes_accessed=int(nbytes), transcendentals=int(trans))


def flip(index, offset):
    bit = 1
    while bit <= offset:
        if offset & bit:
            index = index + bit - 2 * bit * lax.rem(lax.div(index, bit), 2)
        bit *= 2
    return index


def device(rank, core):
    return {"dp": rank, "tensor": core}


def greet(devices):
    barrier = pltpu.get_barrier_semaphore()
    for target in devices:
        pl.semaphore_signal(barrier, inc=1, device_id=target, device_id_type=pl.DeviceIdType.MESH)
    pl.semaphore_wait(barrier, len(devices))


def remote(src, dst, send, recv, target):
    return pltpu.make_async_remote_copy(
        src_ref=src, dst_ref=dst, send_sem=send, recv_sem=recv,
        device_id=target, device_id_type=pl.DeviceIdType.MESH,
    )


class Deal:
    def __init__(self, source, place, send, recv, local, ranks):
        self.source, self.place, self.ranks = source, place, ranks
        self.send, self.recv, self.local = send, recv, local
        self.me, self.core = lax.axis_index("dp"), lax.axis_index("tensor")

    @staticmethod
    def semaphores(ranks):
        dma = pltpu.SemaphoreType.DMA
        return [dma((ranks,)), dma((ranks,)), dma]

    def own(self):
        return pltpu.make_async_copy(self.source(self.me), self.place(self.me), self.local)

    order = (12, 1, 8, 2, 13, 4, 9, 3, 14, 5, 10, 6, 15, 7, 11)

    def share(self, offset):
        rank = flip(self.me, offset)
        return remote(
            self.source(rank), self.place(self.me), self.send.at[offset], self.recv.at[offset],
            device(rank, self.core),
        )

    def each(self, body):
        for offset in self.order:
            body(self.share(offset))

    def start(self, pieces=1):
        self.own().start()
        for piece in range(pieces):
            for offset in self.order:
                rank = flip(self.me, offset)
                source, place = self.source(rank), self.place(self.me)
                rows = source.shape[0] // pieces
                here = pl.ds(piece * rows, rows)
                remote(
                    source.at[here], place.at[here], self.send.at[offset], self.recv.at[offset],
                    device(rank, self.core),
                ).start()

    def wait(self):
        self.own().wait()
        self.each(lambda copy: copy.wait())


def all_and_core(ranks):
    me, core = lax.axis_index("dp"), lax.axis_index("tensor")
    return [device(lax.rem(me + k, ranks), core) for k in range(1, ranks)] + [device(me, 1 - core)]


class Gather:
    order = (0, 1, 4, 2, 5, 3, 6)
    turns = 9

    def __init__(self, own_ref, out_ref, sems, which):
        self.own_ref, self.out_ref = own_ref, out_ref
        self.own_sem, self.z_send, self.z_recv, self.s_send, self.s_recv, self.f_send, self.f_recv = (
            sem.at[which] for sem in sems
        )
        self.cut = own_ref.shape[1] // 2 // LANES * LANES
        self.me, self.core = lax.axis_index("dp"), lax.axis_index("tensor")
        self.z = lax.div(self.me, 4)
        self.up, self.down = lax.min(self.me + 4, 15), lax.max(self.me - 4, 0)
        self.sides_of = (flip(self.me, 1), flip(self.me, 2))

    @staticmethod
    def semaphores(count):
        dma = pltpu.SemaphoreType.DMA
        return [dma((count,)), dma((count, 6)), dma((count, 6))] + [dma((count, 2, 7))] * 4

    def rank_at(self, place):
        return self.me - 4 * place if place <= 3 else self.me + 4 * (place - 3)

    def at(self, place, body):
        if place == 0:
            body()
        else:
            pl.when(self.z >= place if place <= 3 else self.z + (place - 3) <= 3)(body)

    def own_copy(self):
        return pltpu.make_async_copy(self.own_ref, self.out_ref.at[self.me], self.own_sem)

    def z_copy(self, rank, step, upward):
        index = step - 1 if upward else step + 2
        return remote(
            self.own_ref if step == 1 else self.out_ref.at[rank], self.out_ref.at[rank],
            self.z_send.at[index], self.z_recv.at[index],
            device(self.up if upward else self.down, self.core),
        )

    def side_copy(self, rank, place, axis):
        return remote(
            self.own_ref if place == 0 else self.out_ref.at[rank], self.out_ref.at[rank],
            self.s_send.at[axis, place], self.s_recv.at[axis, place],
            device(self.sides_of[axis], self.core),
        )

    def onward_copy(self, rank, place, axis):
        width = self.own_ref.shape[1]
        columns = pl.ds(0, self.cut) if axis == 0 else pl.ds(self.cut, width - self.cut)
        part = self.out_ref.at[rank, :, columns]
        return remote(
            part, part, self.f_send.at[axis, place], self.f_recv.at[axis, place],
            device(self.sides_of[1 - axis], self.core),
        )

    def begin(self):
        self.own_copy().start()
        pl.when(self.z < 3)(lambda: self.z_copy(self.me, 1, True).start())
        pl.when(self.z > 0)(lambda: self.z_copy(self.me, 1, False).start())
        for axis in range(2):
            self.side_copy(self.me, 0, axis).start()

    def arrive(self, place):
        upward = place <= 3
        step = place if upward else place - 3
        rank = self.rank_at(place)
        self.z_copy(rank, step, upward).wait_recv()
        if step < 3:
            further = self.z < 3 if upward else self.z > 0
            pl.when(further)(lambda: self.z_copy(rank, step + 1, upward).start())
        for axis in range(2):
            self.side_copy(rank, place, axis).start()

    def onward(self, place):
        for axis in range(2):
            rank = flip(self.rank_at(place), 1 + axis)
            self.side_copy(rank, place, axis).wait_recv()
            self.onward_copy(rank, place, axis).start()

    def turn(self, index):
        if index < 7:
            self.at(self.order[index], functools.partial(self.arrive, self.order[index]))
        if index >= 2:
            self.at(self.order[index - 2], functools.partial(self.onward, self.order[index - 2]))

    def finish(self, place):
        for axis in range(2):
            rank = flip(self.rank_at(place), 1 + axis)
            self.side_copy(self.rank_at(place), place, axis).wait_send()
            self.onward_copy(rank, place, axis).wait_send()
            self.onward_copy(flip(self.rank_at(place), 3), place, axis).wait_recv()

    def end(self):
        z = self.z
        for place in self.order:
            self.at(place, functools.partial(self.finish, place))
        for step in range(1, 4):
            pl.when((z < 3) & (z >= step - 1))(
                lambda step=step: self.z_copy(self.me - 4 * (step - 1), step, True).wait_send()
            )
            pl.when((z > 0) & (z + step - 1 <= 3))(
                lambda step=step: self.z_copy(self.me + 4 * (step - 1), step, False).wait_send()
            )
        self.own_copy().wait()


def gather_kernel(
    wq_ref, wk_ref, wv_ref, wo_ref, small_ref, sg_ref, su_ref, sd_ref, eg_ref, eu_ref, ed_ref,
    first_out, shared_out, early_out, late_out,
    first_s, shared_s, raw_s, packed_s, load, store, *sems,
):
    loads = [
        pltpu.make_async_copy(ref, raw_s.at[kind], load.at[kind])
        for kind, ref in enumerate((eg_ref, eu_ref, ed_ref))
    ]
    for copy in loads:
        copy.start()
    pairs = wq_ref.shape[1] // LANES
    for pair in range(pairs):
        columns = slice(pair * LANES, (pair + 1) * LANES)
        for kind, ref in enumerate((wq_ref, wk_ref, wv_ref)):
            start = (3 * pair + kind) * LANES
            first_s[:, start : start + LANES] = ref[:, columns].astype(BF16)
    first_s[:, 3 * pairs * LANES : 4 * pairs * LANES] = wo_ref[...].astype(BF16)
    first_s[:, 4 * pairs * LANES :] = small_ref[...].astype(BF16)
    hidden = sg_ref.shape[1]
    for kind, ref in enumerate((sg_ref, su_ref, sd_ref)):
        shared_s[:, kind * hidden : (kind + 1) * hidden] = ref[...].astype(BF16)

    gathers = Gather(first_s, first_out, sems, 0), Gather(shared_s, shared_out, sems, 1)
    z, core = gathers[0].z, gathers[0].core
    barrier = pltpu.get_barrier_semaphore()

    def hello(rank):
        pl.semaphore_signal(
            barrier, inc=1, device_id=device(rank, core), device_id_type=pl.DeviceIdType.MESH
        )

    for rank in gathers[0].sides_of:
        hello(rank)
    pl.when(z < 3)(lambda: hello(gathers[0].up))
    pl.when(z > 0)(lambda: hello(gathers[0].down))
    pl.semaphore_wait(barrier, 2 + lax.min(z, 1) + lax.min(3 - z, 1))
    for gather in gathers:
        gather.begin()
    _, rows, experts, _ = raw_s.shape
    part = packed_s.shape[-1]
    for copy in loads:
        copy.wait()
    for turn in range(1, Gather.turns):
        for gather in gathers:
            gather.turn(turn)
        for expert in range(turn - 1, experts, Gather.turns - 1):
            for kind in range(3):
                for half in range(2):
                    packed_s[half, expert, kind * rows : (kind + 1) * rows, :] = raw_s[
                        kind, :, expert, half * part : (half + 1) * part
                    ].astype(BF16)
    count = early_out.shape[0] // experts
    stores = [
        pltpu.make_async_copy(
            packed_s.at[0], early_out.at[pl.ds(index * experts, experts)], store.at[index]
        )
        for index in range(count)
    ] + [pltpu.make_async_copy(packed_s.at[1], late_out, store.at[count])]
    for copy in stores:
        copy.start()
    for copy in stores:
        copy.wait()
    for gather in gathers:
        gather.end()


def gather_weights(attention, small, shared, expert):
    ranks = lax.axis_size("dp")
    rows, heads_width = attention[0].shape
    columns = 4 * heads_width + LANES
    hidden = shared[0].shape[1]
    if ranks != 16:
        pairs = heads_width // LANES
        qkv = jnp.stack(attention[:3], axis=1).reshape(rows, 3, pairs, LANES)
        qkv = qkv.transpose(0, 2, 1, 3).reshape(rows, 3 * heads_width)
        first = jnp.concatenate([qkv, attention[3], small], axis=1).astype(BF16)
        stack = jnp.stack(expert, axis=0).astype(BF16).transpose(2, 0, 1, 3)
        stack = stack.reshape(stack.shape[0], 3 * rows, hidden)
        early, late = stack[:, :, : hidden // 2], stack[:, :, hidden // 2 :]
        early = jnp.concatenate([early] * (ranks // early.shape[0]), axis=0)
        return (
            to_all(first), to_all(jnp.concatenate(shared, axis=1).astype(BF16)), early, late
        )
    vmem = pl.BlockSpec(memory_space=pltpu.VMEM)
    far = pl.BlockSpec(memory_space=pl.ANY)
    experts = expert[0].shape[1]
    return pl.pallas_call(
        gather_kernel,
        in_specs=[vmem] * 8 + [far] * 3,
        out_specs=[far] * 4,
        out_shape=[
            jax.ShapeDtypeStruct((ranks, rows, columns), BF16),
            jax.ShapeDtypeStruct((ranks, rows, 3 * hidden), BF16),
            jax.ShapeDtypeStruct((ranks, 3 * rows, hidden // 2), BF16),
            jax.ShapeDtypeStruct((experts, 3 * rows, hidden // 2), BF16),
        ],
        scratch_shapes=[
            pltpu.VMEM((rows, columns), BF16),
            pltpu.VMEM((rows, 3 * hidden), BF16),
            pltpu.VMEM((3, rows, experts, hidden), F32),
            pltpu.VMEM((2, experts, 3 * rows, hidden // 2), BF16),
            pltpu.SemaphoreType.DMA((3,)),
            pltpu.SemaphoreType.DMA((ranks // experts + 1,)),
        ]
        + Gather.semaphores(2),
        compiler_params=pltpu.CompilerParams(
            collective_id=1, has_side_effects=True, vmem_limit_bytes=VMEM_LIMIT
        ),
        cost_estimate=cost(1e6, 100e6),
        name="gather_weights",
    )(*attention, small, *shared, *expert)


def partner(values):
    lane = lax.broadcasted_iota(jnp.int32, values.shape, 1)
    return jnp.where(
        lane % HD < HD // 2,
        pltpu.roll(values, LANES - HD // 2, 1),
        pltpu.roll(values, HD // 2, 1),
    )


def head_lanes(shape, head):
    lane = lax.broadcasted_iota(jnp.int32, shape, 1)
    return (lane // HD) == head


def offsets(count):
    return sorted(range(1, count), key=lambda k: (bin(k).count("1"), k))


class Trip:
    def __init__(self, ins, outs, send, recv, core_send, core_recv, local, part):
        self.ins, self.outs, self.part = ins, outs, part
        self.send, self.recv, self.local = send, recv, local
        self.core_send, self.core_recv = core_send, core_recv
        self.me, self.core = lax.axis_index("dp"), lax.axis_index("tensor")
        self.count = ins.shape[0]

    def copy(self, k):
        return remote(
            self.ins.at[k], self.outs.at[k, 0],
            self.send.at[self.part, k], self.recv.at[self.part, k],
            device(flip(self.me, k), self.core),
        )

    def core_copy(self, k):
        src = self.ins.at[0] if k == 0 else self.outs.at[k, 0]
        return remote(
            src, self.outs.at[k, 1],
            self.core_send.at[self.part, k], self.core_recv.at[self.part, k],
            device(self.me, 1 - self.core),
        )

    def own(self):
        return pltpu.make_async_copy(self.ins.at[0], self.outs.at[0, 0], self.local.at[self.part])

    def go(self, k):
        if k:
            self.copy(k).start()
        else:
            self.own().start()
            self.core_copy(0).start()

    def pass_on(self, k):
        self.copy(k).wait_recv()
        self.core_copy(k).start()

    def end(self):
        self.own().wait()
        for k in range(self.count):
            self.core_copy(k).wait()
            if k:
                self.copy(k).wait_send()


def cluster_and_core(count):
    me, core = lax.axis_index("dp"), lax.axis_index("tensor")
    return [device(flip(me, k), core) for k in range(1, count)] + [device(me, 1 - core)]


def rms(values):
    return values * lax.rsqrt(jnp.mean(values * values, axis=-1, keepdims=True) + EPS)


def whole(shape):
    return pl.BlockSpec(shape, lambda i: (0,) * len(shape), pipeline_mode=pl.Buffered(1))


def attn_fwd_kernel(
    len_ref, x_ref, c_ref, routes_ref, w_ref, wo_ref, small_ref, cos_ref, sin_ref, shared_ref,
    a_ref, qkv_ref, ctx_ref, h_ref, b_ref, d_ref, places_ref, rows_ref, gates_ref, y_ref, dx_ref, dr, xr, gr, og_ref,
    ds, xs, gs, ag, au, ad, shared_w, part, x_in, h_in, b_out, b_in, c_out, c_in,
    send, recv, core_send, core_recv, local, pair_send, pair_recv, load, *, block,
):
    step = pl.program_id(0)
    me, core = lax.axis_index("dp"), lax.axis_index("tensor")
    other = device(me, 1 - core)
    experts, slots, _ = ds.shape
    trips = [
        Trip(ins, outs, send, recv, core_send, core_recv, local, index)
        for index, (ins, outs) in enumerate(((ds, dr), (xs, xr), (gs, gr)))
    ]
    slot = core * slots + lax.broadcasted_iota(jnp.int32, (slots, a_ref.shape[0]), 0)
    slot = slot.astype(F32)
    mine = lax.rem(me, experts)
    span, width = a_ref.shape
    half = span // 2
    length = len_ref[0]
    own = pl.ds(pl.multiple_of(core * half, half), half)
    away = pl.ds(pl.multiple_of((1 - core) * half, half), half)
    pairs = pl.num_programs(0)

    def to_other(src, dst, index):
        return remote(src, dst, pair_send.at[index], pair_recv.at[index], other)

    @pl.when(step == 0)
    def _():
        greet(cluster_and_core(experts))
        pltpu.make_async_copy(shared_ref, shared_w, load).start()
        token = core * half + lax.broadcasted_iota(jnp.int32, c_ref.shape, 0)
        valid = jnp.where(token < length, c_ref[...].astype(F32), 0.0).astype(BF16)
        c_out[...] = valid
        d_ref[own, :] = valid
        swap_c = to_other(c_out, c_in, 0)
        swap_c.start()
        swap_x = to_other(x_ref, x_in, 1)
        swap_x.start()

        name = lax.broadcasted_iota(jnp.int32, (experts, span), 0)
        chosen = (name == routes_ref[0:1, :]) | (name == routes_ref[1:2, :])
        earlier = lax.broadcasted_iota(jnp.int32, (span, span), 0) < lax.broadcasted_iota(
            jnp.int32, (span, span), 1
        )
        counts = mm(
            jnp.where(chosen, 1.0, 0.0).astype(BF16), jnp.where(earlier, 1.0, 0.0).astype(BF16), NN
        )
        places_ref[...] = jnp.where(chosen, counts, -1.0)

        swap_c.wait_recv()
        d_ref[away, :] = c_in[...]
        for k in offsets(experts) + [0]:
            place = places_ref[pl.ds(flip(mine, k), 1), :]
            hot = jnp.where(slot == place, 1.0, 0.0).astype(BF16)
            ds[k] = mm(hot, d_ref[...], NN).astype(BF16)
            trips[0].go(k)
        rows_ref[...] = small_ref[...].astype(F32).T[: rows_ref.shape[0], :]
        swap_x.wait_recv()
        gain = rows_ref[0:1, :]
        a_ref[own, :] = (rms(x_ref[...].astype(F32)) * gain).astype(BF16)
        a_ref[away, :] = (rms(x_in[...].astype(F32)) * gain).astype(BF16)
        part[...] = jnp.zeros_like(part)
        swap_c.wait_send()
        swap_x.wait_send()

    raw = mm(a_ref[...], w_ref[...], NN)
    cosine, sine = cos_ref[...], sin_ref[...]
    query, key = raw[:, :LANES], raw[:, LANES : 2 * LANES]
    qkv_ref[:, :LANES] = (query * cosine + partner(query) * sine).astype(BF16)
    qkv_ref[:, LANES : 2 * LANES] = (key * cosine + partner(key) * sine).astype(BF16)
    qkv_ref[:, 2 * LANES :] = raw[:, 2 * LANES :].astype(BF16)
    for index in range(span // block):
        keys = (index + 1) * block
        query_rows = qkv_ref[index * block : keys, :LANES] * jnp.asarray(HD**-0.5, BF16)
        key_rows = qkv_ref[:keys, LANES : 2 * LANES]
        value_rows = qkv_ref[:keys, 2 * LANES :]
        row = index * block + lax.broadcasted_iota(jnp.int32, (block, keys), 0)
        column = lax.broadcasted_iota(jnp.int32, (block, keys), 1)
        allowed = (column <= row) & (column < length)
        parts = []
        for head in range(LANES // HD):
            masked_query = jnp.where(
                head_lanes(query_rows.shape, head), query_rows, jnp.zeros_like(query_rows)
            )
            scores = jnp.where(allowed, mm(masked_query, key_rows, NT), -1e30)
            peak = jnp.max(scores, axis=1, keepdims=True)
            powers = jnp.exp(scores - peak)
            total = jnp.sum(powers, axis=1, keepdims=True)
            prob = (powers * (1.0 / total)).astype(BF16)
            parts.append(mm(prob, value_rows, NN))
        context = jnp.where(head_lanes(parts[0].shape, 0), parts[0], parts[1]).astype(BF16)
        ctx_ref[index * block : keys, :] = context
        part[index * block : keys, :] += mm(context, wo_ref[...], NT)

    @pl.when(step == pairs - 1)
    def _():
        swap_h = to_other(part.at[away], h_in, 2)
        swap_h.start()
        rows = x_ref[...].astype(F32) + part[own, :]
        swap_h.wait_recv()
        rows = rows + h_in[...]
        h_ref[...] = rows
        normed = (rms(rows) * rows_ref[1:2, :]).astype(BF16)
        b_out[...] = normed
        swap_b = to_other(b_out, b_in, 3)
        swap_b.start()
        b_ref[own, :] = normed
        swap_b.wait_recv()
        b_ref[away, :] = b_in[...]
        chosen = places_ref[...] >= 0
        logits = mm(rows_ref[2 : 2 + experts, :].astype(BF16), b_ref[...], NT)
        top = jnp.max(jnp.where(chosen, logits, -1e30), axis=0, keepdims=True)
        powers = jnp.where(chosen, jnp.exp(jnp.minimum(logits - top, 0.0)), 0.0)
        gates_ref[...] = powers / jnp.sum(powers, axis=0, keepdims=True)
        for k in offsets(experts) + [0]:
            target = pl.ds(flip(mine, k), 1)
            found = slot == places_ref[target, :]
            xs[k] = mm(jnp.where(found, 1.0, 0.0).astype(BF16), b_ref[...], NN).astype(BF16)
            trips[1].go(k)
            gate = jnp.sum(jnp.where(found, gates_ref[target, :], 0.0), axis=1, keepdims=True)
            gs[k] = jnp.broadcast_to(row_of(gate), gs.shape[1:])
            trips[2].go(k)
        swap_h.wait_send()
        swap_b.wait_send()
        for total in (ag, au, ad):
            total[...] = jnp.zeros_like(total)
        pltpu.make_async_copy(shared_ref, shared_w, load).wait()
        hidden = ag.shape[1]

        def matrix(index):
            return shared_w[:, :, index * hidden : (index + 1) * hidden].reshape(width, hidden)

        def branch(index, carry):
            rows = pl.ds(pl.multiple_of(index * block, block), block)
            out, row_grad, _ = ffn_block(
                b_ref[rows, :], d_ref[rows, :], None, matrix(0), matrix(1), matrix(2), (ag, au, ad)
            )
            y_ref[rows, :] = out.astype(BF16)
            dx_ref[rows, :] = row_grad.astype(BF16)
            return carry

        lax.fori_loop(0, span // block, branch, 0)
        for index, total in enumerate((ag, au, ad)):
            shared_w[:, :, index * hidden : (index + 1) * hidden] = (
                total[...].astype(BF16).reshape(shared_w.shape[0], -1, hidden)
            )
        write = pltpu.make_async_copy(shared_w, og_ref, load)
        write.start()
        for trip in trips:
            for k in offsets(experts):
                trip.pass_on(k)
        for trip in trips:
            trip.end()
        write.wait()


def attn_forward(length, rows, cotangent, routes, first_all, shared_all, cosine, sine, experts, slots):
    half, width = rows.shape
    span = 2 * half
    pairs = (first_all.shape[1] - LANES) // (4 * LANES)
    far = pl.BlockSpec(memory_space=pl.ANY)
    hidden = shared_all.shape[-1] // 3
    return pl.pallas_call(
        functools.partial(attn_fwd_kernel, block=256),
        grid=(pairs,),
        in_specs=[
            pl.BlockSpec(memory_space=pltpu.SMEM),
            whole((half, width)),
            whole((half, width)),
            whole(routes.shape),
            pl.BlockSpec((width, 3 * LANES), lambda i: (0, i)),
            pl.BlockSpec((width, LANES), lambda i: (0, 3 * pairs + i)),
            pl.BlockSpec((width, LANES), lambda i: (0, 4 * pairs)),
            whole((span, LANES)),
            whole((span, LANES)),
        ]
        + [far],
        out_specs=[
            whole((span, width)),
            pl.BlockSpec((span, 3 * LANES), lambda i: (0, i)),
            pl.BlockSpec((span, LANES), lambda i: (0, i)),
            whole((half, width)),
            whole((span, width)),
            whole((span, width)),
            whole((experts, span)),
            whole((16, width)),
            whole((experts, span)),
            whole((span, width)),
            whole((span, width)),
        ]
        + [far] * 4,
        out_shape=[
            jax.ShapeDtypeStruct((span, width), BF16),
            jax.ShapeDtypeStruct((span, pairs * 3 * LANES), BF16),
            jax.ShapeDtypeStruct((span, pairs * LANES), BF16),
            jax.ShapeDtypeStruct((half, width), F32),
            jax.ShapeDtypeStruct((span, width), BF16),
            jax.ShapeDtypeStruct((span, width), BF16),
            jax.ShapeDtypeStruct((experts, span), F32),
            jax.ShapeDtypeStruct((16, width), F32),
            jax.ShapeDtypeStruct((experts, span), F32),
            jax.ShapeDtypeStruct((span, width), BF16),
            jax.ShapeDtypeStruct((span, width), BF16),
            jax.ShapeDtypeStruct((experts, 2, slots, width), BF16),
            jax.ShapeDtypeStruct((experts, 2, slots, width), BF16),
            jax.ShapeDtypeStruct((experts, 2, 8, slots), F32),
            jax.ShapeDtypeStruct(shared_all.shape, BF16),
        ],
        scratch_shapes=[
            pltpu.VMEM((experts, slots, width), BF16),
            pltpu.VMEM((experts, slots, width), BF16),
            pltpu.VMEM((experts, 8, slots), F32),
            pltpu.VMEM((width, hidden), F32),
            pltpu.VMEM((width, hidden), F32),
            pltpu.VMEM((width, hidden), F32),
            pltpu.VMEM(shared_all.shape, BF16),
            pltpu.VMEM((span, width), F32),
            pltpu.VMEM((half, width), BF16),
            pltpu.VMEM((half, width), F32),
        ]
        + [pltpu.VMEM((half, width), BF16)] * 4
        + [pltpu.SemaphoreType.DMA((3, experts))] * 4
        + [pltpu.SemaphoreType.DMA((3,))]
        + [pltpu.SemaphoreType.DMA((4,))] * 2
        + [pltpu.SemaphoreType.DMA],
        compiler_params=remote_params(4),
        cost_estimate=cost(20e9, 60e6, 6e6),
        name="attn_fwd",
    )(length, rows, cotangent, routes, first_all, first_all, first_all, cosine, sine, shared_all)


def norm_back(grad, values, gain):
    factor = lax.rsqrt(jnp.mean(values * values, axis=-1, keepdims=True) + EPS)
    normed = values * factor
    hat = grad * gain
    back = factor * (hat - normed * jnp.mean(hat * normed, axis=-1, keepdims=True))
    return back, jnp.sum(grad * normed, axis=0, keepdims=True)


def slot_table(places, experts, slots, offset):
    slot = lax.broadcasted_iota(jnp.int32, (places.shape[0], slots), 1) + offset
    slot = slot.astype(F32)
    return jnp.concatenate(
        [jnp.where(slot == places[:, e : e + 1], 1.0, 0.0).astype(BF16) for e in range(experts)],
        axis=1,
    )


def attn_bwd_kernel(
    len_ref, places_ref, gates_ref, rows_ref, dx_ref, dg_ref, base_ref, b_ref, h_ref, d_ref,
    x_ref, a_ref, w_ref, wo_ref, qkv_ref, ctx_ref, cos_ref, sin_ref, sy_ref, y_ref, share_ref,
    gi_ref, lo_ref, *rest, block, ranks, halves, sends,
):
    if sends:
        go_ref, total_ref, small_in = rest[:3]
        sum_x, sum_y, in_x, in_y, sums, in_z, step_send, step_recv = rest[3:11]
        rest = rest[11:]
    else:
        gw_ref, gs_ref = rest[:2]
        rest = rest[2:]
    (
        db_s, dl_s, db_out, y_out, db_in, dh_s, grad_s, da_s, sums_s, sums_in, turned_s,
        yh_s, gw_s, dctx_s, dq_s, dk_s, dv_s, send, recv, local, pair_send, pair_recv,
        y_send, y_recv, y_local, z_send, z_recv,
    ) = rest
    step = pl.program_id(0)
    last = pl.num_programs(0) - 1
    me, core = lax.axis_index("dp"), lax.axis_index("tensor")
    other = device(me, 1 - core)
    experts, slots, width = dx_ref.shape
    span = a_ref.shape[0]
    half = span // 2
    length = len_ref[0]
    own = pl.ds(pl.multiple_of(core * half, half), half)
    away = pl.ds(pl.multiple_of((1 - core) * half, half), half)
    shard = width // ranks
    pairs = gw_s.shape[0]

    def to_other(src, dst, index):
        return remote(src, dst, pair_send.at[index], pair_recv.at[index], other)

    if sends:
        rows_at = lambda rank: pl.ds(pl.multiple_of(rank * shard, shard), shard)
        small = Deal(
            lambda rank: turned_s.at[rows_at(rank)], lambda rank: small_in.at[rank],
            send.at[0], recv.at[0], local.at[0], ranks,
        )

    x, y, x_rank, y_rank = sides(me)
    z = lax.div(me, 4)
    cut = gw_s.shape[-1] // 2
    low, high = slice(0, cut), slice(cut, 2 * cut)

    def step_copy(src, dst, index, pair, rank):
        return remote(
            src, dst, step_send.at[index, pair], step_recv.at[index, pair], device(rank, core)
        )

    def sides_first(pair):
        return (
            step_copy(gw_s.at[pair, :, :, 1 - x, :, low], sum_x.at[pair], 0, pair, x_rank),
            step_copy(gw_s.at[pair, :, 1 - y, :, :, high], sum_y.at[pair], 1, pair, y_rank),
        )

    def sides_second(pair):
        return (
            step_copy(sum_x.at[pair, :, 1 - y], in_x.at[pair], 2, pair, y_rank),
            step_copy(sum_y.at[pair, :, 1 - x], in_y.at[pair], 3, pair, x_rank),
        )

    def along_z(pair):
        copies = []
        for offset in range(1, 4):
            rank = flip(me, 4 * offset)
            copies.append(
                step_copy(
                    sums.at[pair, lax.div(rank, 4)], in_z.at[pair, offset - 1], 3 + offset, pair, rank
                )
            )
        return copies

    def begin_sum(pair):
        for copy in sides_first(pair):
            copy.start()

    def go_on(pair):
        for copy in sides_first(pair):
            copy.wait()
        own_x = gw_s[pair, :, :, pl.ds(x, 1), :, low].reshape(sum_x.shape[1:])
        own_y = gw_s[pair, :, pl.ds(y, 1), :, :, high].reshape(sum_y.shape[1:])
        sum_x[pair] = (sum_x[pair].astype(F32) + own_x.astype(F32)).astype(BF16)
        sum_y[pair] = (sum_y[pair].astype(F32) + own_y.astype(F32)).astype(BF16)
        for copy in sides_second(pair):
            copy.start()

    def go_along(pair):
        for copy in sides_second(pair):
            copy.wait()
        own_x = sum_x[pair, :, pl.ds(y, 1)].reshape(in_x.shape[1:])
        own_y = sum_y[pair, :, pl.ds(x, 1)].reshape(in_y.shape[1:])
        sums[pair, :, :, low] = (in_x[pair].astype(F32) + own_x.astype(F32)).astype(BF16)
        sums[pair, :, :, high] = (in_y[pair].astype(F32) + own_y.astype(F32)).astype(BF16)
        for copy in along_z(pair):
            copy.start()

    def end_sum(pair):
        for copy in along_z(pair):
            copy.wait()
        total = sums[pair, pl.ds(z, 1)].reshape(shard, 2 * cut).astype(F32)
        for offset in range(3):
            total += in_z[pair, offset].astype(F32)
        go_ref[pair] = total

    def y_copy(k):
        return remote(
            y_ref.at[k], yh_s.at[k], y_send.at[k], y_recv.at[k], device(flip(me, k), core)
        )

    def z_copy(k):
        rank = flip(me, 4 * k)
        return remote(
            share_ref.at[lax.div(rank, 4)], total_ref.at[k], z_send.at[k], z_recv.at[k],
            device(rank, core),
        )

    def own_rows():
        copies = [pltpu.make_async_copy(y_ref.at[0], yh_s.at[0], y_local.at[0])]
        if halves:
            copies.append(
                pltpu.make_async_copy(share_ref.at[lax.div(me, 4)], total_ref.at[0], y_local.at[1])
            )
        return copies

    def put_together(table, values, index, tokens):
        here = pl.ds(pl.multiple_of(index * tokens, tokens), tokens)
        places = table(here)
        hot = slot_table(places, experts, slots, core * slots)
        return here, places, mm(hot, values[...].reshape(experts * slots, width), NN)

    @pl.when(step == 0)
    def _():
        if sends:
            greet([device(lax.rem(me + k, ranks), core) for k in range(1, ranks)] + [other])
        else:
            greet(cluster_and_core(experts))
        for copy in own_rows():
            copy.start()
        for k in range(1, experts):
            y_copy(k).start()
        if sends:
            for k in range(1, 4):
                z_copy(k).start()
        router = rows_ref[2 : 2 + experts, :]
        tokens = 256

        def gather(index, carry):
            here, places, total = put_together(
                lambda rows: places_ref[:, rows].T, dx_ref, index, tokens
            )
            gate = gates_ref[:, here].T
            slot = lax.broadcasted_iota(jnp.int32, (tokens, 2 * slots), 1)
            slot = jnp.where(slot < slots, slot + core * slots, slot - core * slots).astype(F32)
            lane = lax.broadcasted_iota(jnp.int32, (tokens, experts), 1)
            gate_grad = jnp.zeros((tokens, experts), F32)
            for e in range(experts):
                found = jnp.where(slot == places[:, e : e + 1], dg_ref[e, 0:1, :], 0.0)
                gate_grad = jnp.where(lane == e, jnp.sum(found, axis=1, keepdims=True), gate_grad)
            mean = jnp.sum(gate * gate_grad, axis=1, keepdims=True)
            logit_grad = gate * (gate_grad - mean)
            dl_s[here, :] = logit_grad
            total += lax.dot_general(
                logit_grad, router, NN, precision=HIGHEST, preferred_element_type=F32
            )
            db_s[here, :] = total + base_ref[here, :].astype(F32)
            return carry

        lax.fori_loop(0, span // tokens, gather, 0)
        db_out[...] = db_s[away, :].astype(BF16)
        swap_b = to_other(db_out, db_in.at[0], 0)
        swap_b.start()
        sums_s[...] = jnp.zeros_like(sums_s)
        sums_s[2 : 2 + experts, :] = lax.dot_general(
            dl_s[...], b_ref[...].astype(F32), TN, precision=HIGHEST, preferred_element_type=F32
        )
        swap_b.wait()
        db = db_s[own, :] + db_in[0].astype(F32)
        back, sums_s[1:2, :] = norm_back(db, h_ref[...], rows_ref[1:2, :])
        rows = d_ref[own, :].astype(F32) + back
        dh_s[...] = rows
        db_out[...] = rows.astype(BF16)
        grad_s[own, :] = rows.astype(BF16)
        swap_a = to_other(db_out, db_in.at[1], 1)
        swap_a.start()
        da_s[...] = jnp.zeros_like(da_s)
        swap_a.wait()
        grad_s[away, :] = db_in[1]

    grad_rows = grad_s[...]
    dctx_s[...] = mm(grad_rows, wo_ref[...], NN).astype(BF16)
    out_grads = mm(grad_rows, ctx_ref[...], TN).astype(BF16)
    dk_s[...] = jnp.zeros_like(dk_s)
    dv_s[...] = jnp.zeros_like(dv_s)
    scale = jnp.asarray(HD**-0.5, BF16)
    for index in range(span // block):
        keys = (index + 1) * block
        start = index * block
        query_rows = qkv_ref[start:keys, :LANES] * scale
        key_rows = qkv_ref[:keys, LANES : 2 * LANES]
        value_rows = qkv_ref[:keys, 2 * LANES :]
        context_grad = dctx_s[start:keys, :]
        row = lax.broadcasted_iota(jnp.int32, (keys, block), 0)
        column = start + lax.broadcasted_iota(jnp.int32, (keys, block), 1)
        allowed = (row <= column) & (row < length)
        dq_total = None
        for head in range(LANES // HD):
            lanes = head_lanes((block, LANES), head)
            masked_query = jnp.where(lanes, query_rows, jnp.zeros_like(query_rows))
            masked_grad = jnp.where(lanes, context_grad, jnp.zeros_like(context_grad))
            scores = jnp.where(allowed, mm(key_rows, masked_query, NT), -1e30)
            peak = jnp.max(scores, axis=0, keepdims=True)
            powers = jnp.exp(scores - peak)
            total = jnp.sum(powers, axis=0, keepdims=True)
            prob = powers * (1.0 / total)
            prob_grad = mm(value_rows, masked_grad, NT)
            inner = jnp.sum(prob * prob_grad, axis=0, keepdims=True)
            score_grad = (prob * (prob_grad - inner)).astype(BF16)
            dk_s[:keys, :] += mm(score_grad, masked_query, NN)
            dv_s[:keys, :] += mm(prob.astype(BF16), masked_grad, NN)
            dq_part = mm(score_grad, key_rows, TN)
            dq_total = dq_part if head == 0 else jnp.where(lanes, dq_part, dq_total)
        dq_s[start:keys, :] = dq_total * (HD**-0.5)
    cosine, sine = cos_ref[...], sin_ref[...]
    dq, dk = dq_s[...], dk_s[...]
    dq = (dq * cosine - partner(dq) * sine).astype(BF16)
    dk = (dk * cosine - partner(dk) * sine).astype(BF16)
    grads = jnp.concatenate([dq, dk, dv_s[...].astype(BF16)], axis=1)
    in_grads = mm(a_ref[...], grads, TN).astype(BF16)
    shape = gw_s.shape[1:-1]
    gw_s[step, ..., : 3 * LANES] = in_grads.reshape(*shape, 3 * LANES)
    gw_s[step, ..., 3 * LANES :] = out_grads.reshape(*shape, LANES)
    if sends:
        for pair in range(pairs):
            pl.when(step == pair)(functools.partial(begin_sum, pair))
            pl.when(step == pair + 1)(functools.partial(go_on, pair))
            pl.when(step == pair + 2)(functools.partial(go_along, pair))
    else:
        gw_ref[step] = gw_s[step]
    da_s[...] += mm(grads, w_ref[...], NT)

    @pl.when(step == last)
    def _():
        db_out[...] = da_s[away, :].astype(BF16)
        swap_d = to_other(db_out, db_in.at[0], 2)
        swap_d.start()

        for copy in own_rows():
            copy.wait()
        for k in range(1, experts):
            y_copy(k).wait()
        mine = lax.rem(me, experts)

        def near(rows):
            table = [places_ref[pl.ds(flip(mine, k), 1), rows] for k in range(experts)]
            return jnp.concatenate(table, axis=0).T

        def add(index, carry):
            here, _, total = put_together(near, yh_s, index, 256)
            db_s[here, :] = total + sy_ref[here, :].astype(F32)
            return carry

        lax.fori_loop(0, span // 256, add, 0)
        y_out[...] = db_s[away, :].astype(BF16)
        swap_y = to_other(y_out, db_in.at[2], 4)
        swap_y.start()

        swap_d.wait()
        da = da_s[own, :] + db_in[0].astype(F32)
        back, sums_s[0:1, :] = norm_back(da, x_ref[...].astype(F32), rows_ref[0:1, :])
        swap_s = to_other(sums_s, sums_in, 3)
        swap_s.start()
        if sends:
            go_on(pairs - 1)
            go_along(pairs - 2)
        gi_ref[...] = (dh_s[...] + back).astype(BF16)
        swap_s.wait()
        turned = (sums_s[...] + sums_in[...]).T
        if sends:
            turned_s[...] = jnp.zeros_like(turned_s)
            turned_s[:, : turned.shape[1]] = turned
            small.start()
            go_along(pairs - 1)
        else:
            gs_ref[:, : turned.shape[1]] = turned
        swap_y.wait()
        out = db_s[own, :] + db_in[2].astype(F32)
        lo_ref[...] = (h_ref[...] + out).astype(BF16)
        if sends:
            for k in range(1, 4):
                z_copy(k).wait()
            for pair in range(pairs):
                end_sum(pair)
            small.wait()


def attn_backward(
    length, places, gates, rows, dx_home, gate_grads, y_near, shared_y, shares,
    shared_dx, ffn_in, hidden_rows, grad_ffn, layer_rows, attn_in, first_all, qkv_rot, context,
    cosine, sine, ranks, halves,
):
    span, width = attn_in.shape
    half = span // 2
    experts = places.shape[0]
    pairs = context.shape[1] // LANES
    shard = width // ranks
    sends = halves
    far = pl.BlockSpec(memory_space=pl.ANY)
    if sends:
        outs = [
            (whole((pairs, shard, 4 * LANES)), (pairs, shard, 4 * LANES), F32),
            (far, shares.shape, BF16),
            (far, (ranks, shard, LANES), F32),
        ]
        extra = [
            pltpu.VMEM((pairs, 4, 2, shard, 2 * LANES), BF16),
            pltpu.VMEM((pairs, 4, 2, shard, 2 * LANES), BF16),
            pltpu.VMEM((pairs, 4, shard, 2 * LANES), BF16),
            pltpu.VMEM((pairs, 4, shard, 2 * LANES), BF16),
            pltpu.VMEM((pairs, 4, shard, 4 * LANES), BF16),
            pltpu.VMEM((pairs, 3, shard, 4 * LANES), BF16),
            pltpu.SemaphoreType.DMA((7, pairs)),
            pltpu.SemaphoreType.DMA((7, pairs)),
        ]
        blocks = (4, 2, 2, shard)
    else:
        forms = (pairs, width, 4 * LANES), (width, LANES)
        outs = [(whole(forms[0]), forms[0], BF16), (whole(forms[1]), forms[1], F32)]
        extra = []
        blocks = (width,)
    outs = [(whole((half, width)), (half, width), BF16)] * 2 + outs
    return pl.pallas_call(
        functools.partial(attn_bwd_kernel, block=256, ranks=ranks, halves=halves, sends=sends),
        grid=(pairs,),
        in_specs=[pl.BlockSpec(memory_space=pltpu.SMEM)]
        + [
            whole(v.shape)
            for v in (
                places, gates, rows, dx_home, gate_grads, shared_dx, ffn_in, hidden_rows, grad_ffn,
                layer_rows, attn_in,
            )
        ]
        + [
            pl.BlockSpec((width, 3 * LANES), lambda i: (0, i)),
            pl.BlockSpec((width, LANES), lambda i: (0, 3 * pairs + i)),
            pl.BlockSpec((span, 3 * LANES), lambda i: (0, i)),
            pl.BlockSpec((span, LANES), lambda i: (0, i)),
            whole((span, LANES)),
            whole((span, LANES)),
            whole((span, width)),
        ]
        + [far] * 2,
        out_specs=[spec for spec, _, _ in outs],
        out_shape=[jax.ShapeDtypeStruct(form, kind) for _, form, kind in outs],
        scratch_shapes=extra
        + [
            pltpu.VMEM((span, width), F32),
            pltpu.VMEM((span, experts), F32),
            pltpu.VMEM((half, width), BF16),
            pltpu.VMEM((half, width), BF16),
            pltpu.VMEM((3, half, width), BF16),
            pltpu.VMEM((half, width), F32),
            pltpu.VMEM((span, width), BF16),
            pltpu.VMEM((span, width), F32),
            pltpu.VMEM((16, width), F32),
            pltpu.VMEM((16, width), F32),
            pltpu.VMEM((width, LANES), F32),
            pltpu.VMEM(y_near.shape, BF16),
            pltpu.VMEM((pairs,) + blocks + (4 * LANES,), BF16),
            pltpu.VMEM((span, LANES), BF16),
            pltpu.VMEM((span, LANES), F32),
            pltpu.VMEM((span, LANES), F32),
            pltpu.VMEM((span, LANES), F32),
            pltpu.SemaphoreType.DMA((1, ranks)),
            pltpu.SemaphoreType.DMA((1, ranks)),
            pltpu.SemaphoreType.DMA((1,)),
            pltpu.SemaphoreType.DMA((5,)),
            pltpu.SemaphoreType.DMA((5,)),
            pltpu.SemaphoreType.DMA((experts,)),
            pltpu.SemaphoreType.DMA((experts,)),
            pltpu.SemaphoreType.DMA((3,)),
            pltpu.SemaphoreType.DMA((4,)),
            pltpu.SemaphoreType.DMA((4,)),
        ],
        compiler_params=remote_params(5),
        cost_estimate=cost(40e9, 40e6, 6e6),
        name="attn_bwd",
    )(
        length, places, gates, rows, dx_home, gate_grads, shared_dx, ffn_in, hidden_rows, grad_ffn,
        layer_rows, attn_in, first_all, first_all, qkv_rot, context, cosine, sine, shared_y,
        y_near, shares,
    )


def finish_kernel(
    gi_in, lo_in, proj_ref, early_ref, late_ref, total_ref, small_ref, gi_ref, lo_ref, *refs
):
    gi_ref[...] = gi_in[...]
    lo_ref[...] = lo_in[...]
    for pair in range(proj_ref.shape[0]):
        for kind in range(4):
            refs[kind][:, pair * LANES : (pair + 1) * LANES] = proj_ref[
                pair, :, kind * LANES : (kind + 1) * LANES
            ]
    experts = refs[4].shape[1]
    part = early_ref.shape[-1]
    for kind in range(3):
        for index, ref in enumerate((early_ref, late_ref)):
            for expert in range(experts):
                total = ref[expert, kind].astype(F32)
                for rank in range(expert + experts, ref.shape[0], experts):
                    total += ref[rank, kind].astype(F32)
                refs[4 + kind][:, expert, index * part : (index + 1) * part] = total
    hidden = total_ref.shape[-1] // 3
    for kind in range(3):
        columns = slice(kind * hidden, (kind + 1) * hidden)
        total = total_ref[0, :, columns].astype(F32)
        for place in range(1, total_ref.shape[0]):
            total += total_ref[place, :, columns].astype(F32)
        refs[7 + kind][...] = total
    total = small_ref[0]
    for rank in range(1, small_ref.shape[0]):
        total += small_ref[rank]
    refs[10][...] = total


def finish(rows, outputs, proj, early, late, total, small, experts):
    pairs, shard, _ = proj.shape
    hidden = total.shape[-1] // 3
    forms = (
        [(rows.shape, BF16)] * 2
        + [((shard, pairs * LANES), F32)] * 4
        + [((shard, experts, hidden), F32)] * 3
        + [((shard, hidden), F32)] * 3
        + [((shard, LANES), F32)]
    )
    args = (rows, outputs, proj, early, late, total, small)
    return pl.pallas_call(
        finish_kernel,
        grid=(1,),
        in_specs=[whole(v.shape) for v in args],
        out_specs=[whole(form) for form, _ in forms],
        out_shape=[jax.ShapeDtypeStruct(form, kind) for form, kind in forms],
        compiler_params=params(1),
        cost_estimate=cost(1e7, 2e7),
        name="finish",
    )(*args)


def column_of(row):
    count = row.shape[1]
    shape = (count, count)
    same = lax.broadcasted_iota(jnp.int32, shape, 0) == lax.broadcasted_iota(jnp.int32, shape, 1)
    return jnp.sum(jnp.where(same, row, 0.0), axis=1, keepdims=True)


def row_of(column):
    count = column.shape[0]
    shape = (count, count)
    same = lax.broadcasted_iota(jnp.int32, shape, 0) == lax.broadcasted_iota(jnp.int32, shape, 1)
    return jnp.sum(jnp.where(same, column, 0.0), axis=0, keepdims=True)


def ffn_block(x, grad, gate, gate_w, up_w, down_w, sums):
    gate_pre = mm(x, gate_w, NN)
    up_pre = mm(x, up_w, NN)
    sig = jax.nn.sigmoid(gate_pre)
    act = gate_pre * sig
    inner = (act * up_pre).astype(BF16)
    out = mm(inner, down_w, NT)
    gate_grad, out_grad = None, grad
    if gate is not None:
        wide = grad.astype(F32)
        gate_grad = jnp.sum(out * wide, axis=1, keepdims=True)
        out = out * gate
        out_grad = (wide * gate).astype(BF16)
    inner_grad = mm(out_grad, down_w, NN)
    gate_pre_grad = (inner_grad * up_pre * (sig + act * (1.0 - sig))).astype(BF16)
    up_pre_grad = (inner_grad * act).astype(BF16)
    row_grad = mm(gate_pre_grad, gate_w, NT) + mm(up_pre_grad, up_w, NT)
    sums[0][...] += mm(x, gate_pre_grad, TN)
    sums[1][...] += mm(x, up_pre_grad, TN)
    sums[2][...] += mm(out_grad, inner, TN)
    return out, row_grad, gate_grad


def sides(rank):
    x, y = lax.rem(rank, 2), lax.rem(lax.div(rank, 2), 2)
    return x, y, flip(rank, 1), flip(rank, 2)


def block_of(x_ref, d_ref, g_ref, w_refs, sums):
    slots, width = x_ref.shape[1:]
    shape = (width, w_refs[0].shape[-1])
    gate = column_of(jnp.concatenate([g_ref[0, 0:1, :], g_ref[1, 0:1, :]], axis=1))
    return ffn_block(
        x_ref[...].reshape(2 * slots, width), d_ref[...].reshape(2 * slots, width), gate,
        *(w_ref[...].reshape(shape) for w_ref in w_refs), sums,
    )


def put_sums(og_ref, sums):
    for index, total in enumerate(sums):
        og_ref[:, index] = total[...].astype(BF16).reshape(og_ref.shape[0], *og_ref.shape[2:])


def expert_first_kernel(
    x_ref, d_ref, g_ref, wg_ref, wu_ref, wd_ref, share_ref, late_ref,
    y_ref, dx_ref, dg_ref, og_ref, sx_ref, sy_ref, late_out,
    ag, au, ad, own_x, own_y, in_x, in_y, send, recv, local, *sems,
    experts, ranks, halves,
):
    step = pl.program_id(0)
    sums = (ag, au, ad)
    me, core = lax.axis_index("dp"), lax.axis_index("tensor")
    x, y, x_rank, y_rank = sides(me)
    cut = share_ref.shape[-1] // 2
    low, high = pl.ds(0, cut), pl.ds(cut, cut)

    def over_x(place):
        return share_ref.at[:, :, place, :, low]

    def over_y(place):
        return share_ref.at[:, place, :, :, high]

    deal = Deal(
        lambda rank: late_ref.at[lax.rem(rank, experts)], lambda rank: late_out.at[rank], *sems, ranks
    )

    def copies():
        return (
            remote(over_x(1 - x), in_x, send.at[0], recv.at[0], device(x_rank, core)),
            remote(over_y(1 - y), in_y, send.at[1], recv.at[1], device(y_rank, core)),
        )

    def loads():
        return (
            pltpu.make_async_copy(over_x(x), own_x, local.at[0]),
            pltpu.make_async_copy(over_y(y), own_y, local.at[1]),
        )

    @pl.when(step == 0)
    def _():
        for total in sums:
            total[...] = jnp.zeros_like(total)
        if halves:
            greet(all_and_core(ranks))
            for copy in copies() + loads():
                copy.start()
            deal.start(3)

    out, row_grad, gate_grad = block_of(x_ref, d_ref, g_ref, (wg_ref, wu_ref, wd_ref), sums)
    y_ref[...] = out
    dx_ref[...] = row_grad
    dg_ref[...] = jnp.broadcast_to(row_of(gate_grad), dg_ref.shape)

    @pl.when(step == pl.num_programs(0) - 1)
    def _():
        put_sums(og_ref, sums)
        if halves:
            for copy in copies() + loads():
                copy.wait()
            sx_ref[...] = (own_x[...].astype(F32) + in_x[...].astype(F32)).astype(BF16)
            sy_ref[...] = (own_y[...].astype(F32) + in_y[...].astype(F32)).astype(BF16)
            deal.wait()


def expert_specs(experts, slots, width, weights, order):
    def group(shape):
        return pl.BlockSpec((None,) + shape, lambda i: (order(i),) + (0,) * len(shape))

    parts, _, shard, hidden = weights.shape
    matrices = [
        pl.BlockSpec(
            (parts, None, shard, hidden), lambda i, k=k: (0, k, 0, 0),
            pipeline_mode=pl.Buffered(1),
        )
        for k in range(3)
    ]
    return group, matrices, [pltpu.VMEM((width, hidden), F32)] * 3


def expert_first(x_slots, d_slots, g_slots, weights, shares, late, halves):
    experts, _, slots, width = x_slots.shape
    hidden = weights.shape[-1]
    ranks = lax.axis_size("dp")
    group, matrices, sums = expert_specs(experts, slots, width, weights, lambda i: i)
    rows = group((2, slots, width))
    if halves:
        _, _, _, shard, columns = shares.shape
        part = (shares.shape[0], 2, shard, columns // 2)
    else:
        part = (1, 1, 16, LANES)
    return pl.pallas_call(
        functools.partial(expert_first_kernel, experts=experts, ranks=ranks, halves=halves),
        grid=(experts,),
        in_specs=[rows, rows, group((2, 8, slots))]
        + matrices
        + [pl.BlockSpec(memory_space=pl.ANY)] * 2,
        out_specs=[group((2 * slots, width))] * 2
        + [group((8, 2 * slots)), whole(weights.shape), whole(part), whole(part)]
        + [pl.BlockSpec(memory_space=pl.ANY)],
        out_shape=[jax.ShapeDtypeStruct((experts, 2 * slots, width), F32)] * 2
        + [
            jax.ShapeDtypeStruct((experts, 8, 2 * slots), F32),
            jax.ShapeDtypeStruct(weights.shape, BF16),
            jax.ShapeDtypeStruct(part, BF16),
            jax.ShapeDtypeStruct(part, BF16),
            jax.ShapeDtypeStruct((ranks,) + late.shape[1:] if halves else (1, 16, LANES), BF16),
        ],
        scratch_shapes=sums
        + [pltpu.VMEM(part, BF16)] * 4
        + [pltpu.SemaphoreType.DMA((2,))] * 3
        + Deal.semaphores(ranks),
        compiler_params=remote_params(6) if halves else params(1),
        cost_estimate=cost(36 * experts * slots * width * hidden, 40e6),
        name="expert_first",
    )(x_slots, d_slots, g_slots, weights, weights, weights, shares, late)


def expert_second_kernel(
    x_ref, d_ref, g_ref, wg_ref, wu_ref, wd_ref, yf_ref, dxf_ref, dgf_ref, sx_ref, sy_ref,
    y_ref, dx_home, dg_home, og_ref, share_ref,
    ag, au, ad, own_y, own_dx, ys, dxs, yp, dxp, dgs, out_x, out_y, in_x, in_y,
    core_send, core_recv, send, recv, local, share_send, share_recv, *, experts, halves,
):
    step = pl.program_id(0)
    block = experts - 1 - step
    sums = (ag, au, ad)
    me, core = lax.axis_index("dp"), lax.axis_index("tensor")
    mine = lax.rem(me, experts)
    other = device(me, 1 - core)
    slots = x_ref.shape[1]
    x, y, x_rank, y_rank = sides(me)

    def rank_at(k):
        total, bit = me - mine, 1
        while bit < experts:
            total += bit * lax.rem(lax.div(mine, bit) + lax.div(k, bit), 2)
            bit *= 2
        return total

    def core_copy(k, part):
        src, dst = ((ys, yp), (dxs, dxp))[part]
        return remote(
            src.at[lax.rem(k, 2)], dst.at[k], core_send.at[part, k], core_recv.at[part, k], other
        )

    def home_copy(k, part):
        src, dst = ((dxp, dx_home), (dgs, dg_home))[part]
        return remote(
            src.at[k], dst.at[mine], send.at[part, k], recv.at[part, k],
            device(rank_at(k), core),
        )

    def own_copy(part):
        src, dst = ((dxp, dx_home), (dgs, dg_home))[part]
        return pltpu.make_async_copy(src.at[0], dst.at[mine], local.at[part])

    def go_home(k, part):
        @pl.when(k == 0)
        def _():
            own_copy(part).start()

        @pl.when(k > 0)
        def _():
            home_copy(k, part).start()

    def share_copies():
        return (
            remote(out_x, in_x, share_send.at[0], share_recv.at[0], device(y_rank, core)),
            remote(out_y, in_y, share_send.at[1], share_recv.at[1], device(x_rank, core)),
        )

    @pl.when(step == 0)
    def _():
        greet(cluster_and_core(experts))
        for total in sums:
            total[...] = jnp.zeros_like(total)
        if halves:
            out_x[...] = sx_ref[:, pl.ds(1 - y, 1)]
            out_y[...] = sy_ref[:, pl.ds(1 - x, 1)]
            for copy in share_copies():
                copy.start()

    def settle(k):
        for part in (1, 0):
            core_copy(k, part).wait_recv()
            own, shared = ((own_y, yp), (own_dx, dxp))[part]
            total = (own[...] + shared[k].astype(F32)).astype(BF16)
            if part:
                dxp[k] = total
                go_home(k, 0)
            else:
                y_ref[...] = total

    @pl.when(step < experts)
    def _():
        out, row_grad, gate_grad = block_of(x_ref, d_ref, g_ref, (wg_ref, wu_ref, wd_ref), sums)
        out += yf_ref[...]
        row_grad += dxf_ref[...]

        @pl.when(step >= 1)
        def _():
            settle(block + 1)

        for part in (1, 0):

            @pl.when(step >= 2)
            def _():
                core_copy(block + 2, part).wait_send()

            own, half = ((own_y, ys), (own_dx, dxs))[part]
            value = (out, row_grad)[part]
            own[...] = value[:slots]
            half[lax.rem(block, 2)] = value[slots:].astype(BF16)
            core_copy(block, part).start()
        dgs[block] = jnp.broadcast_to(row_of(gate_grad), dgs.shape[1:]) + dgf_ref[...]
        go_home(block, 1)

    @pl.when(step == experts)
    def _():
        settle(block + 1)
        put_sums(og_ref, sums)
        if halves:
            cut = out_x.shape[-1]
            for copy in share_copies():
                copy.wait()
            kept_x, kept_y = sx_ref[:, pl.ds(y, 1)], sy_ref[:, pl.ds(x, 1)]
            total_x = kept_x.astype(F32) + in_x[...].astype(F32)
            total_y = kept_y.astype(F32) + in_y[...].astype(F32)
            share_ref[:, :, :cut] = total_x.astype(BF16).reshape(share_ref.shape[0], -1, cut)
            share_ref[:, :, cut:] = total_y.astype(BF16).reshape(share_ref.shape[0], -1, cut)
        for part in (0, 1):
            for k in (0, 1):
                core_copy(k, part).wait_send()
            own_copy(part).wait()
            for k in range(1, experts):
                home_copy(k, part).wait()


def expert_second(x_slots, d_slots, g_slots, weights, first, halves):
    experts, _, slots, width = x_slots.shape
    hidden = weights.shape[-1]
    y_first, dx_first, dg_first, sx, sy = first
    far = pl.BlockSpec(memory_space=pl.ANY)
    group, matrices, sums = expert_specs(
        experts, slots, width, weights, lambda i: jnp.maximum(experts - 1 - i, 0)
    )
    rows = group((2, slots, width))
    long, _, shard, cut = sx.shape
    share = (long, shard, 2 * cut)
    return pl.pallas_call(
        functools.partial(expert_second_kernel, experts=experts, halves=halves),
        grid=(experts + 1,),
        in_specs=[rows, rows, group((2, 8, slots))]
        + matrices
        + [group((2 * slots, width))] * 2
        + [group((8, 2 * slots)), whole(sx.shape), whole(sy.shape)],
        out_specs=[
            pl.BlockSpec((None, slots, width), lambda i: (jnp.minimum(experts - i, experts - 1), 0, 0)),
            far,
            far,
            whole(weights.shape),
            whole(share),
        ],
        out_shape=[
            jax.ShapeDtypeStruct((experts, slots, width), BF16),
            jax.ShapeDtypeStruct((experts, slots, width), BF16),
            jax.ShapeDtypeStruct((experts, 8, 2 * slots), F32),
            jax.ShapeDtypeStruct(weights.shape, BF16),
            jax.ShapeDtypeStruct(share, BF16),
        ],
        scratch_shapes=sums
        + [pltpu.VMEM((slots, width), F32)] * 2
        + [pltpu.VMEM((2, slots, width), BF16)] * 2
        + [pltpu.VMEM((experts, slots, width), BF16)] * 2
        + [pltpu.VMEM((experts, 8, 2 * slots), F32)]
        + [pltpu.VMEM((long, 1, shard, cut), BF16)] * 4
        + [pltpu.SemaphoreType.DMA((2, experts))] * 4
        + [pltpu.SemaphoreType.DMA((2,))] * 3,
        compiler_params=remote_params(3),
        cost_estimate=cost(36 * experts * slots * width * hidden, 40e6),
        name="expert_second",
    )(x_slots, d_slots, g_slots, weights, weights, weights, y_first, dx_first, dg_first, sx, sy)


def to_all(values, groups=None):
    count = lax.axis_size("dp") if groups is None else len(groups[0])
    copies = jnp.broadcast_to(values[None], (count,) + values.shape)
    return lax.all_to_all(copies, "dp", 0, 0, axis_index_groups=groups, tiled=True)


def after(values, *earlier):
    return lax.optimization_barrier((values,) + earlier)[0]


def per_device(
    layer_input, seq_lengths, expert_routes, w_query, w_key, w_value, w_output,
    gain_attn, gain_ffn, router_weight, expert_gate, expert_up, expert_down,
    shared_gate, shared_up, shared_down, out_cotangent,
):
    ranks = lax.axis_size("dp")
    _, own_len, width = layer_input.shape
    span = 2 * own_len
    shard = w_query.shape[0]
    pairs = w_query.shape[1] // LANES
    experts, hidden = expert_gate.shape[1:]
    capacity = 4 * span // experts
    slots = capacity // 2
    groups = [list(range(s, s + experts)) for s in range(0, ranks, experts)]

    small_own = jnp.concatenate(
        [gain_attn[:, None], gain_ffn[:, None], router_weight], axis=1
    )
    small_own = jnp.pad(small_own, ((0, 0), (0, LANES - small_own.shape[1])))
    first_all, shared_all, early_own, late_own = gather_weights(
        (w_query, w_key, w_value, w_output), small_own, (shared_gate, shared_up, shared_down),
        (expert_gate, expert_up, expert_down),
    )
    first_all = first_all.reshape(width, first_all.shape[-1])
    if shard % 16:
        shared_all = shared_all.reshape(1, width, shared_all.shape[-1])

    half = HD // 2
    inverse = np.exp(np.arange(half, dtype=np.float32) * np.float32(-math.log(10000.0) / half))
    angles = np.arange(span, dtype=np.float32)[:, None] * inverse[None, :]
    cos_half, sin_half = np.cos(angles), np.sin(angles)
    cosine = np.concatenate([cos_half] * 4, axis=1)
    sine = np.concatenate([-sin_half, sin_half] * 2, axis=1)

    direct = shard % 16 == 0
    halves = ranks == 16

    def matrices(gathered):
        gathered = gathered.reshape(ranks, 3, shard, gathered.shape[-1])
        if direct:
            return gathered
        return gathered.transpose(1, 0, 2, 3).reshape(1, 3, width, gathered.shape[-1])

    def from_experts(grads):
        if not direct:
            grads = grads.reshape(3, ranks, shard, grads.shape[-1]).transpose(1, 0, 2, 3)
        return lax.all_to_all(grads, "dp", 0, 0, tiled=True)

    def to_outputs(grads):
        grads = grads.reshape(ranks // experts, experts, 3, shard, grads.shape[-1])
        return jnp.sum(grads.astype(F32), axis=0)

    early = lax.all_to_all(early_own, "dp", 0, 0, tiled=True)
    (
        attn_in, qkv_rot, context, hidden_rows, ffn_in, grad_ffn, places, small, gates, shared_y,
        shared_dx, d_slots, x_slots, g_slots, shared_grads,
    ) = attn_forward(
        seq_lengths, layer_input[0], out_cotangent[0], expert_routes.reshape(span, 2).T,
        first_all, shared_all, cosine, sine, experts, slots,
    )

    if halves:
        shares = shared_grads.reshape(4, 2, 2, shard, 3 * hidden)
    else:
        shares = shared_grads[0, :16, :LANES]
        shared_grads = lax.all_to_all(
            shared_grads.reshape(ranks, shard, 3 * hidden), "dp", 0, 0, tiled=True
        )

    y_first, dx_first, dg_first, early_grads, sx, sy, late = expert_first(
        x_slots, d_slots, g_slots, matrices(early), shares, late_own, halves
    )
    if not halves:
        late = jnp.concatenate([late_own] * (ranks // experts), axis=0)
        late = lax.all_to_all(late, "dp", 0, 0, tiled=True)
    early_grads = from_experts(early_grads)
    y_near, dx_home, gate_grads, late_grads, shares = expert_second(
        x_slots, d_slots, g_slots, matrices(late), (y_first, dx_first, dg_first, sx, sy), halves
    )
    late_grads = from_experts(after(late_grads, early_grads))

    grad_input, layer_output, *grads = attn_backward(
        seq_lengths, places, gates, small, dx_home, gate_grads, y_near, shared_y, shares,
        shared_dx, ffn_in, hidden_rows, grad_ffn, layer_input[0], attn_in,
        first_all, qkv_rot, context, cosine, sine, ranks, halves,
    )
    if halves:
        proj, total, small_in = grads
        grad_input, layer_output, *grads = finish(
            grad_input, layer_output, proj, early_grads, late_grads, total, small_in, experts
        )
        attn_grads, expert_grads, shared_grads, small_grads = (
            grads[:4], grads[4:7], grads[7:10], grads[10]
        )
    else:
        attn_grads = grads[0].reshape(pairs, ranks, shard, 4 * LANES).transpose(1, 0, 2, 3)
        attn_grads = lax.all_to_all(attn_grads, "dp", 0, 0, tiled=True)
        attn_grads = jnp.sum(attn_grads.astype(F32), axis=0).reshape(pairs, shard, 4, LANES)
        attn_grads = [
            attn_grads[:, :, k].transpose(1, 0, 2).reshape(shard, pairs * LANES) for k in range(4)
        ]
        small_grads = lax.all_to_all(grads[1].reshape(ranks, shard, LANES), "dp", 0, 0, tiled=True)
        small_grads = jnp.sum(small_grads, axis=0)
        shared_grads = jnp.sum(shared_grads.astype(F32), axis=0)
        shared_grads = [shared_grads[:, k * hidden : (k + 1) * hidden] for k in range(3)]
        expert_grads = jnp.concatenate([to_outputs(early_grads), to_outputs(late_grads)], axis=-1)
        expert_grads = [expert_grads[:, k].transpose(1, 0, 2) for k in range(3)]
    return (
        layer_output[None], grad_input[None],
        attn_grads[0], attn_grads[1], attn_grads[2], attn_grads[3],
        small_grads[:, 0], small_grads[:, 1], small_grads[:, 2 : 2 + experts],
        expert_grads[0], expert_grads[1], expert_grads[2],
        shared_grads[0], shared_grads[1], shared_grads[2],
    )


def solution(mesh):
    tokens = P("dp", "tensor", None)
    matrix = P("dp", "tensor")
    expert = P("dp", None, "tensor")
    in_specs = (
        (tokens, P("dp"), P("dp", None, None))
        + (matrix,) * 4
        + (P("dp"), P("dp"), P("dp", None))
        + (expert,) * 3
        + (matrix,) * 3
        + (tokens,)
    )
    out_specs = (
        (tokens, tokens)
        + (matrix,) * 4
        + (P("dp"), P("dp"), P("dp", None))
        + (expert,) * 3
        + (matrix,) * 3
    )
    return jax.shard_map(
        per_device, mesh=mesh, in_specs=in_specs, out_specs=out_specs, check_vma=False
    )
```
